32 devices in a mesh: req: 32 (over z, y, x, core), kv: 1.
Axes of the slice: x: 2, y: 2, z: 4, core: 2. Of those that a mesh axis runs over, the one named last changes fastest.
Arguments:
- hidden: bfloat16 [256, 2048], P('req'), may hold values from -1.796875 to 1.796875
- queries: bfloat16 [256, 2048], P('req', 'kv'), may hold values from -30 to 30
- fresh_key_value: bfloat16 [256, 4, 256], P('req', 'kv'), may hold values from -6 to 6
- kv_pool: bfloat16 [3328, 32, 4, 256], P('req', None, 'kv'), may hold values from -6 to 6
- page_table: int32 [256, 20], P('req'), may hold values from 0 to 103, as said below
- lengths: int32 [256], P('req'), may hold values from 256 to 639, as said below
- out_weight: bfloat16 [2048, 2048], P('kv'), may hold values from -0.5 to 0.5
- norm_gain: bfloat16 [2048], replicated, may hold values from 0.099609375 to 1.8984375
- router_weight: bfloat16 [16, 2048], replicated, may hold values from -0.03125 to 0.03125
- expert_ids: int32 [256, 6], P('req'), may hold values from 0 to 15, all different within a row; in each aligned block of 8 rows (0 to 7, 8 to 15, ...) at most 4 rows name the same one
- expert_gate_up: bfloat16 [32, 2, 704, 2048], P('req', None, 'kv'), may hold values from -0.125 to 0.125
- expert_down: bfloat16 [32, 704, 2048], P('req', 'kv'), may hold values from -0.15625 to 0.15625
Outputs:
- out_hidden: bfloat16 [256, 2048], P('req')
- updated_pool: bfloat16 [3328, 32, 4, 256], P('req', None, 'kv')
- hidden_norms: float32 [256], P('req')
- max_logit: float32 [256], P('req')
The draws below stay inside these ranges and needn't reach their ends.
Inputs may be any that keep to these rules, and one draw needn't show every extreme that they name: `page_table`: entries index the block of 104 pages of the request's own index of req. Requests of one index of req share their first pages, a common prompt of 8 or more pages; every other page is named by one request alone, and the page holding position lengths[r] is always one of request r's own. `lengths`: every request's length covers its shared prompt. `expert_ids`: within the 8 rows of one index of req, at most 4 rows name one expert, a bound that some block reaches of them.
All inputs are finite; a program needn't handle non-finite values.
Results may differ from the reference program's by a relative error of at most 0.015.
Values may be sent and summed in bfloat16 or wider, within the bound.
No kernel may reach another device: no remote copies, remote signals or barrier semaphores. Data moves between devices by JAX's collectives and lax.ppermute only.
A program may use at most 128 MiB of HBM per device.

```python
import math
import jax
import jax.numpy as jnp
import numpy as np
from jax import lax

D = 2048
QUERY_HEADS = 16
KEY_VALUE_HEADS = 4
HEAD_SIZE = 128
FFE = 1408
TOPK = 6
SHARD_REQUESTS = 8
PAGE_TOKENS = 32
TABLE_PAGES = 20
SHARED_MIN = 8
EXPERTS = 16
CAP = 4
TOTAL_REQUESTS = 256
PAGES_PER_SHARD = 104
TOTAL_PAGES = 3328
N_KV = 1


def layout(key):
    base = jax.random.fold_in(key, 71)
    first_key, second_key, third_key, fourth_key = jax.random.split(base, 4)
    shard_count = TOTAL_REQUESTS // SHARD_REQUESTS
    shared = jax.random.randint(first_key, (shard_count,), SHARED_MIN, TABLE_PAGES)
    perms = jax.vmap(lambda one_key: jax.random.permutation(one_key, PAGES_PER_SHARD))(jax.random.split(second_key, shard_count))
    request_ids = jnp.arange(TOTAL_REQUESTS, dtype=jnp.int32)
    device_ids = request_ids // SHARD_REQUESTS
    local_ids = request_ids % SHARD_REQUESTS
    shared_req = shared[device_ids]
    page_ids = jnp.arange(TABLE_PAGES, dtype=jnp.int32)
    own_index = shared_req[:, None] + local_ids[:, None] * (TABLE_PAGES - shared_req[:, None]) + page_ids[None, :] - shared_req[:, None]
    index = jnp.where(page_ids[None, :] < shared_req[:, None], page_ids[None, :], own_index)
    table = jnp.take_along_axis(perms[device_ids], index, axis=1)
    span = (TABLE_PAGES - shared_req) * PAGE_TOKENS
    extra = jax.random.randint(third_key, (TOTAL_REQUESTS,), 0, 1 << 20) % span
    lengths = shared_req * PAGE_TOKENS + extra
    longest = jax.random.randint(fourth_key, (), 0, TOTAL_REQUESTS)
    lengths = jnp.where(request_ids == longest, TABLE_PAGES * PAGE_TOKENS - 1, lengths)
    return (table.astype(jnp.int32), lengths.astype(jnp.int32))


def draw_page_table(key, part):
    return layout(key)[0]


def draw_lengths(key, part):
    return layout(key)[1]


def draw_kv_pool(key, part):
    own_key = jax.random.fold_in(key, 91)
    array_shape = (TOTAL_PAGES, PAGE_TOKENS, KEY_VALUE_HEADS, 2 * HEAD_SIZE)
    values = jnp.clip(jax.random.normal(own_key, array_shape, jnp.float32), -6.0, 6.0)
    return values.astype(jnp.bfloat16)


def draw_queries(key, part):
    own_key = jax.random.fold_in(key, 97)
    array_shape = (TOTAL_REQUESTS, QUERY_HEADS * HEAD_SIZE)
    values = jnp.clip(jax.random.normal(own_key, array_shape, jnp.float32), -6.0, 6.0)
    return values.astype(jnp.bfloat16)


def level_of(key, dims, pieces, smallest, top_value):
    loudness, own = 1.0, jax.random.fold_in(key, 6)
    for dim, parts in pieces:
        steps = jnp.exp(jax.random.uniform(jax.random.fold_in(own, dim), (parts,), jnp.float32, smallest / len(pieces), top_value / len(pieces)))
        loudness = loudness * jnp.repeat(steps, dims[dim] // parts).reshape([-1 if axis == dim else 1 for axis in range(len(dims))])
    return loudness


def assign_block(rng, own, number, rows, count, top, limit, slope):
    sequence = jax.random.permutation(rng, count)
    heavy_load, usual = portions_of(count, rows * top, limit, slope, True), portions_of(count, rows * top, limit, slope, False)
    places = jnp.arange(count)

    def named(sizes, rotation):
        used = int((sizes > 0).sum())
        fixed = max(1, used // 4)
        passed = fixed + (places - fixed + rotation * (used - fixed)) % max(1, count - fixed)
        return jnp.zeros((count,), jnp.int32).at[sequence[jnp.where(places < fixed, places, passed)]].set(jnp.asarray(sizes, jnp.int32))

    sizes = jnp.where(number % 4 == 0, named(heavy_load, number // 4), named(usual, number - number // 4 - 1))
    mixed = jax.random.permutation(jax.random.fold_in(own, 3), count)
    donor, sink = mixed[0:count // 2 * 2:2], mixed[1:count // 2 * 2:2]
    slack = jnp.minimum(sizes[donor] - 1, limit - sizes[sink]) // 2
    slack = jnp.where((donor == sequence[0]) | (sink == sequence[0]) | (sizes[sink] == 0), 0, jnp.maximum(slack, 0))
    passed = jax.random.randint(jax.random.fold_in(own, 4), (count // 2,), 0, 1 << 20) % (slack + 1)
    sizes = sizes.at[donor].add(-passed).at[sink].add(passed)
    members = jnp.searchsorted(jnp.cumsum(sizes), jnp.arange(rows * top), side="right").astype(jnp.int32)
    listing = members.reshape(top, rows).T
    listing = listing[jax.random.permutation(jax.random.fold_in(own, 1), rows)]
    rotation = jax.random.randint(jax.random.fold_in(own, 2), (rows, 1), 0, top)
    return jnp.take_along_axis(listing, (jnp.arange(top)[None, :] + rotation) % top, axis=1)


def portions_of(amount, total, limit, lean, full):
    portions = [(1 << 20) // math.isqrt(grade ** lean) + 1 for grade in range(1, amount + 1)]
    largest = limit if full else min(limit, max(-(-total // amount), total * portions[0] // sum(portions)))
    least = 1 if total - largest >= amount - 1 else 0
    given, spare = [largest] + [least] * (amount - 1), total - largest - least * (amount - 1)
    while spare > 0:
        free = [i for i in range(1, amount) if given[i] < largest] or [i for i in range(1, amount) if given[i] < limit]
        mass, left = sum([portions[i] for i in free]), spare
        for i in free:
            more = min(limit - given[i], max(1, left * portions[i] // mass), spare)
            given[i] = given[i] + more
            spare = spare - more
    return np.array(given)


def normal_values(key, dims, width, reach, pieces=(), kind=jnp.bfloat16):
    entries = width * jax.random.normal(key, dims, jnp.float32)
    if pieces:
        entries = entries * level_of(key, dims, pieces, -0.22, 0.18)
    return jnp.clip(entries, -reach, reach).astype(kind)


def setup_inputs(seed: int = 0) -> dict:
    keys = jax.random.split(jax.random.key(seed), 13)
    hidden = normal_values(keys[0], (TOTAL_REQUESTS, D), 0.3, 1.796875, ((0, 32),))
    queries = draw_queries(jax.random.fold_in(keys[12], 71), 0)
    fresh_key_value = normal_values(keys[2], (TOTAL_REQUESTS, KEY_VALUE_HEADS, 2 * HEAD_SIZE), 1.0, 6.0, ((0, 32),))
    kv_pool = draw_kv_pool(jax.random.fold_in(keys[12], 71), 0)
    page_table = draw_page_table(jax.random.fold_in(keys[12], 71), 0)
    lengths = draw_lengths(jax.random.fold_in(keys[12], 71), 0)
    out_weight = normal_values(keys[6], (QUERY_HEADS * HEAD_SIZE, D), HEAD_SIZE ** -0.5, 0.5)
    norm_gain = jnp.clip(1.0 + 0.18 * jax.random.normal(keys[7], (D,), jnp.float32), 0.099609375, 1.8984375).astype(jnp.bfloat16)
    router_weight = normal_values(keys[8], (EXPERTS, D), (16 * D) ** -0.5, 0.03125)
    expert_ids_keys = jax.random.split(jax.random.fold_in(keys[9], 1), TOTAL_REQUESTS // SHARD_REQUESTS)
    expert_ids_turns = jax.random.permutation(jax.random.fold_in(keys[9], 3), TOTAL_REQUESTS // SHARD_REQUESTS)
    expert_ids = jax.vmap(lambda own, number: assign_block(jax.random.fold_in(keys[9], 2), own, number, SHARD_REQUESTS, EXPERTS, TOPK, CAP, 2))(expert_ids_keys, expert_ids_turns).reshape((TOTAL_REQUESTS, TOPK))
    expert_gate_up = normal_values(keys[10], (2 * EXPERTS, 2, FFE // 2, D), D ** -0.5, 0.125, ((0, 32),))
    expert_down = normal_values(keys[11], (2 * EXPERTS, FFE // 2, D), FFE ** -0.5, 0.15625, ((0, 32),))
    return dict(hidden=hidden, queries=queries, fresh_key_value=fresh_key_value, kv_pool=kv_pool, page_table=page_table, lengths=lengths, out_weight=out_weight, norm_gain=norm_gain, router_weight=router_weight, expert_ids=expert_ids, expert_gate_up=expert_gate_up, expert_down=expert_down)


def reference(hidden, queries, fresh_key_value, kv_pool, page_table, lengths, out_weight, norm_gain, router_weight, expert_ids, expert_gate_up, expert_down):
    shard_count = TOTAL_REQUESTS // SHARD_REQUESTS
    request_ids = jnp.arange(TOTAL_REQUESTS, dtype=jnp.int32)
    slot_page = jnp.take_along_axis(page_table, (lengths // PAGE_TOKENS)[:, None].astype(jnp.int32), axis=1)[:, 0]
    global_page = request_ids // SHARD_REQUESTS * PAGES_PER_SHARD + slot_page
    refreshed_pool = kv_pool.at[global_page, lengths % PAGE_TOKENS].set(fresh_key_value)
    query_groups = QUERY_HEADS // KEY_VALUE_HEADS
    grouped_queries = queries.reshape(shard_count, SHARD_REQUESTS, KEY_VALUE_HEADS, query_groups, HEAD_SIZE)
    shard_page_pools = refreshed_pool.reshape(shard_count, PAGES_PER_SHARD, PAGE_TOKENS, KEY_VALUE_HEADS, 2 * HEAD_SIZE)
    tables = page_table.reshape(shard_count, SHARD_REQUESTS, TABLE_PAGES)
    device_lengths = lengths.reshape(shard_count, SHARD_REQUESTS)

    def attend_device(device_items):
        query_dev, shard_pool, shard_page_table, length_dev = device_items
        collected_pages = shard_pool[shard_page_table].reshape(SHARD_REQUESTS, TABLE_PAGES * PAGE_TOKENS, KEY_VALUE_HEADS, 2 * HEAD_SIZE)
        key_rows = collected_pages[..., :HEAD_SIZE].astype(jnp.float32)
        value_rows = collected_pages[..., HEAD_SIZE:].astype(jnp.float32)
        scores = jnp.einsum('rhgd,rphd->rhgp', query_dev.astype(jnp.float32), key_rows, precision=lax.Precision.HIGHEST) / math.sqrt(HEAD_SIZE)
        positions = jnp.arange(TABLE_PAGES * PAGE_TOKENS, dtype=jnp.int32)
        visible = positions[None, :] <= length_dev[:, None]
        scores = jnp.where(visible[:, None, None, :], scores, -1e+30)
        top_score = lax.optimization_barrier(jnp.max(scores, axis=-1))
        exponent = jnp.exp(scores - top_score[..., None])
        denominator = lax.optimization_barrier(jnp.sum(exponent, axis=-1))
        probs = lax.optimization_barrier(exponent.astype(jnp.bfloat16)).astype(jnp.float32)
        summed = jnp.einsum('rhgp,rphd->rhgd', probs, value_rows, precision=lax.Precision.HIGHEST)
        attended_dev = (summed / denominator[..., None]).astype(jnp.bfloat16)
        return attended_dev.reshape(SHARD_REQUESTS, QUERY_HEADS * HEAD_SIZE)
    attended = lax.map(attend_device, (grouped_queries, shard_page_pools, tables, device_lengths)).reshape(TOTAL_REQUESTS, QUERY_HEADS * HEAD_SIZE)
    projected = jnp.dot(attended, out_weight, preferred_element_type=jnp.float32)
    mixed_state = (hidden.astype(jnp.float32) + projected).astype(jnp.bfloat16)
    mixed_float = mixed_state.astype(jnp.float32)
    hidden_norms = jnp.sqrt(lax.optimization_barrier(jnp.mean(mixed_float * mixed_float, axis=-1)) + 1e-06)
    normed = (mixed_float / hidden_norms[:, None] * norm_gain.astype(jnp.float32)).astype(jnp.bfloat16)
    logits = jnp.dot(normed, router_weight.T, preferred_element_type=jnp.float32)
    max_logit = lax.optimization_barrier(jnp.max(logits, axis=-1))
    onehot = expert_ids[:, :, None] == jnp.arange(EXPERTS, dtype=jnp.int32)[None, None, :]
    picked = lax.optimization_barrier(jnp.sum(jnp.where(onehot, logits[:, None, :], 0.0), axis=-1))
    exponent = jnp.exp(picked)
    gate_weights = exponent / lax.optimization_barrier(jnp.sum(exponent, axis=-1, keepdims=True))
    flat_hot = onehot.reshape(shard_count, SHARD_REQUESTS * TOPK, EXPERTS)
    counts = jnp.cumsum(flat_hot.astype(jnp.int32), axis=1)
    slot_rank = (lax.optimization_barrier(jnp.sum(jnp.where(flat_hot, counts, 0), axis=-1)) - 1).reshape(TOTAL_REQUESTS, TOPK)
    source = request_ids // SHARD_REQUESTS
    buffer_row = source[:, None] * CAP + slot_rank
    buffers = jnp.zeros((EXPERTS, shard_count * CAP, D), jnp.bfloat16)
    buffers = buffers.at[expert_ids, buffer_row].set(jnp.broadcast_to(normed[:, None, :], (TOTAL_REQUESTS, TOPK, D)))
    block_units = FFE // (2 * N_KV)
    gate_blocks = expert_gate_up.reshape(EXPERTS, 2, 2, N_KV, block_units, D)
    gate_blocks = jnp.transpose(gate_blocks, (0, 1, 3, 2, 4, 5)).reshape(EXPERTS, 2 * N_KV, 2, block_units, D)
    down_blocks = expert_down.reshape(EXPERTS, 2 * N_KV, block_units, D)

    def expert(expert_items):
        rows, gate_up, down = expert_items

        def one_block(block_gate, block_down):
            gate_proj = jnp.dot(rows, block_gate[0].T, preferred_element_type=jnp.float32)
            up_proj = jnp.dot(rows, block_gate[1].T, preferred_element_type=jnp.float32)
            activated = (jax.nn.silu(gate_proj) * up_proj).astype(jnp.bfloat16)
            return jnp.dot(activated, block_down, preferred_element_type=jnp.float32).astype(jnp.bfloat16)
        block_outs = jax.vmap(one_block)(gate_up, down)
        return lax.optimization_barrier(jnp.sum(block_outs.astype(jnp.float32), axis=0))
    results = lax.map(expert, (buffers, gate_blocks, down_blocks))
    expert_out = results[expert_ids, buffer_row]
    routed = lax.optimization_barrier(jnp.sum(gate_weights[..., None] * expert_out, axis=1))
    out_hidden = (mixed_float + routed).astype(jnp.bfloat16)
    return (out_hidden, refreshed_pool, hidden_norms, max_logit)
```

```python
import math

import jax
import jax.numpy as jnp
from jax import lax
from jax.sharding import PartitionSpec as P


def body(
    hidden,
    queries,
    fresh_key_value,
    kv_pool,
    page_table,
    lengths,
    out_weight,
    norm_gain,
    router_weight,
    expert_ids,
    expert_gate_up,
    expert_down,
):
    req_dev = hidden.shape[0]
    model_width = hidden.shape[1]
    req_count = lax.axis_size("req")
    heads_kv = fresh_key_value.shape[1]
    head_dim = fresh_key_value.shape[2] // 2
    page_len = kv_pool.shape[1]
    max_pages = page_table.shape[1]
    slot_page = jnp.take_along_axis(page_table, (lengths // page_len)[:, None], axis=1)[:, 0]
    refreshed_pool = kv_pool.at[slot_page, lengths % page_len].set(fresh_key_value)
    collected_pages = refreshed_pool[page_table].reshape(
        req_dev, max_pages * page_len, heads_kv, 2 * head_dim
    )
    query_heads = queries.reshape(req_dev, heads_kv, -1, head_dim)
    scores = jnp.einsum(
        "rhgd,rphd->rhgp",
        query_heads,
        collected_pages[..., :head_dim],
        preferred_element_type=jnp.float32,
    ) / math.sqrt(head_dim)
    positions = jnp.arange(max_pages * page_len, dtype=jnp.int32)
    visible = positions[None, :] <= lengths[:, None]
    scores = jnp.where(visible[:, None, None, :], scores, -1e30)
    top_score = jnp.max(scores, axis=-1)
    exponent = jnp.exp(scores - top_score[..., None])
    denominator = jnp.sum(exponent, axis=-1)
    probs = exponent.astype(jnp.bfloat16)
    summed = jnp.einsum(
        "rhgp,rphd->rhgd",
        probs,
        collected_pages[..., head_dim:],
        preferred_element_type=jnp.float32,
    )
    attended = (summed / denominator[..., None]).astype(jnp.bfloat16).reshape(req_dev, -1)
    partial_proj = jnp.dot(attended, out_weight, preferred_element_type=jnp.float32)
    projected = lax.psum(partial_proj.astype(jnp.bfloat16), "kv").astype(jnp.float32)
    mixed_state = (hidden.astype(jnp.float32) + projected).astype(jnp.bfloat16)
    mixed_float = mixed_state.astype(jnp.float32)
    hidden_norms = jnp.sqrt(jnp.mean(mixed_float * mixed_float, axis=-1) + 1e-06)
    normed = (mixed_float / hidden_norms[:, None] * norm_gain.astype(jnp.float32)).astype(
        jnp.bfloat16
    )
    logits = jnp.dot(normed, router_weight.T, preferred_element_type=jnp.float32)
    max_logit = jnp.max(logits, axis=-1)
    experts = router_weight.shape[0]
    copies = req_count // experts
    chosen_count = expert_ids.shape[1]
    onehot = expert_ids[:, :, None] == jnp.arange(experts, dtype=jnp.int32)[None, None, :]
    picked = jnp.sum(jnp.where(onehot, logits[:, None, :], 0.0), axis=-1)
    exponent_gate = jnp.exp(picked)
    gate_weights = exponent_gate / jnp.sum(exponent_gate, axis=-1, keepdims=True)
    combine = jnp.sum(jnp.where(onehot, gate_weights[:, :, None], 0.0), axis=1)
    combine_hi = combine.astype(jnp.bfloat16)
    combine_lo = (combine - combine_hi.astype(jnp.float32)).astype(jnp.bfloat16)
    pad = jnp.zeros((req_dev, -(2 * experts) % 128), jnp.bfloat16)
    payload = jnp.concatenate([normed, combine_hi, combine_lo, pad], axis=1)
    gathered = lax.all_gather(payload, "req", axis=0, tiled=True)
    rows = gathered[:, :model_width]
    expert = lax.axis_index("req") // copies
    weights = gathered[:, model_width:].astype(jnp.float32)
    column = jnp.arange(weights.shape[1], dtype=jnp.int32)
    chosen = ((column == expert) | (column == expert + experts)).astype(jnp.float32)
    row_weight = jnp.sum(weights * chosen[None, :], axis=1)
    gate_up = expert_gate_up[0]
    down_local = expert_down[0]
    gate_proj = jnp.einsum("rd,fd->rf", rows, gate_up[0], preferred_element_type=jnp.float32)
    up_proj = jnp.einsum("rd,fd->rf", rows, gate_up[1], preferred_element_type=jnp.float32)
    activated = (jax.nn.silu(gate_proj) * up_proj).astype(jnp.bfloat16)
    terms = jnp.dot(activated, down_local, preferred_element_type=jnp.float32)
    weighted = (terms * row_weight[:, None]).astype(jnp.bfloat16)
    partial_routed = lax.psum_scatter(weighted, "req", scatter_dimension=0, tiled=True)
    routed = lax.psum(partial_routed, "kv").astype(jnp.float32)
    out_hidden = (mixed_float + routed).astype(jnp.bfloat16)
    return (out_hidden, refreshed_pool, hidden_norms, max_logit)


def solution(mesh):
    in_specs = (
        P("req", None),
        P("req", "kv"),
        P("req", "kv", None),
        P("req", None, "kv", None),
        P("req", None),
        P("req"),
        P("kv", None),
        P(),
        P(),
        P("req", None),
        P("req", None, "kv", None),
        P("req", "kv", None),
    )
    out_specs = (P("req", None), P("req", None, "kv", None), P("req"), P("req"))
    return jax.shard_map(body, mesh=mesh, in_specs=in_specs, out_specs=out_specs, check_vma=False)
```

```python
import math

import jax
import jax.numpy as jnp
from jax import lax
from jax.sharding import PartitionSpec as P


def body(
    hidden,
    queries,
    fresh_key_value,
    kv_pool,
    page_table,
    lengths,
    out_weight,
    norm_gain,
    router_weight,
    expert_ids,
    expert_gate_up,
    expert_down,
):
    req_dev = hidden.shape[0]
    model_width = hidden.shape[1]
    req_count = lax.axis_size("req")
    heads_kv = fresh_key_value.shape[1]
    head_dim = fresh_key_value.shape[2] // 2
    page_len = kv_pool.shape[1]
    max_pages = page_table.shape[1]
    slot_page = jnp.take_along_axis(page_table, (lengths // page_len)[:, None], axis=1)[:, 0]
    refreshed_pool = kv_pool.at[slot_page, lengths % page_len].set(fresh_key_value)
    collected_pages = refreshed_pool[page_table].reshape(
        req_dev, max_pages * page_len, heads_kv, 2 * head_dim
    )
    query_heads = queries.reshape(req_dev, heads_kv, -1, head_dim)
    scores = jnp.einsum(
        "rhgd,rphd->rhgp",
        query_heads,
        collected_pages[..., :head_dim],
        preferred_element_type=jnp.float32,
    ) / math.sqrt(head_dim)
    positions = jnp.arange(max_pages * page_len, dtype=jnp.int32)
    visible = positions[None, :] <= lengths[:, None]
    scores = jnp.where(visible[:, None, None, :], scores, -1e30)
    top_score = jnp.max(scores, axis=-1)
    exponent = jnp.exp(scores - top_score[..., None])
    denominator = jnp.sum(exponent, axis=-1)
    probs = exponent.astype(jnp.bfloat16)
    summed = jnp.einsum(
        "rhgp,rphd->rhgd",
        probs,
        collected_pages[..., head_dim:],
        preferred_element_type=jnp.float32,
    )
    attended = (summed / denominator[..., None]).astype(jnp.bfloat16).reshape(req_dev, -1)
    partial_proj = jnp.dot(attended, out_weight, preferred_element_type=jnp.float32)
    projected = lax.psum(partial_proj.astype(jnp.bfloat16), "kv").astype(jnp.float32)
    mixed_state = (hidden.astype(jnp.float32) + projected).astype(jnp.bfloat16)
    mixed_float = mixed_state.astype(jnp.float32)
    hidden_norms = jnp.sqrt(jnp.mean(mixed_float * mixed_float, axis=-1) + 1e-06)
    normed = (mixed_float / hidden_norms[:, None] * norm_gain.astype(jnp.float32)).astype(
        jnp.bfloat16
    )
    logits = jnp.dot(normed, router_weight.T, preferred_element_type=jnp.float32)
    max_logit = jnp.max(logits, axis=-1)
    experts = router_weight.shape[0]
    copies = req_count // experts
    chosen_count = expert_ids.shape[1]
    onehot = expert_ids[:, :, None] == jnp.arange(experts, dtype=jnp.int32)[None, None, :]
    picked = jnp.sum(jnp.where(onehot, logits[:, None, :], 0.0), axis=-1)
    exponent_gate = jnp.exp(picked)
    gate_weights = exponent_gate / jnp.sum(exponent_gate, axis=-1, keepdims=True)
    flat_hot = onehot.reshape(req_dev * chosen_count, experts)
    counts = jnp.cumsum(flat_hot.astype(jnp.int32), axis=0)
    slot_rank = (jnp.sum(jnp.where(flat_hot, counts, 0), axis=-1) - 1).reshape(
        req_dev, chosen_count
    )
    capacity = 2 * max(1, (req_dev * chosen_count + 2 * experts - 1) // (2 * experts))
    slot_index = expert_ids * capacity + slot_rank
    slot_count = experts * capacity
    assigned = slot_index[None, :, :] == jnp.arange(slot_count, dtype=jnp.int32)[:, None, None]
    dispatch_mat = jnp.sum(assigned.astype(jnp.float32), axis=-1).astype(jnp.bfloat16)
    outgoing = (
        jnp.dot(dispatch_mat, normed, preferred_element_type=jnp.float32)
        .astype(jnp.bfloat16)
        .reshape(experts, capacity, model_width)
    )
    combine_mat = jnp.sum(jnp.where(assigned, gate_weights[None, :, :], 0.0), axis=-1).T
    same_part = [list(range(part, req_count, copies)) for part in range(copies)]
    swap = [(index, index ^ 1) for index in range(req_count)]
    gate_up = expert_gate_up[0]
    down_local = expert_down[0]
    arrived = lax.all_to_all(
        outgoing, "req", split_axis=0, concat_axis=0, tiled=True, axis_index_groups=same_part
    )
    partner = lax.ppermute(arrived, "req", swap)
    rows = jnp.concatenate([arrived, partner], axis=0).reshape(-1, model_width)
    gate_proj = jnp.einsum("rd,fd->rf", rows, gate_up[0], preferred_element_type=jnp.float32)
    up_proj = jnp.einsum("rd,fd->rf", rows, gate_up[1], preferred_element_type=jnp.float32)
    activated = (jax.nn.silu(gate_proj) * up_proj).astype(jnp.bfloat16)
    terms = jnp.dot(activated, down_local, preferred_element_type=jnp.float32).astype(jnp.bfloat16)
    own_terms, partner_terms = jnp.split(terms, 2, axis=0)
    swapped = lax.ppermute(partner_terms, "req", swap)
    expert_out = (own_terms.astype(jnp.float32) + swapped.astype(jnp.float32)).astype(jnp.bfloat16)
    returned = lax.all_to_all(
        expert_out.reshape(arrived.shape),
        "req",
        split_axis=0,
        concat_axis=0,
        tiled=True,
        axis_index_groups=same_part,
    )
    partial_routed = jnp.dot(
        combine_mat,
        returned.reshape(-1, model_width).astype(jnp.float32),
        precision=lax.Precision.HIGHEST,
    )
    routed = lax.psum(partial_routed.astype(jnp.bfloat16), "kv").astype(jnp.float32)
    out_hidden = (mixed_float + routed).astype(jnp.bfloat16)
    return (out_hidden, refreshed_pool, hidden_norms, max_logit)


def solution(mesh):
    in_specs = (
        P("req", None),
        P("req", "kv"),
        P("req", "kv", None),
        P("req", None, "kv", None),
        P("req", None),
        P("req"),
        P("kv", None),
        P(),
        P(),
        P("req", None),
        P("req", None, "kv", None),
        P("req", "kv", None),
    )
    out_specs = (P("req", None), P("req", None, "kv", None), P("req"), P("req"))
    return jax.shard_map(body, mesh=mesh, in_specs=in_specs, out_specs=out_specs, check_vma=False)
```

```python
import math

import jax
import jax.numpy as jnp
from jax import lax
from jax.sharding import PartitionSpec as P


def body(
    hidden,
    queries,
    fresh_key_value,
    kv_pool,
    page_table,
    lengths,
    out_weight,
    norm_gain,
    router_weight,
    expert_ids,
    expert_gate_up,
    expert_down,
):
    req_dev = hidden.shape[0]
    model_width = hidden.shape[1]
    req_count = lax.axis_size("req")
    heads_kv = fresh_key_value.shape[1]
    head_dim = fresh_key_value.shape[2] // 2
    page_len = kv_pool.shape[1]
    max_pages = page_table.shape[1]
    slot_page = jnp.take_along_axis(page_table, (lengths // page_len)[:, None], axis=1)[:, 0]
    refreshed_pool = kv_pool.at[slot_page, lengths % page_len].set(fresh_key_value)
    collected_pages = refreshed_pool[page_table].reshape(
        req_dev, max_pages * page_len, heads_kv, 2 * head_dim
    )
    query_heads = queries.reshape(req_dev, heads_kv, -1, head_dim)
    scores = jnp.einsum(
        "rhgd,rphd->rhgp",
        query_heads,
        collected_pages[..., :head_dim],
        preferred_element_type=jnp.float32,
    ) / math.sqrt(head_dim)
    positions = jnp.arange(max_pages * page_len, dtype=jnp.int32)
    visible = positions[None, :] <= lengths[:, None]
    scores = jnp.where(visible[:, None, None, :], scores, -1e30)
    top_score = jnp.max(scores, axis=-1)
    exponent = jnp.exp(scores - top_score[..., None])
    denominator = jnp.sum(exponent, axis=-1)
    probs = exponent.astype(jnp.bfloat16)
    summed = jnp.einsum(
        "rhgp,rphd->rhgd",
        probs,
        collected_pages[..., head_dim:],
        preferred_element_type=jnp.float32,
    )
    attended = (summed / denominator[..., None]).astype(jnp.bfloat16).reshape(req_dev, -1)
    partial_proj = jnp.dot(attended, out_weight, preferred_element_type=jnp.float32)
    projected = lax.psum(partial_proj.astype(jnp.bfloat16), "kv").astype(jnp.float32)
    mixed_state = (hidden.astype(jnp.float32) + projected).astype(jnp.bfloat16)
    mixed_float = mixed_state.astype(jnp.float32)
    hidden_norms = jnp.sqrt(jnp.mean(mixed_float * mixed_float, axis=-1) + 1e-06)
    normed = (mixed_float / hidden_norms[:, None] * norm_gain.astype(jnp.float32)).astype(
        jnp.bfloat16
    )
    logits = jnp.dot(normed, router_weight.T, preferred_element_type=jnp.float32)
    max_logit = jnp.max(logits, axis=-1)
    experts = router_weight.shape[0]
    copies = req_count // experts
    chosen_count = expert_ids.shape[1]
    onehot = expert_ids[:, :, None] == jnp.arange(experts, dtype=jnp.int32)[None, None, :]
    picked = jnp.sum(jnp.where(onehot, logits[:, None, :], 0.0), axis=-1)
    exponent_gate = jnp.exp(picked)
    gate_weights = exponent_gate / jnp.sum(exponent_gate, axis=-1, keepdims=True)
    flat_hot = onehot.reshape(req_dev * chosen_count, experts)
    counts = jnp.cumsum(flat_hot.astype(jnp.int32), axis=0)
    slot_rank = (jnp.sum(jnp.where(flat_hot, counts, 0), axis=-1) - 1).reshape(
        req_dev, chosen_count
    )
    capacity = 2 * max(1, (req_dev * chosen_count + 2 * experts - 1) // (2 * experts))
    chip = lax.axis_index("req") // copies
    slot_index = (expert_ids ^ chip) * capacity + slot_rank
    slot_count = experts * capacity
    assigned = slot_index[None, :, :] == jnp.arange(slot_count, dtype=jnp.int32)[:, None, None]
    dispatch_mat = jnp.sum(assigned.astype(jnp.float32), axis=-1).astype(jnp.bfloat16)
    outgoing = (
        jnp.dot(dispatch_mat, normed, preferred_element_type=jnp.float32)
        .astype(jnp.bfloat16)
        .reshape(experts, capacity, model_width)
    )
    combine_mat = jnp.sum(jnp.where(assigned, gate_weights[None, :, :], 0.0), axis=-1).T
    routes = [
        [(index, index ^ (copies * step)) for index in range(req_count)] for step in range(experts)
    ]
    swap = [(index, index ^ 1) for index in range(req_count)]
    gate_up = expert_gate_up[0]
    down_local = expert_down[0]
    arrived = jnp.stack(
        [outgoing[0]]
        + [lax.ppermute(outgoing[step], "req", routes[step]) for step in range(1, experts)]
    )
    partner = lax.ppermute(arrived, "req", swap)
    rows = jnp.concatenate([arrived, partner], axis=0).reshape(-1, model_width)
    gate_proj = jnp.einsum("rd,fd->rf", rows, gate_up[0], preferred_element_type=jnp.float32)
    up_proj = jnp.einsum("rd,fd->rf", rows, gate_up[1], preferred_element_type=jnp.float32)
    activated = (jax.nn.silu(gate_proj) * up_proj).astype(jnp.bfloat16)
    terms = jnp.dot(activated, down_local, preferred_element_type=jnp.float32).astype(jnp.bfloat16)
    own_terms, partner_terms = jnp.split(terms, 2, axis=0)
    swapped = lax.ppermute(partner_terms, "req", swap)
    expert_out = (own_terms.astype(jnp.float32) + swapped.astype(jnp.float32)).astype(jnp.bfloat16)
    leaving = expert_out.reshape(arrived.shape)
    returned = jnp.stack(
        [leaving[0]]
        + [lax.ppermute(leaving[step], "req", routes[step]) for step in range(1, experts)]
    )
    partial_routed = jnp.dot(
        combine_mat,
        returned.reshape(-1, model_width).astype(jnp.float32),
        precision=lax.Precision.HIGHEST,
    )
    routed = lax.psum(partial_routed.astype(jnp.bfloat16), "kv").astype(jnp.float32)
    out_hidden = (mixed_float + routed).astype(jnp.bfloat16)
    return (out_hidden, refreshed_pool, hidden_norms, max_logit)


def solution(mesh):
    in_specs = (
        P("req", None),
        P("req", "kv"),
        P("req", "kv", None),
        P("req", None, "kv", None),
        P("req", None),
        P("req"),
        P("kv", None),
        P(),
        P(),
        P("req", None),
        P("req", None, "kv", None),
        P("req", "kv", None),
    )
    out_specs = (P("req", None), P("req", None, "kv", None), P("req"), P("req"))
    return jax.shard_map(body, mesh=mesh, in_specs=in_specs, out_specs=out_specs, check_vma=False)
```

```python
import functools
import math

import jax
import jax.numpy as jnp
from jax import lax
from jax.experimental import pallas as pl
from jax.experimental.pallas import tpu as pltpu
from jax.sharding import PartitionSpec as P

BF16 = jnp.bfloat16
F32 = jnp.float32
NT = (((1,), (1,)), ((), ()))
NN = (((1,), (0,)), ((), ()))
SLAB = 16
MIB = 1 << 20


def dot(a, b, dims=NN, precision=None):
    return lax.dot_general(a, b, dims, precision=precision, preferred_element_type=F32)


def iota(shape, dim):
    return lax.broadcasted_iota(jnp.int32, shape, dim)


def pool_loads(pool, keys, values, sems):
    half = keys.shape[-1]
    return [
        pltpu.make_async_copy(pool.at[:, :, :, pl.ds(i * half, half)], kept, sems.at[i])
        for i, kept in enumerate((keys, values))
    ]


def attend(table, lengths, q_ref, fresh, weight, pool, new_pool, keys, values, kept_weight, qs, att, sems):
    requests, max_pages = table.shape
    pages, page_len, heads_kv, head_dim = keys.shape
    heads = q_ref.shape[1] // head_dim
    group = heads // heads_kv
    page_rows = page_len * heads_kv
    loads = pool_loads(pool, keys, values, sems)
    weight_load = pltpu.make_async_copy(weight, kept_weight, sems.at[2])
    for copy in loads:
        copy.start()
    weight_load.start()
    for h in range(heads):
        qs[pl.ds(h * requests, requests), :] = q_ref[:, pl.ds(h * head_dim, head_dim)].astype(F32)
    for copy in loads:
        copy.wait()
    for r in range(requests):
        page = table[r, lengths[r] // page_len]
        slot = lengths[r] % page_len
        row = fresh[r]
        keys[page, slot] = row[:, :head_dim]
        values[page, slot] = row[:, head_dim:]
    stores = [
        pltpu.make_async_copy(kept, new_pool.at[:, :, :, pl.ds(i * head_dim, head_dim)], sems.at[3 + i])
        for i, kept in enumerate((keys, values))
    ]
    for copy in stores:
        copy.start()
    key_pages = keys.reshape(pages, page_rows, head_dim)
    value_pages = values.reshape(pages, page_rows, head_dim)
    columns = max_pages * page_rows
    lane = iota((heads, columns), 1)
    own_head = lane % heads_kv == iota((heads, columns), 0) // group
    position = lane // heads_kv
    for r in range(requests):
        chosen = [table[r, j] for j in range(max_pages)]
        query = qs[pl.ds(r, heads, stride=requests), :].astype(BF16)
        gathered = jnp.concatenate([key_pages[page] for page in chosen], axis=0)
        scores = dot(query, gathered, NT) * (1.0 / math.sqrt(head_dim))
        scores = jnp.where(own_head & (position <= lengths[r]), scores, -1e30)
        top = jnp.max(scores, axis=1, keepdims=True)
        exponent = jnp.exp(scores - top)
        denominator = jnp.sum(exponent, axis=1, keepdims=True)
        gathered = jnp.concatenate([value_pages[page] for page in chosen], axis=0)
        summed = dot(exponent.astype(BF16), gathered)
        att[pl.ds(r, heads, stride=requests), :] = summed / denominator
    attended = jnp.concatenate(
        [att[pl.ds(h * requests, requests), :] for h in range(heads)], axis=1
    ).astype(BF16)
    weight_load.wait()
    projected = dot(attended, kept_weight[...])
    for copy in stores:
        copy.wait()
    return projected


def route(projected, hidden, gain, router, ids, mixed_ref, norms_ref, top_ref, slabs_ref, comb_ref, capacity):
    requests, width = hidden.shape
    experts = router.shape[0]
    parts = SLAB // capacity
    piece = width // parts
    slab_rows = experts * SLAB
    mixed = (hidden[...].astype(F32) + projected).astype(BF16)
    mixed_ref[...] = mixed
    mixed = mixed.astype(F32)
    norms = jnp.sqrt(jnp.mean(mixed * mixed, axis=1, keepdims=True) + 1e-06)
    norms_ref[...] = norms
    normed = (mixed / norms * gain[...].astype(F32)).astype(BF16)
    logits = dot(normed, router[...], NT)
    top_ref[...] = jnp.max(logits, axis=1, keepdims=True)
    column = iota((requests, experts), 1)
    named = column < 0
    for k in range(ids.shape[1]):
        named = named | (ids[:, k : k + 1] == column)
    weights = jnp.where(named, jnp.exp(logits), 0.0)
    weights = weights / jnp.sum(weights, axis=1, keepdims=True)
    earlier = (iota((requests, requests), 1) < iota((requests, requests), 0)).astype(F32)
    rank = dot(earlier, named.astype(F32))
    place = jnp.where(named, rank, -1.0)
    normed = normed.astype(F32)
    stacked = jnp.concatenate([normed[:, p * piece : (p + 1) * piece] for p in range(parts)], axis=0)
    places = jnp.concatenate([place] * parts, axis=0)
    shape = (slab_rows, parts * requests)
    inner = iota(shape, 0) % SLAB
    spread = (iota((slab_rows, experts), 0) // SLAB == iota((slab_rows, experts), 1)).astype(F32)
    picks = (dot(spread, places, NT) == (inner // parts).astype(F32)) & (
        inner % parts == iota(shape, 1) // requests
    )
    slabs_ref[...] = dot(picks.astype(BF16), stacked.astype(BF16)).astype(BF16)
    shape = (experts, slab_rows)
    spread = (iota(shape, 1) // SLAB == iota(shape, 0)).astype(F32)
    inner = iota((requests, slab_rows), 1) % SLAB
    comb_ref[...] = jnp.where(
        dot(place, spread) == (inner // parts).astype(F32),
        dot(weights, spread, precision=lax.Precision.HIGHEST),
        0.0,
    )


def attend_route_kernel(capacity, table, lengths, q_ref, fresh, hidden, gain, router, ids, weight, pool,
                        new_pool, mixed, norms, top, slabs, comb, *scratch):
    projected = attend(table, lengths, q_ref, fresh, weight, pool, new_pool, *scratch)
    route(projected, hidden, gain, router, ids, mixed, norms, top, slabs, comb, capacity)


def attend_kernel(table, lengths, q_ref, fresh, weight, pool, new_pool, projected, *scratch):
    projected[...] = attend(table, lengths, q_ref, fresh, weight, pool, new_pool, *scratch)


def route_kernel(capacity, projected, hidden, gain, router, ids, mixed, norms, top, slabs, comb):
    route(projected[...], hidden, gain, router, ids, mixed, norms, top, slabs, comb, capacity)


def unit_chunks(units):
    return [(start, min(256, units - start)) for start in range(0, units, 256)]


def expert_kernel(capacity, own, partner, gate_up, down, own_out, partner_out, kept_up, kept_down, rows, total, sems):
    units, width = kept_down.shape
    parts = SLAB // capacity
    loads = []
    for i, (start, size) in enumerate(unit_chunks(units)):
        span = pl.ds(start, size)
        loads.append((
            pltpu.make_async_copy(gate_up.at[0, :, span, :], kept_up.at[:, span, :], sems.at[2 * i]),
            pltpu.make_async_copy(down.at[0, span, :], kept_down.at[span, :], sems.at[2 * i + 1]),
        ))
        for copy in loads[-1]:
            copy.start()
    block = 128
    each = block // parts
    shape = (block, block)
    sort = (iota(shape, 1) == iota(shape, 0) % each * parts + iota(shape, 0) // each).astype(BF16)
    row = 0
    for source in (own, partner):
        for start in range(0, source.shape[0], block):
            sorted_rows = dot(sort, source[pl.ds(start, block), :]).astype(BF16)
            rows[pl.ds(row, each), :] = jnp.concatenate(
                [sorted_rows[p * each : (p + 1) * each] for p in range(parts)], axis=1
            )
            row += each
    arrived = rows[...]
    for i, (start, size) in enumerate(unit_chunks(units)):
        span = pl.ds(start, size)
        for copy in loads[i]:
            copy.wait()
        gate = dot(arrived, kept_up[0, span, :], NT)
        up = dot(arrived, kept_up[1, span, :], NT)
        activated = (gate / (1.0 + jnp.exp(-gate)) * up).astype(BF16)
        term = dot(activated, kept_down[span, :])
        if i == 0:
            total[...] = term
        else:
            total[...] += term
    kept = own_out.shape[0]
    own_out[...] = total[pl.ds(0, kept), :].astype(BF16)
    partner_out[...] = total[pl.ds(kept, kept), :].astype(BF16)


def merge_kernel(capacity, own, partner, slabs):
    parts = SLAB // capacity
    block = 128
    each = block // parts
    piece = slabs.shape[1]
    shape = (block, block)
    unsort = (iota(shape, 0) == iota(shape, 1) % each * parts + iota(shape, 1) // each).astype(BF16)
    for i in range(slabs.shape[0] // block):
        span = pl.ds(i * each, each)
        summed = (own[span, :].astype(F32) + partner[span, :].astype(F32)).astype(BF16)
        stacked = jnp.concatenate([summed[:, p * piece : (p + 1) * piece] for p in range(parts)], axis=0)
        slabs[pl.ds(i * block, block), :] = dot(unsort, stacked).astype(BF16)


def gather_terms(comb, slabs, capacity):
    parts = SLAB // capacity
    requests = comb.shape[0]
    weights = comb[...]
    pieces = []
    for _ in range(3):
        piece = weights.astype(BF16).astype(F32)
        weights = weights - piece
        pieces.append(piece)
    part = iota(comb.shape, 1) % parts
    stacked = jnp.concatenate(
        [jnp.where(part == p, piece, 0.0) for p in range(parts) for piece in pieces], axis=0
    ).astype(BF16)
    terms = dot(stacked, slabs[...])
    return jnp.concatenate(
        [
            sum(terms[(3 * p + i) * requests : (3 * p + i + 1) * requests] for i in range(3))
            for p in range(parts)
        ],
        axis=1,
    )


def combine_kernel(capacity, comb, slabs, mixed, out):
    out[...] = (mixed[...].astype(F32) + gather_terms(comb, slabs, capacity)).astype(BF16)


def gather_kernel(capacity, comb, slabs, out):
    out[...] = gather_terms(comb, slabs, capacity).astype(BF16)


def vmem(count):
    return [pl.BlockSpec(memory_space=pltpu.VMEM)] * count


def anywhere(count):
    return [pl.BlockSpec(memory_space=pl.ANY)] * count


def scalars(count):
    return [pl.BlockSpec(memory_space=pltpu.SMEM)] * count


def like(shape, dtype=BF16):
    return jax.ShapeDtypeStruct(shape, dtype)


def body(
    hidden,
    queries,
    fresh_key_value,
    kv_pool,
    page_table,
    lengths,
    out_weight,
    norm_gain,
    router_weight,
    expert_ids,
    expert_gate_up,
    expert_down,
):
    requests, width = hidden.shape
    req_count, kv_count = lax.axis_size("req"), lax.axis_size("kv")
    pages, page_len, heads_kv, pair_dim = kv_pool.shape
    head_dim = pair_dim // 2
    heads = queries.shape[1] // head_dim
    experts = router_weight.shape[0]
    copies = req_count // experts
    chosen = expert_ids.shape[1]
    capacity = 2 * max(1, (requests * chosen + 2 * experts - 1) // (2 * experts))
    parts = SLAB // capacity
    piece = width // parts
    slab_rows = experts * SLAB
    gain = norm_gain.reshape(1, width)

    attend_scratch = [
        pltpu.VMEM((pages, page_len, heads_kv, head_dim), BF16),
        pltpu.VMEM((pages, page_len, heads_kv, head_dim), BF16),
        pltpu.VMEM(out_weight.shape, BF16),
        pltpu.VMEM((heads * requests, head_dim), F32),
        pltpu.VMEM((heads * requests, head_dim), F32),
        pltpu.SemaphoreType.DMA((5,)),
    ]
    routed_shapes = [
        like((requests, width)),
        like((requests, 1), F32),
        like((requests, 1), F32),
        like((slab_rows, piece)),
        like((requests, slab_rows), F32),
    ]
    attend_params = pltpu.CompilerParams(vmem_limit_bytes=32 * MIB)
    if kv_count == 1:
        new_pool, mixed, norms, top, slabs, comb = pl.pallas_call(
            functools.partial(attend_route_kernel, capacity),
            out_shape=[like(kv_pool.shape)] + routed_shapes,
            in_specs=scalars(2) + vmem(6) + anywhere(2),
            out_specs=anywhere(1) + vmem(5),
            scratch_shapes=attend_scratch,
            compiler_params=attend_params,
        )(page_table, lengths, queries, fresh_key_value, hidden, gain, router_weight, expert_ids,
          out_weight, kv_pool)
    else:
        new_pool, projected = pl.pallas_call(
            attend_kernel,
            out_shape=[like(kv_pool.shape), like((requests, width), F32)],
            in_specs=scalars(2) + vmem(2) + anywhere(2),
            out_specs=anywhere(1) + vmem(1),
            scratch_shapes=attend_scratch,
            compiler_params=attend_params,
        )(page_table, lengths, queries, fresh_key_value, out_weight, kv_pool)
        projected = lax.psum(projected, "kv")
        mixed, norms, top, slabs, comb = pl.pallas_call(
            functools.partial(route_kernel, capacity),
            out_shape=routed_shapes,
            in_specs=vmem(5),
            out_specs=vmem(5),
        )(projected, hidden, gain, router_weight, expert_ids)

    same_part = [list(range(part, req_count, copies)) for part in range(copies)]
    swap = [(index, index ^ 1) for index in range(req_count)]

    def exchange(array):
        array = array.reshape(experts, SLAB, piece)
        array = lax.all_to_all(
            array, "req", split_axis=0, concat_axis=0, tiled=True, axis_index_groups=same_part
        )
        return array.reshape(slab_rows, piece)

    arrived = exchange(slabs)
    partner = lax.ppermute(arrived, "req", swap)
    units = expert_down.shape[1]
    kept = experts * capacity
    own_terms, partner_terms = pl.pallas_call(
        functools.partial(expert_kernel, capacity),
        out_shape=[like((kept, width))] * 2,
        in_specs=vmem(2) + anywhere(2),
        out_specs=vmem(2),
        scratch_shapes=[
            pltpu.VMEM((2, units, width), BF16),
            pltpu.VMEM((units, width), BF16),
            pltpu.VMEM((2 * kept, width), BF16),
            pltpu.VMEM((2 * kept, width), F32),
            pltpu.SemaphoreType.DMA((2 * len(unit_chunks(units)),)),
        ],
        compiler_params=pltpu.CompilerParams(vmem_limit_bytes=32 * MIB),
    )(arrived, partner, expert_gate_up, expert_down)
    swapped = lax.ppermute(partner_terms, "req", swap)
    leaving = pl.pallas_call(
        functools.partial(merge_kernel, capacity),
        out_shape=like((slab_rows, piece)),
        in_specs=vmem(2),
        out_specs=pl.BlockSpec(memory_space=pltpu.VMEM),
    )(own_terms, swapped)
    returned = exchange(leaving)
    if kv_count == 1:
        out_hidden = pl.pallas_call(
            functools.partial(combine_kernel, capacity),
            out_shape=like((requests, width)),
            in_specs=vmem(3),
            out_specs=pl.BlockSpec(memory_space=pltpu.VMEM),
        )(comb, returned, mixed)
    else:
        routed = pl.pallas_call(
            functools.partial(gather_kernel, capacity),
            out_shape=like((requests, width)),
            in_specs=vmem(2),
            out_specs=pl.BlockSpec(memory_space=pltpu.VMEM),
        )(comb, returned)
        routed = lax.psum(routed, "kv").astype(F32)
        out_hidden = (mixed.astype(F32) + routed).astype(BF16)
    return out_hidden, new_pool, norms.reshape(requests), top.reshape(requests)


def solution(mesh):
    in_specs = (
        P("req", None),
        P("req", "kv"),
        P("req", "kv", None),
        P("req", None, "kv", None),
        P("req", None),
        P("req"),
        P("kv", None),
        P(),
        P(),
        P("req", None),
        P("req", None, "kv", None),
        P("req", "kv", None),
    )
    out_specs = (P("req", None), P("req", None, "kv", None), P("req"), P("req"))
    return jax.shard_map(body, mesh=mesh, in_specs=in_specs, out_specs=out_specs, check_vma=False)
```

```python
import functools
import math

import jax
import jax.numpy as jnp
from jax import lax
from jax.experimental import pallas as pl
from jax.experimental.pallas import tpu as pltpu
from jax.sharding import PartitionSpec as P

BF16 = jnp.bfloat16
F32 = jnp.float32
NT = (((1,), (1,)), ((), ()))
NN = (((1,), (0,)), ((), ()))
SLAB = 16
MIB = 1 << 20


def dot(a, b, dims=NN, precision=None):
    return lax.dot_general(a, b, dims, precision=precision, preferred_element_type=F32)


def iota(shape, dim):
    return lax.broadcasted_iota(jnp.int32, shape, dim)


def copies(pairs, sems, first=0):
    return [pltpu.make_async_copy(src, dst, sems.at[first + i]) for i, (src, dst) in enumerate(pairs)]


def attend(refs, new_pool, scratch):
    small, (keys, values, kept_weight, qs, att, probs, sums, sems) = scratch
    table, lengths, q_ref, fresh = small[:4]
    requests, max_pages = table.shape
    pages, page_len, heads_kv, head_dim = keys.shape
    heads = q_ref.shape[1] // head_dim
    group = heads // heads_kv
    page_rows = page_len * heads_kv
    pool, weight = refs[-2:]

    def half(array, i):
        return array.at[:, :, :, pl.ds(i * head_dim, head_dim)]

    loads = copies(list(zip(refs[:4], small[:4])), sems)
    key_load, value_load, weight_load = copies(
        [(half(pool, 0), keys), (half(pool, 1), values), (weight, kept_weight)], sems, 4
    )
    later = copies(list(zip(refs[4:-2], small[4:])), sems, 9)
    for copy in loads + [key_load, value_load] + later + [weight_load]:
        copy.start()
    for copy in loads:
        copy.wait()
    for h in range(heads):
        qs[pl.ds(h * requests, requests), :] = q_ref[:, pl.ds(h * head_dim, head_dim)].astype(F32)
    spots = [(table[r, lengths[r] // page_len], lengths[r] % page_len) for r in range(requests)]
    key_store, value_store = copies([(keys, half(new_pool, 0)), (values, half(new_pool, 1))], sems, 7)

    key_load.wait()
    for r, (page, slot) in enumerate(spots):
        keys[page, slot] = fresh[r][:, :head_dim]
    key_store.start()
    key_pages = keys.reshape(pages, page_rows, head_dim)
    value_pages = values.reshape(pages, page_rows, head_dim)
    columns = max_pages * page_rows
    lane = iota((heads, columns), 1)
    own_head = lane % heads_kv == iota((heads, columns), 0) // group
    position = lane // heads_kv
    for r in range(requests):
        query = qs[pl.ds(r, heads, stride=requests), :].astype(BF16)
        gathered = jnp.concatenate([key_pages[table[r, j]] for j in range(max_pages)], axis=0)
        scores = dot(query, gathered, NT) * (1.0 / math.sqrt(head_dim))
        scores = jnp.where(own_head & (position <= lengths[r]), scores, -1e30)
        exponent = jnp.exp(scores - jnp.max(scores, axis=1, keepdims=True))
        sums[r] = jnp.broadcast_to(jnp.sum(exponent, axis=1, keepdims=True), (heads, head_dim))
        probs[r] = exponent.astype(BF16)

    value_load.wait()
    for r, (page, slot) in enumerate(spots):
        values[page, slot] = fresh[r][:, head_dim:]
    value_store.start()
    for r in range(requests):
        gathered = jnp.concatenate([value_pages[table[r, j]] for j in range(max_pages)], axis=0)
        att[pl.ds(r, heads, stride=requests), :] = dot(probs[r], gathered) / sums[r]
    attended = jnp.concatenate(
        [att[pl.ds(h * requests, requests), :] for h in range(heads)], axis=1
    ).astype(BF16)
    weight_load.wait()
    projected = dot(attended, kept_weight[...])
    for copy in later + [key_store, value_store]:
        copy.wait()
    return projected


def route(projected, hidden, gain, router, ids, mixed_ref, norms_ref, top_ref, slabs_ref, comb_ref, capacity):
    requests, width = hidden.shape
    experts = router.shape[0]
    parts = SLAB // capacity
    piece = width // parts
    slab_rows = experts * SLAB
    mixed = (hidden[...].astype(F32) + projected).astype(BF16)
    mixed_ref[...] = mixed
    mixed = mixed.astype(F32)
    norms = jnp.sqrt(jnp.mean(mixed * mixed, axis=1, keepdims=True) + 1e-06)
    norms_ref[...] = norms
    normed = (mixed / norms * gain[...].astype(F32).reshape(1, width)).astype(BF16)
    logits = dot(normed, router[...], NT)
    top_ref[...] = jnp.max(logits, axis=1, keepdims=True)
    column = iota((requests, experts), 1)
    named = column < 0
    for k in range(ids.shape[1]):
        named = named | (ids[:, k : k + 1] == column)
    weights = jnp.where(named, jnp.exp(logits), 0.0)
    weights = weights / jnp.sum(weights, axis=1, keepdims=True)
    earlier = (iota((requests, requests), 1) < iota((requests, requests), 0)).astype(F32)
    rank = dot(earlier, named.astype(F32))
    place = jnp.where(named, rank, -1.0)
    normed = normed.astype(F32)
    stacked = jnp.concatenate([normed[:, p * piece : (p + 1) * piece] for p in range(parts)], axis=0)
    places = jnp.concatenate([place] * parts, axis=0)
    shape = (slab_rows, parts * requests)
    inner = iota(shape, 0) % SLAB
    spread = (iota((slab_rows, experts), 0) // SLAB == iota((slab_rows, experts), 1)).astype(F32)
    picks = (dot(spread, places, NT) == (inner // parts).astype(F32)) & (
        inner % parts == iota(shape, 1) // requests
    )
    slabs_ref[...] = dot(picks.astype(BF16), stacked.astype(BF16)).astype(BF16)
    shape = (experts, slab_rows)
    spread = (iota(shape, 1) // SLAB == iota(shape, 0)).astype(F32)
    inner = iota((requests, slab_rows), 1) % SLAB
    comb_ref[...] = jnp.where(
        dot(place, spread) == (inner // parts).astype(F32),
        dot(weights, spread, precision=lax.Precision.HIGHEST),
        0.0,
    )


def attend_route_kernel(capacity, *refs):
    new_pool, mixed, norms, top, slabs, comb = refs[10:16]
    small, scratch = refs[16:24], refs[24:]
    projected = attend(refs[:10], new_pool, (small, scratch))
    hidden, gain, router, ids = small[4:]
    route(projected, hidden, gain, router, ids, mixed, norms, top, slabs, comb, capacity)


def attend_kernel(*refs):
    new_pool, projected = refs[6:8]
    projected[...] = attend(refs[:6], new_pool, (refs[8:12], refs[12:]))


def route_kernel(capacity, projected, hidden, gain, router, ids, mixed, norms, top, slabs, comb):
    route(projected[...], hidden, gain, router, ids, mixed, norms, top, slabs, comb, capacity)


def unit_chunks(units):
    return [(start, min(256, units - start)) for start in range(0, units, 256)]


def expert_kernel(capacity, own, partner, gate_up, down, own_out, partner_out, kept_up, kept_down, rows, total, sems):
    units, width = kept_down.shape
    parts = SLAB // capacity
    loads = []
    for i, (start, size) in enumerate(unit_chunks(units)):
        span = pl.ds(start, size)
        loads.append((
            pltpu.make_async_copy(gate_up.at[0, :, span, :], kept_up.at[:, span, :], sems.at[2 * i]),
            pltpu.make_async_copy(down.at[0, span, :], kept_down.at[span, :], sems.at[2 * i + 1]),
        ))
        for copy in loads[-1]:
            copy.start()
    block = 128
    each = block // parts
    shape = (block, block)
    sort = (iota(shape, 1) == iota(shape, 0) % each * parts + iota(shape, 0) // each).astype(BF16)
    row = 0
    for source in (own, partner):
        for start in range(0, source.shape[0], block):
            sorted_rows = dot(sort, source[pl.ds(start, block), :]).astype(BF16)
            rows[pl.ds(row, each), :] = jnp.concatenate(
                [sorted_rows[p * each : (p + 1) * each] for p in range(parts)], axis=1
            )
            row += each
    arrived = rows[...]
    for i, (start, size) in enumerate(unit_chunks(units)):
        span = pl.ds(start, size)
        for copy in loads[i]:
            copy.wait()
        gate = dot(arrived, kept_up[0, span, :], NT)
        up = dot(arrived, kept_up[1, span, :], NT)
        activated = (gate / (1.0 + jnp.exp(-gate)) * up).astype(BF16)
        term = dot(activated, kept_down[span, :])
        if i == 0:
            total[...] = term
        else:
            total[...] += term
    kept = own_out.shape[0]
    own_out[...] = total[pl.ds(0, kept), :].astype(BF16)
    partner_out[...] = total[pl.ds(kept, kept), :].astype(BF16)


def merge_kernel(capacity, own, partner, slabs):
    parts = SLAB // capacity
    block = 128
    each = block // parts
    piece = slabs.shape[1]
    shape = (block, block)
    unsort = (iota(shape, 0) == iota(shape, 1) % each * parts + iota(shape, 1) // each).astype(BF16)
    for i in range(slabs.shape[0] // block):
        span = pl.ds(i * each, each)
        summed = (own[span, :].astype(F32) + partner[span, :].astype(F32)).astype(BF16)
        stacked = jnp.concatenate([summed[:, p * piece : (p + 1) * piece] for p in range(parts)], axis=0)
        slabs[pl.ds(i * block, block), :] = dot(unsort, stacked).astype(BF16)


def gather_terms(comb, slabs, capacity):
    parts = SLAB // capacity
    requests = comb.shape[0]
    weights = comb[...]
    pieces = []
    for _ in range(3):
        piece = weights.astype(BF16).astype(F32)
        weights = weights - piece
        pieces.append(piece)
    part = iota(comb.shape, 1) % parts
    stacked = jnp.concatenate(
        [jnp.where(part == p, piece, 0.0) for p in range(parts) for piece in pieces], axis=0
    ).astype(BF16)
    terms = dot(stacked, slabs[...])
    return jnp.concatenate(
        [
            sum(terms[(3 * p + i) * requests : (3 * p + i + 1) * requests] for i in range(3))
            for p in range(parts)
        ],
        axis=1,
    )


def combine_kernel(capacity, comb, slabs, mixed, out):
    out[...] = (mixed[...].astype(F32) + gather_terms(comb, slabs, capacity)).astype(BF16)


def gather_kernel(capacity, comb, slabs, out):
    out[...] = gather_terms(comb, slabs, capacity).astype(BF16)


def vmem(count):
    return [pl.BlockSpec(memory_space=pltpu.VMEM)] * count


def anywhere(count):
    return [pl.BlockSpec(memory_space=pl.ANY)] * count


def in_hbm(count):
    return [pl.BlockSpec(memory_space=pltpu.HBM)] * count


def like(shape, dtype=BF16):
    return jax.ShapeDtypeStruct(shape, dtype)


def body(
    hidden,
    queries,
    fresh_key_value,
    kv_pool,
    page_table,
    lengths,
    out_weight,
    norm_gain,
    router_weight,
    expert_ids,
    expert_gate_up,
    expert_down,
):
    requests, width = hidden.shape
    req_count, kv_count = lax.axis_size("req"), lax.axis_size("kv")
    pages, page_len, heads_kv, pair_dim = kv_pool.shape
    head_dim = pair_dim // 2
    heads = queries.shape[1] // head_dim
    experts = router_weight.shape[0]
    copies = req_count // experts
    chosen = expert_ids.shape[1]
    capacity = 2 * max(1, (requests * chosen + 2 * experts - 1) // (2 * experts))
    parts = SLAB // capacity
    piece = width // parts
    slab_rows = experts * SLAB

    attend_scratch = [
        pltpu.VMEM((pages, page_len, heads_kv, head_dim), BF16),
        pltpu.VMEM((pages, page_len, heads_kv, head_dim), BF16),
        pltpu.VMEM(out_weight.shape, BF16),
        pltpu.VMEM((heads * requests, head_dim), F32),
        pltpu.VMEM((heads * requests, head_dim), F32),
        pltpu.VMEM((requests, heads, page_table.shape[1] * page_len * heads_kv), BF16),
        pltpu.VMEM((requests, heads, head_dim), F32),
        pltpu.SemaphoreType.DMA((13,)),
    ]

    def small(*arrays):
        return [pltpu.VMEM(array.shape, array.dtype) for array in arrays]

    inputs = [pltpu.SMEM(page_table.shape, jnp.int32), pltpu.SMEM(lengths.shape, jnp.int32)]
    inputs += small(queries, fresh_key_value)
    routed_shapes = [
        like((requests, width)),
        like((requests, 1), F32),
        like((requests, 1), F32),
        like((slab_rows, piece)),
        like((requests, slab_rows), F32),
    ]
    attend_params = pltpu.CompilerParams(vmem_limit_bytes=32 * MIB)
    if kv_count == 1:
        new_pool, mixed, norms, top, slabs, comb = pl.pallas_call(
            functools.partial(attend_route_kernel, capacity),
            out_shape=[like(kv_pool.shape)] + routed_shapes,
            in_specs=in_hbm(10),
            out_specs=in_hbm(1) + vmem(5),
            scratch_shapes=inputs + small(hidden, norm_gain, router_weight, expert_ids) + attend_scratch,
            compiler_params=attend_params,
        )(page_table, lengths, queries, fresh_key_value, hidden, norm_gain, router_weight, expert_ids,
          kv_pool, out_weight)
    else:
        new_pool, projected = pl.pallas_call(
            attend_kernel,
            out_shape=[like(kv_pool.shape), like((requests, width), F32)],
            in_specs=in_hbm(6),
            out_specs=in_hbm(1) + vmem(1),
            scratch_shapes=inputs + attend_scratch,
            compiler_params=attend_params,
        )(page_table, lengths, queries, fresh_key_value, kv_pool, out_weight)
        projected = lax.psum(projected, "kv")
        mixed, norms, top, slabs, comb = pl.pallas_call(
            functools.partial(route_kernel, capacity),
            out_shape=routed_shapes,
            in_specs=vmem(5),
            out_specs=vmem(5),
        )(projected, hidden, norm_gain, router_weight, expert_ids)

    same_part = [list(range(part, req_count, copies)) for part in range(copies)]
    swap = [(index, index ^ 1) for index in range(req_count)]

    def exchange(array):
        array = array.reshape(experts, SLAB, piece)
        array = lax.all_to_all(
            array, "req", split_axis=0, concat_axis=0, tiled=True, axis_index_groups=same_part
        )
        return array.reshape(slab_rows, piece)

    arrived = exchange(slabs)
    partner = lax.ppermute(arrived, "req", swap)
    units = expert_down.shape[1]
    kept = experts * capacity
    own_terms, partner_terms = pl.pallas_call(
        functools.partial(expert_kernel, capacity),
        out_shape=[like((kept, width))] * 2,
        in_specs=vmem(2) + anywhere(2),
        out_specs=vmem(2),
        scratch_shapes=[
            pltpu.VMEM((2, units, width), BF16),
            pltpu.VMEM((units, width), BF16),
            pltpu.VMEM((2 * kept, width), BF16),
            pltpu.VMEM((2 * kept, width), F32),
            pltpu.SemaphoreType.DMA((2 * len(unit_chunks(units)),)),
        ],
        compiler_params=pltpu.CompilerParams(vmem_limit_bytes=32 * MIB),
    )(arrived, partner, expert_gate_up, expert_down)
    swapped = lax.ppermute(partner_terms, "req", swap)
    leaving = pl.pallas_call(
        functools.partial(merge_kernel, capacity),
        out_shape=like((slab_rows, piece)),
        in_specs=vmem(2),
        out_specs=pl.BlockSpec(memory_space=pltpu.VMEM),
        compiler_params=pltpu.CompilerParams(vmem_limit_bytes=8 * MIB),
    )(own_terms, swapped)
    returned = exchange(leaving)
    if kv_count == 1:
        out_hidden = pl.pallas_call(
            functools.partial(combine_kernel, capacity),
            out_shape=like((requests, width)),
            in_specs=vmem(3),
            out_specs=pl.BlockSpec(memory_space=pltpu.VMEM),
            compiler_params=pltpu.CompilerParams(vmem_limit_bytes=8 * MIB),
        )(comb, returned, mixed)
    else:
        routed = pl.pallas_call(
            functools.partial(gather_kernel, capacity),
            out_shape=like((requests, width)),
            in_specs=vmem(2),
            out_specs=pl.BlockSpec(memory_space=pltpu.VMEM),
        )(comb, returned)
        routed = lax.psum(routed, "kv").astype(F32)
        out_hidden = (mixed.astype(F32) + routed).astype(BF16)
    return out_hidden, new_pool, norms.reshape(requests), top.reshape(requests)


def solution(mesh):
    in_specs = (
        P("req", None),
        P("req", "kv"),
        P("req", "kv", None),
        P("req", None, "kv", None),
        P("req", None),
        P("req"),
        P("kv", None),
        P(),
        P(),
        P("req", None),
        P("req", None, "kv", None),
        P("req", "kv", None),
    )
    out_specs = (P("req", None), P("req", None, "kv", None), P("req"), P("req"))
    return jax.shard_map(body, mesh=mesh, in_specs=in_specs, out_specs=out_specs, check_vma=False)
```

```python
import functools
import math

import jax
import jax.numpy as jnp
from jax import lax
from jax.experimental import pallas as pl
from jax.experimental.pallas import tpu as pltpu
from jax.sharding import PartitionSpec as P

BF16 = jnp.bfloat16
F32 = jnp.float32
NT = (((1,), (1,)), ((), ()))
NN = (((1,), (0,)), ((), ()))
SLAB = 16
MIB = 1 << 20


def dot(a, b, dims=NN, precision=None):
    return lax.dot_general(a, b, dims, precision=precision, preferred_element_type=F32)


def iota(shape, dim):
    return lax.broadcasted_iota(jnp.int32, shape, dim)


def copies(pairs, sems, first=0):
    return [pltpu.make_async_copy(src, dst, sems.at[first + i]) for i, (src, dst) in enumerate(pairs)]


def attend(refs, new_pool, scratch):
    small, (kept_up, kept_down, keys, values, kept_weight, qs, att, probs, sums, sems) = scratch
    table, lengths, q_ref, fresh = small[:4]
    requests, max_pages = table.shape
    pages, page_len, heads_kv, head_dim = keys.shape
    heads = q_ref.shape[1] // head_dim
    group = heads // heads_kv
    page_rows = page_len * heads_kv
    pool, weight, gate_up, down = refs[-4:]

    def half(array, i):
        return array.at[:, :, :, pl.ds(i * head_dim, head_dim)]

    loads = copies(list(zip(refs[:4], small[:4])), sems)
    key_load, value_load, weight_load = copies(
        [(half(pool, 0), keys), (half(pool, 1), values), (weight, kept_weight)], sems, 4
    )
    later = copies([(gate_up.at[0], kept_up), (down.at[0], kept_down)] + list(zip(refs[4:-4], small[4:])), sems, 9)
    for copy in loads + [key_load, value_load] + later[2:] + [weight_load] + later[:2]:
        copy.start()
    for copy in loads:
        copy.wait()
    for h in range(heads):
        qs[pl.ds(h * requests, requests), :] = q_ref[:, pl.ds(h * head_dim, head_dim)].astype(F32)
    spots = [(table[r, lengths[r] // page_len], lengths[r] % page_len) for r in range(requests)]
    key_store, value_store = copies([(keys, half(new_pool, 0)), (values, half(new_pool, 1))], sems, 7)

    key_load.wait()
    for r, (page, slot) in enumerate(spots):
        keys[page, slot] = fresh[r][:, :head_dim]
    key_store.start()
    key_pages = keys.reshape(pages, page_rows, head_dim)
    value_pages = values.reshape(pages, page_rows, head_dim)
    columns = max_pages * page_rows
    lane = iota((heads, columns), 1)
    own_head = lane % heads_kv == iota((heads, columns), 0) // group
    position = lane // heads_kv
    for r in range(requests):
        query = qs[pl.ds(r, heads, stride=requests), :].astype(BF16)
        gathered = jnp.concatenate([key_pages[table[r, j]] for j in range(max_pages)], axis=0)
        scores = dot(query, gathered, NT) * (1.0 / math.sqrt(head_dim))
        scores = jnp.where(own_head & (position <= lengths[r]), scores, -1e30)
        exponent = jnp.exp(scores - jnp.max(scores, axis=1, keepdims=True))
        sums[r] = jnp.broadcast_to(jnp.sum(exponent, axis=1, keepdims=True), (heads, head_dim))
        probs[r] = exponent.astype(BF16)

    value_load.wait()
    for r, (page, slot) in enumerate(spots):
        values[page, slot] = fresh[r][:, head_dim:]
    value_store.start()
    for r in range(requests):
        gathered = jnp.concatenate([value_pages[table[r, j]] for j in range(max_pages)], axis=0)
        att[pl.ds(r, heads, stride=requests), :] = dot(probs[r], gathered) / sums[r]
    attended = jnp.concatenate(
        [att[pl.ds(h * requests, requests), :] for h in range(heads)], axis=1
    ).astype(BF16)
    weight_load.wait()
    projected = dot(attended, kept_weight[...])
    for copy in later + [key_store, value_store]:
        copy.wait()
    return projected


def route(projected, hidden, gain, router, ids, mixed_ref, norms_ref, top_ref, slabs_ref, comb_ref, capacity):
    requests, width = hidden.shape
    experts = router.shape[0]
    parts = SLAB // capacity
    piece = width // parts
    slab_rows = experts * SLAB
    mixed = (hidden[...].astype(F32) + projected).astype(BF16)
    mixed_ref[...] = mixed
    mixed = mixed.astype(F32)
    norms = jnp.sqrt(jnp.mean(mixed * mixed, axis=1, keepdims=True) + 1e-06)
    norms_ref[...] = norms
    normed = (mixed / norms * gain[...].astype(F32).reshape(1, width)).astype(BF16)
    logits = dot(normed, router[...], NT)
    top_ref[...] = jnp.max(logits, axis=1, keepdims=True)
    column = iota((requests, experts), 1)
    named = column < 0
    for k in range(ids.shape[1]):
        named = named | (ids[:, k : k + 1] == column)
    weights = jnp.where(named, jnp.exp(logits), 0.0)
    weights = weights / jnp.sum(weights, axis=1, keepdims=True)
    earlier = (iota((requests, requests), 1) < iota((requests, requests), 0)).astype(F32)
    rank = dot(earlier, named.astype(F32))
    place = jnp.where(named, rank, -1.0)
    normed = normed.astype(F32)
    stacked = jnp.concatenate([normed[:, p * piece : (p + 1) * piece] for p in range(parts)], axis=0)
    places = jnp.concatenate([place] * parts, axis=0)
    shape = (slab_rows, parts * requests)
    inner = iota(shape, 0) % SLAB
    spread = (iota((slab_rows, experts), 0) // SLAB == iota((slab_rows, experts), 1)).astype(F32)
    picks = (dot(spread, places, NT) == (inner // parts).astype(F32)) & (
        inner % parts == iota(shape, 1) // requests
    )
    slabs_ref[...] = dot(picks.astype(BF16), stacked.astype(BF16)).astype(BF16)
    shape = (experts, slab_rows)
    spread = (iota(shape, 1) // SLAB == iota(shape, 0)).astype(F32)
    inner = iota((requests, slab_rows), 1) % SLAB
    comb_ref[...] = jnp.where(
        dot(place, spread) == (inner // parts).astype(F32),
        dot(weights, spread, precision=lax.Precision.HIGHEST),
        0.0,
    )


def attend_route_kernel(capacity, *refs):
    inputs, (new_pool, kept_up, kept_down, mixed, norms, top, slabs, comb) = refs[:12], refs[12:20]
    small, scratch = refs[20:28], refs[28:]
    projected = attend(inputs, new_pool, (small, (kept_up, kept_down) + scratch))
    hidden, gain, router, ids = small[4:]
    route(projected, hidden, gain, router, ids, mixed, norms, top, slabs, comb, capacity)


def attend_kernel(*refs):
    new_pool, kept_up, kept_down, projected = refs[8:12]
    projected[...] = attend(refs[:8], new_pool, (refs[12:16], (kept_up, kept_down) + refs[16:]))


def route_kernel(capacity, projected, hidden, gain, router, ids, mixed, norms, top, slabs, comb):
    route(projected[...], hidden, gain, router, ids, mixed, norms, top, slabs, comb, capacity)


def unit_chunks(units):
    return [(start, min(256, units - start)) for start in range(0, units, 256)]


def expert_kernel(capacity, own, partner, gate_up, down, own_out, partner_out, rows, total):
    units, width = down.shape
    parts = SLAB // capacity
    block = 128
    each = block // parts
    shape = (block, block)
    sort = (iota(shape, 1) == iota(shape, 0) % each * parts + iota(shape, 0) // each).astype(BF16)
    row = 0
    for source in (own, partner):
        for start in range(0, source.shape[0], block):
            sorted_rows = dot(sort, source[pl.ds(start, block), :]).astype(BF16)
            rows[pl.ds(row, each), :] = jnp.concatenate(
                [sorted_rows[p * each : (p + 1) * each] for p in range(parts)], axis=1
            )
            row += each
    arrived = rows[...]
    for i, (start, size) in enumerate(unit_chunks(units)):
        span = pl.ds(start, size)
        gate = dot(arrived, gate_up[0, span, :], NT)
        up = dot(arrived, gate_up[1, span, :], NT)
        activated = (gate / (1.0 + jnp.exp(-gate)) * up).astype(BF16)
        term = dot(activated, down[span, :])
        if i == 0:
            total[...] = term
        else:
            total[...] += term
    kept = own_out.shape[0]
    own_out[...] = total[pl.ds(0, kept), :].astype(BF16)
    partner_out[...] = total[pl.ds(kept, kept), :].astype(BF16)


def merge_kernel(capacity, own, partner, slabs):
    parts = SLAB // capacity
    block = 128
    each = block // parts
    piece = slabs.shape[1]
    shape = (block, block)
    unsort = (iota(shape, 0) == iota(shape, 1) % each * parts + iota(shape, 1) // each).astype(BF16)
    for i in range(slabs.shape[0] // block):
        span = pl.ds(i * each, each)
        summed = (own[span, :].astype(F32) + partner[span, :].astype(F32)).astype(BF16)
        stacked = jnp.concatenate([summed[:, p * piece : (p + 1) * piece] for p in range(parts)], axis=0)
        slabs[pl.ds(i * block, block), :] = dot(unsort, stacked).astype(BF16)


def gather_terms(comb, slabs, capacity):
    parts = SLAB // capacity
    requests = comb.shape[0]
    weights = comb[...]
    pieces = []
    for _ in range(3):
        piece = weights.astype(BF16).astype(F32)
        weights = weights - piece
        pieces.append(piece)
    part = iota(comb.shape, 1) % parts
    stacked = jnp.concatenate(
        [jnp.where(part == p, piece, 0.0) for p in range(parts) for piece in pieces], axis=0
    ).astype(BF16)
    terms = dot(stacked, slabs[...])
    return jnp.concatenate(
        [
            sum(terms[(3 * p + i) * requests : (3 * p + i + 1) * requests] for i in range(3))
            for p in range(parts)
        ],
        axis=1,
    )


def combine_kernel(capacity, comb, slabs, mixed, out):
    out[...] = (mixed[...].astype(F32) + gather_terms(comb, slabs, capacity)).astype(BF16)


def gather_kernel(capacity, comb, slabs, out):
    out[...] = gather_terms(comb, slabs, capacity).astype(BF16)


def vmem(count):
    return [pl.BlockSpec(memory_space=pltpu.VMEM)] * count


def in_hbm(count):
    return [pl.BlockSpec(memory_space=pltpu.HBM)] * count


def pinned(*arrays):
    return [pltpu.with_memory_space_constraint(array, pltpu.HBM) for array in arrays]


def like(shape, dtype=BF16):
    return jax.ShapeDtypeStruct(shape, dtype)


def body(
    hidden,
    queries,
    fresh_key_value,
    kv_pool,
    page_table,
    lengths,
    out_weight,
    norm_gain,
    router_weight,
    expert_ids,
    expert_gate_up,
    expert_down,
):
    requests, width = hidden.shape
    req_count, kv_count = lax.axis_size("req"), lax.axis_size("kv")
    pages, page_len, heads_kv, pair_dim = kv_pool.shape
    head_dim = pair_dim // 2
    heads = queries.shape[1] // head_dim
    experts = router_weight.shape[0]
    copies = req_count // experts
    chosen = expert_ids.shape[1]
    capacity = 2 * max(1, (requests * chosen + 2 * experts - 1) // (2 * experts))
    parts = SLAB // capacity
    piece = width // parts
    slab_rows = experts * SLAB

    attend_scratch = [
        pltpu.VMEM((pages, page_len, heads_kv, head_dim), BF16),
        pltpu.VMEM((pages, page_len, heads_kv, head_dim), BF16),
        pltpu.VMEM(out_weight.shape, BF16),
        pltpu.VMEM((heads * requests, head_dim), F32),
        pltpu.VMEM((heads * requests, head_dim), F32),
        pltpu.VMEM((requests, heads, page_table.shape[1] * page_len * heads_kv), BF16),
        pltpu.VMEM((requests, heads, head_dim), F32),
        pltpu.SemaphoreType.DMA((15,)),
    ]

    def small(*arrays):
        return [pltpu.VMEM(array.shape, array.dtype) for array in arrays]

    inputs = [pltpu.SMEM(page_table.shape, jnp.int32), pltpu.SMEM(lengths.shape, jnp.int32)]
    inputs += small(queries, fresh_key_value)
    kept_shapes = [like(array) for array in (kv_pool.shape, expert_gate_up.shape[1:], expert_down.shape[1:])]
    routed_shapes = [
        like((requests, width)),
        like((requests, 1), F32),
        like((requests, 1), F32),
        like((slab_rows, piece)),
        like((requests, slab_rows), F32),
    ]
    attend_params = pltpu.CompilerParams(vmem_limit_bytes=32 * MIB)
    if kv_count == 1:
        new_pool, kept_up, kept_down, mixed, norms, top, slabs, comb = pl.pallas_call(
            functools.partial(attend_route_kernel, capacity),
            out_shape=kept_shapes + routed_shapes,
            in_specs=in_hbm(12),
            out_specs=in_hbm(1) + vmem(7),
            scratch_shapes=inputs + small(hidden, norm_gain, router_weight, expert_ids) + attend_scratch,
            compiler_params=attend_params,
        )(*pinned(page_table, lengths, queries, fresh_key_value, hidden, norm_gain, router_weight, expert_ids,
                  kv_pool, out_weight, expert_gate_up, expert_down))
    else:
        new_pool, kept_up, kept_down, projected = pl.pallas_call(
            attend_kernel,
            out_shape=kept_shapes + [like((requests, width), F32)],
            in_specs=in_hbm(8),
            out_specs=in_hbm(1) + vmem(3),
            scratch_shapes=inputs + attend_scratch,
            compiler_params=attend_params,
        )(*pinned(page_table, lengths, queries, fresh_key_value, kv_pool, out_weight, expert_gate_up, expert_down))
        projected = lax.psum(projected, "kv")
        mixed, norms, top, slabs, comb = pl.pallas_call(
            functools.partial(route_kernel, capacity),
            out_shape=routed_shapes,
            in_specs=vmem(5),
            out_specs=vmem(5),
        )(projected, hidden, norm_gain, router_weight, expert_ids)

    same_part = [list(range(part, req_count, copies)) for part in range(copies)]
    swap = [(index, index ^ 1) for index in range(req_count)]

    def exchange(array):
        array = array.reshape(experts, SLAB, piece)
        array = lax.all_to_all(
            array, "req", split_axis=0, concat_axis=0, tiled=True, axis_index_groups=same_part
        )
        return array.reshape(slab_rows, piece)

    arrived = exchange(slabs)
    partner = lax.ppermute(arrived, "req", swap)
    kept = experts * capacity
    own_terms, partner_terms = pl.pallas_call(
        functools.partial(expert_kernel, capacity),
        out_shape=[like((kept, width))] * 2,
        in_specs=vmem(4),
        out_specs=vmem(2),
        scratch_shapes=[pltpu.VMEM((2 * kept, width), BF16), pltpu.VMEM((2 * kept, width), F32)],
        compiler_params=pltpu.CompilerParams(vmem_limit_bytes=28 * MIB),
    )(arrived, partner, kept_up, kept_down)
    swapped = lax.ppermute(partner_terms, "req", swap)
    leaving = pl.pallas_call(
        functools.partial(merge_kernel, capacity),
        out_shape=like((slab_rows, piece)),
        in_specs=vmem(2),
        out_specs=pl.BlockSpec(memory_space=pltpu.VMEM),
        compiler_params=pltpu.CompilerParams(vmem_limit_bytes=8 * MIB),
    )(own_terms, swapped)
    returned = exchange(leaving)
    if kv_count == 1:
        out_hidden = pl.pallas_call(
            functools.partial(combine_kernel, capacity),
            out_shape=like((requests, width)),
            in_specs=vmem(3),
            out_specs=pl.BlockSpec(memory_space=pltpu.VMEM),
            compiler_params=pltpu.CompilerParams(vmem_limit_bytes=8 * MIB),
        )(comb, returned, mixed)
    else:
        routed = pl.pallas_call(
            functools.partial(gather_kernel, capacity),
            out_shape=like((requests, width)),
            in_specs=vmem(2),
            out_specs=pl.BlockSpec(memory_space=pltpu.VMEM),
        )(comb, returned)
        routed = lax.psum(routed, "kv").astype(F32)
        out_hidden = (mixed.astype(F32) + routed).astype(BF16)
    return out_hidden, new_pool, norms.reshape(requests), top.reshape(requests)


def solution(mesh):
    in_specs = (
        P("req", None),
        P("req", "kv"),
        P("req", "kv", None),
        P("req", None, "kv", None),
        P("req", None),
        P("req"),
        P("kv", None),
        P(),
        P(),
        P("req", None),
        P("req", None, "kv", None),
        P("req", "kv", None),
    )
    out_specs = (P("req", None), P("req", None, "kv", None), P("req"), P("req"))
    return jax.shard_map(body, mesh=mesh, in_specs=in_specs, out_specs=out_specs, check_vma=False)
```

```python
import functools
import math

import jax
import jax.numpy as jnp
from jax import lax
from jax.experimental import pallas as pl
from jax.experimental.pallas import tpu as pltpu
from jax.sharding import PartitionSpec as P

BF16 = jnp.bfloat16
F32 = jnp.float32
NT = (((1,), (1,)), ((), ()))
NN = (((1,), (0,)), ((), ()))
SLAB = 16
MIB = 1 << 20


def dot(a, b, dims=NN, precision=None):
    return lax.dot_general(a, b, dims, precision=precision, preferred_element_type=F32)


def iota(shape, dim):
    return lax.broadcasted_iota(jnp.int32, shape, dim)


def copies(pairs, sems, first=0):
    return [pltpu.make_async_copy(src, dst, sems.at[first + i]) for i, (src, dst) in enumerate(pairs)]


def pool_half(array, i):
    head_dim = array.shape[3] // 2
    return array.at[:, :, :, pl.ds(i * head_dim, head_dim)]


def attend(refs, keys, values, scratch):
    small, (kept_weight, qs, att, probs, sums, sems) = scratch
    table, lengths, q_ref, fresh = small[:4]
    requests, max_pages = table.shape
    pages, page_len, heads_kv, head_dim = keys.shape
    heads = q_ref.shape[1] // head_dim
    group = heads // heads_kv
    page_rows = page_len * heads_kv
    pool, weight = refs[-2:]
    loads = copies(list(zip(refs[:4], small[:4])), sems)
    key_load, value_load, weight_load = copies(
        [(pool_half(pool, 0), keys), (pool_half(pool, 1), values), (weight, kept_weight)], sems, 4
    )
    later = copies(list(zip(refs[4:-2], small[4:])), sems, 7)
    for copy in loads + [key_load, value_load] + later + [weight_load]:
        copy.start()
    for copy in loads:
        copy.wait()
    for h in range(heads):
        qs[pl.ds(h * requests, requests), :] = q_ref[:, pl.ds(h * head_dim, head_dim)].astype(F32)
    spots = [(table[r, lengths[r] // page_len], lengths[r] % page_len) for r in range(requests)]

    key_load.wait()
    for r, (page, slot) in enumerate(spots):
        keys[page, slot] = fresh[r][:, :head_dim]
    key_pages = keys.reshape(pages, page_rows, head_dim)
    value_pages = values.reshape(pages, page_rows, head_dim)
    columns = max_pages * page_rows
    lane = iota((heads, columns), 1)
    own_head = lane % heads_kv == iota((heads, columns), 0) // group
    position = lane // heads_kv
    for r in range(requests):
        query = qs[pl.ds(r, heads, stride=requests), :].astype(BF16)
        gathered = jnp.concatenate([key_pages[table[r, j]] for j in range(max_pages)], axis=0)
        scores = dot(query, gathered, NT) * (1.0 / math.sqrt(head_dim))
        scores = jnp.where(own_head & (position <= lengths[r]), scores, -1e30)
        exponent = jnp.exp(scores - jnp.max(scores, axis=1, keepdims=True))
        sums[r] = jnp.broadcast_to(jnp.sum(exponent, axis=1, keepdims=True), (heads, head_dim))
        probs[r] = exponent.astype(BF16)

    value_load.wait()
    for r, (page, slot) in enumerate(spots):
        values[page, slot] = fresh[r][:, head_dim:]
    for r in range(requests):
        gathered = jnp.concatenate([value_pages[table[r, j]] for j in range(max_pages)], axis=0)
        att[pl.ds(r, heads, stride=requests), :] = dot(probs[r], gathered) / sums[r]
    attended = jnp.concatenate(
        [att[pl.ds(h * requests, requests), :] for h in range(heads)], axis=1
    ).astype(BF16)
    weight_load.wait()
    projected = dot(attended, kept_weight[...])
    for copy in later:
        copy.wait()
    return projected


def route(projected, hidden, gain, router, ids, mixed_ref, norms_ref, top_ref, slabs_ref, comb_ref, capacity):
    requests, width = hidden.shape
    experts = router.shape[0]
    parts = SLAB // capacity
    piece = width // parts
    slab_rows = experts * SLAB
    mixed = (hidden[...].astype(F32) + projected).astype(BF16)
    mixed_ref[...] = mixed
    mixed = mixed.astype(F32)
    norms = jnp.sqrt(jnp.mean(mixed * mixed, axis=1, keepdims=True) + 1e-06)
    norms_ref[...] = norms
    normed = (mixed / norms * gain[...].astype(F32).reshape(1, width)).astype(BF16)
    logits = dot(normed, router[...], NT)
    top_ref[...] = jnp.max(logits, axis=1, keepdims=True)
    column = iota((requests, experts), 1)
    named = column < 0
    for k in range(ids.shape[1]):
        named = named | (ids[:, k : k + 1] == column)
    weights = jnp.where(named, jnp.exp(logits), 0.0)
    weights = weights / jnp.sum(weights, axis=1, keepdims=True)
    earlier = (iota((requests, requests), 1) < iota((requests, requests), 0)).astype(F32)
    rank = dot(earlier, named.astype(F32))
    place = jnp.where(named, rank, -1.0)
    normed = normed.astype(F32)
    stacked = jnp.concatenate([normed[:, p * piece : (p + 1) * piece] for p in range(parts)], axis=0)
    places = jnp.concatenate([place] * parts, axis=0)
    shape = (slab_rows, parts * requests)
    inner = iota(shape, 0) % SLAB
    spread = (iota((slab_rows, experts), 0) // SLAB == iota((slab_rows, experts), 1)).astype(F32)
    picks = (dot(spread, places, NT) == (inner // parts).astype(F32)) & (
        inner % parts == iota(shape, 1) // requests
    )
    slabs_ref[...] = dot(picks.astype(BF16), stacked.astype(BF16)).astype(BF16)
    shape = (experts, slab_rows)
    spread = (iota(shape, 1) // SLAB == iota(shape, 0)).astype(F32)
    inner = iota((requests, slab_rows), 1) % SLAB
    comb_ref[...] = jnp.where(
        dot(place, spread) == (inner // parts).astype(F32),
        dot(weights, spread, precision=lax.Precision.HIGHEST),
        0.0,
    )


def attend_route_kernel(capacity, *refs):
    inputs, (keys, values, mixed, norms, top, slabs, comb) = refs[:10], refs[10:17]
    small, scratch = refs[17:25], refs[25:]
    projected = attend(inputs, keys, values, (small, scratch))
    hidden, gain, router, ids = small[4:]
    route(projected, hidden, gain, router, ids, mixed, norms, top, slabs, comb, capacity)


def attend_kernel(*refs):
    keys, values, projected = refs[6:9]
    projected[...] = attend(refs[:6], keys, values, (refs[9:13], refs[13:]))


def store_kernel(keys, values, gate_up, down, new_pool, kept_up, kept_down, sems):
    moves = copies(
        [
            (gate_up.at[0], kept_up),
            (down.at[0], kept_down),
            (keys, pool_half(new_pool, 0)),
            (values, pool_half(new_pool, 1)),
        ],
        sems,
    )
    for copy in moves:
        copy.start()
    for copy in moves:
        copy.wait()


def route_kernel(capacity, projected, hidden, gain, router, ids, mixed, norms, top, slabs, comb):
    route(projected[...], hidden, gain, router, ids, mixed, norms, top, slabs, comb, capacity)


def unit_chunks(units):
    return [(start, min(256, units - start)) for start in range(0, units, 256)]


def expert_kernel(capacity, own, partner, gate_up, down, own_out, partner_out, rows, total):
    units, width = down.shape
    parts = SLAB // capacity
    block = 128
    each = block // parts
    shape = (block, block)
    sort = (iota(shape, 1) == iota(shape, 0) % each * parts + iota(shape, 0) // each).astype(BF16)
    row = 0
    for source in (own, partner):
        for start in range(0, source.shape[0], block):
            sorted_rows = dot(sort, source[pl.ds(start, block), :]).astype(BF16)
            rows[pl.ds(row, each), :] = jnp.concatenate(
                [sorted_rows[p * each : (p + 1) * each] for p in range(parts)], axis=1
            )
            row += each
    arrived = rows[...]
    for i, (start, size) in enumerate(unit_chunks(units)):
        span = pl.ds(start, size)
        gate = dot(arrived, gate_up[0, span, :], NT)
        up = dot(arrived, gate_up[1, span, :], NT)
        activated = (gate / (1.0 + jnp.exp(-gate)) * up).astype(BF16)
        term = dot(activated, down[span, :])
        if i == 0:
            total[...] = term
        else:
            total[...] += term
    kept = own_out.shape[0]
    own_out[...] = total[pl.ds(0, kept), :].astype(BF16)
    partner_out[...] = total[pl.ds(kept, kept), :].astype(BF16)


def merge_kernel(capacity, own, partner, slabs):
    parts = SLAB // capacity
    block = 128
    each = block // parts
    piece = slabs.shape[1]
    shape = (block, block)
    unsort = (iota(shape, 0) == iota(shape, 1) % each * parts + iota(shape, 1) // each).astype(BF16)
    for i in range(slabs.shape[0] // block):
        span = pl.ds(i * each, each)
        summed = (own[span, :].astype(F32) + partner[span, :].astype(F32)).astype(BF16)
        stacked = jnp.concatenate([summed[:, p * piece : (p + 1) * piece] for p in range(parts)], axis=0)
        slabs[pl.ds(i * block, block), :] = dot(unsort, stacked).astype(BF16)


def gather_terms(comb, slabs, capacity):
    parts = SLAB // capacity
    requests = comb.shape[0]
    weights = comb[...]
    pieces = []
    for _ in range(3):
        piece = weights.astype(BF16).astype(F32)
        weights = weights - piece
        pieces.append(piece)
    part = iota(comb.shape, 1) % parts
    stacked = jnp.concatenate(
        [jnp.where(part == p, piece, 0.0) for p in range(parts) for piece in pieces], axis=0
    ).astype(BF16)
    terms = dot(stacked, slabs[...])
    return jnp.concatenate(
        [
            sum(terms[(3 * p + i) * requests : (3 * p + i + 1) * requests] for i in range(3))
            for p in range(parts)
        ],
        axis=1,
    )


def combine_kernel(capacity, comb, slabs, mixed, out):
    out[...] = (mixed[...].astype(F32) + gather_terms(comb, slabs, capacity)).astype(BF16)


def gather_kernel(capacity, comb, slabs, out):
    out[...] = gather_terms(comb, slabs, capacity).astype(BF16)


def vmem(count):
    return [pl.BlockSpec(memory_space=pltpu.VMEM)] * count


def in_hbm(count):
    return [pl.BlockSpec(memory_space=pltpu.HBM)] * count


def pinned(*arrays):
    return [pltpu.with_memory_space_constraint(array, pltpu.HBM) for array in arrays]


def like(shape, dtype=BF16):
    return jax.ShapeDtypeStruct(shape, dtype)


def body(
    hidden,
    queries,
    fresh_key_value,
    kv_pool,
    page_table,
    lengths,
    out_weight,
    norm_gain,
    router_weight,
    expert_ids,
    expert_gate_up,
    expert_down,
):
    requests, width = hidden.shape
    req_count, kv_count = lax.axis_size("req"), lax.axis_size("kv")
    pages, page_len, heads_kv, pair_dim = kv_pool.shape
    head_dim = pair_dim // 2
    heads = queries.shape[1] // head_dim
    experts = router_weight.shape[0]
    copies = req_count // experts
    chosen = expert_ids.shape[1]
    capacity = 2 * max(1, (requests * chosen + 2 * experts - 1) // (2 * experts))
    parts = SLAB // capacity
    piece = width // parts
    slab_rows = experts * SLAB

    attend_scratch = [
        pltpu.VMEM(out_weight.shape, BF16),
        pltpu.VMEM((heads * requests, head_dim), F32),
        pltpu.VMEM((heads * requests, head_dim), F32),
        pltpu.VMEM((requests, heads, page_table.shape[1] * page_len * heads_kv), BF16),
        pltpu.VMEM((requests, heads, head_dim), F32),
        pltpu.SemaphoreType.DMA((11,)),
    ]

    def small(*arrays):
        return [pltpu.VMEM(array.shape, array.dtype) for array in arrays]

    inputs = [pltpu.SMEM(page_table.shape, jnp.int32), pltpu.SMEM(lengths.shape, jnp.int32)]
    inputs += small(queries, fresh_key_value)
    kept_shapes = [like((pages, page_len, heads_kv, head_dim))] * 2
    routed_shapes = [
        like((requests, width)),
        like((requests, 1), F32),
        like((requests, 1), F32),
        like((slab_rows, piece)),
        like((requests, slab_rows), F32),
    ]
    attend_params = pltpu.CompilerParams(vmem_limit_bytes=32 * MIB)
    if kv_count == 1:
        keys, values, mixed, norms, top, slabs, comb = pl.pallas_call(
            functools.partial(attend_route_kernel, capacity),
            out_shape=kept_shapes + routed_shapes,
            in_specs=in_hbm(10),
            out_specs=vmem(7),
            scratch_shapes=inputs + small(hidden, norm_gain, router_weight, expert_ids) + attend_scratch,
            compiler_params=attend_params,
        )(*pinned(page_table, lengths, queries, fresh_key_value, hidden, norm_gain, router_weight, expert_ids,
                  kv_pool, out_weight))
    else:
        keys, values, projected = pl.pallas_call(
            attend_kernel,
            out_shape=kept_shapes + [like((requests, width), F32)],
            in_specs=in_hbm(6),
            out_specs=vmem(3),
            scratch_shapes=inputs + attend_scratch,
            compiler_params=attend_params,
        )(*pinned(page_table, lengths, queries, fresh_key_value, kv_pool, out_weight))
        projected = lax.psum(projected, "kv")
        mixed, norms, top, slabs, comb = pl.pallas_call(
            functools.partial(route_kernel, capacity),
            out_shape=routed_shapes,
            in_specs=vmem(5),
            out_specs=vmem(5),
        )(projected, hidden, norm_gain, router_weight, expert_ids)

    stored = kv_pool.size + expert_gate_up.size + expert_down.size
    new_pool, kept_up, kept_down = pl.pallas_call(
        store_kernel,
        out_shape=[like(array) for array in (kv_pool.shape, expert_gate_up.shape[1:], expert_down.shape[1:])],
        in_specs=vmem(2) + in_hbm(2),
        out_specs=in_hbm(1) + vmem(2),
        scratch_shapes=[pltpu.SemaphoreType.DMA((4,))],
        compiler_params=pltpu.CompilerParams(vmem_limit_bytes=24 * MIB),
        cost_estimate=pl.CostEstimate(flops=0, bytes_accessed=4 * stored, transcendentals=0),
    )(keys, values, *pinned(expert_gate_up, expert_down))

    same_part = [list(range(part, req_count, copies)) for part in range(copies)]
    swap = [(index, index ^ 1) for index in range(req_count)]

    def exchange(array):
        array = array.reshape(experts, SLAB, piece)
        array = lax.all_to_all(
            array, "req", split_axis=0, concat_axis=0, tiled=True, axis_index_groups=same_part
        )
        return array.reshape(slab_rows, piece)

    arrived = exchange(slabs)
    partner = lax.ppermute(arrived, "req", swap)
    kept = experts * capacity
    own_terms, partner_terms = pl.pallas_call(
        functools.partial(expert_kernel, capacity),
        out_shape=[like((kept, width))] * 2,
        in_specs=vmem(4),
        out_specs=vmem(2),
        scratch_shapes=[pltpu.VMEM((2 * kept, width), BF16), pltpu.VMEM((2 * kept, width), F32)],
        compiler_params=pltpu.CompilerParams(vmem_limit_bytes=28 * MIB),
    )(arrived, partner, kept_up, kept_down)
    swapped = lax.ppermute(partner_terms, "req", swap)
    leaving = pl.pallas_call(
        functools.partial(merge_kernel, capacity),
        out_shape=like((slab_rows, piece)),
        in_specs=vmem(2),
        out_specs=pl.BlockSpec(memory_space=pltpu.VMEM),
        compiler_params=pltpu.CompilerParams(vmem_limit_bytes=8 * MIB),
    )(own_terms, swapped)
    returned = exchange(leaving)
    if kv_count == 1:
        out_hidden = pl.pallas_call(
            functools.partial(combine_kernel, capacity),
            out_shape=like((requests, width)),
            in_specs=vmem(3),
            out_specs=pl.BlockSpec(memory_space=pltpu.VMEM),
            compiler_params=pltpu.CompilerParams(vmem_limit_bytes=8 * MIB),
        )(comb, returned, mixed)
    else:
        routed = pl.pallas_call(
            functools.partial(gather_kernel, capacity),
            out_shape=like((requests, width)),
            in_specs=vmem(2),
            out_specs=pl.BlockSpec(memory_space=pltpu.VMEM),
        )(comb, returned)
        routed = lax.psum(routed, "kv").astype(F32)
        out_hidden = (mixed.astype(F32) + routed).astype(BF16)
    return out_hidden, new_pool, norms.reshape(requests), top.reshape(requests)


def solution(mesh):
    in_specs = (
        P("req", None),
        P("req", "kv"),
        P("req", "kv", None),
        P("req", None, "kv", None),
        P("req", None),
        P("req"),
        P("kv", None),
        P(),
        P(),
        P("req", None),
        P("req", None, "kv", None),
        P("req", "kv", None),
    )
    out_specs = (P("req", None), P("req", None, "kv", None), P("req"), P("req"))
    return jax.shard_map(body, mesh=mesh, in_specs=in_specs, out_specs=out_specs, check_vma=False)
```

```python
import functools
import math

import jax
import jax.numpy as jnp
from jax import lax
from jax.experimental import pallas as pl
from jax.experimental.pallas import tpu as pltpu
from jax.sharding import PartitionSpec as P

BF16 = jnp.bfloat16
F32 = jnp.float32
NT = (((1,), (1,)), ((), ()))
NN = (((1,), (0,)), ((), ()))
SLAB = 16
MIB = 1 << 20


def dot(a, b, dims=NN, precision=None):
    return lax.dot_general(a, b, dims, precision=precision, preferred_element_type=F32)


def iota(shape, dim):
    return lax.broadcasted_iota(jnp.int32, shape, dim)


def copies(pairs, sems, first=0):
    return [pltpu.make_async_copy(src, dst, sems.at[first + i]) for i, (src, dst) in enumerate(pairs)]


def pool_half(array, i):
    head_dim = array.shape[3] // 2
    return array.at[:, :, :, pl.ds(i * head_dim, head_dim)]


def attend(refs, keys, values, scratch):
    small, (kept_weight, qs, att, probs, sums, sems) = scratch
    table, lengths, q_ref, fresh = small[:4]
    requests, max_pages = table.shape
    pages, page_len, heads_kv, head_dim = keys.shape
    heads = q_ref.shape[1] // head_dim
    group = heads // heads_kv
    page_rows = page_len * heads_kv
    pool, weight = refs[-2:]
    loads = copies(list(zip(refs[:4], small[:4])), sems)
    key_load, value_load, weight_load = copies(
        [(pool_half(pool, 0), keys), (pool_half(pool, 1), values), (weight, kept_weight)], sems, 4
    )
    later = copies(list(zip(refs[4:-2], small[4:])), sems, 7)
    for copy in loads + [key_load, value_load] + later + [weight_load]:
        copy.start()
    for copy in loads:
        copy.wait()
    for h in range(heads):
        qs[pl.ds(h * requests, requests), :] = q_ref[:, pl.ds(h * head_dim, head_dim)].astype(F32)
    spots = [(table[r, lengths[r] // page_len], lengths[r] % page_len) for r in range(requests)]

    key_load.wait()
    for r, (page, slot) in enumerate(spots):
        keys[page, slot] = fresh[r][:, :head_dim]
    key_pages = keys.reshape(pages, page_rows, head_dim)
    value_pages = values.reshape(pages, page_rows, head_dim)
    columns = max_pages * page_rows
    lane = iota((heads, columns), 1)
    own_head = lane % heads_kv == iota((heads, columns), 0) // group
    position = lane // heads_kv
    for r in range(requests):
        query = qs[pl.ds(r, heads, stride=requests), :].astype(BF16)
        gathered = jnp.concatenate([key_pages[table[r, j]] for j in range(max_pages)], axis=0)
        scores = dot(query, gathered, NT) * (1.0 / math.sqrt(head_dim))
        scores = jnp.where(own_head & (position <= lengths[r]), scores, -1e30)
        exponent = jnp.exp(scores - jnp.max(scores, axis=1, keepdims=True))
        sums[r] = jnp.broadcast_to(jnp.sum(exponent, axis=1, keepdims=True), (heads, head_dim))
        probs[r] = exponent.astype(BF16)

    value_load.wait()
    for r, (page, slot) in enumerate(spots):
        values[page, slot] = fresh[r][:, head_dim:]
    for r in range(requests):
        gathered = jnp.concatenate([value_pages[table[r, j]] for j in range(max_pages)], axis=0)
        att[pl.ds(r, heads, stride=requests), :] = dot(probs[r], gathered) / sums[r]
    attended = jnp.concatenate(
        [att[pl.ds(h * requests, requests), :] for h in range(heads)], axis=1
    ).astype(BF16)
    weight_load.wait()
    projected = dot(attended, kept_weight[...])
    for copy in later:
        copy.wait()
    return projected


def route(projected, hidden, gain, router, ids, mixed_ref, norms_ref, top_ref, slabs_ref, comb_ref, capacity):
    requests, width = hidden.shape
    experts = router.shape[0]
    parts = SLAB // capacity
    piece = width // parts
    slab_rows = experts * SLAB
    mixed = (hidden[...].astype(F32) + projected).astype(BF16)
    mixed_ref[...] = mixed
    mixed = mixed.astype(F32)
    norms = jnp.sqrt(jnp.mean(mixed * mixed, axis=1, keepdims=True) + 1e-06)
    norms_ref[...] = norms
    normed = (mixed / norms * gain[...].astype(F32).reshape(1, width)).astype(BF16)
    logits = dot(normed, router[...], NT)
    top_ref[...] = jnp.max(logits, axis=1, keepdims=True)
    column = iota((requests, experts), 1)
    named = column < 0
    for k in range(ids.shape[1]):
        named = named | (ids[:, k : k + 1] == column)
    weights = jnp.where(named, jnp.exp(logits), 0.0)
    weights = weights / jnp.sum(weights, axis=1, keepdims=True)
    earlier = (iota((requests, requests), 1) < iota((requests, requests), 0)).astype(F32)
    rank = dot(earlier, named.astype(F32))
    place = jnp.where(named, rank, -1.0)
    normed = normed.astype(F32)
    stacked = jnp.concatenate([normed[:, p * piece : (p + 1) * piece] for p in range(parts)], axis=0)
    places = jnp.concatenate([place] * parts, axis=0)
    shape = (slab_rows, parts * requests)
    inner = iota(shape, 0) % SLAB
    spread = (iota((slab_rows, experts), 0) // SLAB == iota((slab_rows, experts), 1)).astype(F32)
    picks = (dot(spread, places, NT) == (inner // parts).astype(F32)) & (
        inner % parts == iota(shape, 1) // requests
    )
    slabs_ref[...] = dot(picks.astype(BF16), stacked.astype(BF16)).astype(BF16)
    shape = (experts, slab_rows)
    spread = (iota(shape, 1) // SLAB == iota(shape, 0)).astype(F32)
    inner = iota((requests, slab_rows), 1) % SLAB
    comb_ref[...] = jnp.where(
        dot(place, spread) == (inner // parts).astype(F32),
        dot(weights, spread, precision=lax.Precision.HIGHEST),
        0.0,
    )


def attend_route_kernel(capacity, *refs):
    inputs, (keys, values, mixed, norms, top, slabs, comb) = refs[:10], refs[10:17]
    small, scratch = refs[17:25], refs[25:]
    projected = attend(inputs, keys, values, (small, scratch))
    hidden, gain, router, ids = small[4:]
    route(projected, hidden, gain, router, ids, mixed, norms, top, slabs, comb, capacity)


def attend_kernel(*refs):
    keys, values, projected = refs[6:9]
    projected[...] = attend(refs[:6], keys, values, (refs[9:13], refs[13:]))


def store_kernel(keys, values, gate_up, down, new_pool, kept_up, kept_down, sems):
    moves = copies(
        [
            (gate_up.at[0], kept_up),
            (down.at[0], kept_down),
            (keys, pool_half(new_pool, 0)),
            (values, pool_half(new_pool, 1)),
        ],
        sems,
    )
    for copy in moves:
        copy.start()
    for copy in moves:
        copy.wait()


def route_kernel(capacity, projected, hidden, gain, router, ids, mixed, norms, top, slabs, comb):
    route(projected[...], hidden, gain, router, ids, mixed, norms, top, slabs, comb, capacity)


def unit_chunks(units):
    return [(start, min(256, units - start)) for start in range(0, units, 256)]


def expert_kernel(capacity, arrived, own_up, own_down, other_up, other_down, slabs, rows, total):
    parts = SLAB // capacity
    piece = slabs.shape[1]
    block = 128
    each = block // parts
    blocks = slabs.shape[0] // block
    shape = (block, block)
    slab_row, sorted_row = iota(shape, 1), iota(shape, 0)
    sort = (slab_row == sorted_row % each * parts + sorted_row // each).astype(BF16)
    for i in range(blocks):
        sorted_rows = dot(sort, arrived[pl.ds(i * block, block), :]).astype(BF16)
        rows[pl.ds(i * each, each), :] = jnp.concatenate(
            [sorted_rows[p * each : (p + 1) * each] for p in range(parts)], axis=1
        )
    states = rows[...]
    first = True
    for gate_up, down in ((own_up, own_down), (other_up.at[0], other_down.at[0])):
        for start, size in unit_chunks(down.shape[0]):
            span = pl.ds(start, size)
            gate = dot(states, gate_up[0, span, :], NT)
            up = dot(states, gate_up[1, span, :], NT)
            activated = (gate / (1.0 + jnp.exp(-gate)) * up).astype(BF16)
            term = dot(activated, down[span, :])
            total[...] = term if first else total[...] + term
            first = False
    slab_row, sorted_row = iota(shape, 0), iota(shape, 1)
    unsort = (slab_row == sorted_row % each * parts + sorted_row // each).astype(BF16)
    for i in range(blocks):
        summed = total[pl.ds(i * each, each), :].astype(BF16)
        stacked = jnp.concatenate([summed[:, p * piece : (p + 1) * piece] for p in range(parts)], axis=0)
        slabs[pl.ds(i * block, block), :] = dot(unsort, stacked).astype(BF16)


def gather_terms(comb, slabs, capacity):
    parts = SLAB // capacity
    requests = comb.shape[0]
    weights = comb[...]
    pieces = []
    for _ in range(3):
        piece = weights.astype(BF16).astype(F32)
        weights = weights - piece
        pieces.append(piece)
    part = iota(comb.shape, 1) % parts
    stacked = jnp.concatenate(
        [jnp.where(part == p, piece, 0.0) for p in range(parts) for piece in pieces], axis=0
    ).astype(BF16)
    terms = dot(stacked, slabs[...])
    return jnp.concatenate(
        [
            sum(terms[(3 * p + i) * requests : (3 * p + i + 1) * requests] for i in range(3))
            for p in range(parts)
        ],
        axis=1,
    )


def combine_kernel(capacity, comb, slabs, mixed, out):
    out[...] = (mixed[...].astype(F32) + gather_terms(comb, slabs, capacity)).astype(BF16)


def gather_kernel(capacity, comb, slabs, out):
    out[...] = gather_terms(comb, slabs, capacity).astype(BF16)


def vmem(count):
    return [pl.BlockSpec(memory_space=pltpu.VMEM)] * count


def in_hbm(count):
    return [pl.BlockSpec(memory_space=pltpu.HBM)] * count


def pinned(*arrays):
    return [pltpu.with_memory_space_constraint(array, pltpu.HBM) for array in arrays]


def like(shape, dtype=BF16):
    return jax.ShapeDtypeStruct(shape, dtype)


def body(
    hidden,
    queries,
    fresh_key_value,
    kv_pool,
    page_table,
    lengths,
    out_weight,
    norm_gain,
    router_weight,
    expert_ids,
    expert_gate_up,
    expert_down,
):
    requests, width = hidden.shape
    req_count, kv_count = lax.axis_size("req"), lax.axis_size("kv")
    pages, page_len, heads_kv, pair_dim = kv_pool.shape
    head_dim = pair_dim // 2
    heads = queries.shape[1] // head_dim
    experts = router_weight.shape[0]
    copies = req_count // experts
    chosen = expert_ids.shape[1]
    capacity = 2 * max(1, (requests * chosen + 2 * experts - 1) // (2 * experts))
    parts = SLAB // capacity
    piece = width // parts
    slab_rows = experts * SLAB

    same_part = [list(range(part, req_count, copies)) for part in range(copies)]
    swap = [(index, index ^ 1) for index in range(req_count)]
    other_up = lax.ppermute(expert_gate_up, "req", swap)
    other_down = lax.ppermute(expert_down, "req", swap)

    attend_scratch = [
        pltpu.VMEM(out_weight.shape, BF16),
        pltpu.VMEM((heads * requests, head_dim), F32),
        pltpu.VMEM((heads * requests, head_dim), F32),
        pltpu.VMEM((requests, heads, page_table.shape[1] * page_len * heads_kv), BF16),
        pltpu.VMEM((requests, heads, head_dim), F32),
        pltpu.SemaphoreType.DMA((11,)),
    ]

    def small(*arrays):
        return [pltpu.VMEM(array.shape, array.dtype) for array in arrays]

    inputs = [pltpu.SMEM(page_table.shape, jnp.int32), pltpu.SMEM(lengths.shape, jnp.int32)]
    inputs += small(queries, fresh_key_value)
    kept_shapes = [like((pages, page_len, heads_kv, head_dim))] * 2
    routed_shapes = [
        like((requests, width)),
        like((requests, 1), F32),
        like((requests, 1), F32),
        like((slab_rows, piece)),
        like((requests, slab_rows), F32),
    ]
    attend_params = pltpu.CompilerParams(vmem_limit_bytes=20 * MIB)
    if kv_count == 1:
        keys, values, mixed, norms, top, slabs, comb = pl.pallas_call(
            functools.partial(attend_route_kernel, capacity),
            out_shape=kept_shapes + routed_shapes,
            in_specs=in_hbm(10),
            out_specs=vmem(7),
            scratch_shapes=inputs + small(hidden, norm_gain, router_weight, expert_ids) + attend_scratch,
            compiler_params=attend_params,
        )(*pinned(page_table, lengths, queries, fresh_key_value, hidden, norm_gain, router_weight, expert_ids,
                  kv_pool, out_weight))
    else:
        keys, values, projected = pl.pallas_call(
            attend_kernel,
            out_shape=kept_shapes + [like((requests, width), F32)],
            in_specs=in_hbm(6),
            out_specs=vmem(3),
            scratch_shapes=inputs + attend_scratch,
            compiler_params=attend_params,
        )(*pinned(page_table, lengths, queries, fresh_key_value, kv_pool, out_weight))
        projected = lax.psum(projected, "kv")
        mixed, norms, top, slabs, comb = pl.pallas_call(
            functools.partial(route_kernel, capacity),
            out_shape=routed_shapes,
            in_specs=vmem(5),
            out_specs=vmem(5),
        )(projected, hidden, norm_gain, router_weight, expert_ids)

    stored = kv_pool.size + expert_gate_up.size + expert_down.size
    new_pool, kept_up, kept_down = pl.pallas_call(
        store_kernel,
        out_shape=[like(array) for array in (kv_pool.shape, expert_gate_up.shape[1:], expert_down.shape[1:])],
        in_specs=vmem(2) + in_hbm(2),
        out_specs=in_hbm(1) + vmem(2),
        scratch_shapes=[pltpu.SemaphoreType.DMA((4,))],
        compiler_params=pltpu.CompilerParams(vmem_limit_bytes=4 * MIB),
        cost_estimate=pl.CostEstimate(flops=0, bytes_accessed=4 * stored, transcendentals=0),
    )(keys, values, *pinned(expert_gate_up, expert_down))

    def exchange(array):
        array = array.reshape(experts, SLAB, piece)
        array = lax.all_to_all(
            array, "req", split_axis=0, concat_axis=0, tiled=True, axis_index_groups=same_part
        )
        return array.reshape(slab_rows, piece)

    arrived = exchange(slabs)
    kept = experts * capacity
    leaving = pl.pallas_call(
        functools.partial(expert_kernel, capacity),
        out_shape=like((slab_rows, piece)),
        in_specs=vmem(5),
        out_specs=pl.BlockSpec(memory_space=pltpu.VMEM),
        scratch_shapes=[pltpu.VMEM((kept, width), BF16), pltpu.VMEM((kept, width), F32)],
        compiler_params=pltpu.CompilerParams(vmem_limit_bytes=12 * MIB),
    )(arrived, kept_up, kept_down, other_up, other_down)
    returned = exchange(leaving)
    if kv_count == 1:
        out_hidden = pl.pallas_call(
            functools.partial(combine_kernel, capacity),
            out_shape=like((requests, width)),
            in_specs=vmem(3),
            out_specs=pl.BlockSpec(memory_space=pltpu.VMEM),
            compiler_params=pltpu.CompilerParams(vmem_limit_bytes=8 * MIB),
        )(comb, returned, mixed)
    else:
        routed = pl.pallas_call(
            functools.partial(gather_kernel, capacity),
            out_shape=like((requests, width)),
            in_specs=vmem(2),
            out_specs=pl.BlockSpec(memory_space=pltpu.VMEM),
        )(comb, returned)
        routed = lax.psum(routed, "kv").astype(F32)
        out_hidden = (mixed.astype(F32) + routed).astype(BF16)
    return out_hidden, new_pool, norms.reshape(requests), top.reshape(requests)


def solution(mesh):
    in_specs = (
        P("req", None),
        P("req", "kv"),
        P("req", "kv", None),
        P("req", None, "kv", None),
        P("req", None),
        P("req"),
        P("kv", None),
        P(),
        P(),
        P("req", None),
        P("req", None, "kv", None),
        P("req", "kv", None),
    )
    out_specs = (P("req", None), P("req", None, "kv", None), P("req"), P("req"))
    return jax.shard_map(body, mesh=mesh, in_specs=in_specs, out_specs=out_specs, check_vma=False)
```

```python
import functools
import math

import jax
import jax.numpy as jnp
from jax import lax
from jax.experimental import pallas as pl
from jax.experimental.pallas import tpu as pltpu
from jax.sharding import PartitionSpec as P

BF16 = jnp.bfloat16
F32 = jnp.float32
NT = (((1,), (1,)), ((), ()))
NN = (((1,), (0,)), ((), ()))
SLAB = 16
MIB = 1 << 20


def dot(a, b, dims=NN, precision=None):
    return lax.dot_general(a, b, dims, precision=precision, preferred_element_type=F32)


def iota(shape, dim):
    return lax.broadcasted_iota(jnp.int32, shape, dim)


def copies(pairs, sems, first=0):
    return [pltpu.make_async_copy(src, dst, sems.at[first + i]) for i, (src, dst) in enumerate(pairs)]


def pool_half(array, i):
    head_dim = array.shape[3] // 2
    return array.at[:, :, :, pl.ds(i * head_dim, head_dim)]


def attend(refs, keys, values, scratch):
    small, (kept_weight, qs, att, probs, sums, sems) = scratch
    table, lengths, q_ref, fresh = small[:4]
    requests, max_pages = table.shape
    pages, page_len, heads_kv, head_dim = keys.shape
    heads = q_ref.shape[1] // head_dim
    group = heads // heads_kv
    page_rows = page_len * heads_kv
    pool, weight = refs[-2:]
    loads = copies(list(zip(refs[:4], small[:4])), sems)
    key_load, value_load, weight_load = copies(
        [(pool_half(pool, 0), keys), (pool_half(pool, 1), values), (weight, kept_weight)], sems, 4
    )
    later = copies(list(zip(refs[4:-2], small[4:])), sems, 7)
    for copy in loads + [key_load, value_load] + later + [weight_load]:
        copy.start()
    for copy in loads:
        copy.wait()
    for h in range(heads):
        qs[pl.ds(h * requests, requests), :] = q_ref[:, pl.ds(h * head_dim, head_dim)].astype(F32)
    spots = [(table[r, lengths[r] // page_len], lengths[r] % page_len) for r in range(requests)]

    key_load.wait()
    for r, (page, slot) in enumerate(spots):
        keys[page, slot] = fresh[r][:, :head_dim]
    key_pages = keys.reshape(pages, page_rows, head_dim)
    value_pages = values.reshape(pages, page_rows, head_dim)
    columns = max_pages * page_rows
    lane = iota((heads, columns), 1)
    own_head = lane % heads_kv == iota((heads, columns), 0) // group
    position = lane // heads_kv
    for r in range(requests):
        query = qs[pl.ds(r, heads, stride=requests), :].astype(BF16)
        gathered = jnp.concatenate([key_pages[table[r, j]] for j in range(max_pages)], axis=0)
        scores = dot(query, gathered, NT) * (1.0 / math.sqrt(head_dim))
        scores = jnp.where(own_head & (position <= lengths[r]), scores, -1e30)
        exponent = jnp.exp(scores - jnp.max(scores, axis=1, keepdims=True))
        sums[r] = jnp.broadcast_to(jnp.sum(exponent, axis=1, keepdims=True), (heads, head_dim))
        probs[r] = exponent.astype(BF16)

    value_load.wait()
    for r, (page, slot) in enumerate(spots):
        values[page, slot] = fresh[r][:, head_dim:]
    for r in range(requests):
        gathered = jnp.concatenate([value_pages[table[r, j]] for j in range(max_pages)], axis=0)
        att[pl.ds(r, heads, stride=requests), :] = dot(probs[r], gathered) / sums[r]
    attended = jnp.concatenate(
        [att[pl.ds(h * requests, requests), :] for h in range(heads)], axis=1
    ).astype(BF16)
    weight_load.wait()
    projected = dot(attended, kept_weight[...])
    for copy in later:
        copy.wait()
    return projected


def route(projected, hidden, gain, router, ids, mixed_ref, norms_ref, top_ref, slabs_ref, comb_ref, capacity, leave=None):
    requests, width = hidden.shape
    experts = router.shape[0]
    parts = SLAB // capacity
    piece = width // parts
    slab_rows = experts * SLAB
    mixed = (hidden[...].astype(F32) + projected).astype(BF16)
    mixed_ref[...] = mixed
    mixed = mixed.astype(F32)
    norms = jnp.sqrt(jnp.mean(mixed * mixed, axis=1, keepdims=True) + 1e-06)
    norms_ref[...] = norms
    normed = (mixed / norms * gain[...].astype(F32).reshape(1, width)).astype(BF16)
    logits = dot(normed, router[...], NT)
    top_ref[...] = jnp.max(logits, axis=1, keepdims=True)
    column = iota((requests, experts), 1)
    named = column < 0
    for k in range(ids.shape[1]):
        named = named | (ids[:, k : k + 1] == column)
    weights = jnp.where(named, jnp.exp(logits), 0.0)
    weights = weights / jnp.sum(weights, axis=1, keepdims=True)
    earlier = (iota((requests, requests), 1) < iota((requests, requests), 0)).astype(F32)
    rank = dot(earlier, named.astype(F32))
    place = jnp.where(named, rank, -1.0)
    normed = normed.astype(F32)
    stacked = jnp.concatenate([normed[:, p * piece : (p + 1) * piece] for p in range(parts)], axis=0)
    places = jnp.concatenate([place] * parts, axis=0)
    shape = (slab_rows, parts * requests)
    inner = iota(shape, 0) % SLAB
    spread = (iota((slab_rows, experts), 0) // SLAB == iota((slab_rows, experts), 1)).astype(F32)
    picks = (dot(spread, places, NT) == (inner // parts).astype(F32)) & (
        inner % parts == iota(shape, 1) // requests
    )
    slabs_ref[...] = dot(picks.astype(BF16), stacked.astype(BF16)).astype(BF16)
    if leave is not None:
        leave()
    shape = (experts, slab_rows)
    spread = (iota(shape, 1) // SLAB == iota(shape, 0)).astype(F32)
    inner = iota((requests, slab_rows), 1) % SLAB
    comb_ref[...] = jnp.where(
        dot(place, spread) == (inner // parts).astype(F32),
        dot(weights, spread, precision=lax.Precision.HIGHEST),
        0.0,
    )


def attend_route_kernel(capacity, *refs):
    inputs, (mixed, norms, top, slabs, comb) = refs[:10], refs[10:15]
    small, scratch = refs[15:23], refs[23:]
    keys, values, kept_slabs = scratch[:3]
    projected = attend(inputs, keys, values, (small, scratch[3:]))
    hidden, gain, router, ids = small[4:]
    leave = pltpu.make_async_copy(kept_slabs, slabs, scratch[-1].at[0])
    route(projected, hidden, gain, router, ids, mixed, norms, top, kept_slabs, comb, capacity, leave.start)
    leave.wait()


def attend_kernel(*refs):
    attended, scratch = refs[6], refs[11:]
    attended[...] = attend(refs[:6], scratch[0], scratch[1], (refs[7:11], scratch[2:]))


def refresh_kernel(table, lengths, fresh, after, pool, new_pool, kept, sems):
    pages, page_len = kept.shape[:2]
    step = -(-pages // 4)
    spans = [pl.ds(start, min(step, pages - start)) for start in range(0, pages, step)]
    loads = copies([(pool.at[span], kept.at[span]) for span in spans], sems)
    stores = copies([(kept.at[span], new_pool.at[span]) for span in spans], sems, len(spans))
    for copy in loads:
        copy.start()
    for copy in loads:
        copy.wait()
    for r in range(table.shape[0]):
        kept[table[r, lengths[r] // page_len], lengths[r] % page_len] = fresh[r]
    for copy in stores:
        copy.start()
    for copy in stores:
        copy.wait()


def route_kernel(capacity, projected, hidden, gain, router, ids, mixed, norms, top, slabs, comb):
    route(projected[...], hidden, gain, router, ids, mixed, norms, top, slabs, comb, capacity)


def unit_chunks(units):
    return [(start, min(256, units - start)) for start in range(0, units, 256)]


def expert_kernel(capacity, arrived, own_up, own_down, other_up, other_down, slabs,
                  slab_rows, kept_up, kept_down, rows, total, sems):
    units = kept_down.shape[1]
    arrive = pltpu.make_async_copy(arrived, slab_rows, sems.at[0])
    arrive.start()
    chunks = []
    for half, (gate_up, down) in enumerate(((own_up, own_down), (other_up, other_down))):
        for start, size in unit_chunks(units):
            span = pl.ds(start, size)
            chunks.append((half, span, copies(
                [
                    (gate_up.at[0, :, span, :], kept_up.at[half, :, span, :]),
                    (down.at[0, span, :], kept_down.at[half, span, :]),
                ],
                sems,
                1 + 2 * len(chunks),
            )))
    for _, _, loads in chunks:
        for copy in loads:
            copy.start()
    arrive.wait()
    parts = SLAB // capacity
    piece = slabs.shape[1]
    block = 128
    each = block // parts
    blocks = slabs.shape[0] // block
    shape = (block, block)
    slab_row, sorted_row = iota(shape, 1), iota(shape, 0)
    sort = (slab_row == sorted_row % each * parts + sorted_row // each).astype(BF16)
    for i in range(blocks):
        sorted_rows = dot(sort, slab_rows[pl.ds(i * block, block), :]).astype(BF16)
        rows[pl.ds(i * each, each), :] = jnp.concatenate(
            [sorted_rows[p * each : (p + 1) * each] for p in range(parts)], axis=1
        )
    states = rows[...]
    for i, (half, span, loads) in enumerate(chunks):
        for copy in loads:
            copy.wait()
        gate = dot(states, kept_up[half, 0, span, :], NT)
        up = dot(states, kept_up[half, 1, span, :], NT)
        activated = (gate / (1.0 + jnp.exp(-gate)) * up).astype(BF16)
        term = dot(activated, kept_down[half, span, :])
        total[...] = term if i == 0 else total[...] + term
    slab_row, sorted_row = iota(shape, 0), iota(shape, 1)
    unsort = (slab_row == sorted_row % each * parts + sorted_row // each).astype(BF16)
    for i in range(blocks):
        summed = total[pl.ds(i * each, each), :].astype(BF16)
        stacked = jnp.concatenate([summed[:, p * piece : (p + 1) * piece] for p in range(parts)], axis=0)
        slabs[pl.ds(i * block, block), :] = dot(unsort, stacked).astype(BF16)


def gather_terms(comb, slabs, capacity):
    parts = SLAB // capacity
    requests = comb.shape[0]
    weights = comb[...]
    pieces = []
    for _ in range(3):
        piece = weights.astype(BF16).astype(F32)
        weights = weights - piece
        pieces.append(piece)
    part = iota(comb.shape, 1) % parts
    stacked = jnp.concatenate(
        [jnp.where(part == p, piece, 0.0) for p in range(parts) for piece in pieces], axis=0
    ).astype(BF16)
    terms = dot(stacked, slabs[...])
    return jnp.concatenate(
        [
            sum(terms[(3 * p + i) * requests : (3 * p + i + 1) * requests] for i in range(3))
            for p in range(parts)
        ],
        axis=1,
    )


def combine_kernel(capacity, comb, slabs, mixed, out):
    out[...] = (mixed[...].astype(F32) + gather_terms(comb, slabs, capacity)).astype(BF16)


def gather_kernel(capacity, comb, slabs, out):
    out[...] = gather_terms(comb, slabs, capacity).astype(BF16)


def vmem(count):
    return [pl.BlockSpec(memory_space=pltpu.VMEM)] * count


def scalars(count):
    return [pl.BlockSpec(memory_space=pltpu.SMEM)] * count


def in_hbm(count):
    return [pl.BlockSpec(memory_space=pltpu.HBM)] * count


def pinned(*arrays):
    return [pltpu.with_memory_space_constraint(array, pltpu.HBM) for array in arrays]


def like(shape, dtype=BF16):
    return jax.ShapeDtypeStruct(shape, dtype)


def body(
    hidden,
    queries,
    fresh_key_value,
    kv_pool,
    page_table,
    lengths,
    out_weight,
    norm_gain,
    router_weight,
    expert_ids,
    expert_gate_up,
    expert_down,
):
    requests, width = hidden.shape
    req_count, kv_count = lax.axis_size("req"), lax.axis_size("kv")
    pages, page_len, heads_kv, pair_dim = kv_pool.shape
    head_dim = pair_dim // 2
    heads = queries.shape[1] // head_dim
    experts = router_weight.shape[0]
    copies = req_count // experts
    chosen = expert_ids.shape[1]
    capacity = 2 * max(1, (requests * chosen + 2 * experts - 1) // (2 * experts))
    parts = SLAB // capacity
    piece = width // parts
    slab_rows = experts * SLAB

    same_part = [list(range(part, req_count, copies)) for part in range(copies)]
    swap = [(index, index ^ 1) for index in range(req_count)]
    other_up = lax.ppermute(expert_gate_up, "req", swap)
    other_down = lax.ppermute(expert_down, "req", swap)

    attend_scratch = [
        pltpu.VMEM((pages, page_len, heads_kv, head_dim), BF16),
        pltpu.VMEM((pages, page_len, heads_kv, head_dim), BF16),
        pltpu.VMEM(out_weight.shape, BF16),
        pltpu.VMEM((heads * requests, head_dim), F32),
        pltpu.VMEM((heads * requests, head_dim), F32),
        pltpu.VMEM((requests, heads, page_table.shape[1] * page_len * heads_kv), BF16),
        pltpu.VMEM((requests, heads, head_dim), F32),
        pltpu.SemaphoreType.DMA((11,)),
    ]

    def small(*arrays):
        return [pltpu.VMEM(array.shape, array.dtype) for array in arrays]

    inputs = [pltpu.SMEM(page_table.shape, jnp.int32), pltpu.SMEM(lengths.shape, jnp.int32)]
    inputs += small(queries, fresh_key_value)
    routed_shapes = [
        like((requests, width)),
        like((requests, 1), F32),
        like((requests, 1), F32),
        like((slab_rows, piece)),
        like((requests, slab_rows), F32),
    ]
    attend_params = pltpu.CompilerParams(vmem_limit_bytes=24 * MIB)
    if kv_count == 1:
        attend_scratch.insert(2, pltpu.VMEM((slab_rows, piece), BF16))
        mixed, norms, top, slabs, comb = pl.pallas_call(
            functools.partial(attend_route_kernel, capacity),
            out_shape=routed_shapes,
            in_specs=in_hbm(10),
            out_specs=vmem(3) + in_hbm(1) + vmem(1),
            scratch_shapes=inputs + small(hidden, norm_gain, router_weight, expert_ids) + attend_scratch,
            compiler_params=attend_params,
        )(*pinned(page_table, lengths, queries, fresh_key_value, hidden, norm_gain, router_weight, expert_ids,
                  kv_pool, out_weight))
    else:
        projected = pl.pallas_call(
            attend_kernel,
            out_shape=like((requests, width), F32),
            in_specs=in_hbm(6),
            out_specs=pl.BlockSpec(memory_space=pltpu.VMEM),
            scratch_shapes=inputs + attend_scratch,
            compiler_params=attend_params,
        )(*pinned(page_table, lengths, queries, fresh_key_value, kv_pool, out_weight))
        projected = lax.psum(projected, "kv")
        mixed, norms, top, slabs, comb = pl.pallas_call(
            functools.partial(route_kernel, capacity),
            out_shape=routed_shapes,
            in_specs=vmem(5),
            out_specs=vmem(5),
        )(projected, hidden, norm_gain, router_weight, expert_ids)

    new_pool = pl.pallas_call(
        refresh_kernel,
        out_shape=like(kv_pool.shape),
        in_specs=scalars(2) + vmem(1) + in_hbm(2),
        out_specs=pl.BlockSpec(memory_space=pltpu.HBM),
        scratch_shapes=[pltpu.VMEM(kv_pool.shape, BF16), pltpu.SemaphoreType.DMA((8,))],
        compiler_params=pltpu.CompilerParams(vmem_limit_bytes=12 * MIB),
        cost_estimate=pl.CostEstimate(flops=0, bytes_accessed=8 * kv_pool.size, transcendentals=0),
    )(page_table, lengths, fresh_key_value, top, *pinned(kv_pool))

    def exchange(array):
        array = array.reshape(experts, SLAB, piece)
        array = lax.all_to_all(
            array, "req", split_axis=0, concat_axis=0, tiled=True, axis_index_groups=same_part
        )
        return array.reshape(slab_rows, piece)

    arrived = exchange(slabs)
    kept = experts * capacity
    units = expert_down.shape[1]
    chunk_count = 2 * len(unit_chunks(units))
    leaving = pl.pallas_call(
        functools.partial(expert_kernel, capacity),
        out_shape=like((slab_rows, piece)),
        in_specs=in_hbm(5),
        out_specs=pl.BlockSpec(memory_space=pltpu.VMEM),
        scratch_shapes=[
            pltpu.VMEM((slab_rows, piece), BF16),
            pltpu.VMEM((2, 2, units, width), BF16),
            pltpu.VMEM((2, units, width), BF16),
            pltpu.VMEM((kept, width), BF16),
            pltpu.VMEM((kept, width), F32),
            pltpu.SemaphoreType.DMA((1 + 2 * chunk_count,)),
        ],
        compiler_params=pltpu.CompilerParams(vmem_limit_bytes=28 * MIB),
    )(arrived, *pinned(expert_gate_up, expert_down), other_up, other_down)
    returned = exchange(leaving)
    if kv_count == 1:
        out_hidden = pl.pallas_call(
            functools.partial(combine_kernel, capacity),
            out_shape=like((requests, width)),
            in_specs=vmem(3),
            out_specs=pl.BlockSpec(memory_space=pltpu.VMEM),
            compiler_params=pltpu.CompilerParams(vmem_limit_bytes=8 * MIB),
        )(comb, returned, mixed)
    else:
        routed = pl.pallas_call(
            functools.partial(gather_kernel, capacity),
            out_shape=like((requests, width)),
            in_specs=vmem(2),
            out_specs=pl.BlockSpec(memory_space=pltpu.VMEM),
        )(comb, returned)
        routed = lax.psum(routed, "kv").astype(F32)
        out_hidden = (mixed.astype(F32) + routed).astype(BF16)
    return out_hidden, new_pool, norms.reshape(requests), top.reshape(requests)


def solution(mesh):
    in_specs = (
        P("req", None),
        P("req", "kv"),
        P("req", "kv", None),
        P("req", None, "kv", None),
        P("req", None),
        P("req"),
        P("kv", None),
        P(),
        P(),
        P("req", None),
        P("req", None, "kv", None),
        P("req", "kv", None),
    )
    out_specs = (P("req", None), P("req", None, "kv", None), P("req"), P("req"))
    return jax.shard_map(body, mesh=mesh, in_specs=in_specs, out_specs=out_specs, check_vma=False)
```

```python
import functools
import math

import jax
import jax.numpy as jnp
from jax import lax
from jax.experimental import pallas as pl
from jax.experimental.pallas import tpu as pltpu
from jax.sharding import PartitionSpec as P

BF16 = jnp.bfloat16
F32 = jnp.float32
NT = (((1,), (1,)), ((), ()))
NN = (((1,), (0,)), ((), ()))
SLAB = 16
MIB = 1 << 20


def dot(a, b, dims=NN, precision=None):
    return lax.dot_general(a, b, dims, precision=precision, preferred_element_type=F32)


def iota(shape, dim):
    return lax.broadcasted_iota(jnp.int32, shape, dim)


def copies(pairs, sems, first=0):
    return [pltpu.make_async_copy(src, dst, sems.at[first + i]) for i, (src, dst) in enumerate(pairs)]


def pool_half(array, i):
    head_dim = array.shape[3] // 2
    return array.at[:, :, :, pl.ds(i * head_dim, head_dim)]


def attend(refs, keys, values, scratch):
    small, (kept_weight, qs, att, probs, sums, sems) = scratch
    table, lengths, q_ref, fresh = small[:4]
    requests, max_pages = table.shape
    pages, page_len, heads_kv, head_dim = keys.shape
    heads = q_ref.shape[1] // head_dim
    group = heads // heads_kv
    page_rows = page_len * heads_kv
    pool, weight = refs[-2:]
    loads = copies(list(zip(refs[:4], small[:4])), sems)
    key_load, value_load, weight_load = copies(
        [(pool_half(pool, 0), keys), (pool_half(pool, 1), values), (weight, kept_weight)], sems, 4
    )
    later = copies(list(zip(refs[4:-2], small[4:])), sems, 7)
    for copy in loads + [key_load, value_load] + later + [weight_load]:
        copy.start()
    for copy in loads:
        copy.wait()
    for h in range(heads):
        qs[pl.ds(h * requests, requests), :] = q_ref[:, pl.ds(h * head_dim, head_dim)].astype(F32)
    spots = [(table[r, lengths[r] // page_len], lengths[r] % page_len) for r in range(requests)]

    key_load.wait()
    for r, (page, slot) in enumerate(spots):
        keys[page, slot] = fresh[r][:, :head_dim]
    key_pages = keys.reshape(pages, page_rows, head_dim)
    value_pages = values.reshape(pages, page_rows, head_dim)
    columns = max_pages * page_rows
    lane = iota((heads, columns), 1)
    own_head = lane % heads_kv == iota((heads, columns), 0) // group
    position = lane // heads_kv
    for r in range(requests):
        query = qs[pl.ds(r, heads, stride=requests), :].astype(BF16)
        gathered = jnp.concatenate([key_pages[table[r, j]] for j in range(max_pages)], axis=0)
        scores = dot(query, gathered, NT) * (1.0 / math.sqrt(head_dim))
        scores = jnp.where(own_head & (position <= lengths[r]), scores, -1e30)
        exponent = jnp.exp(scores - jnp.max(scores, axis=1, keepdims=True))
        sums[r] = jnp.broadcast_to(jnp.sum(exponent, axis=1, keepdims=True), (heads, head_dim))
        probs[r] = exponent.astype(BF16)

    value_load.wait()
    for r, (page, slot) in enumerate(spots):
        values[page, slot] = fresh[r][:, head_dim:]
    for r in range(requests):
        gathered = jnp.concatenate([value_pages[table[r, j]] for j in range(max_pages)], axis=0)
        att[pl.ds(r, heads, stride=requests), :] = dot(probs[r], gathered) / sums[r]
    attended = jnp.concatenate(
        [att[pl.ds(h * requests, requests), :] for h in range(heads)], axis=1
    ).astype(BF16)
    weight_load.wait()
    projected = dot(attended, kept_weight[...])
    for copy in later:
        copy.wait()
    return projected


def route(projected, hidden, gain, router, ids, mixed_ref, norms_ref, top_ref, slabs_ref, comb_ref, capacity, leave=None):
    requests, width = hidden.shape
    experts = router.shape[0]
    parts = SLAB // capacity
    piece = width // parts
    slab_rows = experts * SLAB
    mixed = (hidden[...].astype(F32) + projected).astype(BF16)
    mixed_ref[...] = mixed
    mixed = mixed.astype(F32)
    norms = jnp.sqrt(jnp.mean(mixed * mixed, axis=1, keepdims=True) + 1e-06)
    norms_ref[...] = norms
    normed = (mixed / norms * gain[...].astype(F32).reshape(1, width)).astype(BF16)
    logits = dot(normed, router[...], NT)
    top_ref[...] = jnp.max(logits, axis=1, keepdims=True)
    column = iota((requests, experts), 1)
    named = column < 0
    for k in range(ids.shape[1]):
        named = named | (ids[:, k : k + 1] == column)
    weights = jnp.where(named, jnp.exp(logits), 0.0)
    weights = weights / jnp.sum(weights, axis=1, keepdims=True)
    earlier = (iota((requests, requests), 1) < iota((requests, requests), 0)).astype(F32)
    rank = dot(earlier, named.astype(F32))
    place = jnp.where(named, rank, -1.0)
    normed = normed.astype(F32)
    stacked = jnp.concatenate([normed[:, p * piece : (p + 1) * piece] for p in range(parts)], axis=0)
    places = jnp.concatenate([place] * parts, axis=0)
    shape = (slab_rows, parts * requests)
    inner = iota(shape, 0) % SLAB
    spread = (iota((slab_rows, experts), 0) // SLAB == iota((slab_rows, experts), 1)).astype(F32)
    picks = (dot(spread, places, NT) == (inner // parts).astype(F32)) & (
        inner % parts == iota(shape, 1) // requests
    )
    slabs_ref[...] = dot(picks.astype(BF16), stacked.astype(BF16)).astype(BF16)
    if leave is not None:
        leave()
    shape = (experts, slab_rows)
    spread = (iota(shape, 1) // SLAB == iota(shape, 0)).astype(F32)
    inner = iota((requests, slab_rows), 1) % SLAB
    comb_ref[...] = jnp.where(
        dot(place, spread) == (inner // parts).astype(F32),
        dot(weights, spread, precision=lax.Precision.HIGHEST),
        0.0,
    )


def attend_route_kernel(capacity, *refs):
    inputs, (mixed, norms, top, slabs, comb) = refs[:10], refs[10:15]
    small, scratch = refs[15:23], refs[23:]
    keys, values, kept_slabs = scratch[:3]
    projected = attend(inputs, keys, values, (small, scratch[3:]))
    hidden, gain, router, ids = small[4:]
    leave = pltpu.make_async_copy(kept_slabs, slabs, scratch[-1].at[0])
    route(projected, hidden, gain, router, ids, mixed, norms, top, kept_slabs, comb, capacity, leave.start)
    leave.wait()


def attend_kernel(*refs):
    attended, scratch = refs[6], refs[11:]
    attended[...] = attend(refs[:6], scratch[0], scratch[1], (refs[7:11], scratch[2:]))


def refresh_kernel(table, lengths, fresh, after, pool, new_pool, kept, sems):
    pages, page_len = kept.shape[:2]
    step = -(-pages // 4)
    spans = [pl.ds(start, min(step, pages - start)) for start in range(0, pages, step)]
    loads = copies([(pool.at[span], kept.at[span]) for span in spans], sems)
    stores = copies([(kept.at[span], new_pool.at[span]) for span in spans], sems, len(spans))
    for copy in loads:
        copy.start()
    for copy in loads:
        copy.wait()
    for r in range(table.shape[0]):
        kept[table[r, lengths[r] // page_len], lengths[r] % page_len] = fresh[r]
    for copy in stores:
        copy.start()
    for copy in stores:
        copy.wait()


def route_kernel(capacity, projected, hidden, gain, router, ids, mixed, norms, top, slabs, comb):
    route(projected[...], hidden, gain, router, ids, mixed, norms, top, slabs, comb, capacity)


def unit_chunks(units):
    return [(start, min(256, units - start)) for start in range(0, units, 256)]


def expert_kernel(capacity, arrived, own_up, own_down, other_up, other_down, slabs,
                  slab_rows, kept_up, kept_down, rows, total, sems):
    units = kept_down.shape[0]
    arrive = pltpu.make_async_copy(arrived, slab_rows, sems.at[0])
    arrive.start()
    chunks = []
    for i, (start, size) in enumerate(unit_chunks(units)):
        span = pl.ds(start, size)
        chunks.append((span, copies(
            [(own_up.at[0, :, span, :], kept_up.at[:, span, :]), (own_down.at[0, span, :], kept_down.at[span, :])],
            sems,
            1 + 2 * i,
        )))
    for _, loads in chunks:
        for copy in loads:
            copy.start()
    arrive.wait()
    parts = SLAB // capacity
    piece = slabs.shape[1]
    block = 128
    each = block // parts
    blocks = slabs.shape[0] // block
    shape = (block, block)
    slab_row, sorted_row = iota(shape, 1), iota(shape, 0)
    sort = (slab_row == sorted_row % each * parts + sorted_row // each).astype(BF16)
    for i in range(blocks):
        sorted_rows = dot(sort, slab_rows[pl.ds(i * block, block), :]).astype(BF16)
        rows[pl.ds(i * each, each), :] = jnp.concatenate(
            [sorted_rows[p * each : (p + 1) * each] for p in range(parts)], axis=1
        )
    states = rows[...]
    steps = [(other_up.at[0], other_down.at[0], span, []) for span, _ in chunks]
    steps += [(kept_up, kept_down, span, loads) for span, loads in chunks]
    for i, (gate_up, down, span, loads) in enumerate(steps):
        for copy in loads:
            copy.wait()
        gate = dot(states, gate_up[0, span, :], NT)
        up = dot(states, gate_up[1, span, :], NT)
        activated = (gate / (1.0 + jnp.exp(-gate)) * up).astype(BF16)
        term = dot(activated, down[span, :])
        total[...] = term if i == 0 else total[...] + term
    slab_row, sorted_row = iota(shape, 0), iota(shape, 1)
    unsort = (slab_row == sorted_row % each * parts + sorted_row // each).astype(BF16)
    for i in range(blocks):
        summed = total[pl.ds(i * each, each), :].astype(BF16)
        stacked = jnp.concatenate([summed[:, p * piece : (p + 1) * piece] for p in range(parts)], axis=0)
        slabs[pl.ds(i * block, block), :] = dot(unsort, stacked).astype(BF16)


def gather_terms(comb, slabs, capacity):
    parts = SLAB // capacity
    requests = comb.shape[0]
    weights = comb[...]
    pieces = []
    for _ in range(3):
        piece = weights.astype(BF16).astype(F32)
        weights = weights - piece
        pieces.append(piece)
    part = iota(comb.shape, 1) % parts
    stacked = jnp.concatenate(
        [jnp.where(part == p, piece, 0.0) for p in range(parts) for piece in pieces], axis=0
    ).astype(BF16)
    terms = dot(stacked, slabs[...])
    return jnp.concatenate(
        [
            sum(terms[(3 * p + i) * requests : (3 * p + i + 1) * requests] for i in range(3))
            for p in range(parts)
        ],
        axis=1,
    )


def combine_kernel(capacity, comb, slabs, mixed, out):
    out[...] = (mixed[...].astype(F32) + gather_terms(comb, slabs, capacity)).astype(BF16)


def gather_kernel(capacity, comb, slabs, out):
    out[...] = gather_terms(comb, slabs, capacity).astype(BF16)


def vmem(count):
    return [pl.BlockSpec(memory_space=pltpu.VMEM)] * count


def scalars(count):
    return [pl.BlockSpec(memory_space=pltpu.SMEM)] * count


def in_hbm(count):
    return [pl.BlockSpec(memory_space=pltpu.HBM)] * count


def pinned(*arrays):
    return [pltpu.with_memory_space_constraint(array, pltpu.HBM) for array in arrays]


def like(shape, dtype=BF16):
    return jax.ShapeDtypeStruct(shape, dtype)


def body(
    hidden,
    queries,
    fresh_key_value,
    kv_pool,
    page_table,
    lengths,
    out_weight,
    norm_gain,
    router_weight,
    expert_ids,
    expert_gate_up,
    expert_down,
):
    requests, width = hidden.shape
    req_count, kv_count = lax.axis_size("req"), lax.axis_size("kv")
    pages, page_len, heads_kv, pair_dim = kv_pool.shape
    head_dim = pair_dim // 2
    heads = queries.shape[1] // head_dim
    experts = router_weight.shape[0]
    copies = req_count // experts
    chosen = expert_ids.shape[1]
    capacity = 2 * max(1, (requests * chosen + 2 * experts - 1) // (2 * experts))
    parts = SLAB // capacity
    piece = width // parts
    slab_rows = experts * SLAB

    same_part = [list(range(part, req_count, copies)) for part in range(copies)]
    swap = [(index, index ^ 1) for index in range(req_count)]
    other_up = lax.ppermute(expert_gate_up, "req", swap)
    other_down = lax.ppermute(expert_down, "req", swap)

    attend_scratch = [
        pltpu.VMEM((pages, page_len, heads_kv, head_dim), BF16),
        pltpu.VMEM((pages, page_len, heads_kv, head_dim), BF16),
        pltpu.VMEM(out_weight.shape, BF16),
        pltpu.VMEM((heads * requests, head_dim), F32),
        pltpu.VMEM((heads * requests, head_dim), F32),
        pltpu.VMEM((requests, heads, page_table.shape[1] * page_len * heads_kv), BF16),
        pltpu.VMEM((requests, heads, head_dim), F32),
        pltpu.SemaphoreType.DMA((11,)),
    ]

    def small(*arrays):
        return [pltpu.VMEM(array.shape, array.dtype) for array in arrays]

    inputs = [pltpu.SMEM(page_table.shape, jnp.int32), pltpu.SMEM(lengths.shape, jnp.int32)]
    inputs += small(queries, fresh_key_value)
    routed_shapes = [
        like((requests, width)),
        like((requests, 1), F32),
        like((requests, 1), F32),
        like((slab_rows, piece)),
        like((requests, slab_rows), F32),
    ]
    attend_params = pltpu.CompilerParams(vmem_limit_bytes=24 * MIB)
    if kv_count == 1:
        attend_scratch.insert(2, pltpu.VMEM((slab_rows, piece), BF16))
        mixed, norms, top, slabs, comb = pl.pallas_call(
            functools.partial(attend_route_kernel, capacity),
            out_shape=routed_shapes,
            in_specs=in_hbm(10),
            out_specs=vmem(3) + in_hbm(1) + vmem(1),
            scratch_shapes=inputs + small(hidden, norm_gain, router_weight, expert_ids) + attend_scratch,
            compiler_params=attend_params,
        )(*pinned(page_table, lengths, queries, fresh_key_value, hidden, norm_gain, router_weight, expert_ids,
                  kv_pool, out_weight))
    else:
        projected = pl.pallas_call(
            attend_kernel,
            out_shape=like((requests, width), F32),
            in_specs=in_hbm(6),
            out_specs=pl.BlockSpec(memory_space=pltpu.VMEM),
            scratch_shapes=inputs + attend_scratch,
            compiler_params=attend_params,
        )(*pinned(page_table, lengths, queries, fresh_key_value, kv_pool, out_weight))
        projected = lax.psum(projected, "kv")
        mixed, norms, top, slabs, comb = pl.pallas_call(
            functools.partial(route_kernel, capacity),
            out_shape=routed_shapes,
            in_specs=vmem(5),
            out_specs=vmem(5),
        )(projected, hidden, norm_gain, router_weight, expert_ids)

    new_pool = pl.pallas_call(
        refresh_kernel,
        out_shape=like(kv_pool.shape),
        in_specs=scalars(2) + vmem(1) + in_hbm(2),
        out_specs=pl.BlockSpec(memory_space=pltpu.HBM),
        scratch_shapes=[pltpu.VMEM(kv_pool.shape, BF16), pltpu.SemaphoreType.DMA((8,))],
        compiler_params=pltpu.CompilerParams(vmem_limit_bytes=12 * MIB),
        cost_estimate=pl.CostEstimate(flops=0, bytes_accessed=8 * kv_pool.size, transcendentals=0),
    )(page_table, lengths, fresh_key_value, top, *pinned(kv_pool))

    def exchange(array):
        array = array.reshape(experts, SLAB, piece)
        array = lax.all_to_all(
            array, "req", split_axis=0, concat_axis=0, tiled=True, axis_index_groups=same_part
        )
        return array.reshape(slab_rows, piece)

    arrived = exchange(slabs)
    kept = experts * capacity
    units = expert_down.shape[1]
    leaving = pl.pallas_call(
        functools.partial(expert_kernel, capacity),
        out_shape=like((slab_rows, piece)),
        in_specs=in_hbm(3) + vmem(2),
        out_specs=pl.BlockSpec(memory_space=pltpu.VMEM),
        scratch_shapes=[
            pltpu.VMEM((slab_rows, piece), BF16),
            pltpu.VMEM((2, units, width), BF16),
            pltpu.VMEM((units, width), BF16),
            pltpu.VMEM((kept, width), BF16),
            pltpu.VMEM((kept, width), F32),
            pltpu.SemaphoreType.DMA((1 + 2 * len(unit_chunks(units)),)),
        ],
        compiler_params=pltpu.CompilerParams(vmem_limit_bytes=20 * MIB),
    )(arrived, *pinned(expert_gate_up, expert_down), other_up, other_down)
    returned = exchange(leaving)
    if kv_count == 1:
        out_hidden = pl.pallas_call(
            functools.partial(combine_kernel, capacity),
            out_shape=like((requests, width)),
            in_specs=vmem(3),
            out_specs=pl.BlockSpec(memory_space=pltpu.VMEM),
            compiler_params=pltpu.CompilerParams(vmem_limit_bytes=8 * MIB),
        )(comb, returned, mixed)
    else:
        routed = pl.pallas_call(
            functools.partial(gather_kernel, capacity),
            out_shape=like((requests, width)),
            in_specs=vmem(2),
            out_specs=pl.BlockSpec(memory_space=pltpu.VMEM),
        )(comb, returned)
        routed = lax.psum(routed, "kv").astype(F32)
        out_hidden = (mixed.astype(F32) + routed).astype(BF16)
    return out_hidden, new_pool, norms.reshape(requests), top.reshape(requests)


def solution(mesh):
    in_specs = (
        P("req", None),
        P("req", "kv"),
        P("req", "kv", None),
        P("req", None, "kv", None),
        P("req", None),
        P("req"),
        P("kv", None),
        P(),
        P(),
        P("req", None),
        P("req", None, "kv", None),
        P("req", "kv", None),
    )
    out_specs = (P("req", None), P("req", None, "kv", None), P("req"), P("req"))
    return jax.shard_map(body, mesh=mesh, in_specs=in_specs, out_specs=out_specs, check_vma=False)
```

```python
import functools
import math

import jax
import jax.numpy as jnp
from jax import lax
from jax.experimental import pallas as pl
from jax.experimental.pallas import tpu as pltpu
from jax.sharding import PartitionSpec as P

BF16 = jnp.bfloat16
F32 = jnp.float32
NT = (((1,), (1,)), ((), ()))
NN = (((1,), (0,)), ((), ()))
SLAB = 16
MIB = 1 << 20


def dot(a, b, dims=NN, precision=None):
    return lax.dot_general(a, b, dims, precision=precision, preferred_element_type=F32)


def iota(shape, dim):
    return lax.broadcasted_iota(jnp.int32, shape, dim)


def copies(pairs, sems, first=0):
    return [pltpu.make_async_copy(src, dst, sems.at[first + i]) for i, (src, dst) in enumerate(pairs)]


def pool_half(array, i):
    head_dim = array.shape[3] // 2
    return array.at[:, :, :, pl.ds(i * head_dim, head_dim)]


def attend(refs, keys, values, scratch):
    small, (kept_weight, qs, att, probs, sums, sems) = scratch
    table, lengths, q_ref, fresh = small[:4]
    requests, max_pages = table.shape
    pages, page_len, heads_kv, head_dim = keys.shape
    heads = q_ref.shape[1] // head_dim
    group = heads // heads_kv
    page_rows = page_len * heads_kv
    pool, weight = refs[-2:]
    loads = copies(list(zip(refs[:4], small[:4])), sems)
    key_load, value_load, weight_load = copies(
        [(pool_half(pool, 0), keys), (pool_half(pool, 1), values), (weight, kept_weight)], sems, 4
    )
    later = copies(list(zip(refs[4:-2], small[4:])), sems, 7)
    for copy in loads + [key_load, value_load] + later + [weight_load]:
        copy.start()
    for copy in loads:
        copy.wait()
    for h in range(heads):
        qs[pl.ds(h * requests, requests), :] = q_ref[:, pl.ds(h * head_dim, head_dim)].astype(F32)
    spots = [(table[r, lengths[r] // page_len], lengths[r] % page_len) for r in range(requests)]

    key_load.wait()
    for r, (page, slot) in enumerate(spots):
        keys[page, slot] = fresh[r][:, :head_dim]
    key_pages = keys.reshape(pages, page_rows, head_dim)
    value_pages = values.reshape(pages, page_rows, head_dim)
    columns = max_pages * page_rows
    lane = iota((heads, columns), 1)
    own_head = lane % heads_kv == iota((heads, columns), 0) // group
    position = lane // heads_kv
    for r in range(requests):
        query = qs[pl.ds(r, heads, stride=requests), :].astype(BF16)
        gathered = jnp.concatenate([key_pages[table[r, j]] for j in range(max_pages)], axis=0)
        scores = dot(query, gathered, NT) * (1.0 / math.sqrt(head_dim))
        scores = jnp.where(own_head & (position <= lengths[r]), scores, -1e30)
        exponent = jnp.exp(scores - jnp.max(scores, axis=1, keepdims=True))
        sums[r] = jnp.broadcast_to(jnp.sum(exponent, axis=1, keepdims=True), (heads, head_dim))
        probs[r] = exponent.astype(BF16)

    value_load.wait()
    for r, (page, slot) in enumerate(spots):
        values[page, slot] = fresh[r][:, head_dim:]
    for r in range(requests):
        gathered = jnp.concatenate([value_pages[table[r, j]] for j in range(max_pages)], axis=0)
        att[pl.ds(r, heads, stride=requests), :] = dot(probs[r], gathered) / sums[r]
    attended = jnp.concatenate(
        [att[pl.ds(h * requests, requests), :] for h in range(heads)], axis=1
    ).astype(BF16)
    weight_load.wait()
    projected = dot(attended, kept_weight[...])
    for copy in later:
        copy.wait()
    return projected


def route(projected, hidden, gain, router, ids, mixed_ref, norms_ref, top_ref, slabs_ref, comb_ref, capacity, leave=None):
    requests, width = hidden.shape
    experts = router.shape[0]
    parts = SLAB // capacity
    piece = width // parts
    slab_rows = experts * SLAB
    backwards = lax.axis_index("req") % 2 == 1

    def slab_expert(shape, dim):
        slab = iota(shape, dim) // SLAB
        return jnp.where(backwards, experts - 1 - slab, slab)

    mixed = (hidden[...].astype(F32) + projected).astype(BF16)
    mixed_ref[...] = mixed
    mixed = mixed.astype(F32)
    norms = jnp.sqrt(jnp.mean(mixed * mixed, axis=1, keepdims=True) + 1e-06)
    norms_ref[...] = norms
    normed = (mixed / norms * gain[...].astype(F32).reshape(1, width)).astype(BF16)
    logits = dot(normed, router[...], NT)
    top_ref[...] = jnp.max(logits, axis=1, keepdims=True)
    column = iota((requests, experts), 1)
    named = column < 0
    for k in range(ids.shape[1]):
        named = named | (ids[:, k : k + 1] == column)
    weights = jnp.where(named, jnp.exp(logits), 0.0)
    weights = weights / jnp.sum(weights, axis=1, keepdims=True)
    earlier = (iota((requests, requests), 1) < iota((requests, requests), 0)).astype(F32)
    rank = dot(earlier, named.astype(F32))
    place = jnp.where(named, rank, -1.0)
    normed = normed.astype(F32)
    stacked = jnp.concatenate([normed[:, p * piece : (p + 1) * piece] for p in range(parts)], axis=0)
    places = jnp.concatenate([place] * parts, axis=0)
    shape = (slab_rows, parts * requests)
    inner = iota(shape, 0) % SLAB
    spread = (slab_expert((slab_rows, experts), 0) == iota((slab_rows, experts), 1)).astype(F32)
    picks = (dot(spread, places, NT) == (inner // parts).astype(F32)) & (
        inner % parts == iota(shape, 1) // requests
    )
    slabs_ref[...] = dot(picks.astype(BF16), stacked.astype(BF16)).astype(BF16)
    if leave is not None:
        leave()
    shape = (experts, slab_rows)
    spread = (slab_expert(shape, 1) == iota(shape, 0)).astype(F32)
    inner = iota((requests, slab_rows), 1) % SLAB
    comb_ref[...] = jnp.where(
        dot(place, spread) == (inner // parts).astype(F32),
        dot(weights, spread, precision=lax.Precision.HIGHEST),
        0.0,
    )


def attend_route_kernel(capacity, *refs):
    inputs, (mixed, norms, top, slabs, comb) = refs[:10], refs[10:15]
    small, scratch = refs[15:23], refs[23:]
    keys, values, kept_slabs = scratch[:3]
    projected = attend(inputs, keys, values, (small, scratch[3:]))
    hidden, gain, router, ids = small[4:]
    leave = pltpu.make_async_copy(kept_slabs, slabs, scratch[-1].at[0])
    route(projected, hidden, gain, router, ids, mixed, norms, top, kept_slabs, comb, capacity, leave.start)
    leave.wait()


def attend_kernel(*refs):
    attended, scratch = refs[6], refs[11:]
    attended[...] = attend(refs[:6], scratch[0], scratch[1], (refs[7:11], scratch[2:]))


def refresh_kernel(table, lengths, fresh, after, pool, new_pool, kept, sems):
    pages, page_len = kept.shape[:2]
    step = -(-pages // 4)
    spans = [pl.ds(start, min(step, pages - start)) for start in range(0, pages, step)]
    loads = copies([(pool.at[span], kept.at[span]) for span in spans], sems)
    stores = copies([(kept.at[span], new_pool.at[span]) for span in spans], sems, len(spans))
    for copy in loads:
        copy.start()
    for copy in loads:
        copy.wait()
    for r in range(table.shape[0]):
        kept[table[r, lengths[r] // page_len], lengths[r] % page_len] = fresh[r]
    for copy in stores:
        copy.start()
    for copy in stores:
        copy.wait()


def route_kernel(capacity, projected, hidden, gain, router, ids, mixed, norms, top, slabs, comb):
    route(projected[...], hidden, gain, router, ids, mixed, norms, top, slabs, comb, capacity)


def unit_chunks(units):
    return [(start, min(256, units - start)) for start in range(0, units, 256)]


def expert_kernel(capacity, arrived, own_up, own_down, other_up, other_down, slabs,
                  kept_up, kept_down, rows, total, sems):
    units = kept_down.shape[0]
    chunks = []
    for i, (start, size) in enumerate(unit_chunks(units)):
        span = pl.ds(start, size)
        chunks.append((span, copies(
            [(own_up.at[0, :, span, :], kept_up.at[:, span, :]), (own_down.at[0, span, :], kept_down.at[span, :])],
            sems,
            2 * i,
        )))
    for _, loads in chunks:
        for copy in loads:
            copy.start()
    parts = SLAB // capacity
    piece = slabs.shape[1]
    block = 128
    each = block // parts
    blocks = slabs.shape[0] // block
    shape = (block, block)
    slab_row, sorted_row = iota(shape, 1), iota(shape, 0)
    sort = (slab_row == sorted_row % each * parts + sorted_row // each).astype(BF16)
    for i in range(blocks):
        sorted_rows = dot(sort, arrived[pl.ds(i * block, block), :]).astype(BF16)
        rows[pl.ds(i * each, each), :] = jnp.concatenate(
            [sorted_rows[p * each : (p + 1) * each] for p in range(parts)], axis=1
        )
    states = rows[...]
    steps = [(other_up.at[0], other_down.at[0], span, []) for span, _ in chunks]
    steps += [(kept_up, kept_down, span, loads) for span, loads in chunks]
    for i, (gate_up, down, span, loads) in enumerate(steps):
        for copy in loads:
            copy.wait()
        gate = dot(states, gate_up[0, span, :], NT)
        up = dot(states, gate_up[1, span, :], NT)
        activated = (gate / (1.0 + jnp.exp(-gate)) * up).astype(BF16)
        term = dot(activated, down[span, :])
        total[...] = term if i == 0 else total[...] + term
    slab_row, sorted_row = iota(shape, 0), iota(shape, 1)
    unsort = (slab_row == sorted_row % each * parts + sorted_row // each).astype(BF16)
    for i in range(blocks):
        summed = total[pl.ds(i * each, each), :].astype(BF16)
        stacked = jnp.concatenate([summed[:, p * piece : (p + 1) * piece] for p in range(parts)], axis=0)
        slabs[pl.ds(i * block, block), :] = dot(unsort, stacked).astype(BF16)


def gather_terms(comb, slabs, capacity):
    parts = SLAB // capacity
    requests = comb.shape[0]
    weights = comb[...]
    pieces = []
    for _ in range(3):
        piece = weights.astype(BF16).astype(F32)
        weights = weights - piece
        pieces.append(piece)
    part = iota(comb.shape, 1) % parts
    stacked = jnp.concatenate(
        [jnp.where(part == p, piece, 0.0) for p in range(parts) for piece in pieces], axis=0
    ).astype(BF16)
    terms = dot(stacked, slabs[...])
    return jnp.concatenate(
        [
            sum(terms[(3 * p + i) * requests : (3 * p + i + 1) * requests] for i in range(3))
            for p in range(parts)
        ],
        axis=1,
    )


def combine_kernel(capacity, comb, slabs, mixed, out):
    out[...] = (mixed[...].astype(F32) + gather_terms(comb, slabs, capacity)).astype(BF16)


def gather_kernel(capacity, comb, slabs, out):
    out[...] = gather_terms(comb, slabs, capacity).astype(BF16)


def vmem(count):
    return [pl.BlockSpec(memory_space=pltpu.VMEM)] * count


def scalars(count):
    return [pl.BlockSpec(memory_space=pltpu.SMEM)] * count


def in_hbm(count):
    return [pl.BlockSpec(memory_space=pltpu.HBM)] * count


def pinned(*arrays):
    return [pltpu.with_memory_space_constraint(array, pltpu.HBM) for array in arrays]


def like(shape, dtype=BF16):
    return jax.ShapeDtypeStruct(shape, dtype)


def body(
    hidden,
    queries,
    fresh_key_value,
    kv_pool,
    page_table,
    lengths,
    out_weight,
    norm_gain,
    router_weight,
    expert_ids,
    expert_gate_up,
    expert_down,
):
    requests, width = hidden.shape
    req_count, kv_count = lax.axis_size("req"), lax.axis_size("kv")
    pages, page_len, heads_kv, pair_dim = kv_pool.shape
    head_dim = pair_dim // 2
    heads = queries.shape[1] // head_dim
    experts = router_weight.shape[0]
    copies = req_count // experts
    chosen = expert_ids.shape[1]
    capacity = 2 * max(1, (requests * chosen + 2 * experts - 1) // (2 * experts))
    parts = SLAB // capacity
    piece = width // parts
    slab_rows = experts * SLAB

    same_part = [list(range(part, req_count, copies))[:: -1 if part % 2 else 1] for part in range(copies)]
    swap = [(index, index ^ 1) for index in range(req_count)]
    other_up = lax.ppermute(expert_gate_up, "req", swap)
    other_down = lax.ppermute(expert_down, "req", swap)

    attend_scratch = [
        pltpu.VMEM((pages, page_len, heads_kv, head_dim), BF16),
        pltpu.VMEM((pages, page_len, heads_kv, head_dim), BF16),
        pltpu.VMEM(out_weight.shape, BF16),
        pltpu.VMEM((heads * requests, head_dim), F32),
        pltpu.VMEM((heads * requests, head_dim), F32),
        pltpu.VMEM((requests, heads, page_table.shape[1] * page_len * heads_kv), BF16),
        pltpu.VMEM((requests, heads, head_dim), F32),
        pltpu.SemaphoreType.DMA((11,)),
    ]

    def small(*arrays):
        return [pltpu.VMEM(array.shape, array.dtype) for array in arrays]

    inputs = [pltpu.SMEM(page_table.shape, jnp.int32), pltpu.SMEM(lengths.shape, jnp.int32)]
    inputs += small(queries, fresh_key_value)
    routed_shapes = [
        like((requests, width)),
        like((requests, 1), F32),
        like((requests, 1), F32),
        like((slab_rows, piece)),
        like((requests, slab_rows), F32),
    ]
    attend_params = pltpu.CompilerParams(vmem_limit_bytes=24 * MIB)
    if kv_count == 1:
        attend_scratch.insert(2, pltpu.VMEM((slab_rows, piece), BF16))
        mixed, norms, top, slabs, comb = pl.pallas_call(
            functools.partial(attend_route_kernel, capacity),
            out_shape=routed_shapes,
            in_specs=in_hbm(10),
            out_specs=vmem(3) + in_hbm(1) + vmem(1),
            scratch_shapes=inputs + small(hidden, norm_gain, router_weight, expert_ids) + attend_scratch,
            compiler_params=attend_params,
        )(*pinned(page_table, lengths, queries, fresh_key_value, hidden, norm_gain, router_weight, expert_ids,
                  kv_pool, out_weight))
    else:
        projected = pl.pallas_call(
            attend_kernel,
            out_shape=like((requests, width), F32),
            in_specs=in_hbm(6),
            out_specs=pl.BlockSpec(memory_space=pltpu.VMEM),
            scratch_shapes=inputs + attend_scratch,
            compiler_params=attend_params,
        )(*pinned(page_table, lengths, queries, fresh_key_value, kv_pool, out_weight))
        projected = lax.psum(projected, "kv")
        mixed, norms, top, slabs, comb = pl.pallas_call(
            functools.partial(route_kernel, capacity),
            out_shape=routed_shapes,
            in_specs=vmem(5),
            out_specs=vmem(5),
        )(projected, hidden, norm_gain, router_weight, expert_ids)

    new_pool = pl.pallas_call(
        refresh_kernel,
        out_shape=like(kv_pool.shape),
        in_specs=scalars(2) + vmem(1) + in_hbm(2),
        out_specs=pl.BlockSpec(memory_space=pltpu.HBM),
        scratch_shapes=[pltpu.VMEM(kv_pool.shape, BF16), pltpu.SemaphoreType.DMA((8,))],
        compiler_params=pltpu.CompilerParams(vmem_limit_bytes=12 * MIB),
        cost_estimate=pl.CostEstimate(flops=0, bytes_accessed=8 * kv_pool.size, transcendentals=0),
    )(page_table, lengths, fresh_key_value, top, *pinned(kv_pool))

    def exchange(array):
        array = array.reshape(experts, SLAB, piece)
        array = lax.all_to_all(
            array, "req", split_axis=0, concat_axis=0, tiled=True, axis_index_groups=same_part
        )
        return array.reshape(slab_rows, piece)

    arrived = exchange(slabs)
    kept = experts * capacity
    units = expert_down.shape[1]
    leaving = pl.pallas_call(
        functools.partial(expert_kernel, capacity),
        out_shape=like((slab_rows, piece)),
        in_specs=vmem(1) + in_hbm(2) + vmem(2),
        out_specs=pl.BlockSpec(memory_space=pltpu.VMEM),
        scratch_shapes=[
            pltpu.VMEM((2, units, width), BF16),
            pltpu.VMEM((units, width), BF16),
            pltpu.VMEM((kept, width), BF16),
            pltpu.VMEM((kept, width), F32),
            pltpu.SemaphoreType.DMA((2 * len(unit_chunks(units)),)),
        ],
        compiler_params=pltpu.CompilerParams(vmem_limit_bytes=20 * MIB),
    )(arrived, *pinned(expert_gate_up, expert_down), other_up, other_down)
    returned = exchange(leaving)
    if kv_count == 1:
        out_hidden = pl.pallas_call(
            functools.partial(combine_kernel, capacity),
            out_shape=like((requests, width)),
            in_specs=vmem(3),
            out_specs=pl.BlockSpec(memory_space=pltpu.VMEM),
            compiler_params=pltpu.CompilerParams(vmem_limit_bytes=8 * MIB),
        )(comb, returned, mixed)
    else:
        routed = pl.pallas_call(
            functools.partial(gather_kernel, capacity),
            out_shape=like((requests, width)),
            in_specs=vmem(2),
            out_specs=pl.BlockSpec(memory_space=pltpu.VMEM),
        )(comb, returned)
        routed = lax.psum(routed, "kv").astype(F32)
        out_hidden = (mixed.astype(F32) + routed).astype(BF16)
    return out_hidden, new_pool, norms.reshape(requests), top.reshape(requests)


def solution(mesh):
    in_specs = (
        P("req", None),
        P("req", "kv"),
        P("req", "kv", None),
        P("req", None, "kv", None),
        P("req", None),
        P("req"),
        P("kv", None),
        P(),
        P(),
        P("req", None),
        P("req", None, "kv", None),
        P("req", "kv", None),
    )
    out_specs = (P("req", None), P("req", None, "kv", None), P("req"), P("req"))
    return jax.shard_map(body, mesh=mesh, in_specs=in_specs, out_specs=out_specs, check_vma=False)
```

```python
import functools
import math

import jax
import jax.numpy as jnp
from jax import lax
from jax.experimental import pallas as pl
from jax.experimental.pallas import tpu as pltpu
from jax.sharding import PartitionSpec as P

BF16 = jnp.bfloat16
F32 = jnp.float32
NT = (((1,), (1,)), ((), ()))
NN = (((1,), (0,)), ((), ()))
SHARED_PAGES = 8
SLAB = 16
MIB = 1 << 20


def dot(a, b, dims=NN, precision=None):
    return lax.dot_general(a, b, dims, precision=precision, preferred_element_type=F32)


def iota(shape, dim):
    return lax.broadcasted_iota(jnp.int32, shape, dim)


def copies(pairs, sems, first=0):
    return [pltpu.make_async_copy(src, dst, sems.at[first + i]) for i, (src, dst) in enumerate(pairs)]


def pool_half(array, i):
    head_dim = array.shape[3] // 2
    return array.at[:, :, :, pl.ds(i * head_dim, head_dim)]


def attend(refs, keys, values, scratch):
    small, (kept_weight, qs, att, probs, sums, sems) = scratch
    table, lengths, q_ref, fresh = small[:4]
    requests, max_pages = table.shape
    pages, page_len, heads_kv, head_dim = keys.shape
    heads = q_ref.shape[1] // head_dim
    group = heads // heads_kv
    page_rows = page_len * heads_kv
    pool, weight = refs[-2:]
    loads = copies(list(zip(refs[:4], small[:4])), sems)
    key_load, value_load, weight_load = copies(
        [(pool_half(pool, 0), keys), (pool_half(pool, 1), values), (weight, kept_weight)], sems, 4
    )
    later = copies(list(zip(refs[4:-2], small[4:])), sems, 7)
    for copy in loads + [key_load, value_load] + later + [weight_load]:
        copy.start()
    for copy in loads:
        copy.wait()
    for h in range(heads):
        qs[pl.ds(h * requests, requests), :] = q_ref[:, pl.ds(h * head_dim, head_dim)].astype(F32)
    spots = [(table[r, lengths[r] // page_len], lengths[r] % page_len) for r in range(requests)]

    key_load.wait()
    for r, (page, slot) in enumerate(spots):
        keys[page, slot] = fresh[r][:, :head_dim]
    key_pages = keys.reshape(pages, page_rows, head_dim)
    value_pages = values.reshape(pages, page_rows, head_dim)
    columns = max_pages * page_rows
    lane = iota((heads, columns), 1)
    own_head = lane % heads_kv == iota((heads, columns), 0) // group
    position = lane // heads_kv
    shared_columns = SHARED_PAGES * page_rows

    def pages_of(array, r, first, last):
        return jnp.concatenate([array[table[r, j]] for j in range(first, last)], axis=0)

    query = [qs[pl.ds(r, heads, stride=requests), :] for r in range(requests)]
    shared = dot(jnp.concatenate(query, axis=0).astype(BF16), pages_of(key_pages, 0, 0, SHARED_PAGES), NT)
    for r in range(requests):
        own = dot(query[r].astype(BF16), pages_of(key_pages, r, SHARED_PAGES, max_pages), NT)
        scores = jnp.concatenate([shared[r * heads : (r + 1) * heads], own], axis=1)
        scores = scores * (1.0 / math.sqrt(head_dim))
        scores = jnp.where(own_head & (position <= lengths[r]), scores, -1e30)
        exponent = jnp.exp(scores - jnp.max(scores, axis=1, keepdims=True))
        sums[r] = jnp.broadcast_to(jnp.sum(exponent, axis=1, keepdims=True), (heads, head_dim))
        probs[r] = exponent.astype(BF16)

    value_load.wait()
    for r, (page, slot) in enumerate(spots):
        values[page, slot] = fresh[r][:, head_dim:]
    shared = dot(
        probs[:, :, :shared_columns].reshape(requests * heads, shared_columns),
        pages_of(value_pages, 0, 0, SHARED_PAGES),
    )
    for r in range(requests):
        own = dot(probs[r, :, shared_columns:], pages_of(value_pages, r, SHARED_PAGES, max_pages))
        att[pl.ds(r, heads, stride=requests), :] = (shared[r * heads : (r + 1) * heads] + own) / sums[r]
    attended = jnp.concatenate(
        [att[pl.ds(h * requests, requests), :] for h in range(heads)], axis=1
    ).astype(BF16)
    weight_load.wait()
    projected = dot(attended, kept_weight[...])
    for copy in later:
        copy.wait()
    return projected


def route(projected, hidden, gain, router, ids, mixed_ref, norms_ref, top_ref, slabs_ref, comb_ref, capacity, leave=None):
    requests, width = hidden.shape
    experts = router.shape[0]
    parts = SLAB // capacity
    piece = width // parts
    slab_rows = experts * SLAB
    backwards = lax.axis_index("req") % 2 == 0

    def slab_expert(shape, dim):
        slab = iota(shape, dim) // SLAB
        return jnp.where(backwards, experts - 1 - slab, slab)

    mixed = (hidden[...].astype(F32) + projected).astype(BF16)
    mixed_ref[...] = mixed
    mixed = mixed.astype(F32)
    norms = jnp.sqrt(jnp.mean(mixed * mixed, axis=1, keepdims=True) + 1e-06)
    norms_ref[...] = norms
    normed = (mixed / norms * gain[...].astype(F32).reshape(1, width)).astype(BF16)
    logits = dot(normed, router[...], NT)
    top_ref[...] = jnp.max(logits, axis=1, keepdims=True)
    column = iota((requests, experts), 1)
    named = column < 0
    for k in range(ids.shape[1]):
        named = named | (ids[:, k : k + 1] == column)
    weights = jnp.where(named, jnp.exp(logits), 0.0)
    weights = weights / jnp.sum(weights, axis=1, keepdims=True)
    earlier = (iota((requests, requests), 1) < iota((requests, requests), 0)).astype(F32)
    rank = dot(earlier, named.astype(F32))
    place = jnp.where(named, rank, -1.0)
    normed = normed.astype(F32)
    stacked = jnp.concatenate([normed[:, p * piece : (p + 1) * piece] for p in range(parts)], axis=0)
    places = jnp.concatenate([place] * parts, axis=0)
    shape = (slab_rows, parts * requests)
    inner = iota(shape, 0) % SLAB
    spread = (slab_expert((slab_rows, experts), 0) == iota((slab_rows, experts), 1)).astype(F32)
    picks = (dot(spread, places, NT) == (inner // parts).astype(F32)) & (
        inner % parts == iota(shape, 1) // requests
    )
    slabs_ref[...] = dot(picks.astype(BF16), stacked.astype(BF16)).astype(BF16)
    if leave is not None:
        leave()
    shape = (experts, slab_rows)
    spread = (slab_expert(shape, 1) == iota(shape, 0)).astype(F32)
    inner = iota((requests, slab_rows), 1) % SLAB
    comb_ref[...] = jnp.where(
        dot(place, spread) == (inner // parts).astype(F32),
        dot(weights, spread, precision=lax.Precision.HIGHEST),
        0.0,
    )


def attend_route_kernel(capacity, *refs):
    inputs, (mixed, norms, top, slabs, comb) = refs[:10], refs[10:15]
    small, scratch = refs[15:23], refs[23:]
    keys, values, kept_slabs = scratch[:3]
    projected = attend(inputs, keys, values, (small, scratch[3:]))
    hidden, gain, router, ids = small[4:]
    leave = pltpu.make_async_copy(kept_slabs, slabs, scratch[-1].at[0])
    route(projected, hidden, gain, router, ids, mixed, norms, top, kept_slabs, comb, capacity, leave.start)
    leave.wait()


def attend_kernel(*refs):
    attended, scratch = refs[6], refs[11:]
    attended[...] = attend(refs[:6], scratch[0], scratch[1], (refs[7:11], scratch[2:]))


def refresh_kernel(table, lengths, fresh, after, pool, new_pool, kept, sems):
    pages, page_len = kept.shape[:2]
    step = -(-pages // 4)
    spans = [pl.ds(start, min(step, pages - start)) for start in range(0, pages, step)]
    loads = copies([(pool.at[span], kept.at[span]) for span in spans], sems)
    stores = copies([(kept.at[span], new_pool.at[span]) for span in spans], sems, len(spans))
    for copy in loads:
        copy.start()
    for copy in loads:
        copy.wait()
    for r in range(table.shape[0]):
        kept[table[r, lengths[r] // page_len], lengths[r] % page_len] = fresh[r]
    for copy in stores:
        copy.start()
    for copy in stores:
        copy.wait()


def route_kernel(capacity, projected, hidden, gain, router, ids, mixed, norms, top, slabs, comb):
    route(projected[...], hidden, gain, router, ids, mixed, norms, top, slabs, comb, capacity)


def unit_chunks(units):
    return [(start, min(256, units - start)) for start in range(0, units, 256)]


def expert_kernel(capacity, arrived, own_up, own_down, other_up, other_down, slabs,
                  slab_rows, kept_up, kept_down, rows, total, sems):
    units = kept_down.shape[0]
    arrive = pltpu.make_async_copy(arrived, slab_rows, sems.at[0])
    arrive.start()
    chunks = []
    for i, (start, size) in enumerate(unit_chunks(units)):
        span = pl.ds(start, size)
        chunks.append((span, copies(
            [(own_up.at[0, :, span, :], kept_up.at[:, span, :]), (own_down.at[0, span, :], kept_down.at[span, :])],
            sems,
            1 + 2 * i,
        )))
    for _, loads in chunks:
        for copy in loads:
            copy.start()
    arrive.wait()
    parts = SLAB // capacity
    piece = slabs.shape[1]
    block = 128
    each = block // parts
    blocks = slabs.shape[0] // block
    shape = (block, block)
    slab_row, sorted_row = iota(shape, 1), iota(shape, 0)
    sort = (slab_row == sorted_row % each * parts + sorted_row // each).astype(BF16)
    for i in range(blocks):
        sorted_rows = dot(sort, slab_rows[pl.ds(i * block, block), :]).astype(BF16)
        rows[pl.ds(i * each, each), :] = jnp.concatenate(
            [sorted_rows[p * each : (p + 1) * each] for p in range(parts)], axis=1
        )
    states = rows[...]
    steps = [(other_up.at[0], other_down.at[0], span, []) for span, _ in chunks]
    steps += [(kept_up, kept_down, span, loads) for span, loads in chunks]
    for i, (gate_up, down, span, loads) in enumerate(steps):
        for copy in loads:
            copy.wait()
        gate = dot(states, gate_up[0, span, :], NT)
        up = dot(states, gate_up[1, span, :], NT)
        activated = (gate / (1.0 + jnp.exp(-gate)) * up).astype(BF16)
        term = dot(activated, down[span, :])
        total[...] = term if i == 0 else total[...] + term
    slab_row, sorted_row = iota(shape, 0), iota(shape, 1)
    unsort = (slab_row == sorted_row % each * parts + sorted_row // each).astype(BF16)
    for i in range(blocks):
        summed = total[pl.ds(i * each, each), :].astype(BF16)
        stacked = jnp.concatenate([summed[:, p * piece : (p + 1) * piece] for p in range(parts)], axis=0)
        slabs[pl.ds(i * block, block), :] = dot(unsort, stacked).astype(BF16)


def gather_terms(comb, slabs, capacity):
    parts = SLAB // capacity
    requests = comb.shape[0]
    weights = comb[...]
    pieces = []
    for _ in range(3):
        piece = weights.astype(BF16).astype(F32)
        weights = weights - piece
        pieces.append(piece)
    part = iota(comb.shape, 1) % parts
    stacked = jnp.concatenate(
        [jnp.where(part == p, piece, 0.0) for p in range(parts) for piece in pieces], axis=0
    ).astype(BF16)
    terms = dot(stacked, slabs[...])
    return jnp.concatenate(
        [
            sum(terms[(3 * p + i) * requests : (3 * p + i + 1) * requests] for i in range(3))
            for p in range(parts)
        ],
        axis=1,
    )


def combine_kernel(capacity, comb, slabs, mixed, out):
    out[...] = (mixed[...].astype(F32) + gather_terms(comb, slabs, capacity)).astype(BF16)


def gather_kernel(capacity, comb, slabs, out):
    out[...] = gather_terms(comb, slabs, capacity).astype(BF16)


def vmem(count):
    return [pl.BlockSpec(memory_space=pltpu.VMEM)] * count


def scalars(count):
    return [pl.BlockSpec(memory_space=pltpu.SMEM)] * count


def in_hbm(count):
    return [pl.BlockSpec(memory_space=pltpu.HBM)] * count


def pinned(*arrays):
    return [pltpu.with_memory_space_constraint(array, pltpu.HBM) for array in arrays]


def like(shape, dtype=BF16):
    return jax.ShapeDtypeStruct(shape, dtype)


def body(
    hidden,
    queries,
    fresh_key_value,
    kv_pool,
    page_table,
    lengths,
    out_weight,
    norm_gain,
    router_weight,
    expert_ids,
    expert_gate_up,
    expert_down,
):
    requests, width = hidden.shape
    req_count, kv_count = lax.axis_size("req"), lax.axis_size("kv")
    pages, page_len, heads_kv, pair_dim = kv_pool.shape
    head_dim = pair_dim // 2
    heads = queries.shape[1] // head_dim
    experts = router_weight.shape[0]
    copies = req_count // experts
    chosen = expert_ids.shape[1]
    capacity = 2 * max(1, (requests * chosen + 2 * experts - 1) // (2 * experts))
    parts = SLAB // capacity
    piece = width // parts
    slab_rows = experts * SLAB

    same_part = [list(range(part, req_count, copies))[:: 1 if part % 2 else -1] for part in range(copies)]
    swap = [(index, index ^ 1) for index in range(req_count)]
    other_up = lax.ppermute(expert_gate_up, "req", swap)
    other_down = lax.ppermute(expert_down, "req", swap)

    attend_scratch = [
        pltpu.VMEM((pages, page_len, heads_kv, head_dim), BF16),
        pltpu.VMEM((pages, page_len, heads_kv, head_dim), BF16),
        pltpu.VMEM(out_weight.shape, BF16),
        pltpu.VMEM((heads * requests, head_dim), F32),
        pltpu.VMEM((heads * requests, head_dim), F32),
        pltpu.VMEM((requests, heads, page_table.shape[1] * page_len * heads_kv), BF16),
        pltpu.VMEM((requests, heads, head_dim), F32),
        pltpu.SemaphoreType.DMA((11,)),
    ]

    def small(*arrays):
        return [pltpu.VMEM(array.shape, array.dtype) for array in arrays]

    inputs = [pltpu.SMEM(page_table.shape, jnp.int32), pltpu.SMEM(lengths.shape, jnp.int32)]
    inputs += small(queries, fresh_key_value)
    routed_shapes = [
        like((requests, width)),
        like((requests, 1), F32),
        like((requests, 1), F32),
        like((slab_rows, piece)),
        like((requests, slab_rows), F32),
    ]
    attend_params = pltpu.CompilerParams(vmem_limit_bytes=24 * MIB)
    if kv_count == 1:
        attend_scratch.insert(2, pltpu.VMEM((slab_rows, piece), BF16))
        mixed, norms, top, slabs, comb = pl.pallas_call(
            functools.partial(attend_route_kernel, capacity),
            out_shape=routed_shapes,
            in_specs=in_hbm(10),
            out_specs=vmem(3) + in_hbm(1) + vmem(1),
            scratch_shapes=inputs + small(hidden, norm_gain, router_weight, expert_ids) + attend_scratch,
            compiler_params=attend_params,
        )(*pinned(page_table, lengths, queries, fresh_key_value, hidden, norm_gain, router_weight, expert_ids,
                  kv_pool, out_weight))
    else:
        projected = pl.pallas_call(
            attend_kernel,
            out_shape=like((requests, width), F32),
            in_specs=in_hbm(6),
            out_specs=pl.BlockSpec(memory_space=pltpu.VMEM),
            scratch_shapes=inputs + attend_scratch,
            compiler_params=attend_params,
        )(*pinned(page_table, lengths, queries, fresh_key_value, kv_pool, out_weight))
        projected = lax.psum(projected, "kv")
        mixed, norms, top, slabs, comb = pl.pallas_call(
            functools.partial(route_kernel, capacity),
            out_shape=routed_shapes,
            in_specs=vmem(5),
            out_specs=vmem(5),
        )(projected, hidden, norm_gain, router_weight, expert_ids)

    new_pool = pl.pallas_call(
        refresh_kernel,
        out_shape=like(kv_pool.shape),
        in_specs=scalars(2) + vmem(1) + in_hbm(2),
        out_specs=pl.BlockSpec(memory_space=pltpu.HBM),
        scratch_shapes=[pltpu.VMEM(kv_pool.shape, BF16), pltpu.SemaphoreType.DMA((8,))],
        compiler_params=pltpu.CompilerParams(vmem_limit_bytes=12 * MIB),
        cost_estimate=pl.CostEstimate(flops=0, bytes_accessed=8 * kv_pool.size, transcendentals=0),
    )(page_table, lengths, fresh_key_value, top, *pinned(kv_pool))

    def exchange(array):
        array = array.reshape(experts, SLAB, piece)
        array = lax.all_to_all(
            array, "req", split_axis=0, concat_axis=0, tiled=True, axis_index_groups=same_part
        )
        return array.reshape(slab_rows, piece)

    arrived = exchange(slabs)
    kept = experts * capacity
    units = expert_down.shape[1]
    leaving = pl.pallas_call(
        functools.partial(expert_kernel, capacity),
        out_shape=like((slab_rows, piece)),
        in_specs=in_hbm(3) + vmem(2),
        out_specs=pl.BlockSpec(memory_space=pltpu.VMEM),
        scratch_shapes=[
            pltpu.VMEM((slab_rows, piece), BF16),
            pltpu.VMEM((2, units, width), BF16),
            pltpu.VMEM((units, width), BF16),
            pltpu.VMEM((kept, width), BF16),
            pltpu.VMEM((kept, width), F32),
            pltpu.SemaphoreType.DMA((1 + 2 * len(unit_chunks(units)),)),
        ],
        compiler_params=pltpu.CompilerParams(vmem_limit_bytes=20 * MIB),
    )(arrived, *pinned(expert_gate_up, expert_down), other_up, other_down)
    returned = exchange(leaving)
    if kv_count == 1:
        out_hidden = pl.pallas_call(
            functools.partial(combine_kernel, capacity),
            out_shape=like((requests, width)),
            in_specs=vmem(3),
            out_specs=pl.BlockSpec(memory_space=pltpu.VMEM),
            compiler_params=pltpu.CompilerParams(vmem_limit_bytes=8 * MIB),
        )(comb, returned, mixed)
    else:
        routed = pl.pallas_call(
            functools.partial(gather_kernel, capacity),
            out_shape=like((requests, width)),
            in_specs=vmem(2),
            out_specs=pl.BlockSpec(memory_space=pltpu.VMEM),
        )(comb, returned)
        routed = lax.psum(routed, "kv").astype(F32)
        out_hidden = (mixed.astype(F32) + routed).astype(BF16)
    return out_hidden, new_pool, norms.reshape(requests), top.reshape(requests)


def solution(mesh):
    in_specs = (
        P("req", None),
        P("req", "kv"),
        P("req", "kv", None),
        P("req", None, "kv", None),
        P("req", None),
        P("req"),
        P("kv", None),
        P(),
        P(),
        P("req", None),
        P("req", None, "kv", None),
        P("req", "kv", None),
    )
    out_specs = (P("req", None), P("req", None, "kv", None), P("req"), P("req"))
    return jax.shard_map(body, mesh=mesh, in_specs=in_specs, out_specs=out_specs, check_vma=False)
```

```python
import functools
import math

import jax
import jax.numpy as jnp
from jax import lax
from jax.experimental import pallas as pl
from jax.experimental.pallas import tpu as pltpu
from jax.sharding import PartitionSpec as P

BF16 = jnp.bfloat16
F32 = jnp.float32
NT = (((1,), (1,)), ((), ()))
NN = (((1,), (0,)), ((), ()))
SLAB = 16
MIB = 1 << 20


def dot(a, b, dims=NN, precision=None):
    return lax.dot_general(a, b, dims, precision=precision, preferred_element_type=F32)


def iota(shape, dim):
    return lax.broadcasted_iota(jnp.int32, shape, dim)


def copies(pairs, sems, first=0):
    return [pltpu.make_async_copy(src, dst, sems.at[first + i]) for i, (src, dst) in enumerate(pairs)]


def pool_half(array, i):
    head_dim = array.shape[3] // 2
    return array.at[:, :, :, pl.ds(i * head_dim, head_dim)]


def attend(refs, keys, values, scratch):
    small, (kept_weight, qs, att, probs, sums, sems) = scratch
    table, lengths, q_ref, fresh = small[:4]
    requests, max_pages = table.shape
    pages, page_len, heads_kv, head_dim = keys.shape
    heads = q_ref.shape[1] // head_dim
    group = heads // heads_kv
    page_rows = page_len * heads_kv
    pool, weight = refs[-2:]
    loads = copies(list(zip(refs[:4], small[:4])), sems)
    key_load, value_load, weight_load = copies(
        [(pool_half(pool, 0), keys), (pool_half(pool, 1), values), (weight, kept_weight)], sems, 4
    )
    later = copies(list(zip(refs[4:-2], small[4:])), sems, 7)
    for copy in loads + [key_load]:
        copy.start()
    for copy in loads:
        copy.wait()
    for copy in [value_load, weight_load] + later:
        copy.start()
    for h in range(heads):
        qs[pl.ds(h * requests, requests), :] = q_ref[:, pl.ds(h * head_dim, head_dim)].astype(F32)
    spots = [(table[r, lengths[r] // page_len], lengths[r] % page_len) for r in range(requests)]

    key_load.wait()
    for r, (page, slot) in enumerate(spots):
        keys[page, slot] = fresh[r][:, :head_dim]
    key_pages = keys.reshape(pages, page_rows, head_dim)
    value_pages = values.reshape(pages, page_rows, head_dim)
    columns = max_pages * page_rows
    lane = iota((heads, columns), 1)
    own_head = lane % heads_kv == iota((heads, columns), 0) // group
    position = lane // heads_kv
    for r in range(requests):
        query = qs[pl.ds(r, heads, stride=requests), :].astype(BF16)
        gathered = jnp.concatenate([key_pages[table[r, j]] for j in range(max_pages)], axis=0)
        scores = dot(query, gathered, NT) * (1.0 / math.sqrt(head_dim))
        scores = jnp.where(own_head & (position <= lengths[r]), scores, -1e30)
        exponent = jnp.exp(scores - jnp.max(scores, axis=1, keepdims=True))
        sums[r] = jnp.broadcast_to(jnp.sum(exponent, axis=1, keepdims=True), (heads, head_dim))
        probs[r] = exponent.astype(BF16)

    value_load.wait()
    for r, (page, slot) in enumerate(spots):
        values[page, slot] = fresh[r][:, head_dim:]
    for r in range(requests):
        gathered = jnp.concatenate([value_pages[table[r, j]] for j in range(max_pages)], axis=0)
        att[pl.ds(r, heads, stride=requests), :] = dot(probs[r], gathered) / sums[r]
    attended = jnp.concatenate(
        [att[pl.ds(h * requests, requests), :] for h in range(heads)], axis=1
    ).astype(BF16)
    weight_load.wait()
    projected = dot(attended, kept_weight[...])
    for copy in later:
        copy.wait()
    return projected


def as_row(column):
    shape = (column.shape[0],) * 2
    return jnp.sum(jnp.where(iota(shape, 0) == iota(shape, 1), column, 0.0), axis=0, keepdims=True)


def route(projected, hidden, gain, router, ids, mixed_ref, norms_ref, top_ref, slabs_ref, comb_ref, capacity):
    requests, width = hidden.shape
    experts = router.shape[0]
    parts = SLAB // capacity
    piece = width // parts
    slab_rows = experts * SLAB
    mixed = (hidden[...].astype(F32) + projected).astype(BF16)
    mixed_ref[...] = mixed
    mixed = mixed.astype(F32)
    norms = jnp.sqrt(jnp.mean(mixed * mixed, axis=1, keepdims=True) + 1e-06)
    norms_ref[...] = as_row(norms)
    normed = (mixed / norms * gain[...].astype(F32).reshape(1, width)).astype(BF16)
    logits = dot(normed, router[...], NT)
    top_ref[...] = as_row(jnp.max(logits, axis=1, keepdims=True))
    column = iota((requests, experts), 1)
    named = column < 0
    for k in range(ids.shape[1]):
        named = named | (ids[:, k : k + 1] == column)
    weights = jnp.where(named, jnp.exp(logits), 0.0)
    weights = weights / jnp.sum(weights, axis=1, keepdims=True)
    earlier = (iota((requests, requests), 1) < iota((requests, requests), 0)).astype(F32)
    rank = dot(earlier, named.astype(F32))
    place = jnp.where(named, rank, -1.0)
    normed = normed.astype(F32)
    stacked = jnp.concatenate([normed[:, p * piece : (p + 1) * piece] for p in range(parts)], axis=0)
    places = jnp.concatenate([place] * parts, axis=0)
    shape = (slab_rows, parts * requests)
    inner = iota(shape, 0) % SLAB
    spread = (iota((slab_rows, experts), 0) // SLAB == iota((slab_rows, experts), 1)).astype(F32)
    picks = (dot(spread, places, NT) == (inner // parts).astype(F32)) & (
        inner % parts == iota(shape, 1) // requests
    )
    slabs_ref[...] = dot(picks.astype(BF16), stacked.astype(BF16)).astype(BF16)
    shape = (experts, slab_rows)
    spread = (iota(shape, 1) // SLAB == iota(shape, 0)).astype(F32)
    inner = iota((requests, slab_rows), 1) % SLAB
    comb_ref[...] = jnp.where(
        dot(place, spread) == (inner // parts).astype(F32),
        dot(weights, spread, precision=lax.Precision.HIGHEST),
        0.0,
    )


def attend_route_kernel(capacity, *refs):
    inputs, (keys, values, mixed, norms, top, slabs, comb) = refs[:10], refs[10:17]
    small, scratch = refs[17:25], refs[25:]
    projected = attend(inputs, keys, values, (small, scratch))
    hidden, gain, router, ids = small[4:]
    route(projected, hidden, gain, router, ids, mixed, norms, top, slabs, comb, capacity)


def attend_kernel(*refs):
    keys, values, projected = refs[6:9]
    projected[...] = attend(refs[:6], keys, values, (refs[9:13], refs[13:]))


def route_kernel(capacity, projected, hidden, gain, router, ids, mixed, norms, top, slabs, comb):
    route(projected[...], hidden, gain, router, ids, mixed, norms, top, slabs, comb, capacity)


def unit_chunks(units):
    return [(start, min(256, units - start)) for start in range(0, units, 256)]


def expert_kernel(capacity, arrived, own_up, own_down, other_up, other_down, keys, values, slabs, new_pool,
                  slab_rows, kept_up, kept_down, rows, total, sems):
    units = kept_down.shape[0]
    arrive = pltpu.make_async_copy(arrived, slab_rows, sems.at[0])
    arrive.start()
    chunks = []
    for i, (start, size) in enumerate(unit_chunks(units)):
        span = pl.ds(start, size)
        chunks.append((span, copies(
            [(own_up.at[0, :, span, :], kept_up.at[:, span, :]), (own_down.at[0, span, :], kept_down.at[span, :])],
            sems,
            1 + 2 * i,
        )))
    stores = copies(
        [(keys, pool_half(new_pool, 0)), (values, pool_half(new_pool, 1))], sems, 1 + 2 * len(chunks)
    )
    for copy in [copy for _, loads in chunks for copy in loads] + stores:
        copy.start()
    arrive.wait()
    parts = SLAB // capacity
    piece = slabs.shape[1]
    block = 128
    each = block // parts
    blocks = slabs.shape[0] // block
    shape = (block, block)
    slab_row, sorted_row = iota(shape, 1), iota(shape, 0)
    sort = (slab_row == sorted_row % each * parts + sorted_row // each).astype(BF16)
    for i in range(blocks):
        sorted_rows = dot(sort, slab_rows[pl.ds(i * block, block), :]).astype(BF16)
        rows[pl.ds(i * each, each), :] = jnp.concatenate(
            [sorted_rows[p * each : (p + 1) * each] for p in range(parts)], axis=1
        )
    states = rows[...]
    steps = [(other_up.at[0], other_down.at[0], span, []) for span, _ in chunks]
    steps += [(kept_up, kept_down, span, loads) for span, loads in chunks]
    for i, (gate_up, down, span, loads) in enumerate(steps):
        for copy in loads:
            copy.wait()
        gate = dot(states, gate_up[0, span, :], NT)
        up = dot(states, gate_up[1, span, :], NT)
        activated = (gate / (1.0 + jnp.exp(-gate)) * up).astype(BF16)
        term = dot(activated, down[span, :])
        total[...] = term if i == 0 else total[...] + term
    slab_row, sorted_row = iota(shape, 0), iota(shape, 1)
    unsort = (slab_row == sorted_row % each * parts + sorted_row // each).astype(BF16)
    for i in range(blocks):
        summed = total[pl.ds(i * each, each), :].astype(BF16)
        stacked = jnp.concatenate([summed[:, p * piece : (p + 1) * piece] for p in range(parts)], axis=0)
        slabs[pl.ds(i * block, block), :] = dot(unsort, stacked).astype(BF16)
    for copy in stores:
        copy.wait()


def gather_terms(comb, slabs, capacity):
    parts = SLAB // capacity
    requests = comb.shape[0]
    weights = comb[...]
    pieces = []
    for _ in range(3):
        piece = weights.astype(BF16).astype(F32)
        weights = weights - piece
        pieces.append(piece)
    part = iota(comb.shape, 1) % parts
    stacked = jnp.concatenate(
        [jnp.where(part == p, piece, 0.0) for p in range(parts) for piece in pieces], axis=0
    ).astype(BF16)
    terms = dot(stacked, slabs[...])
    return jnp.concatenate(
        [
            sum(terms[(3 * p + i) * requests : (3 * p + i + 1) * requests] for i in range(3))
            for p in range(parts)
        ],
        axis=1,
    )


def combine_kernel(capacity, comb, slabs, mixed, out):
    out[...] = (mixed[...].astype(F32) + gather_terms(comb, slabs, capacity)).astype(BF16)


def gather_kernel(capacity, comb, slabs, out):
    out[...] = gather_terms(comb, slabs, capacity).astype(BF16)


def vmem(count):
    return [pl.BlockSpec(memory_space=pltpu.VMEM)] * count


def in_hbm(count):
    return [pl.BlockSpec(memory_space=pltpu.HBM)] * count


def pinned(*arrays):
    return [pltpu.with_memory_space_constraint(array, pltpu.HBM) for array in arrays]


def like(shape, dtype=BF16):
    return jax.ShapeDtypeStruct(shape, dtype)


def body(
    hidden,
    queries,
    fresh_key_value,
    kv_pool,
    page_table,
    lengths,
    out_weight,
    norm_gain,
    router_weight,
    expert_ids,
    expert_gate_up,
    expert_down,
):
    requests, width = hidden.shape
    req_count, kv_count = lax.axis_size("req"), lax.axis_size("kv")
    pages, page_len, heads_kv, pair_dim = kv_pool.shape
    head_dim = pair_dim // 2
    heads = queries.shape[1] // head_dim
    experts = router_weight.shape[0]
    copies = req_count // experts
    chosen = expert_ids.shape[1]
    capacity = 2 * max(1, (requests * chosen + 2 * experts - 1) // (2 * experts))
    parts = SLAB // capacity
    piece = width // parts
    slab_rows = experts * SLAB

    same_part = [list(range(part, req_count, copies)) for part in range(copies)]
    swap = [(index, index ^ 1) for index in range(req_count)]
    other_up = lax.ppermute(expert_gate_up, "req", swap)
    other_down = lax.ppermute(expert_down, "req", swap)

    attend_scratch = [
        pltpu.VMEM(out_weight.shape, BF16),
        pltpu.VMEM((heads * requests, head_dim), F32),
        pltpu.VMEM((heads * requests, head_dim), F32),
        pltpu.VMEM((requests, heads, page_table.shape[1] * page_len * heads_kv), BF16),
        pltpu.VMEM((requests, heads, head_dim), F32),
        pltpu.SemaphoreType.DMA((11,)),
    ]

    def small(*arrays):
        return [pltpu.VMEM(array.shape, array.dtype) for array in arrays]

    inputs = [pltpu.SMEM(page_table.shape, jnp.int32), pltpu.SMEM(lengths.shape, jnp.int32)]
    inputs += small(queries, fresh_key_value)
    kept_shapes = [like((pages, page_len, heads_kv, head_dim))] * 2
    routed_shapes = [
        like((requests, width)),
        like((1, requests), F32),
        like((1, requests), F32),
        like((slab_rows, piece)),
        like((requests, slab_rows), F32),
    ]
    attend_params = pltpu.CompilerParams(vmem_limit_bytes=24 * MIB)
    if kv_count == 1:
        keys, values, mixed, norms, top, slabs, comb = pl.pallas_call(
            functools.partial(attend_route_kernel, capacity),
            out_shape=kept_shapes + routed_shapes,
            in_specs=in_hbm(10),
            out_specs=vmem(7),
            scratch_shapes=inputs + small(hidden, norm_gain, router_weight, expert_ids) + attend_scratch,
            compiler_params=attend_params,
        )(*pinned(page_table, lengths, queries, fresh_key_value, hidden, norm_gain, router_weight, expert_ids,
                  kv_pool, out_weight))
    else:
        keys, values, projected = pl.pallas_call(
            attend_kernel,
            out_shape=kept_shapes + [like((requests, width), F32)],
            in_specs=in_hbm(6),
            out_specs=vmem(3),
            scratch_shapes=inputs + attend_scratch,
            compiler_params=attend_params,
        )(*pinned(page_table, lengths, queries, fresh_key_value, kv_pool, out_weight))
        projected = lax.psum(projected, "kv")
        mixed, norms, top, slabs, comb = pl.pallas_call(
            functools.partial(route_kernel, capacity),
            out_shape=routed_shapes,
            in_specs=vmem(5),
            out_specs=vmem(5),
        )(projected, hidden, norm_gain, router_weight, expert_ids)

    def exchange(array):
        array = array.reshape(experts, SLAB, piece)
        array = lax.all_to_all(
            array, "req", split_axis=0, concat_axis=0, tiled=True, axis_index_groups=same_part
        )
        return array.reshape(slab_rows, piece)

    arrived = exchange(slabs)
    kept = experts * capacity
    units = expert_down.shape[1]
    leaving, new_pool = pl.pallas_call(
        functools.partial(expert_kernel, capacity),
        out_shape=[like((slab_rows, piece)), like(kv_pool.shape)],
        in_specs=in_hbm(3) + vmem(4),
        out_specs=vmem(1) + in_hbm(1),
        scratch_shapes=[
            pltpu.VMEM((slab_rows, piece), BF16),
            pltpu.VMEM((2, units, width), BF16),
            pltpu.VMEM((units, width), BF16),
            pltpu.VMEM((kept, width), BF16),
            pltpu.VMEM((kept, width), F32),
            pltpu.SemaphoreType.DMA((3 + 2 * len(unit_chunks(units)),)),
        ],
        compiler_params=pltpu.CompilerParams(vmem_limit_bytes=20 * MIB),
    )(arrived, *pinned(expert_gate_up, expert_down), other_up, other_down, keys, values)
    returned = exchange(leaving)
    if kv_count == 1:
        out_hidden = pl.pallas_call(
            functools.partial(combine_kernel, capacity),
            out_shape=like((requests, width)),
            in_specs=vmem(3),
            out_specs=pl.BlockSpec(memory_space=pltpu.VMEM),
            compiler_params=pltpu.CompilerParams(vmem_limit_bytes=8 * MIB),
        )(comb, returned, mixed)
    else:
        routed = pl.pallas_call(
            functools.partial(gather_kernel, capacity),
            out_shape=like((requests, width)),
            in_specs=vmem(2),
            out_specs=pl.BlockSpec(memory_space=pltpu.VMEM),
        )(comb, returned)
        routed = lax.psum(routed, "kv").astype(F32)
        out_hidden = (mixed.astype(F32) + routed).astype(BF16)
    return out_hidden, new_pool, norms.reshape(requests), top.reshape(requests)


def solution(mesh):
    in_specs = (
        P("req", None),
        P("req", "kv"),
        P("req", "kv", None),
        P("req", None, "kv", None),
        P("req", None),
        P("req"),
        P("kv", None),
        P(),
        P(),
        P("req", None),
        P("req", None, "kv", None),
        P("req", "kv", None),
    )
    out_specs = (P("req", None), P("req", None, "kv", None), P("req"), P("req"))
    return jax.shard_map(body, mesh=mesh, in_specs=in_specs, out_specs=out_specs, check_vma=False)
```

```python
import functools
import math

import jax
import jax.numpy as jnp
from jax import lax
from jax.experimental import pallas as pl
from jax.experimental.pallas import tpu as pltpu
from jax.sharding import PartitionSpec as P

BF16 = jnp.bfloat16
F32 = jnp.float32
NT = (((1,), (1,)), ((), ()))
NN = (((1,), (0,)), ((), ()))
SLAB = 16
MIB = 1 << 20


def dot(a, b, dims=NN, precision=None):
    return lax.dot_general(a, b, dims, precision=precision, preferred_element_type=F32)


def iota(shape, dim):
    return lax.broadcasted_iota(jnp.int32, shape, dim)


def copies(pairs, sems, first=0):
    return [pltpu.make_async_copy(src, dst, sems.at[first + i]) for i, (src, dst) in enumerate(pairs)]


def pool_half(array, i):
    head_dim = array.shape[3] // 2
    return array.at[:, :, :, pl.ds(i * head_dim, head_dim)]


def attend(refs, keys, values, scratch):
    small, (kept_weight, qs, att, probs, sums, sems) = scratch
    table, lengths, q_ref, fresh = small[:4]
    requests, max_pages = table.shape
    pages, page_len, heads_kv, head_dim = keys.shape
    heads = q_ref.shape[1] // head_dim
    group = heads // heads_kv
    page_rows = page_len * heads_kv
    pool, weight = refs[-2:]
    loads = copies(list(zip(refs[:4], small[:4])), sems)
    key_load, value_load, weight_load = copies(
        [(pool_half(pool, 0), keys), (pool_half(pool, 1), values), (weight, kept_weight)], sems, 4
    )
    later = copies(list(zip(refs[4:-2], small[4:])), sems, 7)
    for copy in loads + [key_load]:
        copy.start()
    for copy in loads:
        copy.wait()
    for copy in [value_load, weight_load] + later:
        copy.start()
    for h in range(heads):
        qs[pl.ds(h * requests, requests), :] = q_ref[:, pl.ds(h * head_dim, head_dim)].astype(F32)
    spots = [(table[r, lengths[r] // page_len], lengths[r] % page_len) for r in range(requests)]

    key_load.wait()
    for r, (page, slot) in enumerate(spots):
        keys[page, slot] = fresh[r][:, :head_dim]
    key_pages = keys.reshape(pages, page_rows, head_dim)
    value_pages = values.reshape(pages, page_rows, head_dim)
    columns = max_pages * page_rows
    lane = iota((heads, columns), 1)
    own_head = lane % heads_kv == iota((heads, columns), 0) // group
    position = lane // heads_kv
    for r in range(requests):
        query = qs[pl.ds(r, heads, stride=requests), :].astype(BF16)
        gathered = jnp.concatenate([key_pages[table[r, j]] for j in range(max_pages)], axis=0)
        scores = dot(query, gathered, NT) * (1.0 / math.sqrt(head_dim))
        scores = jnp.where(own_head & (position <= lengths[r]), scores, -1e30)
        exponent = jnp.exp(scores - jnp.max(scores, axis=1, keepdims=True))
        sums[r] = jnp.broadcast_to(jnp.sum(exponent, axis=1, keepdims=True), (heads, head_dim))
        probs[r] = exponent.astype(BF16)

    value_load.wait()
    for r, (page, slot) in enumerate(spots):
        values[page, slot] = fresh[r][:, head_dim:]
    for r in range(requests):
        gathered = jnp.concatenate([value_pages[table[r, j]] for j in range(max_pages)], axis=0)
        att[pl.ds(r, heads, stride=requests), :] = dot(probs[r], gathered) / sums[r]
    attended = jnp.concatenate(
        [att[pl.ds(h * requests, requests), :] for h in range(heads)], axis=1
    ).astype(BF16)
    weight_load.wait()
    projected = dot(attended, kept_weight[...])
    for copy in later:
        copy.wait()
    return projected


def as_row(column):
    shape = (column.shape[0],) * 2
    return jnp.sum(jnp.where(iota(shape, 0) == iota(shape, 1), column, 0.0), axis=0, keepdims=True)


def route(projected, hidden, gain, router, ids, mixed_ref, norms_ref, top_ref, packet_ref):
    requests, width = hidden.shape
    experts = router.shape[0]
    mixed = (hidden[...].astype(F32) + projected).astype(BF16)
    mixed_ref[...] = mixed
    mixed = mixed.astype(F32)
    norms = jnp.sqrt(jnp.mean(mixed * mixed, axis=1, keepdims=True) + 1e-06)
    norms_ref[...] = as_row(norms)
    normed = (mixed / norms * gain[...].astype(F32).reshape(1, width)).astype(BF16)
    packet_ref[:, :width] = normed
    logits = dot(normed, router[...], NT)
    top_ref[...] = as_row(jnp.max(logits, axis=1, keepdims=True))
    column = iota((requests, experts), 1)
    named = column < 0
    for k in range(ids.shape[1]):
        named = named | (ids[:, k : k + 1] == column)
    weights = jnp.where(named, jnp.exp(logits), 0.0)
    weights = weights / jnp.sum(weights, axis=1, keepdims=True)
    earlier = (iota((requests, requests), 1) < iota((requests, requests), 0)).astype(F32)
    rank = dot(earlier, named.astype(F32))
    fields = [jnp.where(named, rank, -1.0)] + split(weights)
    spare = packet_ref.shape[1] - width - len(fields) * experts
    if spare:
        fields.append(jnp.zeros((requests, spare), F32))
    packet_ref[:, width:] = jnp.concatenate(fields, axis=1).astype(BF16)


def split(values):
    pieces = []
    for _ in range(3):
        pieces.append(values.astype(BF16).astype(F32))
        values = values - pieces[-1]
    return pieces


def dispatch_kernel(capacity, experts, own, partner, slabs_ref, comb_ref):
    rows, piece = slabs_ref.shape
    requests = own.shape[0]
    tokens = 2 * requests
    parts = SLAB // (2 * capacity)
    width = parts * piece
    first = lax.axis_index("req") // (lax.axis_size("req") // 2) * (rows // SLAB)
    packet = jnp.concatenate([own[...].astype(F32), partner[...].astype(F32)], axis=0)
    place = packet[:, width : width + experts]
    source = iota(place.shape, 0) // requests * capacity
    place = jnp.where(place >= 0.0, place + source.astype(F32), -1.0)
    weights = sum(packet[:, width + i * experts : width + (i + 1) * experts] for i in (1, 2, 3))
    stacked = jnp.concatenate([packet[:, p * piece : (p + 1) * piece] for p in range(parts)], axis=0)
    places = jnp.concatenate([place] * parts, axis=0)
    shape = (rows, parts * tokens)
    inner = iota(shape, 0) % SLAB
    spread = (iota((rows, experts), 0) // SLAB + first == iota((rows, experts), 1)).astype(F32)
    picks = (dot(spread, places, NT) == (inner // parts).astype(F32)) & (
        inner % parts == iota(shape, 1) // tokens
    )
    slabs_ref[...] = dot(picks.astype(BF16), stacked.astype(BF16)).astype(BF16)
    shape = (experts, rows)
    spread = (iota(shape, 1) // SLAB + first == iota(shape, 0)).astype(F32)
    inner = iota((tokens, rows), 1) % SLAB
    comb_ref[...] = jnp.where(
        dot(place, spread) == (inner // parts).astype(F32),
        dot(weights, spread, precision=lax.Precision.HIGHEST),
        0.0,
    )


def attend_route_kernel(*refs):
    inputs, outputs = refs[:10], refs[10:14]
    small, scratch = refs[14:22], refs[22:]
    projected = attend(inputs, scratch[0], scratch[1], (small, scratch[2:]))
    hidden, gain, router, ids = small[4:]
    route(projected, hidden, gain, router, ids, *outputs)


def attend_kernel(*refs):
    projected, scratch = refs[6], refs[11:]
    projected[...] = attend(refs[:6], scratch[0], scratch[1], (refs[7:11], scratch[2:]))


def refresh_kernel(table, lengths, fresh, after, pool, new_pool, done, kept, sems):
    done[...] = after[...]
    pages, page_len = kept.shape[:2]
    step = -(-pages // 4)
    spans = [pl.ds(start, min(step, pages - start)) for start in range(0, pages, step)]
    loads = copies([(pool.at[span], kept.at[span]) for span in spans], sems)
    stores = copies([(kept.at[span], new_pool.at[span]) for span in spans], sems, len(spans))
    for copy in loads:
        copy.start()
    for copy in loads:
        copy.wait()
    for r in range(table.shape[0]):
        kept[table[r, lengths[r] // page_len], lengths[r] % page_len] = fresh[r]
    for copy in stores:
        copy.start()
    for copy in stores:
        copy.wait()


def route_kernel(projected, hidden, gain, router, ids, *outputs):
    route(projected[...], hidden, gain, router, ids, *outputs)


def unit_chunks(units):
    return [(start, min(256, units - start)) for start in range(0, units, 256)]


def expert_kernel(slots, arrived, own_up, own_down, other_up, other_down, slabs, done,
                  slab_rows, kept_up, kept_down, rows, total, sems):
    units = kept_down.shape[0]
    arrive = pltpu.make_async_copy(arrived, slab_rows, sems.at[0])
    arrive.start()
    chunks = []
    for i, (start, size) in enumerate(unit_chunks(units)):
        span = pl.ds(start, size)
        chunks.append((span, copies(
            [(own_up.at[0, :, span, :], kept_up.at[:, span, :]), (own_down.at[0, span, :], kept_down.at[span, :])],
            sems,
            1 + 2 * i,
        )))
    for copy in [copy for _, loads in chunks for copy in loads]:
        copy.start()
    arrive.wait()
    parts = SLAB // slots
    piece = slabs.shape[1]
    block = 128
    each = block // parts
    blocks = slabs.shape[0] // block
    shape = (block, block)
    slab_row, sorted_row = iota(shape, 1), iota(shape, 0)
    sort = (slab_row == sorted_row % each * parts + sorted_row // each).astype(BF16)
    for i in range(blocks):
        sorted_rows = dot(sort, slab_rows[pl.ds(i * block, block), :]).astype(BF16)
        rows[pl.ds(i * each, each), :] = jnp.concatenate(
            [sorted_rows[p * each : (p + 1) * each] for p in range(parts)], axis=1
        )
    states = rows[...]
    steps = [(other_up.at[0], other_down.at[0], span, []) for span, _ in chunks]
    steps += [(kept_up, kept_down, span, loads) for span, loads in chunks]
    for i, (gate_up, down, span, loads) in enumerate(steps):
        for copy in loads:
            copy.wait()
        gate = dot(states, gate_up[0, span, :], NT)
        up = dot(states, gate_up[1, span, :], NT)
        activated = (gate / (1.0 + jnp.exp(-gate)) * up).astype(BF16)
        term = dot(activated, down[span, :])
        total[...] = term if i == 0 else total[...] + term
    slab_row, sorted_row = iota(shape, 0), iota(shape, 1)
    unsort = (slab_row == sorted_row % each * parts + sorted_row // each).astype(BF16)
    for i in range(blocks):
        summed = total[pl.ds(i * each, each), :].astype(BF16)
        stacked = jnp.concatenate([summed[:, p * piece : (p + 1) * piece] for p in range(parts)], axis=0)
        slabs[pl.ds(i * block, block), :] = dot(unsort, stacked).astype(BF16)
    done[...] = jnp.zeros(done.shape, F32)


def gather_kernel(slots, comb, slabs, stored, own, partner):
    parts = SLAB // slots
    tokens = comb.shape[0]
    part = iota(comb.shape, 1) % parts
    pieces = split(comb[...])
    stacked = jnp.concatenate(
        [jnp.where(part == p, piece, 0.0) for p in range(parts) for piece in pieces], axis=0
    ).astype(BF16)
    terms = dot(stacked, slabs[...])
    terms = jnp.concatenate(
        [sum(terms[(3 * p + i) * tokens : (3 * p + i + 1) * tokens] for i in range(3)) for p in range(parts)],
        axis=1,
    )
    own[...] = terms[: tokens // 2]
    partner[...] = terms[tokens // 2 :].astype(BF16)


def finish_kernel(mixed, own, partner, out):
    out[...] = (mixed[...].astype(F32) + own[...] + partner[...].astype(F32)).astype(BF16)


def vmem(count):
    return [pl.BlockSpec(memory_space=pltpu.VMEM)] * count


def scalars(count):
    return [pl.BlockSpec(memory_space=pltpu.SMEM)] * count


def in_hbm(count):
    return [pl.BlockSpec(memory_space=pltpu.HBM)] * count


def pinned(*arrays):
    return [pltpu.with_memory_space_constraint(array, pltpu.HBM) for array in arrays]


def like(shape, dtype=BF16):
    return jax.ShapeDtypeStruct(shape, dtype)


def body(
    hidden,
    queries,
    fresh_key_value,
    kv_pool,
    page_table,
    lengths,
    out_weight,
    norm_gain,
    router_weight,
    expert_ids,
    expert_gate_up,
    expert_down,
):
    requests, width = hidden.shape
    req_count, kv_count = lax.axis_size("req"), lax.axis_size("kv")
    pages, page_len, heads_kv, pair_dim = kv_pool.shape
    head_dim = pair_dim // 2
    heads = queries.shape[1] // head_dim
    experts = router_weight.shape[0]
    copies = req_count // experts
    chosen = expert_ids.shape[1]
    capacity = 2 * max(1, (requests * chosen + 2 * experts - 1) // (2 * experts))
    slots = 2 * capacity
    piece = width // (SLAB // slots)
    members = experts // 2
    slab_rows = members * SLAB

    far = req_count // 2
    near = [list(range(base + part, base + far, copies)) for base in (0, far) for part in range(copies)]
    across = [(index, (index + far) % req_count) for index in range(req_count)]
    swap = [(index, index ^ 1) for index in range(req_count)]
    other_up = lax.ppermute(expert_gate_up, "req", swap)
    other_down = lax.ppermute(expert_down, "req", swap)

    attend_scratch = [
        pltpu.VMEM((pages, page_len, heads_kv, head_dim), BF16),
        pltpu.VMEM((pages, page_len, heads_kv, head_dim), BF16),
        pltpu.VMEM(out_weight.shape, BF16),
        pltpu.VMEM((heads * requests, head_dim), F32),
        pltpu.VMEM((heads * requests, head_dim), F32),
        pltpu.VMEM((requests, heads, page_table.shape[1] * page_len * heads_kv), BF16),
        pltpu.VMEM((requests, heads, head_dim), F32),
        pltpu.SemaphoreType.DMA((11,)),
    ]

    def small(*arrays):
        return [pltpu.VMEM(array.shape, array.dtype) for array in arrays]

    inputs = [pltpu.SMEM(page_table.shape, jnp.int32), pltpu.SMEM(lengths.shape, jnp.int32)]
    inputs += small(queries, fresh_key_value)
    routed_shapes = [
        like((requests, width)),
        like((1, requests), F32),
        like((1, requests), F32),
        like((requests, width + -(-4 * experts // 128) * 128)),
    ]
    attend_params = pltpu.CompilerParams(vmem_limit_bytes=24 * MIB)
    if kv_count == 1:
        mixed, norms, top, packet = pl.pallas_call(
            attend_route_kernel,
            out_shape=routed_shapes,
            in_specs=in_hbm(10),
            out_specs=vmem(4),
            scratch_shapes=inputs + small(hidden, norm_gain, router_weight, expert_ids) + attend_scratch,
            compiler_params=attend_params,
        )(*pinned(page_table, lengths, queries, fresh_key_value, hidden, norm_gain, router_weight, expert_ids,
                  kv_pool, out_weight))
    else:
        projected = pl.pallas_call(
            attend_kernel,
            out_shape=like((requests, width), F32),
            in_specs=in_hbm(6),
            out_specs=pl.BlockSpec(memory_space=pltpu.VMEM),
            scratch_shapes=inputs + attend_scratch,
            compiler_params=attend_params,
        )(*pinned(page_table, lengths, queries, fresh_key_value, kv_pool, out_weight))
        projected = lax.psum(projected, "kv")
        mixed, norms, top, packet = pl.pallas_call(
            route_kernel,
            out_shape=routed_shapes,
            in_specs=vmem(5),
            out_specs=vmem(4),
        )(projected, hidden, norm_gain, router_weight, expert_ids)

    def exchange(array):
        array = array.reshape(members, SLAB, piece)
        array = lax.all_to_all(array, "req", split_axis=0, concat_axis=0, tiled=True, axis_index_groups=near)
        return array.reshape(slab_rows, piece)

    small_grant = pltpu.CompilerParams(vmem_limit_bytes=8 * MIB)
    slabs, comb = pl.pallas_call(
        functools.partial(dispatch_kernel, capacity, experts),
        out_shape=[like((slab_rows, piece)), like((2 * requests, slab_rows), F32)],
        in_specs=vmem(2),
        out_specs=vmem(2),
        compiler_params=small_grant,
    )(packet, lax.ppermute(packet, "req", across))
    arrived = exchange(slabs)
    kept = members * slots
    units = expert_down.shape[1]
    leaving, done = pl.pallas_call(
        functools.partial(expert_kernel, slots),
        out_shape=[like((slab_rows, piece)), like((8, 128), F32)],
        in_specs=in_hbm(3) + vmem(2),
        out_specs=vmem(2),
        scratch_shapes=[
            pltpu.VMEM((slab_rows, piece), BF16),
            pltpu.VMEM((2, units, width), BF16),
            pltpu.VMEM((units, width), BF16),
            pltpu.VMEM((kept, width), BF16),
            pltpu.VMEM((kept, width), F32),
            pltpu.SemaphoreType.DMA((1 + 2 * len(unit_chunks(units)),)),
        ],
        compiler_params=pltpu.CompilerParams(vmem_limit_bytes=20 * MIB),
    )(arrived, *pinned(expert_gate_up, expert_down), other_up, other_down)
    new_pool, stored = pl.pallas_call(
        refresh_kernel,
        out_shape=[like(kv_pool.shape), like((8, 128), F32)],
        in_specs=scalars(2) + vmem(2) + in_hbm(1),
        out_specs=in_hbm(1) + vmem(1),
        scratch_shapes=[pltpu.VMEM(kv_pool.shape, BF16), pltpu.SemaphoreType.DMA((8,))],
        compiler_params=pltpu.CompilerParams(vmem_limit_bytes=12 * MIB),
        cost_estimate=pl.CostEstimate(flops=0, bytes_accessed=8 * kv_pool.size, transcendentals=0),
    )(page_table, lengths, fresh_key_value, done, *pinned(kv_pool))
    own_sum, partner_sum = pl.pallas_call(
        functools.partial(gather_kernel, slots),
        out_shape=[like((requests, width), F32), like((requests, width))],
        in_specs=vmem(3),
        out_specs=vmem(2),
        compiler_params=small_grant,
    )(comb, exchange(leaving), stored)
    crossed = lax.ppermute(partner_sum, "req", across)
    if kv_count == 1:
        out_hidden = pl.pallas_call(
            finish_kernel,
            out_shape=like((requests, width)),
            in_specs=vmem(3),
            out_specs=pl.BlockSpec(memory_space=pltpu.VMEM),
            compiler_params=small_grant,
        )(mixed, own_sum, crossed)
    else:
        routed = (own_sum + crossed.astype(F32)).astype(BF16)
        routed = lax.psum(routed, "kv").astype(F32)
        out_hidden = (mixed.astype(F32) + routed).astype(BF16)
    return out_hidden, new_pool, norms.reshape(requests), top.reshape(requests)


def solution(mesh):
    in_specs = (
        P("req", None),
        P("req", "kv"),
        P("req", "kv", None),
        P("req", None, "kv", None),
        P("req", None),
        P("req"),
        P("kv", None),
        P(),
        P(),
        P("req", None),
        P("req", None, "kv", None),
        P("req", "kv", None),
    )
    out_specs = (P("req", None), P("req", None, "kv", None), P("req"), P("req"))
    return jax.shard_map(body, mesh=mesh, in_specs=in_specs, out_specs=out_specs, check_vma=False)
```

```python
import functools
import math

import jax
import jax.numpy as jnp
from jax import lax
from jax.experimental import pallas as pl
from jax.experimental.pallas import tpu as pltpu
from jax.sharding import PartitionSpec as P

BF16 = jnp.bfloat16
F32 = jnp.float32
NT = (((1,), (1,)), ((), ()))
NN = (((1,), (0,)), ((), ()))
SHARED_PAGES = 8
SLAB = 16
MIB = 1 << 20


def dot(a, b, dims=NN, precision=None):
    return lax.dot_general(a, b, dims, precision=precision, preferred_element_type=F32)


def iota(shape, dim):
    return lax.broadcasted_iota(jnp.int32, shape, dim)


def copies(pairs, sems, first=0):
    return [pltpu.make_async_copy(src, dst, sems.at[first + i]) for i, (src, dst) in enumerate(pairs)]


def group_turn(chips, part):
    return chips * 9 // 16 if part % 2 else chips * 3 // 8


def pool_half(array, i):
    head_dim = array.shape[3] // 2
    return array.at[:, :, :, pl.ds(i * head_dim, head_dim)]


def attend(refs, keys, values, scratch):
    small, (kept_weight, qs, att, scores, probs, sems) = scratch
    table, lengths, q_ref, fresh = small[:4]
    requests, max_pages = table.shape
    pages, page_len, heads_kv, head_dim = keys.shape
    heads = q_ref.shape[1] // head_dim
    group = heads // heads_kv
    page_rows = page_len * heads_kv
    pool, weight = refs[-2:]
    loads = copies(list(zip(refs[:4], small[:4])), sems)
    key_load, value_load = copies([(pool_half(pool, 0), keys), (pool_half(pool, 1), values)], sems, 4)
    later = copies(list(zip(refs[4:-2], small[4:])), sems, 6)
    step = weight.shape[0] // 4
    spans = [pl.ds(i * step, step) for i in range(4)]
    weight_loads = copies([(weight.at[span], kept_weight.at[span]) for span in spans], sems, 10)
    for copy in loads + [key_load]:
        copy.start()
    for copy in loads:
        copy.wait()
    for copy in [value_load] + later + weight_loads[:1]:
        copy.start()
    for h in range(heads):
        qs[pl.ds(h * requests, requests), :] = q_ref[:, pl.ds(h * head_dim, head_dim)].astype(F32)
    spots = [(table[r, lengths[r] // page_len], lengths[r] % page_len) for r in range(requests)]

    key_load.wait()
    for r, (page, slot) in enumerate(spots):
        keys[page, slot] = fresh[r][:, :head_dim]
    key_pages = keys.reshape(pages, page_rows, head_dim)
    value_pages = values.reshape(pages, page_rows, head_dim)
    columns = max_pages * page_rows
    shared_columns = SHARED_PAGES * page_rows
    rows = requests * heads

    def pages_of(array, r, first, last):
        return jnp.concatenate([array[table[r, j]] for j in range(first, last)], axis=0)

    weight_loads[1].start()
    query = [qs[pl.ds(r, heads, stride=requests), :] for r in range(requests)]
    query_rows = jnp.concatenate(query, axis=0).astype(BF16)
    scores[:, :shared_columns] = dot(query_rows, pages_of(key_pages, 0, 0, SHARED_PAGES), NT)
    for r in range(requests):
        scores[pl.ds(r * heads, heads), shared_columns:] = dot(
            query[r].astype(BF16), pages_of(key_pages, r, SHARED_PAGES, max_pages), NT
        )
    lane = iota((heads, columns), 1)
    own_head = (lane & (heads_kv - 1)) == iota((heads, columns), 0) // group
    position = lane >> (heads_kv.bit_length() - 1)
    masked = jnp.concatenate(
        [
            jnp.where(own_head & (position <= lengths[r]), scores[pl.ds(r * heads, heads), :], -1e30)
            for r in range(requests)
        ],
        axis=0,
    )
    scale = 1.0 / math.sqrt(head_dim)
    exponent = jnp.exp((masked - jnp.max(masked, axis=1, keepdims=True)) * scale)
    sums = jnp.sum(exponent, axis=1, keepdims=True)
    probs[...] = exponent.astype(BF16)

    value_load.wait()
    for copy in weight_loads[2:]:
        copy.start()
    for r, (page, slot) in enumerate(spots):
        values[page, slot] = fresh[r][:, head_dim:]
    shared = dot(probs[:, :shared_columns], pages_of(value_pages, 0, 0, SHARED_PAGES))
    own = [
        dot(probs[pl.ds(r * heads, heads), shared_columns:], pages_of(value_pages, r, SHARED_PAGES, max_pages))
        for r in range(requests)
    ]
    mean = (shared + jnp.concatenate(own, axis=0)) / sums
    for r in range(requests):
        att[pl.ds(r, heads, stride=requests), :] = mean[r * heads : (r + 1) * heads]
    attended = jnp.concatenate(
        [att[pl.ds(h * requests, requests), :] for h in range(heads)], axis=1
    ).astype(BF16)
    projected = 0.0
    for i, copy in enumerate(weight_loads):
        copy.wait()
        projected = projected + dot(attended[:, i * step : (i + 1) * step], kept_weight[spans[i], :])
    for copy in later:
        copy.wait()
    return projected


def as_row(column):
    shape = (column.shape[0],) * 2
    return jnp.sum(jnp.where(iota(shape, 0) == iota(shape, 1), column, 0.0), axis=0, keepdims=True)


def route(projected, hidden, gain, router, ids, mixed_ref, norms_ref, top_ref, slabs_ref, comb_ref, capacity, leave=None):
    requests, width = hidden.shape
    experts = router.shape[0]
    parts = SLAB // capacity
    piece = width // parts
    slab_rows = experts * SLAB
    turns = jnp.where(lax.axis_index("req") % 2 == 0, group_turn(experts, 0), group_turn(experts, 1))

    def slab_expert(shape, dim):
        return (iota(shape, dim) // SLAB) ^ turns

    mixed = (hidden[...].astype(F32) + projected).astype(BF16)
    mixed_ref[...] = mixed
    mixed = mixed.astype(F32)
    norms = jnp.sqrt(jnp.mean(mixed * mixed, axis=1, keepdims=True) + 1e-06)
    norms_ref[...] = as_row(norms)
    normed = (mixed / norms * gain[...].astype(F32).reshape(1, width)).astype(BF16)
    logits = dot(normed, router[...], NT)
    top_ref[...] = as_row(jnp.max(logits, axis=1, keepdims=True))
    column = iota((requests, experts), 1)
    named = column < 0
    for k in range(ids.shape[1]):
        named = named | (ids[:, k : k + 1] == column)
    weights = jnp.where(named, jnp.exp(logits), 0.0)
    weights = weights / jnp.sum(weights, axis=1, keepdims=True)
    earlier = (iota((requests, requests), 1) < iota((requests, requests), 0)).astype(F32)
    rank = dot(earlier, named.astype(F32))
    place = jnp.where(named, rank, -1.0)
    normed = normed.astype(F32)
    stacked = jnp.concatenate([normed[:, p * piece : (p + 1) * piece] for p in range(parts)], axis=0)
    places = jnp.concatenate([place] * parts, axis=0)
    shape = (slab_rows, parts * requests)
    inner = iota(shape, 0) % SLAB
    spread = (slab_expert((slab_rows, experts), 0) == iota((slab_rows, experts), 1)).astype(F32)
    picks = (dot(spread, places, NT) == (inner // parts).astype(F32)) & (
        inner % parts == iota(shape, 1) // requests
    )
    slabs_ref[...] = dot(picks.astype(BF16), stacked.astype(BF16)).astype(BF16)
    if leave is not None:
        leave()
    shape = (experts, slab_rows)
    spread = (slab_expert(shape, 1) == iota(shape, 0)).astype(F32)
    inner = iota((requests, slab_rows), 1) % SLAB
    comb_ref[...] = jnp.where(
        dot(place, spread) == (inner // parts).astype(F32),
        dot(weights, spread, precision=lax.Precision.HIGHEST),
        0.0,
    )


def attend_route_kernel(capacity, *refs):
    inputs, (mixed, norms, top, slabs, comb) = refs[:10], refs[10:15]
    small, scratch = refs[15:23], refs[23:]
    keys, values, kept_slabs = scratch[:3]
    projected = attend(inputs, keys, values, (small, scratch[3:]))
    hidden, gain, router, ids = small[4:]
    leave = pltpu.make_async_copy(kept_slabs, slabs, scratch[-1].at[0])
    route(projected, hidden, gain, router, ids, mixed, norms, top, kept_slabs, comb, capacity, leave.start)
    leave.wait()


def attend_kernel(*refs):
    attended, scratch = refs[6], refs[11:]
    attended[...] = attend(refs[:6], scratch[0], scratch[1], (refs[7:11], scratch[2:]))


def refresh_kernel(table, lengths, fresh, after, pool, new_pool, kept, sems):
    pages, page_len = kept.shape[:2]
    step = -(-pages // 4)
    spans = [pl.ds(start, min(step, pages - start)) for start in range(0, pages, step)]
    loads = copies([(pool.at[span], kept.at[span]) for span in spans], sems)
    stores = copies([(kept.at[span], new_pool.at[span]) for span in spans], sems, len(spans))
    for copy in loads:
        copy.start()
    spots = [(table[r, lengths[r] // page_len], lengths[r] % page_len) for r in range(table.shape[0])]
    for i, (load, store) in enumerate(zip(loads, stores)):
        load.wait()
        for r, (page, slot) in enumerate(spots):

            @pl.when((page >= i * step) & (page < (i + 1) * step))
            def _():
                kept[page, slot] = fresh[r]

        store.start()
    for copy in stores:
        copy.wait()


def route_kernel(capacity, projected, hidden, gain, router, ids, mixed, norms, top, slabs, comb):
    route(projected[...], hidden, gain, router, ids, mixed, norms, top, slabs, comb, capacity)


def unit_chunks(units):
    whole = units // 256 * 256
    return [(start, size) for start, size in ((0, whole), (whole, units - whole)) if size]


def expert_kernel(capacity, arrived, own_up, own_down, other_up, other_down, slabs,
                  slab_rows, kept_up, kept_down, rows, total, sems):
    units = kept_down.shape[0]
    arrive = pltpu.make_async_copy(arrived, slab_rows, sems.at[0])
    arrive.start()
    chunks = []
    for i, (start, size) in enumerate(unit_chunks(units)):
        span = pl.ds(start, size)
        chunks.append((span, copies(
            [(own_up.at[0, :, span, :], kept_up.at[:, span, :]), (own_down.at[0, span, :], kept_down.at[span, :])],
            sems,
            1 + 2 * i,
        )))
    for _, loads in chunks:
        loads[0].start()
    arrive.wait()
    parts = SLAB // capacity
    piece = slabs.shape[1]
    block = 128
    each = block // parts
    blocks = slabs.shape[0] // block
    shape = (block, block)
    slab_row, sorted_row = iota(shape, 1), iota(shape, 0)
    sort = (slab_row == sorted_row % each * parts + sorted_row // each).astype(BF16)
    for i in range(blocks):
        sorted_rows = dot(sort, slab_rows[pl.ds(i * block, block), :]).astype(BF16)
        rows[pl.ds(i * each, each), :] = jnp.concatenate(
            [sorted_rows[p * each : (p + 1) * each] for p in range(parts)], axis=1
        )
    states = rows[...]
    steps = [(other_up.at[0], other_down.at[0], span, []) for span, _ in chunks]
    steps += [(kept_up, kept_down, span, loads) for span, loads in chunks]

    def add_down(i, activated):
        _, down, span, loads = steps[i]
        if loads:
            loads[1].wait()
        term = dot(activated, down[span, :])
        total[...] = term if i == 0 else total[...] + term

    activated = None
    for i, (gate_up, _, span, loads) in enumerate(steps):
        if loads:
            loads[0].wait()
        gate = dot(states, gate_up[0, span, :], NT)
        up = dot(states, gate_up[1, span, :], NT)
        if i == 0:
            for _, loads in chunks:
                loads[1].start()
        else:
            add_down(i - 1, activated)
        activated = (gate / (1.0 + jnp.exp(-gate)) * up).astype(BF16)
    add_down(len(steps) - 1, activated)
    slab_row, sorted_row = iota(shape, 0), iota(shape, 1)
    unsort = (slab_row == sorted_row % each * parts + sorted_row // each).astype(BF16)
    for i in range(blocks):
        summed = total[pl.ds(i * each, each), :].astype(BF16)
        stacked = jnp.concatenate([summed[:, p * piece : (p + 1) * piece] for p in range(parts)], axis=0)
        slabs[pl.ds(i * block, block), :] = dot(unsort, stacked).astype(BF16)


def gather_terms(comb, slabs, capacity):
    parts = SLAB // capacity
    requests = comb.shape[0]
    weights = comb[...]
    pieces = []
    for _ in range(3):
        piece = weights.astype(BF16).astype(F32)
        weights = weights - piece
        pieces.append(piece)
    part = iota(comb.shape, 1) % parts
    stacked = jnp.concatenate(
        [jnp.where(part == p, piece, 0.0) for p in range(parts) for piece in pieces], axis=0
    ).astype(BF16)
    terms = dot(stacked, slabs[...])
    return jnp.concatenate(
        [
            sum(terms[(3 * p + i) * requests : (3 * p + i + 1) * requests] for i in range(3))
            for p in range(parts)
        ],
        axis=1,
    )


def combine_kernel(capacity, comb, slabs, mixed, out):
    out[...] = (mixed[...].astype(F32) + gather_terms(comb, slabs, capacity)).astype(BF16)


def gather_kernel(capacity, comb, slabs, out):
    out[...] = gather_terms(comb, slabs, capacity).astype(BF16)


def vmem(count):
    return [pl.BlockSpec(memory_space=pltpu.VMEM)] * count


def scalars(count):
    return [pl.BlockSpec(memory_space=pltpu.SMEM)] * count


def in_hbm(count):
    return [pl.BlockSpec(memory_space=pltpu.HBM)] * count


def pinned(*arrays):
    return [pltpu.with_memory_space_constraint(array, pltpu.HBM) for array in arrays]


def like(shape, dtype=BF16):
    return jax.ShapeDtypeStruct(shape, dtype)


def body(
    hidden,
    queries,
    fresh_key_value,
    kv_pool,
    page_table,
    lengths,
    out_weight,
    norm_gain,
    router_weight,
    expert_ids,
    expert_gate_up,
    expert_down,
):
    requests, width = hidden.shape
    req_count, kv_count = lax.axis_size("req"), lax.axis_size("kv")
    pages, page_len, heads_kv, pair_dim = kv_pool.shape
    head_dim = pair_dim // 2
    heads = queries.shape[1] // head_dim
    experts = router_weight.shape[0]
    copies = req_count // experts
    chosen = expert_ids.shape[1]
    capacity = 2 * max(1, (requests * chosen + 2 * experts - 1) // (2 * experts))
    parts = SLAB // capacity
    piece = width // parts
    slab_rows = experts * SLAB

    same_part = [
        [(place ^ group_turn(experts, part)) * copies + part for place in range(experts)] for part in range(copies)
    ]
    swap = [(index, index ^ 1) for index in range(req_count)]
    other_up = lax.ppermute(expert_gate_up, "req", swap)
    other_down = lax.ppermute(expert_down, "req", swap)

    attend_scratch = [
        pltpu.VMEM((pages, page_len, heads_kv, head_dim), BF16),
        pltpu.VMEM((pages, page_len, heads_kv, head_dim), BF16),
        pltpu.VMEM(out_weight.shape, BF16),
        pltpu.VMEM((heads * requests, head_dim), F32),
        pltpu.VMEM((heads * requests, head_dim), F32),
        pltpu.VMEM((requests * heads, page_table.shape[1] * page_len * heads_kv), F32),
        pltpu.VMEM((requests * heads, page_table.shape[1] * page_len * heads_kv), BF16),
        pltpu.SemaphoreType.DMA((14,)),
    ]

    def small(*arrays):
        return [pltpu.VMEM(array.shape, array.dtype) for array in arrays]

    inputs = [pltpu.SMEM(page_table.shape, jnp.int32), pltpu.SMEM(lengths.shape, jnp.int32)]
    inputs += small(queries, fresh_key_value)
    routed_shapes = [
        like((requests, width)),
        like((1, requests), F32),
        like((1, requests), F32),
        like((slab_rows, piece)),
        like((requests, slab_rows), F32),
    ]
    attend_params = pltpu.CompilerParams(vmem_limit_bytes=24 * MIB)
    if kv_count == 1:
        attend_scratch.insert(2, pltpu.VMEM((slab_rows, piece), BF16))
        mixed, norms, top, slabs, comb = pl.pallas_call(
            functools.partial(attend_route_kernel, capacity),
            out_shape=routed_shapes,
            in_specs=in_hbm(10),
            out_specs=vmem(3) + in_hbm(1) + vmem(1),
            scratch_shapes=inputs + small(hidden, norm_gain, router_weight, expert_ids) + attend_scratch,
            compiler_params=attend_params,
        )(*pinned(page_table, lengths, queries, fresh_key_value, hidden, norm_gain, router_weight, expert_ids,
                  kv_pool, out_weight))
    else:
        projected = pl.pallas_call(
            attend_kernel,
            out_shape=like((requests, width), F32),
            in_specs=in_hbm(6),
            out_specs=pl.BlockSpec(memory_space=pltpu.VMEM),
            scratch_shapes=inputs + attend_scratch,
            compiler_params=attend_params,
        )(*pinned(page_table, lengths, queries, fresh_key_value, kv_pool, out_weight))
        projected = lax.psum(projected, "kv")
        mixed, norms, top, slabs, comb = pl.pallas_call(
            functools.partial(route_kernel, capacity),
            out_shape=routed_shapes,
            in_specs=vmem(5),
            out_specs=vmem(5),
        )(projected, hidden, norm_gain, router_weight, expert_ids)

    new_pool = pl.pallas_call(
        refresh_kernel,
        out_shape=like(kv_pool.shape),
        in_specs=scalars(2) + vmem(1) + in_hbm(2),
        out_specs=pl.BlockSpec(memory_space=pltpu.HBM),
        scratch_shapes=[pltpu.VMEM(kv_pool.shape, BF16), pltpu.SemaphoreType.DMA((8,))],
        compiler_params=pltpu.CompilerParams(vmem_limit_bytes=12 * MIB),
        cost_estimate=pl.CostEstimate(flops=0, bytes_accessed=8 * kv_pool.size, transcendentals=0),
    )(page_table, lengths, fresh_key_value, top, *pinned(kv_pool))

    def exchange(array):
        array = array.reshape(experts, SLAB, piece)
        array = lax.all_to_all(
            array, "req", split_axis=0, concat_axis=0, tiled=True, axis_index_groups=same_part
        )
        return array.reshape(slab_rows, piece)

    arrived = exchange(slabs)
    kept = experts * capacity
    units = expert_down.shape[1]
    leaving = pl.pallas_call(
        functools.partial(expert_kernel, capacity),
        out_shape=like((slab_rows, piece)),
        in_specs=in_hbm(3) + vmem(2),
        out_specs=pl.BlockSpec(memory_space=pltpu.VMEM),
        scratch_shapes=[
            pltpu.VMEM((slab_rows, piece), BF16),
            pltpu.VMEM((2, units, width), BF16),
            pltpu.VMEM((units, width), BF16),
            pltpu.VMEM((kept, width), BF16),
            pltpu.VMEM((kept, width), F32),
            pltpu.SemaphoreType.DMA((1 + 2 * len(unit_chunks(units)),)),
        ],
        compiler_params=pltpu.CompilerParams(vmem_limit_bytes=20 * MIB),
    )(arrived, *pinned(expert_gate_up, expert_down), other_up, other_down)
    returned = exchange(leaving)
    if kv_count == 1:
        out_hidden = pl.pallas_call(
            functools.partial(combine_kernel, capacity),
            out_shape=like((requests, width)),
            in_specs=vmem(3),
            out_specs=pl.BlockSpec(memory_space=pltpu.VMEM),
            compiler_params=pltpu.CompilerParams(vmem_limit_bytes=8 * MIB),
        )(comb, returned, mixed)
    else:
        routed = pl.pallas_call(
            functools.partial(gather_kernel, capacity),
            out_shape=like((requests, width)),
            in_specs=vmem(2),
            out_specs=pl.BlockSpec(memory_space=pltpu.VMEM),
        )(comb, returned)
        routed = lax.psum(routed, "kv").astype(F32)
        out_hidden = (mixed.astype(F32) + routed).astype(BF16)
    return out_hidden, new_pool, norms.reshape(requests), top.reshape(requests)


def solution(mesh):
    in_specs = (
        P("req", None),
        P("req", "kv"),
        P("req", "kv", None),
        P("req", None, "kv", None),
        P("req", None),
        P("req"),
        P("kv", None),
        P(),
        P(),
        P("req", None),
        P("req", None, "kv", None),
        P("req", "kv", None),
    )
    out_specs = (P("req", None), P("req", None, "kv", None), P("req"), P("req"))
    return jax.shard_map(body, mesh=mesh, in_specs=in_specs, out_specs=out_specs, check_vma=False)
```

```python
import functools
import math

import jax
import jax.numpy as jnp
from jax import lax
from jax.experimental import pallas as pl
from jax.experimental.pallas import tpu as pltpu
from jax.sharding import PartitionSpec as P

BF16 = jnp.bfloat16
F32 = jnp.float32
NT = (((1,), (1,)), ((), ()))
NN = (((1,), (0,)), ((), ()))
SHARED_PAGES = 8
SLAB = 16
MIB = 1 << 20


def dot(a, b, dims=NN, precision=None):
    return lax.dot_general(a, b, dims, precision=precision, preferred_element_type=F32)


def iota(shape, dim):
    return lax.broadcasted_iota(jnp.int32, shape, dim)


def copies(pairs, sems, first=0):
    return [pltpu.make_async_copy(src, dst, sems.at[first + i]) for i, (src, dst) in enumerate(pairs)]


def group_turn(chips, part):
    return chips * 9 // 16 if part % 2 else chips * 11 // 16


def pool_half(array, i):
    head_dim = array.shape[3] // 2
    return array.at[:, :, :, pl.ds(i * head_dim, head_dim)]


def attend(refs, keys, values, scratch):
    small, (kept_weight, qs, att, scores, probs, sems) = scratch
    table, lengths, q_ref, fresh = small[:4]
    requests, max_pages = table.shape
    pages, page_len, heads_kv, head_dim = keys.shape
    heads = q_ref.shape[1] // head_dim
    group = heads // heads_kv
    page_rows = page_len * heads_kv
    pool, weight = refs[-2:]
    loads = copies(list(zip(refs[:4], small[:4])), sems)
    page_step = -(-pages // 4)
    page_spans = [pl.ds(first, min(page_step, pages - first)) for first in range(0, pages, page_step)]
    key_loads, value_loads = [
        copies(
            [(pool_half(pool, i).at[span], kept.at[span]) for span in page_spans], sems, 4 + i * len(page_spans)
        )
        for i, kept in enumerate((keys, values))
    ]
    step = weight.shape[0] // 2
    spans = [pl.ds(i * step, step) for i in range(2)]
    weight_loads = copies([(weight.at[span], kept_weight.at[span]) for span in spans], sems, 12)
    later = copies(list(zip(refs[4:-2], small[4:])), sems, 14)
    for copy in loads + key_loads + value_loads + weight_loads + later:
        copy.start()
    for copy in loads:
        copy.wait()
    for h in range(heads):
        qs[pl.ds(h * requests, requests), :] = q_ref[:, pl.ds(h * head_dim, head_dim)].astype(F32)
    spots = [(table[r, lengths[r] // page_len], lengths[r] % page_len) for r in range(requests)]

    for copy in key_loads:
        copy.wait()
    for r, (page, slot) in enumerate(spots):
        keys[page, slot] = fresh[r][:, :head_dim]
    key_pages = keys.reshape(pages, page_rows, head_dim)
    value_pages = values.reshape(pages, page_rows, head_dim)
    columns = max_pages * page_rows
    shared_columns = SHARED_PAGES * page_rows
    rows = requests * heads

    def pages_of(array, r, first, last):
        return jnp.concatenate([array[table[r, j]] for j in range(first, last)], axis=0)

    query = [qs[pl.ds(r, heads, stride=requests), :] for r in range(requests)]
    query_rows = jnp.concatenate(query, axis=0).astype(BF16)
    scores[:, :shared_columns] = dot(query_rows, pages_of(key_pages, 0, 0, SHARED_PAGES), NT)
    for r in range(requests):
        scores[pl.ds(r * heads, heads), shared_columns:] = dot(
            query[r].astype(BF16), pages_of(key_pages, r, SHARED_PAGES, max_pages), NT
        )
    lane = iota((heads, columns), 1)
    own_head = (lane & (heads_kv - 1)) == iota((heads, columns), 0) // group
    position = lane >> (heads_kv.bit_length() - 1)
    masked = jnp.concatenate(
        [
            jnp.where(own_head & (position <= lengths[r]), scores[pl.ds(r * heads, heads), :], -1e30)
            for r in range(requests)
        ],
        axis=0,
    )
    scale = 1.0 / math.sqrt(head_dim)
    exponent = jnp.exp((masked - jnp.max(masked, axis=1, keepdims=True)) * scale)
    sums = jnp.sum(exponent, axis=1, keepdims=True)
    probs[...] = exponent.astype(BF16)

    for copy in value_loads:
        copy.wait()
    for r, (page, slot) in enumerate(spots):
        values[page, slot] = fresh[r][:, head_dim:]
    shared = dot(probs[:, :shared_columns], pages_of(value_pages, 0, 0, SHARED_PAGES))
    own = [
        dot(probs[pl.ds(r * heads, heads), shared_columns:], pages_of(value_pages, r, SHARED_PAGES, max_pages))
        for r in range(requests)
    ]
    mean = (shared + jnp.concatenate(own, axis=0)) / sums
    for r in range(requests):
        att[pl.ds(r, heads, stride=requests), :] = mean[r * heads : (r + 1) * heads]
    attended = jnp.concatenate(
        [att[pl.ds(h * requests, requests), :] for h in range(heads)], axis=1
    ).astype(BF16)
    projected = 0.0
    for i, copy in enumerate(weight_loads):
        copy.wait()
        projected = projected + dot(attended[:, i * step : (i + 1) * step], kept_weight[spans[i], :])
    for copy in later:
        copy.wait()
    return projected


def as_row(column):
    shape = (column.shape[0],) * 2
    return jnp.sum(jnp.where(iota(shape, 0) == iota(shape, 1), column, 0.0), axis=0, keepdims=True)


def route(projected, hidden, gain, router, ids, mixed_ref, norms_ref, top_ref, slabs_ref, comb_ref, capacity, leave=None):
    requests, width = hidden.shape
    experts = router.shape[0]
    parts = SLAB // capacity
    piece = width // parts
    slab_rows = experts * SLAB
    turns = jnp.where(lax.axis_index("req") % 2 == 0, group_turn(experts, 0), group_turn(experts, 1))

    def slab_expert(shape, dim):
        return (iota(shape, dim) // SLAB) ^ turns

    mixed = (hidden[...].astype(F32) + projected).astype(BF16)
    mixed_ref[...] = mixed
    mixed = mixed.astype(F32)
    norms = jnp.sqrt(jnp.mean(mixed * mixed, axis=1, keepdims=True) + 1e-06)
    norms_ref[...] = as_row(norms)
    normed = (mixed / norms * gain[...].astype(F32).reshape(1, width)).astype(BF16)
    logits = dot(normed, router[...], NT)
    top_ref[...] = as_row(jnp.max(logits, axis=1, keepdims=True))
    column = iota((requests, experts), 1)
    named = column < 0
    for k in range(ids.shape[1]):
        named = named | (ids[:, k : k + 1] == column)
    weights = jnp.where(named, jnp.exp(logits), 0.0)
    weights = weights / jnp.sum(weights, axis=1, keepdims=True)
    earlier = (iota((requests, requests), 1) < iota((requests, requests), 0)).astype(F32)
    rank = dot(earlier, named.astype(F32))
    place = jnp.where(named, rank, -1.0)
    normed = normed.astype(F32)
    stacked = jnp.concatenate([normed[:, p * piece : (p + 1) * piece] for p in range(parts)], axis=0)
    places = jnp.concatenate([place] * parts, axis=0)
    shape = (slab_rows, parts * requests)
    inner = iota(shape, 0) % SLAB
    spread = (slab_expert((slab_rows, experts), 0) == iota((slab_rows, experts), 1)).astype(F32)
    picks = (dot(spread, places, NT) == (inner // parts).astype(F32)) & (
        inner % parts == iota(shape, 1) // requests
    )
    slabs_ref[...] = dot(picks.astype(BF16), stacked.astype(BF16)).astype(BF16)
    if leave is not None:
        leave()
    shape = (experts, slab_rows)
    spread = (slab_expert(shape, 1) == iota(shape, 0)).astype(F32)
    inner = iota((requests, slab_rows), 1) % SLAB
    comb_ref[...] = jnp.where(
        dot(place, spread) == (inner // parts).astype(F32),
        dot(weights, spread, precision=lax.Precision.HIGHEST),
        0.0,
    )


def attend_route_kernel(capacity, *refs):
    inputs, (mixed, norms, top, slabs, comb) = refs[:10], refs[10:15]
    small, scratch = refs[15:23], refs[23:]
    keys, values, kept_slabs = scratch[:3]
    projected = attend(inputs, keys, values, (small, scratch[3:]))
    hidden, gain, router, ids = small[4:]
    leave = pltpu.make_async_copy(kept_slabs, slabs, scratch[-1].at[0])
    route(projected, hidden, gain, router, ids, mixed, norms, top, kept_slabs, comb, capacity, leave.start)
    leave.wait()


def attend_kernel(*refs):
    attended, scratch = refs[6], refs[11:]
    attended[...] = attend(refs[:6], scratch[0], scratch[1], (refs[7:11], scratch[2:]))


def refresh_kernel(table, lengths, fresh, after, pool, new_pool, kept, sems):
    pages, page_len = kept.shape[:2]
    step = -(-pages // 4)
    spans = [pl.ds(start, min(step, pages - start)) for start in range(0, pages, step)]
    loads = copies([(pool.at[span], kept.at[span]) for span in spans], sems)
    stores = copies([(kept.at[span], new_pool.at[span]) for span in spans], sems, len(spans))
    for copy in loads:
        copy.start()
    spots = [(table[r, lengths[r] // page_len], lengths[r] % page_len) for r in range(table.shape[0])]
    for i, (load, store) in enumerate(zip(loads, stores)):
        load.wait()
        for r, (page, slot) in enumerate(spots):

            @pl.when((page >= i * step) & (page < (i + 1) * step))
            def _():
                kept[page, slot] = fresh[r]

        store.start()
    for copy in stores:
        copy.wait()


def route_kernel(capacity, projected, hidden, gain, router, ids, mixed, norms, top, slabs, comb):
    route(projected[...], hidden, gain, router, ids, mixed, norms, top, slabs, comb, capacity)


def unit_chunks(units):
    whole = units // 256 * 256
    return [(start, size) for start, size in ((0, whole), (whole, units - whole)) if size]


def expert_kernel(capacity, arrived, own_up, own_down, other_up, other_down, slabs,
                  slab_rows, kept_up, kept_down, rows, total, sems):
    units = kept_down.shape[0]
    arrive = pltpu.make_async_copy(arrived, slab_rows, sems.at[0])
    arrive.start()
    chunks = []
    for i, (start, size) in enumerate(unit_chunks(units)):
        span = pl.ds(start, size)
        chunks.append((span, copies(
            [(own_up.at[0, :, span, :], kept_up.at[:, span, :]), (own_down.at[0, span, :], kept_down.at[span, :])],
            sems,
            1 + 2 * i,
        )))
    for _, loads in chunks:
        loads[0].start()
    arrive.wait()
    parts = SLAB // capacity
    piece = slabs.shape[1]
    block = 128
    each = block // parts
    blocks = slabs.shape[0] // block
    shape = (block, block)
    slab_row, sorted_row = iota(shape, 1), iota(shape, 0)
    sort = (slab_row == sorted_row % each * parts + sorted_row // each).astype(BF16)
    for i in range(blocks):
        sorted_rows = dot(sort, slab_rows[pl.ds(i * block, block), :]).astype(BF16)
        rows[pl.ds(i * each, each), :] = jnp.concatenate(
            [sorted_rows[p * each : (p + 1) * each] for p in range(parts)], axis=1
        )
    states = rows[...]
    steps = [(other_up.at[0], other_down.at[0], span, []) for span, _ in chunks]
    steps += [(kept_up, kept_down, span, loads) for span, loads in chunks]

    def add_down(i, activated):
        _, down, span, loads = steps[i]
        if loads:
            loads[1].wait()
        term = dot(activated, down[span, :])
        total[...] = term if i == 0 else total[...] + term

    activated = None
    for i, (gate_up, _, span, loads) in enumerate(steps):
        if loads:
            loads[0].wait()
        gate = dot(states, gate_up[0, span, :], NT)
        up = dot(states, gate_up[1, span, :], NT)
        if i == 0:
            for _, loads in chunks:
                loads[1].start()
        else:
            add_down(i - 1, activated)
        activated = (gate / (1.0 + jnp.exp(-gate)) * up).astype(BF16)
    add_down(len(steps) - 1, activated)
    slab_row, sorted_row = iota(shape, 0), iota(shape, 1)
    unsort = (slab_row == sorted_row % each * parts + sorted_row // each).astype(BF16)
    for i in range(blocks):
        summed = total[pl.ds(i * each, each), :].astype(BF16)
        stacked = jnp.concatenate([summed[:, p * piece : (p + 1) * piece] for p in range(parts)], axis=0)
        slabs[pl.ds(i * block, block), :] = dot(unsort, stacked).astype(BF16)


def gather_terms(comb, slabs, capacity):
    parts = SLAB // capacity
    requests = comb.shape[0]
    weights = comb[...]
    pieces = []
    for _ in range(3):
        piece = weights.astype(BF16).astype(F32)
        weights = weights - piece
        pieces.append(piece)
    part = iota(comb.shape, 1) % parts
    stacked = jnp.concatenate(
        [jnp.where(part == p, piece, 0.0) for p in range(parts) for piece in pieces], axis=0
    ).astype(BF16)
    terms = dot(stacked, slabs[...])
    return jnp.concatenate(
        [
            sum(terms[(3 * p + i) * requests : (3 * p + i + 1) * requests] for i in range(3))
            for p in range(parts)
        ],
        axis=1,
    )


def combine_kernel(capacity, comb, slabs, mixed, out):
    out[...] = (mixed[...].astype(F32) + gather_terms(comb, slabs, capacity)).astype(BF16)


def gather_kernel(capacity, comb, slabs, out):
    out[...] = gather_terms(comb, slabs, capacity).astype(BF16)


def vmem(count):
    return [pl.BlockSpec(memory_space=pltpu.VMEM)] * count


def scalars(count):
    return [pl.BlockSpec(memory_space=pltpu.SMEM)] * count


def in_hbm(count):
    return [pl.BlockSpec(memory_space=pltpu.HBM)] * count


def pinned(*arrays):
    return [pltpu.with_memory_space_constraint(array, pltpu.HBM) for array in arrays]


def like(shape, dtype=BF16):
    return jax.ShapeDtypeStruct(shape, dtype)


def body(
    hidden,
    queries,
    fresh_key_value,
    kv_pool,
    page_table,
    lengths,
    out_weight,
    norm_gain,
    router_weight,
    expert_ids,
    expert_gate_up,
    expert_down,
):
    requests, width = hidden.shape
    req_count, kv_count = lax.axis_size("req"), lax.axis_size("kv")
    pages, page_len, heads_kv, pair_dim = kv_pool.shape
    head_dim = pair_dim // 2
    heads = queries.shape[1] // head_dim
    experts = router_weight.shape[0]
    copies = req_count // experts
    chosen = expert_ids.shape[1]
    capacity = 2 * max(1, (requests * chosen + 2 * experts - 1) // (2 * experts))
    parts = SLAB // capacity
    piece = width // parts
    slab_rows = experts * SLAB

    same_part = [
        [(place ^ group_turn(experts, part)) * copies + part for place in range(experts)] for part in range(copies)
    ]
    swap = [(index, index ^ 1) for index in range(req_count)]
    other_up = lax.ppermute(expert_gate_up, "req", swap)
    other_down = lax.ppermute(expert_down, "req", swap)

    attend_scratch = [
        pltpu.VMEM((pages, page_len, heads_kv, head_dim), BF16),
        pltpu.VMEM((pages, page_len, heads_kv, head_dim), BF16),
        pltpu.VMEM(out_weight.shape, BF16),
        pltpu.VMEM((heads * requests, head_dim), F32),
        pltpu.VMEM((heads * requests, head_dim), F32),
        pltpu.VMEM((requests * heads, page_table.shape[1] * page_len * heads_kv), F32),
        pltpu.VMEM((requests * heads, page_table.shape[1] * page_len * heads_kv), BF16),
        pltpu.SemaphoreType.DMA((18,)),
    ]

    def small(*arrays):
        return [pltpu.VMEM(array.shape, array.dtype) for array in arrays]

    inputs = [pltpu.SMEM(page_table.shape, jnp.int32), pltpu.SMEM(lengths.shape, jnp.int32)]
    inputs += small(queries, fresh_key_value)
    routed_shapes = [
        like((requests, width)),
        like((1, requests), F32),
        like((1, requests), F32),
        like((slab_rows, piece)),
        like((requests, slab_rows), F32),
    ]
    attend_params = pltpu.CompilerParams(vmem_limit_bytes=24 * MIB)
    if kv_count == 1:
        attend_scratch.insert(2, pltpu.VMEM((slab_rows, piece), BF16))
        mixed, norms, top, slabs, comb = pl.pallas_call(
            functools.partial(attend_route_kernel, capacity),
            out_shape=routed_shapes,
            in_specs=in_hbm(10),
            out_specs=vmem(3) + in_hbm(1) + vmem(1),
            scratch_shapes=inputs + small(hidden, norm_gain, router_weight, expert_ids) + attend_scratch,
            compiler_params=attend_params,
        )(*pinned(page_table, lengths, queries, fresh_key_value, hidden, norm_gain, router_weight, expert_ids,
                  kv_pool, out_weight))
    else:
        projected = pl.pallas_call(
            attend_kernel,
            out_shape=like((requests, width), F32),
            in_specs=in_hbm(6),
            out_specs=pl.BlockSpec(memory_space=pltpu.VMEM),
            scratch_shapes=inputs + attend_scratch,
            compiler_params=attend_params,
        )(*pinned(page_table, lengths, queries, fresh_key_value, kv_pool, out_weight))
        projected = lax.psum(projected, "kv")
        mixed, norms, top, slabs, comb = pl.pallas_call(
            functools.partial(route_kernel, capacity),
            out_shape=routed_shapes,
            in_specs=vmem(5),
            out_specs=vmem(5),
        )(projected, hidden, norm_gain, router_weight, expert_ids)

    new_pool = pl.pallas_call(
        refresh_kernel,
        out_shape=like(kv_pool.shape),
        in_specs=scalars(2) + vmem(1) + in_hbm(2),
        out_specs=pl.BlockSpec(memory_space=pltpu.HBM),
        scratch_shapes=[pltpu.VMEM(kv_pool.shape, BF16), pltpu.SemaphoreType.DMA((8,))],
        compiler_params=pltpu.CompilerParams(vmem_limit_bytes=12 * MIB),
        cost_estimate=pl.CostEstimate(flops=0, bytes_accessed=8 * kv_pool.size, transcendentals=0),
    )(page_table, lengths, fresh_key_value, top, *pinned(kv_pool))

    def exchange(array):
        array = array.reshape(experts, SLAB, piece)
        array = lax.all_to_all(
            array, "req", split_axis=0, concat_axis=0, tiled=True, axis_index_groups=same_part
        )
        return array.reshape(slab_rows, piece)

    arrived = exchange(slabs)
    kept = experts * capacity
    units = expert_down.shape[1]
    leaving = pl.pallas_call(
        functools.partial(expert_kernel, capacity),
        out_shape=like((slab_rows, piece)),
        in_specs=in_hbm(3) + vmem(2),
        out_specs=pl.BlockSpec(memory_space=pltpu.VMEM),
        scratch_shapes=[
            pltpu.VMEM((slab_rows, piece), BF16),
            pltpu.VMEM((2, units, width), BF16),
            pltpu.VMEM((units, width), BF16),
            pltpu.VMEM((kept, width), BF16),
            pltpu.VMEM((kept, width), F32),
            pltpu.SemaphoreType.DMA((1 + 2 * len(unit_chunks(units)),)),
        ],
        compiler_params=pltpu.CompilerParams(vmem_limit_bytes=20 * MIB),
    )(arrived, *pinned(expert_gate_up, expert_down), other_up, other_down)
    returned = exchange(leaving)
    if kv_count == 1:
        out_hidden = pl.pallas_call(
            functools.partial(combine_kernel, capacity),
            out_shape=like((requests, width)),
            in_specs=vmem(3),
            out_specs=pl.BlockSpec(memory_space=pltpu.VMEM),
            compiler_params=pltpu.CompilerParams(vmem_limit_bytes=8 * MIB),
        )(comb, returned, mixed)
    else:
        routed = pl.pallas_call(
            functools.partial(gather_kernel, capacity),
            out_shape=like((requests, width)),
            in_specs=vmem(2),
            out_specs=pl.BlockSpec(memory_space=pltpu.VMEM),
        )(comb, returned)
        routed = lax.psum(routed, "kv").astype(F32)
        out_hidden = (mixed.astype(F32) + routed).astype(BF16)
    return out_hidden, new_pool, norms.reshape(requests), top.reshape(requests)


def solution(mesh):
    in_specs = (
        P("req", None),
        P("req", "kv"),
        P("req", "kv", None),
        P("req", None, "kv", None),
        P("req", None),
        P("req"),
        P("kv", None),
        P(),
        P(),
        P("req", None),
        P("req", None, "kv", None),
        P("req", "kv", None),
    )
    out_specs = (P("req", None), P("req", None, "kv", None), P("req"), P("req"))
    return jax.shard_map(body, mesh=mesh, in_specs=in_specs, out_specs=out_specs, check_vma=False)
```

```python
import functools
import math

import jax
import jax.numpy as jnp
from jax import lax
from jax.experimental import pallas as pl
from jax.experimental.pallas import tpu as pltpu
from jax.sharding import PartitionSpec as P

BF16 = jnp.bfloat16
F32 = jnp.float32
NT = (((1,), (1,)), ((), ()))
NN = (((1,), (0,)), ((), ()))
SLAB = 16
MIB = 1 << 20


def dot(a, b, dims=NN, precision=None):
    return lax.dot_general(a, b, dims, precision=precision, preferred_element_type=F32)


def iota(shape, dim):
    return lax.broadcasted_iota(jnp.int32, shape, dim)


def copies(pairs, sems, first=0):
    return [pltpu.make_async_copy(src, dst, sems.at[first + i]) for i, (src, dst) in enumerate(pairs)]


def group_turn(chips, part):
    return chips * 9 // 16 if part % 2 else chips * 3 // 8


def pool_half(array, i):
    head_dim = array.shape[3] // 2
    return array.at[:, :, :, pl.ds(i * head_dim, head_dim)]


def attend(refs, keys, values, scratch):
    small, (kept_weight, qs, att, probs, sums, sems) = scratch
    table, lengths, q_ref, fresh = small[:4]
    requests, max_pages = table.shape
    pages, page_len, heads_kv, head_dim = keys.shape
    heads = q_ref.shape[1] // head_dim
    group = heads // heads_kv
    page_rows = page_len * heads_kv
    pool, weight = refs[-2:]
    loads = copies(list(zip(refs[:4], small[:4])), sems)
    page_step = -(-pages // 4)
    page_spans = [pl.ds(first, min(page_step, pages - first)) for first in range(0, pages, page_step)]
    key_loads, value_loads = [
        copies(
            [(pool_half(pool, i).at[span], kept.at[span]) for span in page_spans], sems, 4 + i * len(page_spans)
        )
        for i, kept in enumerate((keys, values))
    ]
    step = weight.shape[0] // 2
    spans = [pl.ds(i * step, step) for i in range(2)]
    weight_loads = copies([(weight.at[span], kept_weight.at[span]) for span in spans], sems, 12)
    later = copies(list(zip(refs[4:-2], small[4:])), sems, 14)
    for copy in loads + key_loads + value_loads + weight_loads + later:
        copy.start()
    for copy in loads:
        copy.wait()
    for h in range(heads):
        qs[pl.ds(h * requests, requests), :] = q_ref[:, pl.ds(h * head_dim, head_dim)].astype(F32)
    spots = [(table[r, lengths[r] // page_len], lengths[r] % page_len) for r in range(requests)]

    for copy in key_loads:
        copy.wait()
    for r, (page, slot) in enumerate(spots):
        keys[page, slot] = fresh[r][:, :head_dim]
    key_pages = keys.reshape(pages, page_rows, head_dim)
    value_pages = values.reshape(pages, page_rows, head_dim)
    columns = max_pages * page_rows
    lane = iota((heads, columns), 1)
    own_head = (lane & (heads_kv - 1)) == iota((heads, columns), 0) // group
    position = jnp.where(own_head, lane >> (heads_kv.bit_length() - 1), columns)
    scale = math.log2(math.e) / math.sqrt(head_dim)
    for r in range(requests):
        query = qs[pl.ds(r, heads, stride=requests), :].astype(BF16)
        gathered = jnp.concatenate([key_pages[table[r, j]] for j in range(max_pages)], axis=0)
        scores = jnp.where(position <= lengths[r], dot(query, gathered, NT), -1e30)
        exponent = jnp.exp2((scores - jnp.max(scores, axis=1, keepdims=True)) * scale)
        sums[r] = jnp.broadcast_to(jnp.sum(exponent, axis=1, keepdims=True), (heads, head_dim))
        probs[r] = exponent.astype(BF16)

    for copy in value_loads:
        copy.wait()
    for r, (page, slot) in enumerate(spots):
        values[page, slot] = fresh[r][:, head_dim:]
    for r in range(requests):
        gathered = jnp.concatenate([value_pages[table[r, j]] for j in range(max_pages)], axis=0)
        att[pl.ds(r, heads, stride=requests), :] = dot(probs[r], gathered) / sums[r]
    attended = jnp.concatenate(
        [att[pl.ds(h * requests, requests), :] for h in range(heads)], axis=1
    ).astype(BF16)
    projected = 0.0
    for i, copy in enumerate(weight_loads):
        copy.wait()
        projected = projected + dot(attended[:, i * step : (i + 1) * step], kept_weight[spans[i], :])
    for copy in later:
        copy.wait()
    return projected


def as_row(column):
    shape = (column.shape[0],) * 2
    return jnp.sum(jnp.where(iota(shape, 0) == iota(shape, 1), column, 0.0), axis=0, keepdims=True)


def route(projected, hidden, gain, router, ids, mixed_ref, norms_ref, top_ref, slabs_ref, comb_ref, capacity, leave=None):
    requests, width = hidden.shape
    experts = router.shape[0]
    parts = SLAB // capacity
    piece = width // parts
    slab_rows = experts * SLAB
    turns = jnp.where(lax.axis_index("req") % 2 == 0, group_turn(experts, 0), group_turn(experts, 1))

    def slab_expert(shape, dim):
        return (iota(shape, dim) // SLAB) ^ turns

    mixed = (hidden[...].astype(F32) + projected).astype(BF16)
    mixed_ref[...] = mixed
    mixed = mixed.astype(F32)
    norms = jnp.sqrt(jnp.mean(mixed * mixed, axis=1, keepdims=True) + 1e-06)
    norms_ref[...] = as_row(norms)
    normed = (mixed / norms * gain[...].astype(F32).reshape(1, width)).astype(BF16)
    logits = dot(normed, router[...], NT)
    top_ref[...] = as_row(jnp.max(logits, axis=1, keepdims=True))
    column = iota((requests, experts), 1)
    named = column < 0
    for k in range(ids.shape[1]):
        named = named | (ids[:, k : k + 1] == column)
    weights = jnp.where(named, jnp.exp(logits), 0.0)
    weights = weights / jnp.sum(weights, axis=1, keepdims=True)
    earlier = (iota((requests, requests), 1) < iota((requests, requests), 0)).astype(F32)
    rank = dot(earlier, named.astype(F32))
    place = jnp.where(named, rank, -1.0)
    normed = normed.astype(F32)
    stacked = jnp.concatenate([normed[:, p * piece : (p + 1) * piece] for p in range(parts)], axis=0)
    places = jnp.concatenate([place] * parts, axis=0)
    shape = (slab_rows, parts * requests)
    inner = iota(shape, 0) % SLAB
    spread = (slab_expert((slab_rows, experts), 0) == iota((slab_rows, experts), 1)).astype(F32)
    picks = (dot(spread, places, NT) == (inner // parts).astype(F32)) & (
        inner % parts == iota(shape, 1) // requests
    )
    slabs_ref[...] = dot(picks.astype(BF16), stacked.astype(BF16)).astype(BF16)
    if leave is not None:
        leave()
    shape = (experts, slab_rows)
    spread = (slab_expert(shape, 1) == iota(shape, 0)).astype(F32)
    inner = iota((requests, slab_rows), 1) % SLAB
    comb_ref[...] = jnp.where(
        dot(place, spread) == (inner // parts).astype(F32),
        dot(weights, spread, precision=lax.Precision.HIGHEST),
        0.0,
    )


def attend_route_kernel(capacity, *refs):
    inputs, (mixed, norms, top, slabs, comb) = refs[:10], refs[10:15]
    small, scratch = refs[15:23], refs[23:]
    keys, values, kept_slabs = scratch[:3]
    projected = attend(inputs, keys, values, (small, scratch[3:]))
    hidden, gain, router, ids = small[4:]
    leave = pltpu.make_async_copy(kept_slabs, slabs, scratch[-1].at[0])
    route(projected, hidden, gain, router, ids, mixed, norms, top, kept_slabs, comb, capacity, leave.start)
    leave.wait()


def attend_kernel(*refs):
    attended, scratch = refs[6], refs[11:]
    attended[...] = attend(refs[:6], scratch[0], scratch[1], (refs[7:11], scratch[2:]))


def refresh_kernel(table, lengths, fresh, after, pool, new_pool, kept, sems):
    pages, page_len = kept.shape[:2]
    step = -(-pages // 4)
    spans = [pl.ds(start, min(step, pages - start)) for start in range(0, pages, step)]
    loads = copies([(pool.at[span], kept.at[span]) for span in spans], sems)
    stores = copies([(kept.at[span], new_pool.at[span]) for span in spans], sems, len(spans))
    for copy in loads:
        copy.start()
    spots = [(table[r, lengths[r] // page_len], lengths[r] % page_len) for r in range(table.shape[0])]
    for i, (load, store) in enumerate(zip(loads, stores)):
        load.wait()
        for r, (page, slot) in enumerate(spots):

            @pl.when((page >= i * step) & (page < (i + 1) * step))
            def _():
                kept[page, slot] = fresh[r]

        store.start()
    for copy in stores:
        copy.wait()


def route_kernel(capacity, projected, hidden, gain, router, ids, mixed, norms, top, slabs, comb):
    route(projected[...], hidden, gain, router, ids, mixed, norms, top, slabs, comb, capacity)


def unit_chunks(units):
    whole = units // 256 * 256
    return [(start, size) for start, size in ((0, whole), (whole, units - whole)) if size]


def expert_kernel(capacity, arrived, own_up, own_down, other_up, other_down, slabs,
                  slab_rows, kept_up, kept_down, rows, total, sems):
    units = kept_down.shape[0]
    arrive = pltpu.make_async_copy(arrived, slab_rows, sems.at[0])
    arrive.start()
    chunks = []
    for i, (start, size) in enumerate(unit_chunks(units)):
        span = pl.ds(start, size)
        chunks.append((span, copies(
            [(own_up.at[0, :, span, :], kept_up.at[:, span, :]), (own_down.at[0, span, :], kept_down.at[span, :])],
            sems,
            1 + 2 * i,
        )))
    for _, loads in chunks:
        loads[0].start()
    arrive.wait()
    parts = SLAB // capacity
    piece = slabs.shape[1]
    block = 128
    each = block // parts
    blocks = slabs.shape[0] // block
    shape = (block, block)
    slab_row, sorted_row = iota(shape, 1), iota(shape, 0)
    sort = (slab_row == sorted_row % each * parts + sorted_row // each).astype(BF16)
    for i in range(blocks):
        sorted_rows = dot(sort, slab_rows[pl.ds(i * block, block), :]).astype(BF16)
        rows[pl.ds(i * each, each), :] = jnp.concatenate(
            [sorted_rows[p * each : (p + 1) * each] for p in range(parts)], axis=1
        )
    states = rows[...]
    steps = [(other_up.at[0], other_down.at[0], span, []) for span, _ in chunks]
    steps += [(kept_up, kept_down, span, loads) for span, loads in chunks]

    def add_down(i, activated):
        _, down, span, loads = steps[i]
        if loads:
            loads[1].wait()
        term = dot(activated, down[span, :])
        total[...] = term if i == 0 else total[...] + term

    activated = None
    for i, (gate_up, _, span, loads) in enumerate(steps):
        if loads:
            loads[0].wait()
        gate = dot(states, gate_up[0, span, :], NT)
        up = dot(states, gate_up[1, span, :], NT)
        if i == 0:
            for _, loads in chunks:
                loads[1].start()
        else:
            add_down(i - 1, activated)
        activated = (gate / (1.0 + jnp.exp(-gate)) * up).astype(BF16)
    add_down(len(steps) - 1, activated)
    slab_row, sorted_row = iota(shape, 0), iota(shape, 1)
    unsort = (slab_row == sorted_row % each * parts + sorted_row // each).astype(BF16)
    for i in range(blocks):
        summed = total[pl.ds(i * each, each), :].astype(BF16)
        stacked = jnp.concatenate([summed[:, p * piece : (p + 1) * piece] for p in range(parts)], axis=0)
        slabs[pl.ds(i * block, block), :] = dot(unsort, stacked).astype(BF16)


def gather_terms(comb, slabs, capacity):
    parts = SLAB // capacity
    requests = comb.shape[0]
    weights = comb[...]
    pieces = []
    for _ in range(3):
        piece = weights.astype(BF16).astype(F32)
        weights = weights - piece
        pieces.append(piece)
    part = iota(comb.shape, 1) % parts
    stacked = jnp.concatenate(
        [jnp.where(part == p, piece, 0.0) for p in range(parts) for piece in pieces], axis=0
    ).astype(BF16)
    terms = dot(stacked, slabs[...])
    return jnp.concatenate(
        [
            sum(terms[(3 * p + i) * requests : (3 * p + i + 1) * requests] for i in range(3))
            for p in range(parts)
        ],
        axis=1,
    )


def combine_kernel(capacity, comb, slabs, mixed, out):
    out[...] = (mixed[...].astype(F32) + gather_terms(comb, slabs, capacity)).astype(BF16)


def gather_kernel(capacity, comb, slabs, out):
    out[...] = gather_terms(comb, slabs, capacity).astype(BF16)


def vmem(count):
    return [pl.BlockSpec(memory_space=pltpu.VMEM)] * count


def scalars(count):
    return [pl.BlockSpec(memory_space=pltpu.SMEM)] * count


def in_hbm(count):
    return [pl.BlockSpec(memory_space=pltpu.HBM)] * count


def pinned(*arrays):
    return [pltpu.with_memory_space_constraint(array, pltpu.HBM) for array in arrays]


def like(shape, dtype=BF16):
    return jax.ShapeDtypeStruct(shape, dtype)


def body(
    hidden,
    queries,
    fresh_key_value,
    kv_pool,
    page_table,
    lengths,
    out_weight,
    norm_gain,
    router_weight,
    expert_ids,
    expert_gate_up,
    expert_down,
):
    requests, width = hidden.shape
    req_count, kv_count = lax.axis_size("req"), lax.axis_size("kv")
    pages, page_len, heads_kv, pair_dim = kv_pool.shape
    head_dim = pair_dim // 2
    heads = queries.shape[1] // head_dim
    experts = router_weight.shape[0]
    copies = req_count // experts
    chosen = expert_ids.shape[1]
    capacity = 2 * max(1, (requests * chosen + 2 * experts - 1) // (2 * experts))
    parts = SLAB // capacity
    piece = width // parts
    slab_rows = experts * SLAB

    same_part = [
        [(place ^ group_turn(experts, part)) * copies + part for place in range(experts)] for part in range(copies)
    ]
    swap = [(index, index ^ 1) for index in range(req_count)]
    other_up = lax.ppermute(expert_gate_up, "req", swap)
    other_down = lax.ppermute(expert_down, "req", swap)

    attend_scratch = [
        pltpu.VMEM((pages, page_len, heads_kv, head_dim), BF16),
        pltpu.VMEM((pages, page_len, heads_kv, head_dim), BF16),
        pltpu.VMEM(out_weight.shape, BF16),
        pltpu.VMEM((heads * requests, head_dim), F32),
        pltpu.VMEM((heads * requests, head_dim), F32),
        pltpu.VMEM((requests, heads, page_table.shape[1] * page_len * heads_kv), BF16),
        pltpu.VMEM((requests, heads, head_dim), F32),
        pltpu.SemaphoreType.DMA((18,)),
    ]

    def small(*arrays):
        return [pltpu.VMEM(array.shape, array.dtype) for array in arrays]

    inputs = [pltpu.SMEM(page_table.shape, jnp.int32), pltpu.SMEM(lengths.shape, jnp.int32)]
    inputs += small(queries, fresh_key_value)
    routed_shapes = [
        like((requests, width)),
        like((1, requests), F32),
        like((1, requests), F32),
        like((slab_rows, piece)),
        like((requests, slab_rows), F32),
    ]
    attend_params = pltpu.CompilerParams(vmem_limit_bytes=24 * MIB)
    if kv_count == 1:
        attend_scratch.insert(2, pltpu.VMEM((slab_rows, piece), BF16))
        mixed, norms, top, slabs, comb = pl.pallas_call(
            functools.partial(attend_route_kernel, capacity),
            out_shape=routed_shapes,
            in_specs=in_hbm(10),
            out_specs=vmem(3) + in_hbm(1) + vmem(1),
            scratch_shapes=inputs + small(hidden, norm_gain, router_weight, expert_ids) + attend_scratch,
            compiler_params=attend_params,
        )(*pinned(page_table, lengths, queries, fresh_key_value, hidden, norm_gain, router_weight, expert_ids,
                  kv_pool, out_weight))
    else:
        projected = pl.pallas_call(
            attend_kernel,
            out_shape=like((requests, width), F32),
            in_specs=in_hbm(6),
            out_specs=pl.BlockSpec(memory_space=pltpu.VMEM),
            scratch_shapes=inputs + attend_scratch,
            compiler_params=attend_params,
        )(*pinned(page_table, lengths, queries, fresh_key_value, kv_pool, out_weight))
        projected = lax.psum(projected, "kv")
        mixed, norms, top, slabs, comb = pl.pallas_call(
            functools.partial(route_kernel, capacity),
            out_shape=routed_shapes,
            in_specs=vmem(5),
            out_specs=vmem(5),
        )(projected, hidden, norm_gain, router_weight, expert_ids)

    new_pool = pl.pallas_call(
        refresh_kernel,
        out_shape=like(kv_pool.shape),
        in_specs=scalars(2) + vmem(1) + in_hbm(2),
        out_specs=pl.BlockSpec(memory_space=pltpu.HBM),
        scratch_shapes=[pltpu.VMEM(kv_pool.shape, BF16), pltpu.SemaphoreType.DMA((8,))],
        compiler_params=pltpu.CompilerParams(vmem_limit_bytes=12 * MIB),
        cost_estimate=pl.CostEstimate(flops=0, bytes_accessed=8 * kv_pool.size, transcendentals=0),
    )(page_table, lengths, fresh_key_value, top, *pinned(kv_pool))

    def exchange(array):
        array = array.reshape(experts, SLAB, piece)
        array = lax.all_to_all(
            array, "req", split_axis=0, concat_axis=0, tiled=True, axis_index_groups=same_part
        )
        return array.reshape(slab_rows, piece)

    arrived = exchange(slabs)
    kept = experts * capacity
    units = expert_down.shape[1]
    leaving = pl.pallas_call(
        functools.partial(expert_kernel, capacity),
        out_shape=like((slab_rows, piece)),
        in_specs=in_hbm(3) + vmem(2),
        out_specs=pl.BlockSpec(memory_space=pltpu.VMEM),
        scratch_shapes=[
            pltpu.VMEM((slab_rows, piece), BF16),
            pltpu.VMEM((2, units, width), BF16),
            pltpu.VMEM((units, width), BF16),
            pltpu.VMEM((kept, width), BF16),
            pltpu.VMEM((kept, width), F32),
            pltpu.SemaphoreType.DMA((1 + 2 * len(unit_chunks(units)),)),
        ],
        compiler_params=pltpu.CompilerParams(vmem_limit_bytes=20 * MIB),
    )(arrived, *pinned(expert_gate_up, expert_down), other_up, other_down)
    returned = exchange(leaving)
    if kv_count == 1:
        out_hidden = pl.pallas_call(
            functools.partial(combine_kernel, capacity),
            out_shape=like((requests, width)),
            in_specs=vmem(3),
            out_specs=pl.BlockSpec(memory_space=pltpu.VMEM),
            compiler_params=pltpu.CompilerParams(vmem_limit_bytes=8 * MIB),
        )(comb, returned, mixed)
    else:
        routed = pl.pallas_call(
            functools.partial(gather_kernel, capacity),
            out_shape=like((requests, width)),
            in_specs=vmem(2),
            out_specs=pl.BlockSpec(memory_space=pltpu.VMEM),
        )(comb, returned)
        routed = lax.psum(routed, "kv").astype(F32)
        out_hidden = (mixed.astype(F32) + routed).astype(BF16)
    return out_hidden, new_pool, norms.reshape(requests), top.reshape(requests)


def solution(mesh):
    in_specs = (
        P("req", None),
        P("req", "kv"),
        P("req", "kv", None),
        P("req", None, "kv", None),
        P("req", None),
        P("req"),
        P("kv", None),
        P(),
        P(),
        P("req", None),
        P("req", None, "kv", None),
        P("req", "kv", None),
    )
    out_specs = (P("req", None), P("req", None, "kv", None), P("req"), P("req"))
    return jax.shard_map(body, mesh=mesh, in_specs=in_specs, out_specs=out_specs, check_vma=False)
```

```python
import functools
import math

import jax
import jax.numpy as jnp
from jax import lax
from jax.experimental import pallas as pl
from jax.experimental.pallas import tpu as pltpu
from jax.sharding import PartitionSpec as P

BF16 = jnp.bfloat16
F32 = jnp.float32
NT = (((1,), (1,)), ((), ()))
NN = (((1,), (0,)), ((), ()))
STATS = 128
SLAB = 16
MIB = 1 << 20


def dot(a, b, dims=NN, precision=None):
    return lax.dot_general(a, b, dims, precision=precision, preferred_element_type=F32)


def iota(shape, dim):
    return lax.broadcasted_iota(jnp.int32, shape, dim)


def copies(pairs, sems, first=0):
    return [pltpu.make_async_copy(src, dst, sems.at[first + i]) for i, (src, dst) in enumerate(pairs)]


def group_turn(chips, part):
    return chips * 9 // 16 if part % 2 else chips * 3 // 8


def pool_half(array, i):
    head_dim = array.shape[3] // 2
    return array.at[:, :, :, pl.ds(i * head_dim, head_dim)]


def attend(refs, keys, values, scratch):
    small, (kept_weight, qs, att, probs, sums, sems) = scratch
    table, lengths, q_ref, fresh = small[:4]
    requests, max_pages = table.shape
    pages, page_len, heads_kv, head_dim = keys.shape
    heads = q_ref.shape[1] // head_dim
    group = heads // heads_kv
    page_rows = page_len * heads_kv
    pool, weight = refs[-2:]
    loads = copies(list(zip(refs[:4], small[:4])), sems)
    page_step = -(-pages // 4)
    page_spans = [pl.ds(first, min(page_step, pages - first)) for first in range(0, pages, page_step)]
    key_loads, value_loads = [
        copies(
            [(pool_half(pool, i).at[span], kept.at[span]) for span in page_spans], sems, 4 + i * len(page_spans)
        )
        for i, kept in enumerate((keys, values))
    ]
    step = weight.shape[0] // 2
    spans = [pl.ds(i * step, step) for i in range(2)]
    weight_loads = copies([(weight.at[span], kept_weight.at[span]) for span in spans], sems, 12)
    later = copies(list(zip(refs[4:-2], small[4:])), sems, 14)
    for copy in loads + key_loads + value_loads + weight_loads + later:
        copy.start()
    for copy in loads:
        copy.wait()
    for h in range(heads):
        qs[pl.ds(h * requests, requests), :] = q_ref[:, pl.ds(h * head_dim, head_dim)].astype(F32)
    spots = [(table[r, lengths[r] // page_len], lengths[r] % page_len) for r in range(requests)]

    for copy in key_loads:
        copy.wait()
    for r, (page, slot) in enumerate(spots):
        keys[page, slot] = fresh[r][:, :head_dim]
    key_pages = keys.reshape(pages, page_rows, head_dim)
    value_pages = values.reshape(pages, page_rows, head_dim)
    columns = max_pages * page_rows
    lane = iota((heads, columns), 1)
    own_head = (lane & (heads_kv - 1)) == iota((heads, columns), 0) // group
    position = jnp.where(own_head, lane >> (heads_kv.bit_length() - 1), columns)
    scale = math.log2(math.e) / math.sqrt(head_dim)
    for r in range(requests):
        query = qs[pl.ds(r, heads, stride=requests), :].astype(BF16)
        gathered = jnp.concatenate([key_pages[table[r, j]] for j in range(max_pages)], axis=0)
        scores = jnp.where(position <= lengths[r], dot(query, gathered, NT), -1e30)
        exponent = jnp.exp2((scores - jnp.max(scores, axis=1, keepdims=True)) * scale)
        sums[r] = jnp.broadcast_to(jnp.sum(exponent, axis=1, keepdims=True), (heads, head_dim))
        probs[r] = exponent.astype(BF16)

    for copy in value_loads:
        copy.wait()
    for r, (page, slot) in enumerate(spots):
        values[page, slot] = fresh[r][:, head_dim:]
    for r in range(requests):
        gathered = jnp.concatenate([value_pages[table[r, j]] for j in range(max_pages)], axis=0)
        att[pl.ds(r, heads, stride=requests), :] = dot(probs[r], gathered) / sums[r]
    attended = jnp.concatenate(
        [att[pl.ds(h * requests, requests), :] for h in range(heads)], axis=1
    ).astype(BF16)
    projected = 0.0
    for i, copy in enumerate(weight_loads):
        copy.wait()
        projected = projected + dot(attended[:, i * step : (i + 1) * step], kept_weight[spans[i], :])
    for copy in later:
        copy.wait()
    return projected


def as_row(column):
    shape = (column.shape[0],) * 2
    return jnp.sum(jnp.where(iota(shape, 0) == iota(shape, 1), column, 0.0), axis=0, keepdims=True)


def route(projected, hidden, gain, router, ids, mixed_ref, slabs_ref, comb_ref, capacity):
    requests, width = hidden.shape
    experts = router.shape[0]
    parts = SLAB // capacity
    piece = width // parts
    slab_rows = experts * SLAB
    turns = jnp.where(lax.axis_index("req") % 2 == 0, group_turn(experts, 0), group_turn(experts, 1))

    def slab_expert(shape, dim):
        return (iota(shape, dim) // SLAB) ^ turns

    mixed = (hidden[...].astype(F32) + projected).astype(BF16)
    mixed_ref[...] = mixed
    mixed = mixed.astype(F32)
    norms = jnp.sqrt(jnp.mean(mixed * mixed, axis=1, keepdims=True) + 1e-06)
    normed = (mixed / norms * gain[...].astype(F32).reshape(1, width)).astype(BF16)
    logits = dot(normed, router[...], NT)
    top = jnp.max(logits, axis=1, keepdims=True)
    column = iota((requests, experts), 1)
    named = column < 0
    for k in range(ids.shape[1]):
        named = named | (ids[:, k : k + 1] == column)
    weights = jnp.where(named, jnp.exp(logits), 0.0)
    weights = weights / jnp.sum(weights, axis=1, keepdims=True)
    earlier = (iota((requests, requests), 1) < iota((requests, requests), 0)).astype(F32)
    rank = dot(earlier, named.astype(F32))
    place = jnp.where(named, rank, -1.0)
    normed = normed.astype(F32)
    stacked = jnp.concatenate([normed[:, p * piece : (p + 1) * piece] for p in range(parts)], axis=0)
    places = jnp.concatenate([place] * parts, axis=0)
    shape = (slab_rows, parts * requests)
    inner = iota(shape, 0) % SLAB
    spread = (slab_expert((slab_rows, experts), 0) == iota((slab_rows, experts), 1)).astype(F32)
    picks = (dot(spread, places, NT) == (inner // parts).astype(F32)) & (
        inner % parts == iota(shape, 1) // requests
    )
    slabs_ref[...] = dot(picks.astype(BF16), stacked.astype(BF16)).astype(BF16)
    shape = (experts, slab_rows)
    spread = (slab_expert(shape, 1) == iota(shape, 0)).astype(F32)
    inner = iota((requests, slab_rows), 1) % SLAB
    field = iota((requests, STATS), 1)
    comb_ref[:, slab_rows:] = jnp.where(field == 0, norms, jnp.where(field == 1, top, 0.0))
    comb_ref[:, :slab_rows] = jnp.where(
        dot(place, spread) == (inner // parts).astype(F32),
        dot(weights, spread, precision=lax.Precision.HIGHEST),
        0.0,
    )


def attend_route_kernel(capacity, *refs):
    inputs, (mixed, slabs, comb) = refs[:10], refs[10:13]
    small, scratch = refs[13:21], refs[21:]
    projected = attend(inputs, scratch[0], scratch[1], (small, scratch[2:]))
    hidden, gain, router, ids = small[4:]
    route(projected, hidden, gain, router, ids, mixed, slabs, comb, capacity)


def attend_kernel(*refs):
    attended, scratch = refs[6], refs[11:]
    attended[...] = attend(refs[:6], scratch[0], scratch[1], (refs[7:11], scratch[2:]))


def refresh_kernel(table, lengths, fresh, after, pool, new_pool, kept, sems):
    pages, page_len = kept.shape[:2]
    step = -(-pages // 4)
    spans = [pl.ds(start, min(step, pages - start)) for start in range(0, pages, step)]
    loads = copies([(pool.at[span], kept.at[span]) for span in spans], sems)
    stores = copies([(kept.at[span], new_pool.at[span]) for span in spans], sems, len(spans))
    for copy in loads:
        copy.start()
    spots = [(table[r, lengths[r] // page_len], lengths[r] % page_len) for r in range(table.shape[0])]
    for i, (load, store) in enumerate(zip(loads, stores)):
        load.wait()
        for r, (page, slot) in enumerate(spots):

            @pl.when((page >= i * step) & (page < (i + 1) * step))
            def _():
                kept[page, slot] = fresh[r]

        store.start()
    for copy in stores:
        copy.wait()


def route_kernel(capacity, projected, hidden, gain, router, ids, mixed, slabs, comb):
    route(projected[...], hidden, gain, router, ids, mixed, slabs, comb, capacity)


def unit_chunks(units):
    whole = units // 256 * 256
    return [(start, size) for start, size in ((0, whole), (whole, units - whole)) if size]


def expert_kernel(capacity, arrived, own_up, own_down, other_up, other_down, slabs,
                  slab_rows, kept_up, kept_down, rows, total, sems):
    units = kept_down.shape[0]
    arrive = pltpu.make_async_copy(arrived, slab_rows, sems.at[0])
    arrive.start()
    chunks = []
    for i, (start, size) in enumerate(unit_chunks(units)):
        span = pl.ds(start, size)
        chunks.append((span, copies(
            [(own_up.at[0, :, span, :], kept_up.at[:, span, :]), (own_down.at[0, span, :], kept_down.at[span, :])],
            sems,
            1 + 2 * i,
        )))
    for _, loads in chunks:
        loads[0].start()
    arrive.wait()
    parts = SLAB // capacity
    piece = slabs.shape[1]
    block = 128
    each = block // parts
    blocks = slabs.shape[0] // block
    shape = (block, block)
    slab_row, sorted_row = iota(shape, 1), iota(shape, 0)
    sort = (slab_row == sorted_row % each * parts + sorted_row // each).astype(BF16)
    for i in range(blocks):
        sorted_rows = dot(sort, slab_rows[pl.ds(i * block, block), :]).astype(BF16)
        rows[pl.ds(i * each, each), :] = jnp.concatenate(
            [sorted_rows[p * each : (p + 1) * each] for p in range(parts)], axis=1
        )
    states = rows[...]
    steps = [(other_up.at[0], other_down.at[0], span, []) for span, _ in chunks]
    steps += [(kept_up, kept_down, span, loads) for span, loads in chunks]

    def add_down(i, activated):
        _, down, span, loads = steps[i]
        if loads:
            loads[1].wait()
        term = dot(activated, down[span, :])
        total[...] = term if i == 0 else total[...] + term

    activated = None
    for i, (gate_up, _, span, loads) in enumerate(steps):
        if loads:
            loads[0].wait()
        gate = dot(states, gate_up[0, span, :], NT)
        up = dot(states, gate_up[1, span, :], NT)
        if i == 0:
            for _, loads in chunks:
                loads[1].start()
        else:
            add_down(i - 1, activated)
        activated = (gate / (1.0 + jnp.exp(-gate)) * up).astype(BF16)
    add_down(len(steps) - 1, activated)
    slab_row, sorted_row = iota(shape, 0), iota(shape, 1)
    unsort = (slab_row == sorted_row % each * parts + sorted_row // each).astype(BF16)
    for i in range(blocks):
        summed = total[pl.ds(i * each, each), :].astype(BF16)
        stacked = jnp.concatenate([summed[:, p * piece : (p + 1) * piece] for p in range(parts)], axis=0)
        slabs[pl.ds(i * block, block), :] = dot(unsort, stacked).astype(BF16)


def gather_terms(comb, slabs, norms, top, capacity):
    parts = SLAB // capacity
    requests = comb.shape[0]
    used = slabs.shape[0]
    norms[...] = as_row(comb[:, used : used + 1])
    top[...] = as_row(comb[:, used + 1 : used + 2])
    weights = comb[:, :used]
    pieces = []
    for _ in range(3):
        piece = weights.astype(BF16).astype(F32)
        weights = weights - piece
        pieces.append(piece)
    part = iota(weights.shape, 1) % parts
    stacked = jnp.concatenate(
        [jnp.where(part == p, piece, 0.0) for p in range(parts) for piece in pieces], axis=0
    ).astype(BF16)
    terms = dot(stacked, slabs[...])
    return jnp.concatenate(
        [
            sum(terms[(3 * p + i) * requests : (3 * p + i + 1) * requests] for i in range(3))
            for p in range(parts)
        ],
        axis=1,
    )


def combine_kernel(capacity, comb, slabs, mixed, out, norms, top):
    out[...] = (mixed[...].astype(F32) + gather_terms(comb, slabs, norms, top, capacity)).astype(BF16)


def gather_kernel(capacity, comb, slabs, out, norms, top):
    out[...] = gather_terms(comb, slabs, norms, top, capacity).astype(BF16)


def vmem(count):
    return [pl.BlockSpec(memory_space=pltpu.VMEM)] * count


def scalars(count):
    return [pl.BlockSpec(memory_space=pltpu.SMEM)] * count


def in_hbm(count):
    return [pl.BlockSpec(memory_space=pltpu.HBM)] * count


def pinned(*arrays):
    return [pltpu.with_memory_space_constraint(array, pltpu.HBM) for array in arrays]


def like(shape, dtype=BF16):
    return jax.ShapeDtypeStruct(shape, dtype)


def body(
    hidden,
    queries,
    fresh_key_value,
    kv_pool,
    page_table,
    lengths,
    out_weight,
    norm_gain,
    router_weight,
    expert_ids,
    expert_gate_up,
    expert_down,
):
    requests, width = hidden.shape
    req_count, kv_count = lax.axis_size("req"), lax.axis_size("kv")
    pages, page_len, heads_kv, pair_dim = kv_pool.shape
    head_dim = pair_dim // 2
    heads = queries.shape[1] // head_dim
    experts = router_weight.shape[0]
    copies = req_count // experts
    chosen = expert_ids.shape[1]
    capacity = 2 * max(1, (requests * chosen + 2 * experts - 1) // (2 * experts))
    parts = SLAB // capacity
    piece = width // parts
    slab_rows = experts * SLAB

    same_part = [
        [(place ^ group_turn(experts, part)) * copies + part for place in range(experts)] for part in range(copies)
    ]
    swap = [(index, index ^ 1) for index in range(req_count)]
    other_up = lax.ppermute(expert_gate_up, "req", swap)
    other_down = lax.ppermute(expert_down, "req", swap)

    attend_scratch = [
        pltpu.VMEM((pages, page_len, heads_kv, head_dim), BF16),
        pltpu.VMEM((pages, page_len, heads_kv, head_dim), BF16),
        pltpu.VMEM(out_weight.shape, BF16),
        pltpu.VMEM((heads * requests, head_dim), F32),
        pltpu.VMEM((heads * requests, head_dim), F32),
        pltpu.VMEM((requests, heads, page_table.shape[1] * page_len * heads_kv), BF16),
        pltpu.VMEM((requests, heads, head_dim), F32),
        pltpu.SemaphoreType.DMA((18,)),
    ]

    def small(*arrays):
        return [pltpu.VMEM(array.shape, array.dtype) for array in arrays]

    inputs = [pltpu.SMEM(page_table.shape, jnp.int32), pltpu.SMEM(lengths.shape, jnp.int32)]
    inputs += small(queries, fresh_key_value)
    routed_shapes = [like((requests, width)), like((slab_rows, piece)), like((requests, slab_rows + STATS), F32)]
    final_shapes = [like((requests, width)), like((1, requests), F32), like((1, requests), F32)]
    attend_params = pltpu.CompilerParams(vmem_limit_bytes=24 * MIB)
    if kv_count == 1:
        mixed, slabs, comb = pl.pallas_call(
            functools.partial(attend_route_kernel, capacity),
            out_shape=routed_shapes,
            in_specs=in_hbm(10),
            out_specs=vmem(3),
            scratch_shapes=inputs + small(hidden, norm_gain, router_weight, expert_ids) + attend_scratch,
            compiler_params=attend_params,
        )(*pinned(page_table, lengths, queries, fresh_key_value, hidden, norm_gain, router_weight, expert_ids,
                  kv_pool, out_weight))
    else:
        projected = pl.pallas_call(
            attend_kernel,
            out_shape=like((requests, width), F32),
            in_specs=in_hbm(6),
            out_specs=pl.BlockSpec(memory_space=pltpu.VMEM),
            scratch_shapes=inputs + attend_scratch,
            compiler_params=attend_params,
        )(*pinned(page_table, lengths, queries, fresh_key_value, kv_pool, out_weight))
        projected = lax.psum(projected, "kv")
        mixed, slabs, comb = pl.pallas_call(
            functools.partial(route_kernel, capacity),
            out_shape=routed_shapes,
            in_specs=vmem(5),
            out_specs=vmem(3),
        )(projected, hidden, norm_gain, router_weight, expert_ids)

    new_pool = pl.pallas_call(
        refresh_kernel,
        out_shape=like(kv_pool.shape),
        in_specs=scalars(2) + vmem(1) + in_hbm(2),
        out_specs=pl.BlockSpec(memory_space=pltpu.HBM),
        scratch_shapes=[pltpu.VMEM(kv_pool.shape, BF16), pltpu.SemaphoreType.DMA((8,))],
        compiler_params=pltpu.CompilerParams(vmem_limit_bytes=12 * MIB),
        cost_estimate=pl.CostEstimate(flops=0, bytes_accessed=8 * kv_pool.size, transcendentals=0),
    )(page_table, lengths, fresh_key_value, comb, *pinned(kv_pool))

    def exchange(array):
        array = array.reshape(experts, SLAB, piece)
        array = lax.all_to_all(
            array, "req", split_axis=0, concat_axis=0, tiled=True, axis_index_groups=same_part
        )
        return array.reshape(slab_rows, piece)

    arrived = exchange(slabs)
    kept = experts * capacity
    units = expert_down.shape[1]
    leaving = pl.pallas_call(
        functools.partial(expert_kernel, capacity),
        out_shape=like((slab_rows, piece)),
        in_specs=in_hbm(3) + vmem(2),
        out_specs=pl.BlockSpec(memory_space=pltpu.VMEM),
        scratch_shapes=[
            pltpu.VMEM((slab_rows, piece), BF16),
            pltpu.VMEM((2, units, width), BF16),
            pltpu.VMEM((units, width), BF16),
            pltpu.VMEM((kept, width), BF16),
            pltpu.VMEM((kept, width), F32),
            pltpu.SemaphoreType.DMA((1 + 2 * len(unit_chunks(units)),)),
        ],
        compiler_params=pltpu.CompilerParams(vmem_limit_bytes=20 * MIB),
    )(arrived, *pinned(expert_gate_up, expert_down), other_up, other_down)
    returned = exchange(leaving)
    if kv_count == 1:
        out_hidden, norms, top = pl.pallas_call(
            functools.partial(combine_kernel, capacity),
            out_shape=final_shapes,
            in_specs=vmem(3),
            out_specs=vmem(3),
            compiler_params=pltpu.CompilerParams(vmem_limit_bytes=8 * MIB),
        )(comb, returned, mixed)
    else:
        routed, norms, top = pl.pallas_call(
            functools.partial(gather_kernel, capacity),
            out_shape=final_shapes,
            in_specs=vmem(2),
            out_specs=vmem(3),
        )(comb, returned)
        routed = lax.psum(routed, "kv").astype(F32)
        out_hidden = (mixed.astype(F32) + routed).astype(BF16)
    return out_hidden, new_pool, norms.reshape(requests), top.reshape(requests)


def solution(mesh):
    in_specs = (
        P("req", None),
        P("req", "kv"),
        P("req", "kv", None),
        P("req", None, "kv", None),
        P("req", None),
        P("req"),
        P("kv", None),
        P(),
        P(),
        P("req", None),
        P("req", None, "kv", None),
        P("req", "kv", None),
    )
    out_specs = (P("req", None), P("req", None, "kv", None), P("req"), P("req"))
    return jax.shard_map(body, mesh=mesh, in_specs=in_specs, out_specs=out_specs, check_vma=False)
```

```python
import functools
import math

import jax
import jax.numpy as jnp
from jax import lax
from jax.experimental import pallas as pl
from jax.experimental.pallas import tpu as pltpu
from jax.sharding import PartitionSpec as P

BF16 = jnp.bfloat16
F32 = jnp.float32
NT = (((1,), (1,)), ((), ()))
NN = (((1,), (0,)), ((), ()))
STATS = 128
SLAB = 16
MIB = 1 << 20


def dot(a, b, dims=NN, precision=None):
    return lax.dot_general(a, b, dims, precision=precision, preferred_element_type=F32)


def iota(shape, dim):
    return lax.broadcasted_iota(jnp.int32, shape, dim)


def copies(pairs, sems, first=0):
    return [pltpu.make_async_copy(src, dst, sems.at[first + i]) for i, (src, dst) in enumerate(pairs)]


def group_turn(chips, part):
    return chips * 9 // 16 if part % 2 else chips // 4


def pool_half(array, i):
    head_dim = array.shape[3] // 2
    return array.at[:, :, :, pl.ds(i * head_dim, head_dim)]


def attend(refs, keys, values, scratch):
    small, (kept_weight, qs, att, probs, sums, sems) = scratch
    table, lengths, q_ref, fresh = small[:4]
    requests, max_pages = table.shape
    pages, page_len, heads_kv, head_dim = keys.shape
    heads = q_ref.shape[1] // head_dim
    group = heads // heads_kv
    page_rows = page_len * heads_kv
    pool, weight = refs[-2:]
    loads = copies(list(zip(refs[:4], small[:4])), sems)
    page_step = -(-pages // 4)
    page_spans = [pl.ds(first, min(page_step, pages - first)) for first in range(0, pages, page_step)]
    key_loads, value_loads = [
        copies(
            [(pool_half(pool, i).at[span], kept.at[span]) for span in page_spans], sems, 4 + i * len(page_spans)
        )
        for i, kept in enumerate((keys, values))
    ]
    step = weight.shape[0] // 4
    spans = [pl.ds(i * step, step) for i in range(4)]
    weight_loads = copies([(weight.at[span], kept_weight.at[span]) for span in spans], sems, 12)
    later = copies(list(zip(refs[4:-2], small[4:])), sems, 16)
    for copy in loads + key_loads + value_loads + weight_loads[:2] + later:
        copy.start()
    for copy in loads:
        copy.wait()
    for h in range(heads):
        qs[pl.ds(h * requests, requests), :] = q_ref[:, pl.ds(h * head_dim, head_dim)].astype(F32)
    spots = [(table[r, lengths[r] // page_len], lengths[r] % page_len) for r in range(requests)]

    for copy in key_loads:
        copy.wait()
    weight_loads[2].start()
    for r, (page, slot) in enumerate(spots):
        keys[page, slot] = fresh[r][:, :head_dim]
    key_pages = keys.reshape(pages, page_rows, head_dim)
    value_pages = values.reshape(pages, page_rows, head_dim)
    columns = max_pages * page_rows
    lane = iota((heads, columns), 1)
    own_head = (lane & (heads_kv - 1)) == iota((heads, columns), 0) // group
    position = jnp.where(own_head, lane >> (heads_kv.bit_length() - 1), columns)
    scale = math.log2(math.e) / math.sqrt(head_dim)
    for r in range(requests):
        query = qs[pl.ds(r, heads, stride=requests), :].astype(BF16)
        gathered = jnp.concatenate([key_pages[table[r, j]] for j in range(max_pages)], axis=0)
        scores = jnp.where(position <= lengths[r], dot(query, gathered, NT), -1e30)
        exponent = jnp.exp2((scores - jnp.max(scores, axis=1, keepdims=True)) * scale)
        sums[r] = jnp.broadcast_to(jnp.sum(exponent, axis=1, keepdims=True), (heads, head_dim))
        probs[r] = exponent.astype(BF16)

    for copy in value_loads:
        copy.wait()
    weight_loads[3].start()
    for r, (page, slot) in enumerate(spots):
        values[page, slot] = fresh[r][:, head_dim:]
    for r in range(requests):
        gathered = jnp.concatenate([value_pages[table[r, j]] for j in range(max_pages)], axis=0)
        att[pl.ds(r, heads, stride=requests), :] = dot(probs[r], gathered) / sums[r]
    attended = jnp.concatenate(
        [att[pl.ds(h * requests, requests), :] for h in range(heads)], axis=1
    ).astype(BF16)
    projected = 0.0
    for i, copy in enumerate(weight_loads):
        copy.wait()
        projected = projected + dot(attended[:, i * step : (i + 1) * step], kept_weight[spans[i], :])
    for copy in later:
        copy.wait()
    return projected


def as_row(column):
    shape = (column.shape[0],) * 2
    return jnp.sum(jnp.where(iota(shape, 0) == iota(shape, 1), column, 0.0), axis=0, keepdims=True)


def route(projected, hidden, gain, router, ids, mixed_ref, slabs_ref, comb_ref, capacity):
    requests, width = hidden.shape
    experts = router.shape[0]
    parts = SLAB // capacity
    piece = width // parts
    slab_rows = experts * SLAB
    turns = jnp.where(lax.axis_index("req") % 2 == 0, group_turn(experts, 0), group_turn(experts, 1))

    def slab_expert(shape, dim):
        return (iota(shape, dim) // SLAB) ^ turns

    mixed = (hidden[...].astype(F32) + projected).astype(BF16)
    mixed_ref[...] = mixed
    mixed = mixed.astype(F32)
    norms = jnp.sqrt(jnp.mean(mixed * mixed, axis=1, keepdims=True) + 1e-06)
    normed = (mixed / norms * gain[...].astype(F32).reshape(1, width)).astype(BF16)
    logits = dot(normed, router[...], NT)
    top = jnp.max(logits, axis=1, keepdims=True)
    column = iota((requests, experts), 1)
    named = column < 0
    for k in range(ids.shape[1]):
        named = named | (ids[:, k : k + 1] == column)
    weights = jnp.where(named, jnp.exp(logits), 0.0)
    weights = weights / jnp.sum(weights, axis=1, keepdims=True)
    earlier = (iota((requests, requests), 1) < iota((requests, requests), 0)).astype(F32)
    rank = dot(earlier, named.astype(F32))
    place = jnp.where(named, rank, -1.0)
    normed = normed.astype(F32)
    stacked = jnp.concatenate([normed[:, p * piece : (p + 1) * piece] for p in range(parts)], axis=0)
    places = jnp.concatenate([place] * parts, axis=0)
    shape = (slab_rows, parts * requests)
    inner = iota(shape, 0) % SLAB
    spread = (slab_expert((slab_rows, experts), 0) == iota((slab_rows, experts), 1)).astype(F32)
    picks = (dot(spread, places, NT) == (inner // parts).astype(F32)) & (
        inner % parts == iota(shape, 1) // requests
    )
    slabs_ref[...] = dot(picks.astype(BF16), stacked.astype(BF16)).astype(BF16)
    shape = (experts, slab_rows)
    spread = (slab_expert(shape, 1) == iota(shape, 0)).astype(F32)
    inner = iota((requests, slab_rows), 1) % SLAB
    field = iota((requests, STATS), 1)
    comb_ref[:, slab_rows:] = jnp.where(field == 0, norms, jnp.where(field == 1, top, 0.0))
    comb_ref[:, :slab_rows] = jnp.where(
        dot(place, spread) == (inner // parts).astype(F32),
        dot(weights, spread, precision=lax.Precision.HIGHEST),
        0.0,
    )


def attend_route_kernel(capacity, *refs):
    inputs, (mixed, slabs, comb) = refs[:10], refs[10:13]
    small, scratch = refs[13:21], refs[21:]
    projected = attend(inputs, scratch[0], scratch[1], (small, scratch[2:]))
    hidden, gain, router, ids = small[4:]
    route(projected, hidden, gain, router, ids, mixed, slabs, comb, capacity)


def attend_kernel(*refs):
    attended, scratch = refs[6], refs[11:]
    attended[...] = attend(refs[:6], scratch[0], scratch[1], (refs[7:11], scratch[2:]))


def refresh_kernel(table, lengths, fresh, after, pool, new_pool, kept, sems):
    pages, page_len = kept.shape[:2]
    step = -(-pages // 4)
    spans = [pl.ds(start, min(step, pages - start)) for start in range(0, pages, step)]
    loads = copies([(pool.at[span], kept.at[span]) for span in spans], sems)
    stores = copies([(kept.at[span], new_pool.at[span]) for span in spans], sems, len(spans))
    for copy in loads:
        copy.start()
    spots = [(table[r, lengths[r] // page_len], lengths[r] % page_len) for r in range(table.shape[0])]
    for i, (load, store) in enumerate(zip(loads, stores)):
        load.wait()
        for r, (page, slot) in enumerate(spots):

            @pl.when((page >= i * step) & (page < (i + 1) * step))
            def _():
                kept[page, slot] = fresh[r]

        store.start()
    for copy in stores:
        copy.wait()


def route_kernel(capacity, projected, hidden, gain, router, ids, mixed, slabs, comb):
    route(projected[...], hidden, gain, router, ids, mixed, slabs, comb, capacity)


def unit_chunks(units):
    whole = units // 256 * 256
    return [(start, size) for start, size in ((0, whole), (whole, units - whole)) if size]


def expert_kernel(capacity, arrived, own_up, own_down, other_up, other_down, slabs,
                  slab_rows, kept_up, kept_down, rows, total, sems):
    units = kept_down.shape[0]
    arrive = pltpu.make_async_copy(arrived, slab_rows, sems.at[0])
    arrive.start()
    chunks = []
    for i, (start, size) in enumerate(unit_chunks(units)):
        span = pl.ds(start, size)
        chunks.append((span, copies(
            [(own_up.at[0, :, span, :], kept_up.at[:, span, :]), (own_down.at[0, span, :], kept_down.at[span, :])],
            sems,
            1 + 2 * i,
        )))
    for _, loads in chunks:
        loads[0].start()
    arrive.wait()
    parts = SLAB // capacity
    piece = slabs.shape[1]
    block = 128
    each = block // parts
    blocks = slabs.shape[0] // block
    shape = (block, block)
    slab_row, sorted_row = iota(shape, 1), iota(shape, 0)
    sort = (slab_row == sorted_row % each * parts + sorted_row // each).astype(BF16)
    for i in range(blocks):
        sorted_rows = dot(sort, slab_rows[pl.ds(i * block, block), :]).astype(BF16)
        rows[pl.ds(i * each, each), :] = jnp.concatenate(
            [sorted_rows[p * each : (p + 1) * each] for p in range(parts)], axis=1
        )
    states = rows[...]
    steps = [(other_up.at[0], other_down.at[0], span, []) for span, _ in chunks]
    steps += [(kept_up, kept_down, span, loads) for span, loads in chunks]

    def add_down(i, activated):
        _, down, span, loads = steps[i]
        if loads:
            loads[1].wait()
        term = dot(activated, down[span, :])
        total[...] = term if i == 0 else total[...] + term

    activated = None
    for i, (gate_up, _, span, loads) in enumerate(steps):
        if loads:
            loads[0].wait()
        gate = dot(states, gate_up[0, span, :], NT)
        up = dot(states, gate_up[1, span, :], NT)
        if i == 0:
            for _, loads in chunks:
                loads[1].start()
        else:
            add_down(i - 1, activated)
        activated = (gate / (1.0 + jnp.exp(-gate)) * up).astype(BF16)
    add_down(len(steps) - 1, activated)
    slab_row, sorted_row = iota(shape, 0), iota(shape, 1)
    unsort = (slab_row == sorted_row % each * parts + sorted_row // each).astype(BF16)
    for i in range(blocks):
        summed = total[pl.ds(i * each, each), :].astype(BF16)
        stacked = jnp.concatenate([summed[:, p * piece : (p + 1) * piece] for p in range(parts)], axis=0)
        slabs[pl.ds(i * block, block), :] = dot(unsort, stacked).astype(BF16)


def gather_terms(comb, slabs, norms, top, capacity):
    parts = SLAB // capacity
    requests = comb.shape[0]
    used = slabs.shape[0]
    norms[...] = as_row(comb[:, used : used + 1])
    top[...] = as_row(comb[:, used + 1 : used + 2])
    weights = comb[:, :used]
    pieces = []
    for _ in range(3):
        piece = weights.astype(BF16).astype(F32)
        weights = weights - piece
        pieces.append(piece)
    part = iota(weights.shape, 1) % parts
    stacked = jnp.concatenate(
        [jnp.where(part == p, piece, 0.0) for p in range(parts) for piece in pieces], axis=0
    ).astype(BF16)
    terms = dot(stacked, slabs[...])
    return jnp.concatenate(
        [
            sum(terms[(3 * p + i) * requests : (3 * p + i + 1) * requests] for i in range(3))
            for p in range(parts)
        ],
        axis=1,
    )


def combine_kernel(capacity, comb, slabs, mixed, out, norms, top):
    out[...] = (mixed[...].astype(F32) + gather_terms(comb, slabs, norms, top, capacity)).astype(BF16)


def gather_kernel(capacity, comb, slabs, out, norms, top):
    out[...] = gather_terms(comb, slabs, norms, top, capacity).astype(BF16)


def vmem(count):
    return [pl.BlockSpec(memory_space=pltpu.VMEM)] * count


def scalars(count):
    return [pl.BlockSpec(memory_space=pltpu.SMEM)] * count


def in_hbm(count):
    return [pl.BlockSpec(memory_space=pltpu.HBM)] * count


def pinned(*arrays):
    return [pltpu.with_memory_space_constraint(array, pltpu.HBM) for array in arrays]


def like(shape, dtype=BF16):
    return jax.ShapeDtypeStruct(shape, dtype)


def body(
    hidden,
    queries,
    fresh_key_value,
    kv_pool,
    page_table,
    lengths,
    out_weight,
    norm_gain,
    router_weight,
    expert_ids,
    expert_gate_up,
    expert_down,
):
    requests, width = hidden.shape
    req_count, kv_count = lax.axis_size("req"), lax.axis_size("kv")
    pages, page_len, heads_kv, pair_dim = kv_pool.shape
    head_dim = pair_dim // 2
    heads = queries.shape[1] // head_dim
    experts = router_weight.shape[0]
    copies = req_count // experts
    chosen = expert_ids.shape[1]
    capacity = 2 * max(1, (requests * chosen + 2 * experts - 1) // (2 * experts))
    parts = SLAB // capacity
    piece = width // parts
    slab_rows = experts * SLAB

    same_part = [
        [(place ^ group_turn(experts, part)) * copies + part for place in range(experts)] for part in range(copies)
    ]
    swap = [(index, index ^ 1) for index in range(req_count)]
    other_up = lax.ppermute(expert_gate_up, "req", swap)
    other_down = lax.ppermute(expert_down, "req", swap)

    attend_scratch = [
        pltpu.VMEM((pages, page_len, heads_kv, head_dim), BF16),
        pltpu.VMEM((pages, page_len, heads_kv, head_dim), BF16),
        pltpu.VMEM(out_weight.shape, BF16),
        pltpu.VMEM((heads * requests, head_dim), F32),
        pltpu.VMEM((heads * requests, head_dim), F32),
        pltpu.VMEM((requests, heads, page_table.shape[1] * page_len * heads_kv), BF16),
        pltpu.VMEM((requests, heads, head_dim), F32),
        pltpu.SemaphoreType.DMA((20,)),
    ]

    def small(*arrays):
        return [pltpu.VMEM(array.shape, array.dtype) for array in arrays]

    inputs = [pltpu.SMEM(page_table.shape, jnp.int32), pltpu.SMEM(lengths.shape, jnp.int32)]
    inputs += small(queries, fresh_key_value)
    routed_shapes = [like((requests, width)), like((slab_rows, piece)), like((requests, slab_rows + STATS), F32)]
    final_shapes = [like((requests, width)), like((1, requests), F32), like((1, requests), F32)]
    attend_params = pltpu.CompilerParams(vmem_limit_bytes=24 * MIB)
    if kv_count == 1:
        mixed, slabs, comb = pl.pallas_call(
            functools.partial(attend_route_kernel, capacity),
            out_shape=routed_shapes,
            in_specs=in_hbm(10),
            out_specs=vmem(3),
            scratch_shapes=inputs + small(hidden, norm_gain, router_weight, expert_ids) + attend_scratch,
            compiler_params=attend_params,
        )(*pinned(page_table, lengths, queries, fresh_key_value, hidden, norm_gain, router_weight, expert_ids,
                  kv_pool, out_weight))
    else:
        projected = pl.pallas_call(
            attend_kernel,
            out_shape=like((requests, width), F32),
            in_specs=in_hbm(6),
            out_specs=pl.BlockSpec(memory_space=pltpu.VMEM),
            scratch_shapes=inputs + attend_scratch,
            compiler_params=attend_params,
        )(*pinned(page_table, lengths, queries, fresh_key_value, kv_pool, out_weight))
        projected = lax.psum(projected, "kv")
        mixed, slabs, comb = pl.pallas_call(
            functools.partial(route_kernel, capacity),
            out_shape=routed_shapes,
            in_specs=vmem(5),
            out_specs=vmem(3),
        )(projected, hidden, norm_gain, router_weight, expert_ids)

    new_pool = pl.pallas_call(
        refresh_kernel,
        out_shape=like(kv_pool.shape),
        in_specs=scalars(2) + vmem(1) + in_hbm(2),
        out_specs=pl.BlockSpec(memory_space=pltpu.HBM),
        scratch_shapes=[pltpu.VMEM(kv_pool.shape, BF16), pltpu.SemaphoreType.DMA((8,))],
        compiler_params=pltpu.CompilerParams(vmem_limit_bytes=12 * MIB),
        cost_estimate=pl.CostEstimate(flops=0, bytes_accessed=8 * kv_pool.size, transcendentals=0),
    )(page_table, lengths, fresh_key_value, comb, *pinned(kv_pool))

    def exchange(array):
        array = array.reshape(experts, SLAB, piece)
        array = lax.all_to_all(
            array, "req", split_axis=0, concat_axis=0, tiled=True, axis_index_groups=same_part
        )
        return array.reshape(slab_rows, piece)

    arrived = exchange(slabs)
    kept = experts * capacity
    units = expert_down.shape[1]
    leaving = pl.pallas_call(
        functools.partial(expert_kernel, capacity),
        out_shape=like((slab_rows, piece)),
        in_specs=in_hbm(3) + vmem(2),
        out_specs=pl.BlockSpec(memory_space=pltpu.VMEM),
        scratch_shapes=[
            pltpu.VMEM((slab_rows, piece), BF16),
            pltpu.VMEM((2, units, width), BF16),
            pltpu.VMEM((units, width), BF16),
            pltpu.VMEM((kept, width), BF16),
            pltpu.VMEM((kept, width), F32),
            pltpu.SemaphoreType.DMA((1 + 2 * len(unit_chunks(units)),)),
        ],
        compiler_params=pltpu.CompilerParams(vmem_limit_bytes=20 * MIB),
    )(arrived, *pinned(expert_gate_up, expert_down), other_up, other_down)
    returned = exchange(leaving)
    if kv_count == 1:
        out_hidden, norms, top = pl.pallas_call(
            functools.partial(combine_kernel, capacity),
            out_shape=final_shapes,
            in_specs=vmem(3),
            out_specs=vmem(3),
            compiler_params=pltpu.CompilerParams(vmem_limit_bytes=8 * MIB),
        )(comb, returned, mixed)
    else:
        routed, norms, top = pl.pallas_call(
            functools.partial(gather_kernel, capacity),
            out_shape=final_shapes,
            in_specs=vmem(2),
            out_specs=vmem(3),
        )(comb, returned)
        routed = lax.psum(routed, "kv").astype(F32)
        out_hidden = (mixed.astype(F32) + routed).astype(BF16)
    return out_hidden, new_pool, norms.reshape(requests), top.reshape(requests)


def solution(mesh):
    in_specs = (
        P("req", None),
        P("req", "kv"),
        P("req", "kv", None),
        P("req", None, "kv", None),
        P("req", None),
        P("req"),
        P("kv", None),
        P(),
        P(),
        P("req", None),
        P("req", None, "kv", None),
        P("req", "kv", None),
    )
    out_specs = (P("req", None), P("req", None, "kv", None), P("req"), P("req"))
    return jax.shard_map(body, mesh=mesh, in_specs=in_specs, out_specs=out_specs, check_vma=False)
```

```python
import functools
import math

import jax
import jax.numpy as jnp
from jax import lax
from jax.experimental import pallas as pl
from jax.experimental.pallas import tpu as pltpu
from jax.sharding import PartitionSpec as P

BF16 = jnp.bfloat16
F32 = jnp.float32
NT = (((1,), (1,)), ((), ()))
NN = (((1,), (0,)), ((), ()))
STATS = 128
SLAB = 16
MIB = 1 << 20


def dot(a, b, dims=NN, precision=None):
    return lax.dot_general(a, b, dims, precision=precision, preferred_element_type=F32)


def iota(shape, dim):
    return lax.broadcasted_iota(jnp.int32, shape, dim)


def copies(pairs, sems, first=0):
    return [pltpu.make_async_copy(src, dst, sems.at[first + i]) for i, (src, dst) in enumerate(pairs)]


def group_turn(chips, part):
    return chips * 9 // 16 if part % 2 else chips * 7 // 16


def pool_half(array, i):
    head_dim = array.shape[3] // 2
    return array.at[:, :, :, pl.ds(i * head_dim, head_dim)]


def attend(refs, keys, values, scratch, prepare):
    small, (kept_weight, qs, att, probs, sums, sems) = scratch
    table, lengths, q_ref, fresh = small[:4]
    requests, max_pages = table.shape
    pages, page_len, heads_kv, head_dim = keys.shape
    heads = q_ref.shape[1] // head_dim
    group = heads // heads_kv
    page_rows = page_len * heads_kv
    pool, weight = refs[-2:]
    loads = copies(list(zip(refs[:4], small[:4])), sems)
    page_step = -(-pages // 4)
    page_spans = [pl.ds(first, min(page_step, pages - first)) for first in range(0, pages, page_step)]
    key_loads, value_loads = [
        copies(
            [(pool_half(pool, i).at[span], kept.at[span]) for span in page_spans], sems, 4 + i * len(page_spans)
        )
        for i, kept in enumerate((keys, values))
    ]
    step = weight.shape[0] // 2
    spans = [pl.ds(i * step, step) for i in range(2)]
    weight_loads = copies([(weight.at[span], kept_weight.at[span]) for span in spans], sems, 12)
    later = copies(list(zip(refs[4:-2], small[4:])), sems, 14)
    for copy in loads + key_loads + value_loads + weight_loads + later:
        copy.start()
    for copy in loads:
        copy.wait()
    for h in range(heads):
        qs[pl.ds(h * requests, requests), :] = q_ref[:, pl.ds(h * head_dim, head_dim)].astype(F32)
    spots = [(table[r, lengths[r] // page_len], lengths[r] % page_len) for r in range(requests)]

    for copy in key_loads:
        copy.wait()
    for r, (page, slot) in enumerate(spots):
        keys[page, slot] = fresh[r][:, :head_dim]
    key_pages = keys.reshape(pages, page_rows, head_dim)
    value_pages = values.reshape(pages, page_rows, head_dim)
    columns = max_pages * page_rows
    lane = iota((heads, columns), 1)
    own_head = (lane & (heads_kv - 1)) == iota((heads, columns), 0) // group
    position = jnp.where(own_head, lane >> (heads_kv.bit_length() - 1), columns)
    scale = math.log2(math.e) / math.sqrt(head_dim)
    for r in range(requests):
        query = qs[pl.ds(r, heads, stride=requests), :].astype(BF16)
        gathered = jnp.concatenate([key_pages[table[r, j]] for j in range(max_pages)], axis=0)
        scores = jnp.where(position <= lengths[r], dot(query, gathered, NT), -1e30)
        exponent = jnp.exp2((scores - jnp.max(scores, axis=1, keepdims=True)) * scale)
        sums[r] = jnp.broadcast_to(jnp.sum(exponent, axis=1, keepdims=True), (heads, head_dim))
        probs[r] = exponent.astype(BF16)

    for copy in later:
        copy.wait()
    prepared = prepare()
    for copy in value_loads:
        copy.wait()
    for r, (page, slot) in enumerate(spots):
        values[page, slot] = fresh[r][:, head_dim:]
    for r in range(requests):
        gathered = jnp.concatenate([value_pages[table[r, j]] for j in range(max_pages)], axis=0)
        att[pl.ds(r, heads, stride=requests), :] = dot(probs[r], gathered) / sums[r]
    attended = jnp.concatenate(
        [att[pl.ds(h * requests, requests), :] for h in range(heads)], axis=1
    ).astype(BF16)
    projected = 0.0
    for i, copy in enumerate(weight_loads):
        copy.wait()
        projected = projected + dot(attended[:, i * step : (i + 1) * step], kept_weight[spans[i], :])
    return projected, prepared


def as_row(column):
    shape = (column.shape[0],) * 2
    return jnp.sum(jnp.where(iota(shape, 0) == iota(shape, 1), column, 0.0), axis=0, keepdims=True)


def split(values):
    pieces = []
    for _ in range(3):
        pieces.append(values.astype(BF16).astype(F32))
        values = values - pieces[-1]
    return pieces


def plan(ids, requests, experts, slab_rows, capacity):
    parts = SLAB // capacity
    turns = jnp.where(lax.axis_index("req") % 2 == 0, group_turn(experts, 0), group_turn(experts, 1))

    def slab_expert(shape, dim):
        return (iota(shape, dim) // SLAB) ^ turns

    column = iota((requests, experts), 1)
    named = column < 0
    for k in range(ids.shape[1]):
        named = named | (ids[:, k : k + 1] == column)
    named = named.astype(F32)
    earlier = (iota((requests, requests), 1) < iota((requests, requests), 0)).astype(F32)
    rank = dot(earlier, named)
    place = jnp.where(named > 0.0, rank, -1.0)
    places = jnp.concatenate([place] * parts, axis=0)
    shape = (slab_rows, parts * requests)
    inner = iota(shape, 0) % SLAB
    spread = (slab_expert((slab_rows, experts), 0) == iota((slab_rows, experts), 1)).astype(F32)
    picks = (dot(spread, places, NT) == (inner // parts).astype(F32)) & (
        inner % parts == iota(shape, 1) // requests
    )
    shape = (experts, slab_rows)
    spread = (slab_expert(shape, 1) == iota(shape, 0)).astype(F32)
    inner = iota((requests, slab_rows), 1) % SLAB
    holds = (dot(place, spread) == (inner // parts).astype(F32)).astype(F32)
    return named, picks.astype(BF16), spread.astype(BF16), holds


def route(projected, planned, hidden, gain, router, mixed_ref, slabs_ref, comb_ref, capacity):
    named, picks, spread, holds = planned
    requests, width = hidden.shape
    parts = SLAB // capacity
    piece = width // parts
    slab_rows = slabs_ref.shape[0]
    mixed = (hidden[...].astype(F32) + projected).astype(BF16)
    mixed_ref[...] = mixed
    mixed = mixed.astype(F32)
    norms = jnp.sqrt(jnp.mean(mixed * mixed, axis=1, keepdims=True) + 1e-06)
    normed = (mixed / norms * gain[...].astype(F32).reshape(1, width)).astype(BF16)
    wide = normed.astype(F32)
    stacked = jnp.concatenate([wide[:, p * piece : (p + 1) * piece] for p in range(parts)], axis=0)
    slabs_ref[...] = dot(picks, stacked.astype(BF16)).astype(BF16)
    logits = dot(normed, router[...], NT)
    top = jnp.max(logits, axis=1, keepdims=True)
    weights = jnp.where(named > 0.0, jnp.exp(logits), 0.0)
    weights = weights / jnp.sum(weights, axis=1, keepdims=True)
    spread_weights = dot(jnp.concatenate(split(weights), axis=0).astype(BF16), spread)
    spread_weights = sum(spread_weights[i * requests : (i + 1) * requests] for i in range(3))
    field = iota((requests, STATS), 1)
    comb_ref[:, slab_rows:] = jnp.where(field == 0, norms, jnp.where(field == 1, top, 0.0))
    comb_ref[:, :slab_rows] = jnp.where(holds > 0.0, spread_weights, 0.0)


def attend_route_kernel(capacity, *refs):
    inputs, (mixed, slabs, comb) = refs[:10], refs[10:13]
    small, scratch = refs[13:21], refs[21:]
    hidden, gain, router, ids = small[4:]

    def prepare():
        return plan(ids, ids.shape[0], router.shape[0], slabs.shape[0], capacity)

    projected, planned = attend(inputs, scratch[0], scratch[1], (small, scratch[2:]), prepare)
    route(projected, planned, hidden, gain, router, mixed, slabs, comb, capacity)


def attend_kernel(*refs):
    projected, scratch = refs[6], refs[11:]
    projected[...] = attend(refs[:6], scratch[0], scratch[1], (refs[7:11], scratch[2:]), lambda: None)[0]


def refresh_kernel(table, lengths, fresh, after, pool, new_pool, kept, sems):
    pages, page_len = kept.shape[:2]
    step = -(-pages // 4)
    spans = [pl.ds(start, min(step, pages - start)) for start in range(0, pages, step)]
    loads = copies([(pool.at[span], kept.at[span]) for span in spans], sems)
    stores = copies([(kept.at[span], new_pool.at[span]) for span in spans], sems, len(spans))
    for copy in loads:
        copy.start()
    spots = [(table[r, lengths[r] // page_len], lengths[r] % page_len) for r in range(table.shape[0])]
    for i, (load, store) in enumerate(zip(loads, stores)):
        load.wait()
        for r, (page, slot) in enumerate(spots):

            @pl.when((page >= i * step) & (page < (i + 1) * step))
            def _():
                kept[page, slot] = fresh[r]

        store.start()
    for copy in stores:
        copy.wait()


def route_kernel(capacity, projected, hidden, gain, router, ids, mixed, slabs, comb):
    planned = plan(ids, ids.shape[0], router.shape[0], slabs.shape[0], capacity)
    route(projected[...], planned, hidden, gain, router, mixed, slabs, comb, capacity)


def unit_chunks(units):
    whole = units // 256 * 256
    return [(start, size) for start, size in ((0, whole), (whole, units - whole)) if size]


def expert_kernel(capacity, arrived, own_up, own_down, other_up, other_down, slabs,
                  slab_rows, kept_up, kept_down, rows, total, sems):
    units = kept_down.shape[0]
    arrive = pltpu.make_async_copy(arrived, slab_rows, sems.at[0])
    arrive.start()
    chunks = []
    for i, (start, size) in enumerate(unit_chunks(units)):
        span = pl.ds(start, size)
        chunks.append((span, copies(
            [(own_up.at[0, :, span, :], kept_up.at[:, span, :]), (own_down.at[0, span, :], kept_down.at[span, :])],
            sems,
            1 + 2 * i,
        )))
    for _, loads in chunks:
        loads[0].start()
    arrive.wait()
    parts = SLAB // capacity
    piece = slabs.shape[1]
    block = 128
    each = block // parts
    blocks = slabs.shape[0] // block
    shape = (block, block)
    slab_row, sorted_row = iota(shape, 1), iota(shape, 0)
    sort = (slab_row == sorted_row % each * parts + sorted_row // each).astype(BF16)
    for i in range(blocks):
        sorted_rows = dot(sort, slab_rows[pl.ds(i * block, block), :]).astype(BF16)
        rows[pl.ds(i * each, each), :] = jnp.concatenate(
            [sorted_rows[p * each : (p + 1) * each] for p in range(parts)], axis=1
        )
    states = rows[...]
    steps = [(other_up.at[0], other_down.at[0], span, []) for span, _ in chunks]
    steps += [(kept_up, kept_down, span, loads) for span, loads in chunks]

    def add_down(i, activated):
        _, down, span, loads = steps[i]
        if loads:
            loads[1].wait()
        term = dot(activated, down[span, :])
        total[...] = term if i == 0 else total[...] + term

    activated = None
    for i, (gate_up, _, span, loads) in enumerate(steps):
        if loads:
            loads[0].wait()
        gate = dot(states, gate_up[0, span, :], NT)
        up = dot(states, gate_up[1, span, :], NT)
        if i == 0:
            for _, loads in chunks:
                loads[1].start()
        else:
            add_down(i - 1, activated)
        activated = (gate / (1.0 + jnp.exp(-gate)) * up).astype(BF16)
    add_down(len(steps) - 1, activated)
    slab_row, sorted_row = iota(shape, 0), iota(shape, 1)
    unsort = (slab_row == sorted_row % each * parts + sorted_row // each).astype(BF16)
    for i in range(blocks):
        summed = total[pl.ds(i * each, each), :].astype(BF16)
        stacked = jnp.concatenate([summed[:, p * piece : (p + 1) * piece] for p in range(parts)], axis=0)
        slabs[pl.ds(i * block, block), :] = dot(unsort, stacked).astype(BF16)


def gather_terms(comb, slabs, norms, top, capacity):
    parts = SLAB // capacity
    requests = comb.shape[0]
    used = slabs.shape[0]
    norms[...] = as_row(comb[:, used : used + 1])
    top[...] = as_row(comb[:, used + 1 : used + 2])
    weights = comb[:, :used]
    pieces = []
    for _ in range(3):
        piece = weights.astype(BF16).astype(F32)
        weights = weights - piece
        pieces.append(piece)
    part = iota(weights.shape, 1) % parts
    stacked = jnp.concatenate(
        [jnp.where(part == p, piece, 0.0) for p in range(parts) for piece in pieces], axis=0
    ).astype(BF16)
    terms = dot(stacked, slabs[...])
    return jnp.concatenate(
        [
            sum(terms[(3 * p + i) * requests : (3 * p + i + 1) * requests] for i in range(3))
            for p in range(parts)
        ],
        axis=1,
    )


def combine_kernel(capacity, comb, slabs, mixed, out, norms, top):
    out[...] = (mixed[...].astype(F32) + gather_terms(comb, slabs, norms, top, capacity)).astype(BF16)


def gather_kernel(capacity, comb, slabs, out, norms, top):
    out[...] = gather_terms(comb, slabs, norms, top, capacity).astype(BF16)


def vmem(count):
    return [pl.BlockSpec(memory_space=pltpu.VMEM)] * count


def scalars(count):
    return [pl.BlockSpec(memory_space=pltpu.SMEM)] * count


def in_hbm(count):
    return [pl.BlockSpec(memory_space=pltpu.HBM)] * count


def pinned(*arrays):
    return [pltpu.with_memory_space_constraint(array, pltpu.HBM) for array in arrays]


def like(shape, dtype=BF16):
    return jax.ShapeDtypeStruct(shape, dtype)


def body(
    hidden,
    queries,
    fresh_key_value,
    kv_pool,
    page_table,
    lengths,
    out_weight,
    norm_gain,
    router_weight,
    expert_ids,
    expert_gate_up,
    expert_down,
):
    requests, width = hidden.shape
    req_count, kv_count = lax.axis_size("req"), lax.axis_size("kv")
    pages, page_len, heads_kv, pair_dim = kv_pool.shape
    head_dim = pair_dim // 2
    heads = queries.shape[1] // head_dim
    experts = router_weight.shape[0]
    copies = req_count // experts
    chosen = expert_ids.shape[1]
    capacity = 2 * max(1, (requests * chosen + 2 * experts - 1) // (2 * experts))
    parts = SLAB // capacity
    piece = width // parts
    slab_rows = experts * SLAB

    same_part = [
        [(place ^ group_turn(experts, part)) * copies + part for place in range(experts)] for part in range(copies)
    ]
    swap = [(index, index ^ 1) for index in range(req_count)]
    other_up = lax.ppermute(expert_gate_up, "req", swap)
    other_down = lax.ppermute(expert_down, "req", swap)

    attend_scratch = [
        pltpu.VMEM((pages, page_len, heads_kv, head_dim), BF16),
        pltpu.VMEM((pages, page_len, heads_kv, head_dim), BF16),
        pltpu.VMEM(out_weight.shape, BF16),
        pltpu.VMEM((heads * requests, head_dim), F32),
        pltpu.VMEM((heads * requests, head_dim), F32),
        pltpu.VMEM((requests, heads, page_table.shape[1] * page_len * heads_kv), BF16),
        pltpu.VMEM((requests, heads, head_dim), F32),
        pltpu.SemaphoreType.DMA((18,)),
    ]

    def small(*arrays):
        return [pltpu.VMEM(array.shape, array.dtype) for array in arrays]

    inputs = [pltpu.SMEM(page_table.shape, jnp.int32), pltpu.SMEM(lengths.shape, jnp.int32)]
    inputs += small(queries, fresh_key_value)
    routed_shapes = [like((requests, width)), like((slab_rows, piece)), like((requests, slab_rows + STATS), F32)]
    final_shapes = [like((requests, width)), like((1, requests), F32), like((1, requests), F32)]
    attend_params = pltpu.CompilerParams(vmem_limit_bytes=24 * MIB)
    if kv_count == 1:
        mixed, slabs, comb = pl.pallas_call(
            functools.partial(attend_route_kernel, capacity),
            out_shape=routed_shapes,
            in_specs=in_hbm(10),
            out_specs=vmem(3),
            scratch_shapes=inputs + small(hidden, norm_gain, router_weight, expert_ids) + attend_scratch,
            compiler_params=attend_params,
        )(*pinned(page_table, lengths, queries, fresh_key_value, hidden, norm_gain, router_weight, expert_ids,
                  kv_pool, out_weight))
    else:
        projected = pl.pallas_call(
            attend_kernel,
            out_shape=like((requests, width), F32),
            in_specs=in_hbm(6),
            out_specs=pl.BlockSpec(memory_space=pltpu.VMEM),
            scratch_shapes=inputs + attend_scratch,
            compiler_params=attend_params,
        )(*pinned(page_table, lengths, queries, fresh_key_value, kv_pool, out_weight))
        projected = lax.psum(projected, "kv")
        mixed, slabs, comb = pl.pallas_call(
            functools.partial(route_kernel, capacity),
            out_shape=routed_shapes,
            in_specs=vmem(5),
            out_specs=vmem(3),
        )(projected, hidden, norm_gain, router_weight, expert_ids)

    new_pool = pl.pallas_call(
        refresh_kernel,
        out_shape=like(kv_pool.shape),
        in_specs=scalars(2) + vmem(1) + in_hbm(2),
        out_specs=pl.BlockSpec(memory_space=pltpu.HBM),
        scratch_shapes=[pltpu.VMEM(kv_pool.shape, BF16), pltpu.SemaphoreType.DMA((8,))],
        compiler_params=pltpu.CompilerParams(vmem_limit_bytes=12 * MIB),
        cost_estimate=pl.CostEstimate(flops=0, bytes_accessed=8 * kv_pool.size, transcendentals=0),
    )(page_table, lengths, fresh_key_value, comb, *pinned(kv_pool))

    def exchange(array):
        array = array.reshape(experts, SLAB, piece)
        array = lax.all_to_all(
            array, "req", split_axis=0, concat_axis=0, tiled=True, axis_index_groups=same_part
        )
        return array.reshape(slab_rows, piece)

    arrived = exchange(slabs)
    kept = experts * capacity
    units = expert_down.shape[1]
    leaving = pl.pallas_call(
        functools.partial(expert_kernel, capacity),
        out_shape=like((slab_rows, piece)),
        in_specs=in_hbm(3) + vmem(2),
        out_specs=pl.BlockSpec(memory_space=pltpu.VMEM),
        scratch_shapes=[
            pltpu.VMEM((slab_rows, piece), BF16),
            pltpu.VMEM((2, units, width), BF16),
            pltpu.VMEM((units, width), BF16),
            pltpu.VMEM((kept, width), BF16),
            pltpu.VMEM((kept, width), F32),
            pltpu.SemaphoreType.DMA((1 + 2 * len(unit_chunks(units)),)),
        ],
        compiler_params=pltpu.CompilerParams(vmem_limit_bytes=20 * MIB),
    )(arrived, *pinned(expert_gate_up, expert_down), other_up, other_down)
    returned = exchange(leaving)
    if kv_count == 1:
        out_hidden, norms, top = pl.pallas_call(
            functools.partial(combine_kernel, capacity),
            out_shape=final_shapes,
            in_specs=vmem(3),
            out_specs=vmem(3),
            compiler_params=pltpu.CompilerParams(vmem_limit_bytes=8 * MIB),
        )(comb, returned, mixed)
    else:
        routed, norms, top = pl.pallas_call(
            functools.partial(gather_kernel, capacity),
            out_shape=final_shapes,
            in_specs=vmem(2),
            out_specs=vmem(3),
        )(comb, returned)
        routed = lax.psum(routed, "kv").astype(F32)
        out_hidden = (mixed.astype(F32) + routed).astype(BF16)
    return out_hidden, new_pool, norms.reshape(requests), top.reshape(requests)


def solution(mesh):
    in_specs = (
        P("req", None),
        P("req", "kv"),
        P("req", "kv", None),
        P("req", None, "kv", None),
        P("req", None),
        P("req"),
        P("kv", None),
        P(),
        P(),
        P("req", None),
        P("req", None, "kv", None),
        P("req", "kv", None),
    )
    out_specs = (P("req", None), P("req", None, "kv", None), P("req"), P("req"))
    return jax.shard_map(body, mesh=mesh, in_specs=in_specs, out_specs=out_specs, check_vma=False)
```

```python
import functools
import math

import jax
import jax.numpy as jnp
from jax import lax
from jax.experimental import pallas as pl
from jax.experimental.pallas import tpu as pltpu
from jax.sharding import PartitionSpec as P

BF16 = jnp.bfloat16
F32 = jnp.float32
NT = (((1,), (1,)), ((), ()))
NN = (((1,), (0,)), ((), ()))
STATS = 128
SLAB = 16
MIB = 1 << 20


def dot(a, b, dims=NN, precision=None):
    return lax.dot_general(a, b, dims, precision=precision, preferred_element_type=F32)


def iota(shape, dim):
    return lax.broadcasted_iota(jnp.int32, shape, dim)


def copies(pairs, sems, first=0):
    return [pltpu.make_async_copy(src, dst, sems.at[first + i]) for i, (src, dst) in enumerate(pairs)]


def group_turn(chips, part):
    return chips * 9 // 16 if part % 2 else chips * 3 // 8


def pool_half(array, i):
    head_dim = array.shape[3] // 2
    return array.at[:, :, :, pl.ds(i * head_dim, head_dim)]


def attend(refs, keys, values, scratch, prepare):
    small, (kept_weight, qs, att, probs, sums, sems) = scratch
    table, lengths, q_ref, fresh = small[:4]
    requests, max_pages = table.shape
    pages, page_len, heads_kv, head_dim = keys.shape
    heads = q_ref.shape[1] // head_dim
    group = heads // heads_kv
    page_rows = page_len * heads_kv
    pool, weight = refs[-2:]
    loads = copies(list(zip(refs[:4], small[:4])), sems)
    page_step = -(-pages // 4)
    page_spans = [pl.ds(first, min(page_step, pages - first)) for first in range(0, pages, page_step)]
    key_loads, value_loads = [
        copies(
            [(pool_half(pool, i).at[span], kept.at[span]) for span in page_spans], sems, 4 + i * len(page_spans)
        )
        for i, kept in enumerate((keys, values))
    ]
    step = weight.shape[0] // 2
    spans = [pl.ds(i * step, step) for i in range(2)]
    weight_loads = copies([(weight.at[span], kept_weight.at[span]) for span in spans], sems, 12)
    later = copies(list(zip(refs[4:-2], small[4:])), sems, 14)
    for copy in loads + later + key_loads + value_loads + weight_loads:
        copy.start()
    for copy in loads:
        copy.wait()
    for h in range(heads):
        qs[pl.ds(h * requests, requests), :] = q_ref[:, pl.ds(h * head_dim, head_dim)].astype(F32)
    spots = [(table[r, lengths[r] // page_len], lengths[r] % page_len) for r in range(requests)]

    for copy in later:
        copy.wait()
    prepared = prepare()
    for copy in key_loads:
        copy.wait()
    for r, (page, slot) in enumerate(spots):
        keys[page, slot] = fresh[r][:, :head_dim]
    key_pages = keys.reshape(pages, page_rows, head_dim)
    value_pages = values.reshape(pages, page_rows, head_dim)
    columns = max_pages * page_rows
    lane = iota((heads, columns), 1)
    own_head = (lane & (heads_kv - 1)) == iota((heads, columns), 0) // group
    position = jnp.where(own_head, lane >> (heads_kv.bit_length() - 1), columns)
    scale = math.log2(math.e) / math.sqrt(head_dim)
    for r in range(requests):
        query = qs[pl.ds(r, heads, stride=requests), :].astype(BF16)
        gathered = jnp.concatenate([key_pages[table[r, j]] for j in range(max_pages)], axis=0)
        scores = jnp.where(position <= lengths[r], dot(query, gathered, NT), -1e30)
        exponent = jnp.exp2((scores - jnp.max(scores, axis=1, keepdims=True)) * scale)
        sums[r] = jnp.broadcast_to(jnp.sum(exponent, axis=1, keepdims=True), (heads, head_dim))
        probs[r] = exponent.astype(BF16)

    for copy in value_loads:
        copy.wait()
    for r, (page, slot) in enumerate(spots):
        values[page, slot] = fresh[r][:, head_dim:]
    for r in range(requests):
        gathered = jnp.concatenate([value_pages[table[r, j]] for j in range(max_pages)], axis=0)
        att[pl.ds(r, heads, stride=requests), :] = dot(probs[r], gathered) / sums[r]
    attended = jnp.concatenate(
        [att[pl.ds(h * requests, requests), :] for h in range(heads)], axis=1
    ).astype(BF16)
    projected = 0.0
    for i, copy in enumerate(weight_loads):
        copy.wait()
        projected = projected + dot(attended[:, i * step : (i + 1) * step], kept_weight[spans[i], :])
    return projected, prepared


def as_row(column):
    shape = (column.shape[0],) * 2
    return jnp.sum(jnp.where(iota(shape, 0) == iota(shape, 1), column, 0.0), axis=0, keepdims=True)


def split(values):
    pieces = []
    for _ in range(3):
        pieces.append(values.astype(BF16).astype(F32))
        values = values - pieces[-1]
    return pieces


def plan(ids, requests, experts, slab_rows, capacity):
    parts = SLAB // capacity
    turns = jnp.where(lax.axis_index("req") % 2 == 0, group_turn(experts, 0), group_turn(experts, 1))

    def slab_expert(shape, dim):
        return (iota(shape, dim) // SLAB) ^ turns

    column = iota((requests, experts), 1)
    named = column < 0
    for k in range(ids.shape[1]):
        named = named | (ids[:, k : k + 1] == column)
    named = named.astype(F32)
    earlier = (iota((requests, requests), 1) < iota((requests, requests), 0)).astype(F32)
    rank = dot(earlier, named)
    place = jnp.where(named > 0.0, rank, -1.0)
    places = jnp.concatenate([place] * parts, axis=0)
    shape = (slab_rows, parts * requests)
    inner = iota(shape, 0) % SLAB
    spread = (slab_expert((slab_rows, experts), 0) == iota((slab_rows, experts), 1)).astype(F32)
    picks = (dot(spread, places, NT) == (inner // parts).astype(F32)) & (
        inner % parts == iota(shape, 1) // requests
    )
    shape = (experts, slab_rows)
    spread = (slab_expert(shape, 1) == iota(shape, 0)).astype(F32)
    inner = iota((requests, slab_rows), 1) % SLAB
    holds = (dot(place, spread) == (inner // parts).astype(F32)).astype(F32)
    return named, picks.astype(BF16), spread.astype(BF16), holds


def route(projected, planned, hidden, gain, router, mixed_ref, slabs_ref, comb_ref, capacity):
    named, picks, spread, holds = planned
    requests, width = hidden.shape
    parts = SLAB // capacity
    piece = width // parts
    slab_rows = slabs_ref.shape[0]
    mixed = (hidden[...].astype(F32) + projected).astype(BF16)
    mixed_ref[...] = mixed
    mixed = mixed.astype(F32)
    norms = jnp.sqrt(jnp.mean(mixed * mixed, axis=1, keepdims=True) + 1e-06)
    normed = (mixed / norms * gain[...].astype(F32).reshape(1, width)).astype(BF16)
    wide = normed.astype(F32)
    stacked = jnp.concatenate([wide[:, p * piece : (p + 1) * piece] for p in range(parts)], axis=0)
    slabs_ref[...] = dot(picks, stacked.astype(BF16)).astype(BF16)
    logits = dot(normed, router[...], NT)
    top = jnp.max(logits, axis=1, keepdims=True)
    weights = jnp.where(named > 0.0, jnp.exp(logits), 0.0)
    weights = weights / jnp.sum(weights, axis=1, keepdims=True)
    spread_weights = dot(jnp.concatenate(split(weights), axis=0).astype(BF16), spread)
    spread_weights = sum(spread_weights[i * requests : (i + 1) * requests] for i in range(3))
    field = iota((requests, STATS), 1)
    comb_ref[:, slab_rows:] = jnp.where(field == 0, norms, jnp.where(field == 1, top, 0.0))
    comb_ref[:, :slab_rows] = jnp.where(holds > 0.0, spread_weights, 0.0)


def attend_route_kernel(capacity, *refs):
    inputs, (mixed, slabs, comb) = refs[:10], refs[10:13]
    small, scratch = refs[13:21], refs[21:]
    hidden, gain, router, ids = small[4:]

    def prepare():
        return plan(ids, ids.shape[0], router.shape[0], slabs.shape[0], capacity)

    projected, planned = attend(inputs, scratch[0], scratch[1], (small, scratch[2:]), prepare)
    route(projected, planned, hidden, gain, router, mixed, slabs, comb, capacity)


def attend_kernel(*refs):
    projected, scratch = refs[6], refs[11:]
    projected[...] = attend(refs[:6], scratch[0], scratch[1], (refs[7:11], scratch[2:]), lambda: None)[0]


def refresh_kernel(table, lengths, fresh, after, pool, new_pool, kept, sems):
    pages, page_len = kept.shape[:2]
    step = -(-pages // 4)
    spans = [pl.ds(start, min(step, pages - start)) for start in range(0, pages, step)]
    loads = copies([(pool.at[span], kept.at[span]) for span in spans], sems)
    stores = copies([(kept.at[span], new_pool.at[span]) for span in spans], sems, len(spans))
    for copy in loads:
        copy.start()
    spots = [(table[r, lengths[r] // page_len], lengths[r] % page_len) for r in range(table.shape[0])]
    for i, (load, store) in enumerate(zip(loads, stores)):
        load.wait()
        for r, (page, slot) in enumerate(spots):

            @pl.when((page >= i * step) & (page < (i + 1) * step))
            def _():
                kept[page, slot] = fresh[r]

        store.start()
    for copy in stores:
        copy.wait()


def route_kernel(capacity, projected, hidden, gain, router, ids, mixed, slabs, comb):
    planned = plan(ids, ids.shape[0], router.shape[0], slabs.shape[0], capacity)
    route(projected[...], planned, hidden, gain, router, mixed, slabs, comb, capacity)


def unit_chunks(units):
    whole = units // 256 * 256
    return [(start, size) for start, size in ((0, whole), (whole, units - whole)) if size]


def expert_kernel(capacity, arrived, own_up, own_down, other_up, other_down, slabs,
                  slab_rows, kept_up, kept_down, rows, total, sems):
    units = kept_down.shape[0]
    arrive = pltpu.make_async_copy(arrived, slab_rows, sems.at[0])
    arrive.start()
    chunks = []
    for i, (start, size) in enumerate(unit_chunks(units)):
        span = pl.ds(start, size)
        chunks.append((span, copies(
            [(own_up.at[0, :, span, :], kept_up.at[:, span, :]), (own_down.at[0, span, :], kept_down.at[span, :])],
            sems,
            1 + 2 * i,
        )))
    for _, loads in chunks:
        loads[0].start()
    arrive.wait()
    parts = SLAB // capacity
    piece = slabs.shape[1]
    block = 128
    each = block // parts
    blocks = slabs.shape[0] // block
    shape = (block, block)
    slab_row, sorted_row = iota(shape, 1), iota(shape, 0)
    sort = (slab_row == sorted_row % each * parts + sorted_row // each).astype(BF16)
    for i in range(blocks):
        sorted_rows = dot(sort, slab_rows[pl.ds(i * block, block), :]).astype(BF16)
        rows[pl.ds(i * each, each), :] = jnp.concatenate(
            [sorted_rows[p * each : (p + 1) * each] for p in range(parts)], axis=1
        )
    states = rows[...]
    steps = [(other_up.at[0], other_down.at[0], span, []) for span, _ in chunks]
    steps += [(kept_up, kept_down, span, loads) for span, loads in chunks]

    def add_down(i, activated):
        _, down, span, loads = steps[i]
        if loads:
            loads[1].wait()
        term = dot(activated, down[span, :])
        total[...] = term if i == 0 else total[...] + term

    activated = None
    for i, (gate_up, _, span, loads) in enumerate(steps):
        if loads:
            loads[0].wait()
        gate = dot(states, gate_up[0, span, :], NT)
        up = dot(states, gate_up[1, span, :], NT)
        if i == 0:
            for _, loads in chunks:
                loads[1].start()
        else:
            add_down(i - 1, activated)
        activated = (gate / (1.0 + jnp.exp(-gate)) * up).astype(BF16)
    add_down(len(steps) - 1, activated)
    slab_row, sorted_row = iota(shape, 0), iota(shape, 1)
    unsort = (slab_row == sorted_row % each * parts + sorted_row // each).astype(BF16)
    for i in range(blocks):
        summed = total[pl.ds(i * each, each), :].astype(BF16)
        stacked = jnp.concatenate([summed[:, p * piece : (p + 1) * piece] for p in range(parts)], axis=0)
        slabs[pl.ds(i * block, block), :] = dot(unsort, stacked).astype(BF16)


def gather_terms(comb, slabs, norms, top, capacity):
    parts = SLAB // capacity
    requests = comb.shape[0]
    used = slabs.shape[0]
    norms[...] = as_row(comb[:, used : used + 1])
    top[...] = as_row(comb[:, used + 1 : used + 2])
    weights = comb[:, :used]
    pieces = []
    for _ in range(3):
        piece = weights.astype(BF16).astype(F32)
        weights = weights - piece
        pieces.append(piece)
    part = iota(weights.shape, 1) % parts
    stacked = jnp.concatenate(
        [jnp.where(part == p, piece, 0.0) for p in range(parts) for piece in pieces], axis=0
    ).astype(BF16)
    terms = dot(stacked, slabs[...])
    return jnp.concatenate(
        [
            sum(terms[(3 * p + i) * requests : (3 * p + i + 1) * requests] for i in range(3))
            for p in range(parts)
        ],
        axis=1,
    )


def combine_kernel(capacity, comb, slabs, mixed, out, norms, top):
    out[...] = (mixed[...].astype(F32) + gather_terms(comb, slabs, norms, top, capacity)).astype(BF16)


def gather_kernel(capacity, comb, slabs, out, norms, top):
    out[...] = gather_terms(comb, slabs, norms, top, capacity).astype(BF16)


def vmem(count):
    return [pl.BlockSpec(memory_space=pltpu.VMEM)] * count


def scalars(count):
    return [pl.BlockSpec(memory_space=pltpu.SMEM)] * count


def in_hbm(count):
    return [pl.BlockSpec(memory_space=pltpu.HBM)] * count


def pinned(*arrays):
    return [pltpu.with_memory_space_constraint(array, pltpu.HBM) for array in arrays]


def like(shape, dtype=BF16):
    return jax.ShapeDtypeStruct(shape, dtype)


def body(
    hidden,
    queries,
    fresh_key_value,
    kv_pool,
    page_table,
    lengths,
    out_weight,
    norm_gain,
    router_weight,
    expert_ids,
    expert_gate_up,
    expert_down,
):
    requests, width = hidden.shape
    req_count, kv_count = lax.axis_size("req"), lax.axis_size("kv")
    pages, page_len, heads_kv, pair_dim = kv_pool.shape
    head_dim = pair_dim // 2
    heads = queries.shape[1] // head_dim
    experts = router_weight.shape[0]
    copies = req_count // experts
    chosen = expert_ids.shape[1]
    capacity = 2 * max(1, (requests * chosen + 2 * experts - 1) // (2 * experts))
    parts = SLAB // capacity
    piece = width // parts
    slab_rows = experts * SLAB

    same_part = [
        [(place ^ group_turn(experts, part)) * copies + part for place in range(experts)] for part in range(copies)
    ]
    swap = [(index, index ^ 1) for index in range(req_count)]
    other_up = lax.ppermute(expert_gate_up, "req", swap)
    other_down = lax.ppermute(expert_down, "req", swap)

    attend_scratch = [
        pltpu.VMEM((pages, page_len, heads_kv, head_dim), BF16),
        pltpu.VMEM((pages, page_len, heads_kv, head_dim), BF16),
        pltpu.VMEM(out_weight.shape, BF16),
        pltpu.VMEM((heads * requests, head_dim), F32),
        pltpu.VMEM((heads * requests, head_dim), F32),
        pltpu.VMEM((requests, heads, page_table.shape[1] * page_len * heads_kv), BF16),
        pltpu.VMEM((requests, heads, head_dim), F32),
        pltpu.SemaphoreType.DMA((18,)),
    ]

    def small(*arrays):
        return [pltpu.VMEM(array.shape, array.dtype) for array in arrays]

    inputs = [pltpu.SMEM(page_table.shape, jnp.int32), pltpu.SMEM(lengths.shape, jnp.int32)]
    inputs += small(queries, fresh_key_value)
    routed_shapes = [like((requests, width)), like((slab_rows, piece)), like((requests, slab_rows + STATS), F32)]
    final_shapes = [like((requests, width)), like((1, requests), F32), like((1, requests), F32)]
    attend_params = pltpu.CompilerParams(vmem_limit_bytes=24 * MIB)
    if kv_count == 1:
        mixed, slabs, comb = pl.pallas_call(
            functools.partial(attend_route_kernel, capacity),
            out_shape=routed_shapes,
            in_specs=in_hbm(10),
            out_specs=vmem(3),
            scratch_shapes=inputs + small(hidden, norm_gain, router_weight, expert_ids) + attend_scratch,
            compiler_params=attend_params,
        )(*pinned(page_table, lengths, queries, fresh_key_value, hidden, norm_gain, router_weight, expert_ids,
                  kv_pool, out_weight))
    else:
        projected = pl.pallas_call(
            attend_kernel,
            out_shape=like((requests, width), F32),
            in_specs=in_hbm(6),
            out_specs=pl.BlockSpec(memory_space=pltpu.VMEM),
            scratch_shapes=inputs + attend_scratch,
            compiler_params=attend_params,
        )(*pinned(page_table, lengths, queries, fresh_key_value, kv_pool, out_weight))
        projected = lax.psum(projected, "kv")
        mixed, slabs, comb = pl.pallas_call(
            functools.partial(route_kernel, capacity),
            out_shape=routed_shapes,
            in_specs=vmem(5),
            out_specs=vmem(3),
        )(projected, hidden, norm_gain, router_weight, expert_ids)

    new_pool = pl.pallas_call(
        refresh_kernel,
        out_shape=like(kv_pool.shape),
        in_specs=scalars(2) + vmem(1) + in_hbm(2),
        out_specs=pl.BlockSpec(memory_space=pltpu.HBM),
        scratch_shapes=[pltpu.VMEM(kv_pool.shape, BF16), pltpu.SemaphoreType.DMA((8,))],
        compiler_params=pltpu.CompilerParams(vmem_limit_bytes=12 * MIB),
        cost_estimate=pl.CostEstimate(flops=0, bytes_accessed=8 * kv_pool.size, transcendentals=0),
    )(page_table, lengths, fresh_key_value, comb, *pinned(kv_pool))

    def exchange(array):
        array = array.reshape(experts, SLAB, piece)
        array = lax.all_to_all(
            array, "req", split_axis=0, concat_axis=0, tiled=True, axis_index_groups=same_part
        )
        return array.reshape(slab_rows, piece)

    arrived = exchange(slabs)
    kept = experts * capacity
    units = expert_down.shape[1]
    leaving = pl.pallas_call(
        functools.partial(expert_kernel, capacity),
        out_shape=like((slab_rows, piece)),
        in_specs=in_hbm(3) + vmem(2),
        out_specs=pl.BlockSpec(memory_space=pltpu.VMEM),
        scratch_shapes=[
            pltpu.VMEM((slab_rows, piece), BF16),
            pltpu.VMEM((2, units, width), BF16),
            pltpu.VMEM((units, width), BF16),
            pltpu.VMEM((kept, width), BF16),
            pltpu.VMEM((kept, width), F32),
            pltpu.SemaphoreType.DMA((1 + 2 * len(unit_chunks(units)),)),
        ],
        compiler_params=pltpu.CompilerParams(vmem_limit_bytes=20 * MIB),
    )(arrived, *pinned(expert_gate_up, expert_down), other_up, other_down)
    returned = exchange(leaving)
    if kv_count == 1:
        out_hidden, norms, top = pl.pallas_call(
            functools.partial(combine_kernel, capacity),
            out_shape=final_shapes,
            in_specs=vmem(3),
            out_specs=vmem(3),
            compiler_params=pltpu.CompilerParams(vmem_limit_bytes=8 * MIB),
        )(comb, returned, mixed)
    else:
        routed, norms, top = pl.pallas_call(
            functools.partial(gather_kernel, capacity),
            out_shape=final_shapes,
            in_specs=vmem(2),
            out_specs=vmem(3),
        )(comb, returned)
        routed = lax.psum(routed, "kv").astype(F32)
        out_hidden = (mixed.astype(F32) + routed).astype(BF16)
    return out_hidden, new_pool, norms.reshape(requests), top.reshape(requests)


def solution(mesh):
    in_specs = (
        P("req", None),
        P("req", "kv"),
        P("req", "kv", None),
        P("req", None, "kv", None),
        P("req", None),
        P("req"),
        P("kv", None),
        P(),
        P(),
        P("req", None),
        P("req", None, "kv", None),
        P("req", "kv", None),
    )
    out_specs = (P("req", None), P("req", None, "kv", None), P("req"), P("req"))
    return jax.shard_map(body, mesh=mesh, in_specs=in_specs, out_specs=out_specs, check_vma=False)
```

```python
import functools
import math

import jax
import jax.numpy as jnp
from jax import lax
from jax.experimental import pallas as pl
from jax.experimental.pallas import tpu as pltpu
from jax.sharding import PartitionSpec as P

BF16 = jnp.bfloat16
F32 = jnp.float32
NT = (((1,), (1,)), ((), ()))
NN = (((1,), (0,)), ((), ()))
STATS = 128
SLAB = 16
MIB = 1 << 20


def dot(a, b, dims=NN, precision=None):
    return lax.dot_general(a, b, dims, precision=precision, preferred_element_type=F32)


def iota(shape, dim):
    return lax.broadcasted_iota(jnp.int32, shape, dim)


def copies(pairs, sems, first=0):
    return [pltpu.make_async_copy(src, dst, sems.at[first + i]) for i, (src, dst) in enumerate(pairs)]


def chip_at(position, chips, part):
    return position ^ (chips * 9 // 16) if part % 2 else (position + chips * 5 // 16) % chips


def pool_half(array, i):
    head_dim = array.shape[3] // 2
    return array.at[:, :, :, pl.ds(i * head_dim, head_dim)]


def attend(refs, keys, values, scratch):
    small, (kept_weight, qs, att, probs, sums, sems) = scratch
    table, lengths, q_ref, fresh = small[:4]
    requests, max_pages = table.shape
    pages, page_len, heads_kv, head_dim = keys.shape
    heads = q_ref.shape[1] // head_dim
    group = heads // heads_kv
    page_rows = page_len * heads_kv
    pool, weight = refs[-2:]
    loads = copies(list(zip(refs[:4], small[:4])), sems)
    page_step = -(-pages // 4)
    page_spans = [pl.ds(first, min(page_step, pages - first)) for first in range(0, pages, page_step)]
    key_loads, value_loads = [
        copies(
            [(pool_half(pool, i).at[span], kept.at[span]) for span in page_spans], sems, 4 + i * len(page_spans)
        )
        for i, kept in enumerate((keys, values))
    ]
    step = weight.shape[0] // 2
    spans = [pl.ds(i * step, step) for i in range(2)]
    weight_loads = copies([(weight.at[span], kept_weight.at[span]) for span in spans], sems, 12)
    later = copies(list(zip(refs[4:-2], small[4:])), sems, 14)
    for copy in loads + key_loads + value_loads + weight_loads + later:
        copy.start()
    for copy in loads:
        copy.wait()
    for h in range(heads):
        qs[pl.ds(h * requests, requests), :] = q_ref[:, pl.ds(h * head_dim, head_dim)].astype(F32)
    spots = [(table[r, lengths[r] // page_len], lengths[r] % page_len) for r in range(requests)]

    for copy in key_loads:
        copy.wait()
    for r, (page, slot) in enumerate(spots):
        keys[page, slot] = fresh[r][:, :head_dim]
    key_pages = keys.reshape(pages, page_rows, head_dim)
    value_pages = values.reshape(pages, page_rows, head_dim)
    columns = max_pages * page_rows
    lane = iota((heads, columns), 1)
    own_head = (lane & (heads_kv - 1)) == iota((heads, columns), 0) // group
    position = jnp.where(own_head, lane >> (heads_kv.bit_length() - 1), columns)
    scale = math.log2(math.e) / math.sqrt(head_dim)
    for r in range(requests):
        query = qs[pl.ds(r, heads, stride=requests), :].astype(BF16)
        gathered = jnp.concatenate([key_pages[table[r, j]] for j in range(max_pages)], axis=0)
        scores = jnp.where(position <= lengths[r], dot(query, gathered, NT), -1e30)
        exponent = jnp.exp2((scores - jnp.max(scores, axis=1, keepdims=True)) * scale)
        sums[r] = jnp.broadcast_to(jnp.sum(exponent, axis=1, keepdims=True), (heads, head_dim))
        probs[r] = exponent.astype(BF16)

    for copy in value_loads:
        copy.wait()
    for r, (page, slot) in enumerate(spots):
        values[page, slot] = fresh[r][:, head_dim:]
    for r in range(requests):
        gathered = jnp.concatenate([value_pages[table[r, j]] for j in range(max_pages)], axis=0)
        att[pl.ds(r, heads, stride=requests), :] = dot(probs[r], gathered) / sums[r]
    attended = jnp.concatenate(
        [att[pl.ds(h * requests, requests), :] for h in range(heads)], axis=1
    ).astype(BF16)
    projected = 0.0
    for i, copy in enumerate(weight_loads):
        copy.wait()
        projected = projected + dot(attended[:, i * step : (i + 1) * step], kept_weight[spans[i], :])
    for copy in later:
        copy.wait()
    return projected


def as_row(column):
    shape = (column.shape[0],) * 2
    return jnp.sum(jnp.where(iota(shape, 0) == iota(shape, 1), column, 0.0), axis=0, keepdims=True)


def route(projected, hidden, gain, router, ids, mixed_ref, slabs_ref, comb_ref, capacity):
    requests, width = hidden.shape
    experts = router.shape[0]
    parts = SLAB // capacity
    piece = width // parts
    slab_rows = experts * SLAB
    even = lax.axis_index("req") % 2 == 0

    def slab_expert(shape, dim):
        slab = iota(shape, dim) // SLAB
        return jnp.where(even, chip_at(slab, experts, 0), chip_at(slab, experts, 1))

    mixed = (hidden[...].astype(F32) + projected).astype(BF16)
    mixed_ref[...] = mixed
    mixed = mixed.astype(F32)
    norms = jnp.sqrt(jnp.mean(mixed * mixed, axis=1, keepdims=True) + 1e-06)
    normed = (mixed / norms * gain[...].astype(F32).reshape(1, width)).astype(BF16)
    logits = dot(normed, router[...], NT)
    top = jnp.max(logits, axis=1, keepdims=True)
    column = iota((requests, experts), 1)
    named = column < 0
    for k in range(ids.shape[1]):
        named = named | (ids[:, k : k + 1] == column)
    weights = jnp.where(named, jnp.exp(logits), 0.0)
    weights = weights / jnp.sum(weights, axis=1, keepdims=True)
    earlier = (iota((requests, requests), 1) < iota((requests, requests), 0)).astype(F32)
    rank = dot(earlier, named.astype(F32))
    place = jnp.where(named, rank, -1.0)
    normed = normed.astype(F32)
    stacked = jnp.concatenate([normed[:, p * piece : (p + 1) * piece] for p in range(parts)], axis=0)
    places = jnp.concatenate([place] * parts, axis=0)
    shape = (slab_rows, parts * requests)
    inner = iota(shape, 0) % SLAB
    spread = (slab_expert((slab_rows, experts), 0) == iota((slab_rows, experts), 1)).astype(F32)
    picks = (dot(spread, places, NT) == (inner // parts).astype(F32)) & (
        inner % parts == iota(shape, 1) // requests
    )
    slabs_ref[...] = dot(picks.astype(BF16), stacked.astype(BF16)).astype(BF16)
    shape = (experts, slab_rows)
    spread = (slab_expert(shape, 1) == iota(shape, 0)).astype(F32)
    inner = iota((requests, slab_rows), 1) % SLAB
    field = iota((requests, STATS), 1)
    comb_ref[:, slab_rows:] = jnp.where(field == 0, norms, jnp.where(field == 1, top, 0.0))
    comb_ref[:, :slab_rows] = jnp.where(
        dot(place, spread) == (inner // parts).astype(F32),
        dot(weights, spread, precision=lax.Precision.HIGHEST),
        0.0,
    )


def attend_route_kernel(capacity, *refs):
    inputs, (mixed, slabs, comb) = refs[:10], refs[10:13]
    small, scratch = refs[13:21], refs[21:]
    projected = attend(inputs, scratch[0], scratch[1], (small, scratch[2:]))
    hidden, gain, router, ids = small[4:]
    route(projected, hidden, gain, router, ids, mixed, slabs, comb, capacity)


def attend_kernel(*refs):
    attended, scratch = refs[6], refs[11:]
    attended[...] = attend(refs[:6], scratch[0], scratch[1], (refs[7:11], scratch[2:]))


def refresh_kernel(table, lengths, fresh, after, pool, new_pool, kept, sems):
    pages, page_len = kept.shape[:2]
    step = -(-pages // 4)
    spans = [pl.ds(start, min(step, pages - start)) for start in range(0, pages, step)]
    loads = copies([(pool.at[span], kept.at[span]) for span in spans], sems)
    stores = copies([(kept.at[span], new_pool.at[span]) for span in spans], sems, len(spans))
    for copy in loads:
        copy.start()
    spots = [(table[r, lengths[r] // page_len], lengths[r] % page_len) for r in range(table.shape[0])]
    for i, (load, store) in enumerate(zip(loads, stores)):
        load.wait()
        for r, (page, slot) in enumerate(spots):

            @pl.when((page >= i * step) & (page < (i + 1) * step))
            def _():
                kept[page, slot] = fresh[r]

        store.start()
    for copy in stores:
        copy.wait()


def route_kernel(capacity, projected, hidden, gain, router, ids, mixed, slabs, comb):
    route(projected[...], hidden, gain, router, ids, mixed, slabs, comb, capacity)


def unit_chunks(units):
    whole = units // 256 * 256
    return [(start, size) for start, size in ((0, whole), (whole, units - whole)) if size]


def expert_kernel(capacity, arrived, own_up, own_down, other_up, other_down, slabs,
                  slab_rows, kept_up, kept_down, rows, total, sems):
    units = kept_down.shape[0]
    arrive = pltpu.make_async_copy(arrived, slab_rows, sems.at[0])
    arrive.start()
    chunks = []
    for i, (start, size) in enumerate(unit_chunks(units)):
        span = pl.ds(start, size)
        chunks.append((span, copies(
            [(own_up.at[0, :, span, :], kept_up.at[:, span, :]), (own_down.at[0, span, :], kept_down.at[span, :])],
            sems,
            1 + 2 * i,
        )))
    for _, loads in chunks:
        loads[0].start()
    arrive.wait()
    parts = SLAB // capacity
    piece = slabs.shape[1]
    block = 128
    each = block // parts
    blocks = slabs.shape[0] // block
    shape = (block, block)
    slab_row, sorted_row = iota(shape, 1), iota(shape, 0)
    sort = (slab_row == sorted_row % each * parts + sorted_row // each).astype(BF16)
    for i in range(blocks):
        sorted_rows = dot(sort, slab_rows[pl.ds(i * block, block), :]).astype(BF16)
        rows[pl.ds(i * each, each), :] = jnp.concatenate(
            [sorted_rows[p * each : (p + 1) * each] for p in range(parts)], axis=1
        )
    states = rows[...]
    steps = [(other_up.at[0], other_down.at[0], span, []) for span, _ in chunks]
    steps += [(kept_up, kept_down, span, loads) for span, loads in chunks]

    def add_down(i, activated):
        _, down, span, loads = steps[i]
        if loads:
            loads[1].wait()
        term = dot(activated, down[span, :])
        total[...] = term if i == 0 else total[...] + term

    activated = None
    for i, (gate_up, _, span, loads) in enumerate(steps):
        if loads:
            loads[0].wait()
        gate = dot(states, gate_up[0, span, :], NT)
        up = dot(states, gate_up[1, span, :], NT)
        if i == 0:
            for _, loads in chunks:
                loads[1].start()
        else:
            add_down(i - 1, activated)
        activated = (gate / (1.0 + jnp.exp(-gate)) * up).astype(BF16)
    add_down(len(steps) - 1, activated)
    slab_row, sorted_row = iota(shape, 0), iota(shape, 1)
    unsort = (slab_row == sorted_row % each * parts + sorted_row // each).astype(BF16)
    for i in range(blocks):
        summed = total[pl.ds(i * each, each), :].astype(BF16)
        stacked = jnp.concatenate([summed[:, p * piece : (p + 1) * piece] for p in range(parts)], axis=0)
        slabs[pl.ds(i * block, block), :] = dot(unsort, stacked).astype(BF16)


def gather_terms(comb, slabs, norms, top, capacity):
    parts = SLAB // capacity
    requests = comb.shape[0]
    used = slabs.shape[0]
    norms[...] = as_row(comb[:, used : used + 1])
    top[...] = as_row(comb[:, used + 1 : used + 2])
    weights = comb[:, :used]
    pieces = []
    for _ in range(3):
        piece = weights.astype(BF16).astype(F32)
        weights = weights - piece
        pieces.append(piece)
    part = iota(weights.shape, 1) % parts
    stacked = jnp.concatenate(
        [jnp.where(part == p, piece, 0.0) for p in range(parts) for piece in pieces], axis=0
    ).astype(BF16)
    terms = dot(stacked, slabs[...])
    return jnp.concatenate(
        [
            sum(terms[(3 * p + i) * requests : (3 * p + i + 1) * requests] for i in range(3))
            for p in range(parts)
        ],
        axis=1,
    )


def combine_kernel(capacity, comb, slabs, mixed, out, norms, top):
    out[...] = (mixed[...].astype(F32) + gather_terms(comb, slabs, norms, top, capacity)).astype(BF16)


def gather_kernel(capacity, comb, slabs, out, norms, top):
    out[...] = gather_terms(comb, slabs, norms, top, capacity).astype(BF16)


def vmem(count):
    return [pl.BlockSpec(memory_space=pltpu.VMEM)] * count


def scalars(count):
    return [pl.BlockSpec(memory_space=pltpu.SMEM)] * count


def in_hbm(count):
    return [pl.BlockSpec(memory_space=pltpu.HBM)] * count


def pinned(*arrays):
    return [pltpu.with_memory_space_constraint(array, pltpu.HBM) for array in arrays]


def like(shape, dtype=BF16):
    return jax.ShapeDtypeStruct(shape, dtype)


def body(
    hidden,
    queries,
    fresh_key_value,
    kv_pool,
    page_table,
    lengths,
    out_weight,
    norm_gain,
    router_weight,
    expert_ids,
    expert_gate_up,
    expert_down,
):
    requests, width = hidden.shape
    req_count, kv_count = lax.axis_size("req"), lax.axis_size("kv")
    pages, page_len, heads_kv, pair_dim = kv_pool.shape
    head_dim = pair_dim // 2
    heads = queries.shape[1] // head_dim
    experts = router_weight.shape[0]
    copies = req_count // experts
    chosen = expert_ids.shape[1]
    capacity = 2 * max(1, (requests * chosen + 2 * experts - 1) // (2 * experts))
    parts = SLAB // capacity
    piece = width // parts
    slab_rows = experts * SLAB

    same_part = [
        [chip_at(place, experts, part) * copies + part for place in range(experts)] for part in range(copies)
    ]
    swap = [(index, index ^ 1) for index in range(req_count)]
    other_up = lax.ppermute(expert_gate_up, "req", swap)
    other_down = lax.ppermute(expert_down, "req", swap)

    attend_scratch = [
        pltpu.VMEM((pages, page_len, heads_kv, head_dim), BF16),
        pltpu.VMEM((pages, page_len, heads_kv, head_dim), BF16),
        pltpu.VMEM(out_weight.shape, BF16),
        pltpu.VMEM((heads * requests, head_dim), F32),
        pltpu.VMEM((heads * requests, head_dim), F32),
        pltpu.VMEM((requests, heads, page_table.shape[1] * page_len * heads_kv), BF16),
        pltpu.VMEM((requests, heads, head_dim), F32),
        pltpu.SemaphoreType.DMA((18,)),
    ]

    def small(*arrays):
        return [pltpu.VMEM(array.shape, array.dtype) for array in arrays]

    inputs = [pltpu.SMEM(page_table.shape, jnp.int32), pltpu.SMEM(lengths.shape, jnp.int32)]
    inputs += small(queries, fresh_key_value)
    routed_shapes = [like((requests, width)), like((slab_rows, piece)), like((requests, slab_rows + STATS), F32)]
    final_shapes = [like((requests, width)), like((1, requests), F32), like((1, requests), F32)]
    attend_params = pltpu.CompilerParams(vmem_limit_bytes=24 * MIB)
    if kv_count == 1:
        mixed, slabs, comb = pl.pallas_call(
            functools.partial(attend_route_kernel, capacity),
            out_shape=routed_shapes,
            in_specs=in_hbm(10),
            out_specs=vmem(3),
            scratch_shapes=inputs + small(hidden, norm_gain, router_weight, expert_ids) + attend_scratch,
            compiler_params=attend_params,
        )(*pinned(page_table, lengths, queries, fresh_key_value, hidden, norm_gain, router_weight, expert_ids,
                  kv_pool, out_weight))
    else:
        projected = pl.pallas_call(
            attend_kernel,
            out_shape=like((requests, width), F32),
            in_specs=in_hbm(6),
            out_specs=pl.BlockSpec(memory_space=pltpu.VMEM),
            scratch_shapes=inputs + attend_scratch,
            compiler_params=attend_params,
        )(*pinned(page_table, lengths, queries, fresh_key_value, kv_pool, out_weight))
        projected = lax.psum(projected, "kv")
        mixed, slabs, comb = pl.pallas_call(
            functools.partial(route_kernel, capacity),
            out_shape=routed_shapes,
            in_specs=vmem(5),
            out_specs=vmem(3),
        )(projected, hidden, norm_gain, router_weight, expert_ids)

    new_pool = pl.pallas_call(
        refresh_kernel,
        out_shape=like(kv_pool.shape),
        in_specs=scalars(2) + vmem(1) + in_hbm(2),
        out_specs=pl.BlockSpec(memory_space=pltpu.HBM),
        scratch_shapes=[pltpu.VMEM(kv_pool.shape, BF16), pltpu.SemaphoreType.DMA((8,))],
        compiler_params=pltpu.CompilerParams(vmem_limit_bytes=12 * MIB),
        cost_estimate=pl.CostEstimate(flops=0, bytes_accessed=8 * kv_pool.size, transcendentals=0),
    )(page_table, lengths, fresh_key_value, comb, *pinned(kv_pool))

    def exchange(array):
        array = array.reshape(experts, SLAB, piece)
        array = lax.all_to_all(
            array, "req", split_axis=0, concat_axis=0, tiled=True, axis_index_groups=same_part
        )
        return array.reshape(slab_rows, piece)

    arrived = exchange(slabs)
    kept = experts * capacity
    units = expert_down.shape[1]
    leaving = pl.pallas_call(
        functools.partial(expert_kernel, capacity),
        out_shape=like((slab_rows, piece)),
        in_specs=in_hbm(3) + vmem(2),
        out_specs=pl.BlockSpec(memory_space=pltpu.VMEM),
        scratch_shapes=[
            pltpu.VMEM((slab_rows, piece), BF16),
            pltpu.VMEM((2, units, width), BF16),
            pltpu.VMEM((units, width), BF16),
            pltpu.VMEM((kept, width), BF16),
            pltpu.VMEM((kept, width), F32),
            pltpu.SemaphoreType.DMA((1 + 2 * len(unit_chunks(units)),)),
        ],
        compiler_params=pltpu.CompilerParams(vmem_limit_bytes=20 * MIB),
    )(arrived, *pinned(expert_gate_up, expert_down), other_up, other_down)
    returned = exchange(leaving)
    if kv_count == 1:
        out_hidden, norms, top = pl.pallas_call(
            functools.partial(combine_kernel, capacity),
            out_shape=final_shapes,
            in_specs=vmem(3),
            out_specs=vmem(3),
            compiler_params=pltpu.CompilerParams(vmem_limit_bytes=8 * MIB),
        )(comb, returned, mixed)
    else:
        routed, norms, top = pl.pallas_call(
            functools.partial(gather_kernel, capacity),
            out_shape=final_shapes,
            in_specs=vmem(2),
            out_specs=vmem(3),
        )(comb, returned)
        routed = lax.psum(routed, "kv").astype(F32)
        out_hidden = (mixed.astype(F32) + routed).astype(BF16)
    return out_hidden, new_pool, norms.reshape(requests), top.reshape(requests)


def solution(mesh):
    in_specs = (
        P("req", None),
        P("req", "kv"),
        P("req", "kv", None),
        P("req", None, "kv", None),
        P("req", None),
        P("req"),
        P("kv", None),
        P(),
        P(),
        P("req", None),
        P("req", None, "kv", None),
        P("req", "kv", None),
    )
    out_specs = (P("req", None), P("req", None, "kv", None), P("req"), P("req"))
    return jax.shard_map(body, mesh=mesh, in_specs=in_specs, out_specs=out_specs, check_vma=False)
```

```python
import functools
import math

import jax
import jax.numpy as jnp
from jax import lax
from jax.experimental import pallas as pl
from jax.experimental.pallas import tpu as pltpu
from jax.sharding import PartitionSpec as P

BF16 = jnp.bfloat16
F32 = jnp.float32
NT = (((1,), (1,)), ((), ()))
NN = (((1,), (0,)), ((), ()))
STATS = 128
SLAB = 16
MIB = 1 << 20


def dot(a, b, dims=NN, precision=None):
    return lax.dot_general(a, b, dims, precision=precision, preferred_element_type=F32)


def iota(shape, dim):
    return lax.broadcasted_iota(jnp.int32, shape, dim)


def copies(pairs, sems, first=0):
    return [pltpu.make_async_copy(src, dst, sems.at[first + i]) for i, (src, dst) in enumerate(pairs)]


def chip_at(position, chips, part):
    return (position + chips * (9 if part % 2 else 5) // 16) % chips


def pool_half(array, i):
    head_dim = array.shape[3] // 2
    return array.at[:, :, :, pl.ds(i * head_dim, head_dim)]


def attend(refs, keys, values, scratch):
    small, (kept_weight, qs, att, probs, sums, sems) = scratch
    table, lengths, q_ref, fresh = small[:4]
    requests, max_pages = table.shape
    pages, page_len, heads_kv, head_dim = keys.shape
    heads = q_ref.shape[1] // head_dim
    group = heads // heads_kv
    page_rows = page_len * heads_kv
    pool, weight = refs[-2:]
    loads = copies(list(zip(refs[:4], small[:4])), sems)
    page_step = -(-pages // 4)
    page_spans = [pl.ds(first, min(page_step, pages - first)) for first in range(0, pages, page_step)]
    key_loads, value_loads = [
        copies(
            [(pool_half(pool, i).at[span], kept.at[span]) for span in page_spans], sems, 4 + i * len(page_spans)
        )
        for i, kept in enumerate((keys, values))
    ]
    step = weight.shape[0] // 2
    spans = [pl.ds(i * step, step) for i in range(2)]
    weight_loads = copies([(weight.at[span], kept_weight.at[span]) for span in spans], sems, 12)
    later = copies(list(zip(refs[4:-2], small[4:])), sems, 14)
    for copy in loads + key_loads + value_loads + weight_loads + later:
        copy.start()
    for copy in loads:
        copy.wait()
    for h in range(heads):
        qs[pl.ds(h * requests, requests), :] = q_ref[:, pl.ds(h * head_dim, head_dim)].astype(F32)
    spots = [(table[r, lengths[r] // page_len], lengths[r] % page_len) for r in range(requests)]

    for copy in key_loads:
        copy.wait()
    for r, (page, slot) in enumerate(spots):
        keys[page, slot] = fresh[r][:, :head_dim]
    key_pages = keys.reshape(pages, page_rows, head_dim)
    value_pages = values.reshape(pages, page_rows, head_dim)
    columns = max_pages * page_rows
    lane = iota((heads, columns), 1)
    own_head = (lane & (heads_kv - 1)) == iota((heads, columns), 0) // group
    position = jnp.where(own_head, lane >> (heads_kv.bit_length() - 1), columns)
    scale = math.log2(math.e) / math.sqrt(head_dim)
    for r in range(requests):
        query = qs[pl.ds(r, heads, stride=requests), :].astype(BF16)
        gathered = jnp.concatenate([key_pages[table[r, j]] for j in range(max_pages)], axis=0)
        scores = jnp.where(position <= lengths[r], dot(query, gathered, NT), -1e30)
        exponent = jnp.exp2((scores - jnp.max(scores, axis=1, keepdims=True)) * scale)
        sums[r] = jnp.broadcast_to(jnp.sum(exponent, axis=1, keepdims=True), (heads, head_dim))
        probs[r] = exponent.astype(BF16)

    for copy in value_loads:
        copy.wait()
    for r, (page, slot) in enumerate(spots):
        values[page, slot] = fresh[r][:, head_dim:]
    for r in range(requests):
        gathered = jnp.concatenate([value_pages[table[r, j]] for j in range(max_pages)], axis=0)
        att[pl.ds(r, heads, stride=requests), :] = dot(probs[r], gathered) / sums[r]
    attended = jnp.concatenate(
        [att[pl.ds(h * requests, requests), :] for h in range(heads)], axis=1
    ).astype(BF16)
    projected = 0.0
    for i, copy in enumerate(weight_loads):
        copy.wait()
        projected = projected + dot(attended[:, i * step : (i + 1) * step], kept_weight[spans[i], :])
    for copy in later:
        copy.wait()
    return projected


def as_row(column):
    shape = (column.shape[0],) * 2
    return jnp.sum(jnp.where(iota(shape, 0) == iota(shape, 1), column, 0.0), axis=0, keepdims=True)


def route(projected, hidden, gain, router, ids, mixed_ref, slabs_ref, comb_ref, capacity):
    requests, width = hidden.shape
    experts = router.shape[0]
    parts = SLAB // capacity
    piece = width // parts
    slab_rows = experts * SLAB
    even = lax.axis_index("req") % 2 == 0

    def slab_expert(shape, dim):
        slab = iota(shape, dim) // SLAB
        return jnp.where(even, chip_at(slab, experts, 0), chip_at(slab, experts, 1))

    mixed = (hidden[...].astype(F32) + projected).astype(BF16)
    mixed_ref[...] = mixed
    mixed = mixed.astype(F32)
    norms = jnp.sqrt(jnp.mean(mixed * mixed, axis=1, keepdims=True) + 1e-06)
    normed = (mixed / norms * gain[...].astype(F32).reshape(1, width)).astype(BF16)
    logits = dot(normed, router[...], NT)
    top = jnp.max(logits, axis=1, keepdims=True)
    column = iota((requests, experts), 1)
    named = column < 0
    for k in range(ids.shape[1]):
        named = named | (ids[:, k : k + 1] == column)
    weights = jnp.where(named, jnp.exp(logits), 0.0)
    weights = weights / jnp.sum(weights, axis=1, keepdims=True)
    earlier = (iota((requests, requests), 1) < iota((requests, requests), 0)).astype(F32)
    rank = dot(earlier, named.astype(F32))
    place = jnp.where(named, rank, -1.0)
    normed = normed.astype(F32)
    stacked = jnp.concatenate([normed[:, p * piece : (p + 1) * piece] for p in range(parts)], axis=0)
    places = jnp.concatenate([place] * parts, axis=0)
    shape = (slab_rows, parts * requests)
    inner = iota(shape, 0) % SLAB
    spread = (slab_expert((slab_rows, experts), 0) == iota((slab_rows, experts), 1)).astype(F32)
    picks = (dot(spread, places, NT) == (inner // parts).astype(F32)) & (
        inner % parts == iota(shape, 1) // requests
    )
    slabs_ref[...] = dot(picks.astype(BF16), stacked.astype(BF16)).astype(BF16)
    shape = (experts, slab_rows)
    spread = (slab_expert(shape, 1) == iota(shape, 0)).astype(F32)
    inner = iota((requests, slab_rows), 1) % SLAB
    field = iota((requests, STATS), 1)
    comb_ref[:, slab_rows:] = jnp.where(field == 0, norms, jnp.where(field == 1, top, 0.0))
    comb_ref[:, :slab_rows] = jnp.where(
        dot(place, spread) == (inner // parts).astype(F32),
        dot(weights, spread, precision=lax.Precision.HIGHEST),
        0.0,
    )


def attend_route_kernel(capacity, *refs):
    inputs, (mixed, slabs, comb) = refs[:10], refs[10:13]
    small, scratch = refs[13:21], refs[21:]
    projected = attend(inputs, scratch[0], scratch[1], (small, scratch[2:]))
    hidden, gain, router, ids = small[4:]
    route(projected, hidden, gain, router, ids, mixed, slabs, comb, capacity)


def attend_kernel(*refs):
    attended, scratch = refs[6], refs[11:]
    attended[...] = attend(refs[:6], scratch[0], scratch[1], (refs[7:11], scratch[2:]))


def refresh_kernel(table, lengths, fresh, after, pool, new_pool, kept, sems):
    pages, page_len = kept.shape[:2]
    step = -(-pages // 4)
    spans = [pl.ds(start, min(step, pages - start)) for start in range(0, pages, step)]
    loads = copies([(pool.at[span], kept.at[span]) for span in spans], sems)
    stores = copies([(kept.at[span], new_pool.at[span]) for span in spans], sems, len(spans))
    for copy in loads:
        copy.start()
    spots = [(table[r, lengths[r] // page_len], lengths[r] % page_len) for r in range(table.shape[0])]
    for i, (load, store) in enumerate(zip(loads, stores)):
        load.wait()
        for r, (page, slot) in enumerate(spots):

            @pl.when((page >= i * step) & (page < (i + 1) * step))
            def _():
                kept[page, slot] = fresh[r]

        store.start()
    for copy in stores:
        copy.wait()


def route_kernel(capacity, projected, hidden, gain, router, ids, mixed, slabs, comb):
    route(projected[...], hidden, gain, router, ids, mixed, slabs, comb, capacity)


def unit_chunks(units):
    whole = units // 256 * 256
    return [(start, size) for start, size in ((0, whole), (whole, units - whole)) if size]


def expert_kernel(capacity, arrived, own_up, own_down, other_up, other_down, slabs,
                  slab_rows, kept_up, kept_down, rows, total, sems):
    units = kept_down.shape[0]
    arrive = pltpu.make_async_copy(arrived, slab_rows, sems.at[0])
    arrive.start()
    chunks = []
    for i, (start, size) in enumerate(unit_chunks(units)):
        span = pl.ds(start, size)
        chunks.append((span, copies(
            [(own_up.at[0, :, span, :], kept_up.at[:, span, :]), (own_down.at[0, span, :], kept_down.at[span, :])],
            sems,
            1 + 2 * i,
        )))
    for _, loads in chunks:
        loads[0].start()
    arrive.wait()
    parts = SLAB // capacity
    piece = slabs.shape[1]
    block = 128
    each = block // parts
    blocks = slabs.shape[0] // block
    shape = (block, block)
    slab_row, sorted_row = iota(shape, 1), iota(shape, 0)
    sort = (slab_row == sorted_row % each * parts + sorted_row // each).astype(BF16)
    for i in range(blocks):
        sorted_rows = dot(sort, slab_rows[pl.ds(i * block, block), :]).astype(BF16)
        rows[pl.ds(i * each, each), :] = jnp.concatenate(
            [sorted_rows[p * each : (p + 1) * each] for p in range(parts)], axis=1
        )
    states = rows[...]
    steps = [(other_up.at[0], other_down.at[0], span, []) for span, _ in chunks]
    steps += [(kept_up, kept_down, span, loads) for span, loads in chunks]

    def add_down(i, activated):
        _, down, span, loads = steps[i]
        if loads:
            loads[1].wait()
        term = dot(activated, down[span, :])
        total[...] = term if i == 0 else total[...] + term

    activated = None
    for i, (gate_up, _, span, loads) in enumerate(steps):
        if loads:
            loads[0].wait()
        gate = dot(states, gate_up[0, span, :], NT)
        up = dot(states, gate_up[1, span, :], NT)
        if i == 0:
            for _, loads in chunks:
                loads[1].start()
        else:
            add_down(i - 1, activated)
        activated = (gate / (1.0 + jnp.exp(-gate)) * up).astype(BF16)
    add_down(len(steps) - 1, activated)
    slab_row, sorted_row = iota(shape, 0), iota(shape, 1)
    unsort = (slab_row == sorted_row % each * parts + sorted_row // each).astype(BF16)
    for i in range(blocks):
        summed = total[pl.ds(i * each, each), :].astype(BF16)
        stacked = jnp.concatenate([summed[:, p * piece : (p + 1) * piece] for p in range(parts)], axis=0)
        slabs[pl.ds(i * block, block), :] = dot(unsort, stacked).astype(BF16)


def gather_terms(comb, slabs, norms, top, capacity):
    parts = SLAB // capacity
    requests = comb.shape[0]
    used = slabs.shape[0]
    norms[...] = as_row(comb[:, used : used + 1])
    top[...] = as_row(comb[:, used + 1 : used + 2])
    weights = comb[:, :used]
    pieces = []
    for _ in range(3):
        piece = weights.astype(BF16).astype(F32)
        weights = weights - piece
        pieces.append(piece)
    part = iota(weights.shape, 1) % parts
    stacked = jnp.concatenate(
        [jnp.where(part == p, piece, 0.0) for p in range(parts) for piece in pieces], axis=0
    ).astype(BF16)
    terms = dot(stacked, slabs[...])
    return jnp.concatenate(
        [
            sum(terms[(3 * p + i) * requests : (3 * p + i + 1) * requests] for i in range(3))
            for p in range(parts)
        ],
        axis=1,
    )


def combine_kernel(capacity, comb, slabs, mixed, out, norms, top):
    out[...] = (mixed[...].astype(F32) + gather_terms(comb, slabs, norms, top, capacity)).astype(BF16)


def gather_kernel(capacity, comb, slabs, out, norms, top):
    out[...] = gather_terms(comb, slabs, norms, top, capacity).astype(BF16)


def vmem(count):
    return [pl.BlockSpec(memory_space=pltpu.VMEM)] * count


def scalars(count):
    return [pl.BlockSpec(memory_space=pltpu.SMEM)] * count


def in_hbm(count):
    return [pl.BlockSpec(memory_space=pltpu.HBM)] * count


def pinned(*arrays):
    return [pltpu.with_memory_space_constraint(array, pltpu.HBM) for array in arrays]


def like(shape, dtype=BF16):
    return jax.ShapeDtypeStruct(shape, dtype)


def body(
    hidden,
    queries,
    fresh_key_value,
    kv_pool,
    page_table,
    lengths,
    out_weight,
    norm_gain,
    router_weight,
    expert_ids,
    expert_gate_up,
    expert_down,
):
    requests, width = hidden.shape
    req_count, kv_count = lax.axis_size("req"), lax.axis_size("kv")
    pages, page_len, heads_kv, pair_dim = kv_pool.shape
    head_dim = pair_dim // 2
    heads = queries.shape[1] // head_dim
    experts = router_weight.shape[0]
    copies = req_count // experts
    chosen = expert_ids.shape[1]
    capacity = 2 * max(1, (requests * chosen + 2 * experts - 1) // (2 * experts))
    parts = SLAB // capacity
    piece = width // parts
    slab_rows = experts * SLAB

    same_part = [
        [chip_at(place, experts, part) * copies + part for place in range(experts)] for part in range(copies)
    ]
    swap = [(index, index ^ 1) for index in range(req_count)]
    other_up = lax.ppermute(expert_gate_up, "req", swap)
    other_down = lax.ppermute(expert_down, "req", swap)

    attend_scratch = [
        pltpu.VMEM((pages, page_len, heads_kv, head_dim), BF16),
        pltpu.VMEM((pages, page_len, heads_kv, head_dim), BF16),
        pltpu.VMEM(out_weight.shape, BF16),
        pltpu.VMEM((heads * requests, head_dim), F32),
        pltpu.VMEM((heads * requests, head_dim), F32),
        pltpu.VMEM((requests, heads, page_table.shape[1] * page_len * heads_kv), BF16),
        pltpu.VMEM((requests, heads, head_dim), F32),
        pltpu.SemaphoreType.DMA((18,)),
    ]

    def small(*arrays):
        return [pltpu.VMEM(array.shape, array.dtype) for array in arrays]

    inputs = [pltpu.SMEM(page_table.shape, jnp.int32), pltpu.SMEM(lengths.shape, jnp.int32)]
    inputs += small(queries, fresh_key_value)
    routed_shapes = [like((requests, width)), like((slab_rows, piece)), like((requests, slab_rows + STATS), F32)]
    final_shapes = [like((requests, width)), like((1, requests), F32), like((1, requests), F32)]
    attend_params = pltpu.CompilerParams(vmem_limit_bytes=24 * MIB)
    if kv_count == 1:
        mixed, slabs, comb = pl.pallas_call(
            functools.partial(attend_route_kernel, capacity),
            out_shape=routed_shapes,
            in_specs=in_hbm(10),
            out_specs=vmem(3),
            scratch_shapes=inputs + small(hidden, norm_gain, router_weight, expert_ids) + attend_scratch,
            compiler_params=attend_params,
        )(*pinned(page_table, lengths, queries, fresh_key_value, hidden, norm_gain, router_weight, expert_ids,
                  kv_pool, out_weight))
    else:
        projected = pl.pallas_call(
            attend_kernel,
            out_shape=like((requests, width), F32),
            in_specs=in_hbm(6),
            out_specs=pl.BlockSpec(memory_space=pltpu.VMEM),
            scratch_shapes=inputs + attend_scratch,
            compiler_params=attend_params,
        )(*pinned(page_table, lengths, queries, fresh_key_value, kv_pool, out_weight))
        projected = lax.psum(projected, "kv")
        mixed, slabs, comb = pl.pallas_call(
            functools.partial(route_kernel, capacity),
            out_shape=routed_shapes,
            in_specs=vmem(5),
            out_specs=vmem(3),
        )(projected, hidden, norm_gain, router_weight, expert_ids)

    new_pool = pl.pallas_call(
        refresh_kernel,
        out_shape=like(kv_pool.shape),
        in_specs=scalars(2) + vmem(1) + in_hbm(2),
        out_specs=pl.BlockSpec(memory_space=pltpu.HBM),
        scratch_shapes=[pltpu.VMEM(kv_pool.shape, BF16), pltpu.SemaphoreType.DMA((8,))],
        compiler_params=pltpu.CompilerParams(vmem_limit_bytes=12 * MIB),
        cost_estimate=pl.CostEstimate(flops=0, bytes_accessed=8 * kv_pool.size, transcendentals=0),
    )(page_table, lengths, fresh_key_value, comb, *pinned(kv_pool))

    def exchange(array):
        array = array.reshape(experts, SLAB, piece)
        array = lax.all_to_all(
            array, "req", split_axis=0, concat_axis=0, tiled=True, axis_index_groups=same_part
        )
        return array.reshape(slab_rows, piece)

    arrived = exchange(slabs)
    kept = experts * capacity
    units = expert_down.shape[1]
    leaving = pl.pallas_call(
        functools.partial(expert_kernel, capacity),
        out_shape=like((slab_rows, piece)),
        in_specs=in_hbm(3) + vmem(2),
        out_specs=pl.BlockSpec(memory_space=pltpu.VMEM),
        scratch_shapes=[
            pltpu.VMEM((slab_rows, piece), BF16),
            pltpu.VMEM((2, units, width), BF16),
            pltpu.VMEM((units, width), BF16),
            pltpu.VMEM((kept, width), BF16),
            pltpu.VMEM((kept, width), F32),
            pltpu.SemaphoreType.DMA((1 + 2 * len(unit_chunks(units)),)),
        ],
        compiler_params=pltpu.CompilerParams(vmem_limit_bytes=20 * MIB),
    )(arrived, *pinned(expert_gate_up, expert_down), other_up, other_down)
    returned = exchange(leaving)
    if kv_count == 1:
        out_hidden, norms, top = pl.pallas_call(
            functools.partial(combine_kernel, capacity),
            out_shape=final_shapes,
            in_specs=vmem(3),
            out_specs=vmem(3),
            compiler_params=pltpu.CompilerParams(vmem_limit_bytes=8 * MIB),
        )(comb, returned, mixed)
    else:
        routed, norms, top = pl.pallas_call(
            functools.partial(gather_kernel, capacity),
            out_shape=final_shapes,
            in_specs=vmem(2),
            out_specs=vmem(3),
        )(comb, returned)
        routed = lax.psum(routed, "kv").astype(F32)
        out_hidden = (mixed.astype(F32) + routed).astype(BF16)
    return out_hidden, new_pool, norms.reshape(requests), top.reshape(requests)


def solution(mesh):
    in_specs = (
        P("req", None),
        P("req", "kv"),
        P("req", "kv", None),
        P("req", None, "kv", None),
        P("req", None),
        P("req"),
        P("kv", None),
        P(),
        P(),
        P("req", None),
        P("req", None, "kv", None),
        P("req", "kv", None),
    )
    out_specs = (P("req", None), P("req", None, "kv", None), P("req"), P("req"))
    return jax.shard_map(body, mesh=mesh, in_specs=in_specs, out_specs=out_specs, check_vma=False)
```
